32 devices in a mesh: seq: 8 (over z, x), head: 4 (over y, core).
Axes of the slice: x: 2, y: 2, z: 4, core: 2. Of those that a mesh axis runs over, the one named last changes fastest.
Arguments:
- tokens_in: bfloat16 [4, 2048, 768], P(None, 'seq', 'head'), may hold values from -6 to 6
- out_grad: bfloat16 [4, 2048, 768], P(None, 'seq', 'head'), may hold values from -6 to 6
- lengths: int32 [4, 4], replicated, may hold values from 1 to 1920, as said below
- norm_gain: bfloat16 [768], P('head'), may hold values from 0.5 to 1.5
- proj_z: bfloat16 [768, 1536], P(None, 'head'), may hold values from -0.21875 to 0.21875
- proj_x: bfloat16 [768, 1536], P(None, 'head'), may hold values from -0.21875 to 0.21875
- proj_bc: bfloat16 [768, 256], P(None, 'head'), may hold values from -0.21875 to 0.21875
- proj_dt: bfloat16 [768, 24], P(None, 'head'), may hold values from -0.21875 to 0.21875
- conv_x: bfloat16 [4, 1536], P(None, 'head'), may hold values from -3 to 3
- conv_bc: bfloat16 [4, 256], P(None, 'head'), may hold values from -3 to 3
- bias_x: bfloat16 [1536], P('head'), may hold values from -3 to 3
- bias_bc: bfloat16 [256], P('head'), may hold values from -3 to 3
- dt_bias: bfloat16 [24], P('head'), may hold values from -5 to -3
- a_log: bfloat16 [24], P('head'), may hold values from -12 to 1
- d_skip: bfloat16 [24], P('head'), may hold values from 0.5 to 1.5
- gate_gain: bfloat16 [1536], P('head'), may hold values from 0.5 to 1.5
- proj_out: bfloat16 [1536, 768], P('head'), may hold values from -0.15625 to 0.15625
Outputs:
- block_out: bfloat16 [4, 2048, 768], P(None, 'seq', 'head')
- in_grad: float32 [4, 2048, 768], P(None, 'seq', 'head')
- grad_norm_gain: float32 [768], P('head')
- grad_proj_z: float32 [768, 1536], P(None, 'head')
- grad_proj_x: float32 [768, 1536], P(None, 'head')
- grad_proj_bc: float32 [768, 256], P(None, 'head')
- grad_proj_dt: float32 [768, 24], P(None, 'head')
- grad_conv_x: float32 [4, 1536], P(None, 'head')
- grad_conv_bc: float32 [4, 256], P(None, 'head')
- grad_bias_x: float32 [1536], P('head')
- grad_bias_bc: float32 [256], P('head')
- grad_dt_bias: float32 [24], P('head')
- grad_a_log: float32 [24], P('head')
- grad_d_skip: float32 [24], P('head')
- grad_gate_gain: float32 [1536], P('head')
- grad_proj_out: float32 [1536, 768], P('head')
The draws below stay inside these ranges and needn't reach their ends.
Inputs may be any that keep to these rules, and one draw needn't show every extreme that they name: Each row holds 4 lengths that sum to 2048; exactly one of them is 2048 minus half of 256, the others share the rest.
All inputs are finite; a program needn't handle non-finite values.
Results may differ from the reference program's by a relative error of at most 0.012.
The reference program's roundings to bfloat16 on the way (of `normed` and `gated`) count: a program that leaves them out, or rounds other values in their place, can miss the bound.
Values may be sent and summed in bfloat16 or wider, within the bound.
No kernel may reach another device: no remote copies, remote signals or barrier semaphores. Data moves between devices by JAX's collectives and lax.ppermute only.
A program may use at most 192 MiB of HBM per device.

```python
import math
import jax
import jax.numpy as jnp
from jax import lax

D = 768
H = 24
P_SIZE = 64
NS = 128
KW = 4
TOK_DEV = 256
PACKS = 4
NSEQ = 4
DI = 1536
TOKENS = 2048


def draw_lengths(key, part):
    key = jax.random.fold_in(key, 11)
    short_total = TOK_DEV // 2

    def one_row(row_key):
        key_long, key_cut = jax.random.split(row_key)
        cuts = jnp.sort(jax.random.permutation(key_cut, short_total - 1)[:NSEQ - 2] + 1).astype(jnp.int32)
        bounds = jnp.concatenate([jnp.zeros((1,), jnp.int32), cuts, jnp.full((1,), short_total, jnp.int32)])
        shorts = bounds[1:] - bounds[:-1]
        place = jax.random.randint(key_long, (), 0, NSEQ)
        slots = jnp.arange(NSEQ, dtype=jnp.int32)
        short_index = jnp.clip(slots - (slots > place).astype(jnp.int32), 0, NSEQ - 2)
        return jnp.where(slots == place, TOKENS - short_total, shorts[short_index]).astype(jnp.int32)
    return jax.vmap(one_row)(jax.random.split(key, PACKS))


def draw_a_log(key, part):
    key = jax.random.fold_in(key, 23)
    unit = jax.random.uniform(key, (H,), jnp.float32)
    low_end = math.log(50.0 / TOKENS)
    high_end = math.log(1.5)
    return (low_end + unit * (high_end - low_end)).astype(jnp.bfloat16)


def shard_levels(own_key, extent, cuts, smallest, high):
    gain, own = 1.0, jax.random.fold_in(own_key, 6)
    for position, shards_of in cuts:
        heights = jnp.exp(jax.random.uniform(jax.random.fold_in(own, position), (shards_of,), jnp.float32, smallest / len(cuts), high / len(cuts)))
        gain = gain * jnp.repeat(heights, extent[position] // shards_of).reshape([-1 if axis == position else 1 for axis in range(len(extent))])
    return gain


def noise(own_key, shape, spread, reach, pieces=(), kind=jnp.bfloat16):
    values = spread * jax.random.normal(own_key, shape, jnp.float32)
    if pieces:
        values = values * shard_levels(own_key, shape, pieces, -0.22, 0.18)
    return jnp.clip(values, -reach, reach).astype(kind)


def setup_inputs(seed: int = 0) -> dict:
    key_of = jax.random.split(jax.random.key(seed), 18)
    return {
        "tokens_in": noise(key_of[0], (PACKS, TOKENS, D), 1.0, 6.0, ((1, 8), (2, 4))),
        "out_grad": noise(key_of[1], (PACKS, TOKENS, D), 1.0, 6.0, ((1, 8), (2, 4))),
        "lengths": draw_lengths(jax.random.fold_in(key_of[17], 71), 0),
        "norm_gain": jnp.clip(1.0 + 0.1 * jax.random.normal(key_of[3], (D,), jnp.float32), 0.5, 1.5).astype(jnp.bfloat16),
        "proj_z": noise(key_of[4], (D, DI), D ** -0.5, 0.21875, ((1, 4),)),
        "proj_x": noise(key_of[5], (D, DI), D ** -0.5, 0.21875, ((1, 4),)),
        "proj_bc": noise(key_of[6], (D, 2 * NS), D ** -0.5, 0.21875, ((1, 4),)),
        "proj_dt": noise(key_of[7], (D, H), D ** -0.5, 0.21875, ((1, 4),)),
        "conv_x": noise(key_of[8], (KW, DI), KW ** -0.5, 3.0, ((1, 4),)),
        "conv_bc": noise(key_of[9], (KW, 2 * NS), KW ** -0.5, 3.0, ((1, 4),)),
        "bias_x": noise(key_of[10], (DI,), 0.5, 3.0, ((0, 4),)),
        "bias_bc": noise(key_of[11], (2 * NS,), 0.5, 3.0, ((0, 4),)),
        "dt_bias": jnp.clip(-5.0 + 2.0 * jax.random.uniform(key_of[12], (H,), jnp.float32) ** shard_levels(key_of[12], (H,), ((0, 4),), -0.2, 0.2), -5.0, -3.0).astype(jnp.bfloat16),
        "a_log": draw_a_log(jax.random.fold_in(key_of[17], 71), 0),
        "d_skip": jnp.clip(0.5 + 1.0 * jax.random.uniform(key_of[14], (H,), jnp.float32) ** shard_levels(key_of[14], (H,), ((0, 4),), -0.2, 0.2), 0.5, 1.5).astype(jnp.bfloat16),
        "gate_gain": jnp.clip(1.0 + 0.1 * jax.random.normal(key_of[15], (DI,), jnp.float32), 0.5, 1.5).astype(jnp.bfloat16),
        "proj_out": noise(key_of[16], (DI, D), DI ** -0.5, 0.15625, ((0, 4),)),
    }


EPSILON = 1e-05
PRECISE = lax.Precision.HIGHEST

@jax.custom_vjp
def low(v):
    return lax.optimization_barrier(v.astype(jnp.bfloat16)).astype(jnp.float32)

@jax.custom_vjp
def low_back(v):
    return v

def low_keep(v):
    return (low(v), None)

def low_pass(kept, grad):
    return (grad,)

def back_keep(v):
    return (v, None)

def back_low(kept, grad):
    return (low(grad),)
low.defvjp(low_keep, low_pass)
low_back.defvjp(back_keep, back_low)

def matmul(left, right):
    return jnp.dot(left, right, precision=PRECISE, preferred_element_type=jnp.float32)

def causal_conv(raw_vals, kernel, offset, segment):
    width = kernel.shape[0]
    total = raw_vals.shape[0]
    padded = jnp.concatenate([jnp.zeros((width - 1, raw_vals.shape[1]), jnp.float32), raw_vals], axis=0)
    seg_pad = jnp.concatenate([jnp.full((width - 1,), -1, jnp.int32), segment], axis=0)
    summed = jnp.broadcast_to(offset[None, :], raw_vals.shape)
    for lag_index in range(width):
        keep_rows = (seg_pad[lag_index:lag_index + total] == segment).astype(jnp.float32)
        summed = summed + kernel[lag_index][None, :] * padded[lag_index:lag_index + total] * keep_rows[:, None]
    return jax.nn.silu(summed)

def scan_block_step(state_in, block):
    x_block, b_block, c_block, dt_block, rate_block, seg_block, cont_block = block
    count = x_block.shape[0]
    cum_decay = jnp.cumsum(rate_block, axis=0)
    row_ids = jnp.arange(count, dtype=jnp.int32)
    below_diag = row_ids[:, None] >= row_ids[None, :]
    same_seq = ((seg_block[:, None] == seg_block[None, :]) & below_diag)[:, :, None]
    decay_mat = jnp.where(same_seq, jnp.exp(jnp.where(same_seq, cum_decay[:, None, :] - cum_decay[None, :, :], 0.0)), 0.0)
    scores = matmul(c_block, b_block.T)
    scaled = x_block * dt_block[:, :, None]
    inner = jnp.einsum('tsh,shp->thp', scores[:, :, None] * decay_mat, scaled, precision=PRECISE)
    carried = jnp.einsum('hpn,tn->thp', state_in, c_block, precision=PRECISE)
    output = inner + (cont_block[:, None] * jnp.exp(cum_decay))[:, :, None] * carried
    keep_end = (seg_block == seg_block[-1])[:, None]
    end_weight = jnp.where(keep_end, jnp.exp(jnp.where(keep_end, cum_decay[-1][None, :] - cum_decay, 0.0)), 0.0)
    local_state = jnp.einsum('sh,shp,sn->hpn', end_weight, scaled, b_block, precision=PRECISE)
    carry_decay = cont_block[-1] * jnp.exp(cum_decay[-1])
    return (carry_decay[:, None, None] * state_in + local_state, output)

def block_forward(params, tokens, segment, carry_flag):
    norm_gain, proj_z, proj_x, proj_bc, proj_dt, conv_x, conv_bc, bias_x, bias_bc, dt_bias, a_log, d_skip, gate_gain, proj_out = params
    total = tokens.shape[0]
    normed = low(tokens * lax.rsqrt(lax.optimization_barrier(jnp.mean(tokens * tokens, axis=-1, keepdims=True)) + EPSILON) * norm_gain)
    gate_raw = low_back(low(matmul(normed, proj_z)))
    x_raw = low_back(low(matmul(normed, proj_x)))
    bc_raw = low_back(low(matmul(normed, proj_bc)))
    dt_raw = low_back(low(matmul(normed, proj_dt)))
    x_conv = low(causal_conv(x_raw, conv_x, bias_x, segment))
    bc_conv = low(causal_conv(bc_raw, conv_bc, bias_bc, segment))
    b_vals = bc_conv[:, :NS]
    c_vals = bc_conv[:, NS:]
    dt_vals = jax.nn.softplus(dt_raw + dt_bias)
    rate_vals = dt_vals * -jnp.exp(a_log)
    x_heads = x_conv.reshape(total, H, P_SIZE)
    block_count = total // TOK_DEV

    def split_blocks(array_in):
        return array_in.reshape((block_count, TOK_DEV) + array_in.shape[1:])
    blocks = tuple((split_blocks(member) for member in (x_heads, b_vals, c_vals, dt_vals, rate_vals, segment, carry_flag)))
    final_state, outputs = lax.scan(jax.checkpoint(scan_block_step), jnp.zeros((H, P_SIZE, NS), jnp.float32), blocks)
    ssd_out = outputs.reshape(total, H, P_SIZE) + x_heads * d_skip[None, :, None]
    mixed = ssd_out.reshape(total, DI) * jax.nn.silu(gate_raw)
    inv_gate = lax.rsqrt(lax.optimization_barrier(jnp.mean(mixed * mixed, axis=-1, keepdims=True)) + EPSILON)
    gated = low(mixed * inv_gate * gate_gain)
    return tokens + matmul(gated, proj_out)

def segment_ids(lens_row):
    seq_ends = jnp.cumsum(lens_row).astype(jnp.int32)
    positions = jnp.arange(TOKENS, dtype=jnp.int32)
    segment = lax.optimization_barrier(jnp.sum((positions[:, None] >= seq_ends[None, :]).astype(jnp.int32), axis=1)).astype(jnp.int32)
    prev_index = (positions // TOK_DEV * TOK_DEV - 1).astype(jnp.int32)
    prev_seg = jnp.where(prev_index >= 0, segment[jnp.maximum(prev_index, 0)], -1)
    carry_flag = (segment == prev_seg).astype(jnp.float32)
    return (segment, carry_flag)

def reference(tokens_in, out_grad, lengths, norm_gain, proj_z, proj_x, proj_bc, proj_dt, conv_x, conv_bc, bias_x, bias_bc, dt_bias, a_log, d_skip, gate_gain, proj_out):
    params = tuple((weight.astype(jnp.float32) for weight in (norm_gain, proj_z, proj_x, proj_bc, proj_dt, conv_x, conv_bc, bias_x, bias_bc, dt_bias, a_log, d_skip, gate_gain, proj_out)))

    def per_pack(totals, member):
        tokens, cotangent, lens_row = member
        segment, carry_flag = segment_ids(lens_row)

        def run_block(param_set, values):
            return block_forward(param_set, values, segment, carry_flag)
        result, pullback = jax.vjp(run_block, params, tokens.astype(jnp.float32))
        param_grads, token_grad = pullback(cotangent.astype(jnp.float32))
        totals = jax.tree.map(lambda left, right: left + right, totals, param_grads)
        return (totals, (result.astype(jnp.bfloat16), token_grad))
    zero_grads = jax.tree.map(jnp.zeros_like, params)
    totals, (block_out, in_grad) = lax.scan(per_pack, zero_grads, (tokens_in, out_grad, lengths))
    return (block_out, in_grad, totals[0], totals[1], totals[2], totals[3], totals[4], totals[5], totals[6], totals[7], totals[8], totals[9], totals[10], totals[11], totals[12], totals[13])
```

```python
import functools

import jax
import jax.numpy as jnp
from jax import lax
from jax.experimental import pallas as pl
from jax.experimental.pallas import tpu as pltpu
from jax.sharding import PartitionSpec as P

EPSILON = 1e-05
bf16 = jnp.bfloat16
f32 = jnp.float32
LANES = 128
EDGE = 16
VMEM_LIMIT = 60 * 1024 * 1024
STEPS = 32000.0
UNIT = 16384.0
LN2 = 0.6931471805599453


def swap(x, axis, bit):
    return lax.ppermute(x, axis, [(i, i ^ bit) for i in range(lax.axis_size(axis))])


def shift(x, axis, distance):
    n = lax.axis_size(axis)
    return lax.ppermute(x, axis, [(i, i + distance) for i in range(n) if 0 <= i + distance < n])


def head_pieces(x):
    far = swap(x, "head", 2)
    near = swap(x, "head", 1)
    return x, near, far, swap(far, "head", 1)


def nn(a, b):
    return lax.dot_general(a, b, (((1,), (0,)), ((), ())), preferred_element_type=f32)


def nt(a, b):
    return lax.dot_general(a, b, (((1,), (1,)), ((), ())), preferred_element_type=f32)


def tn(a, b):
    return lax.dot_general(a, b, (((0,), (0,)), ((), ())), preferred_element_type=f32)


def split2(v):
    hi = v.astype(bf16)
    return hi, (v - hi.astype(f32)).astype(bf16)


def split3(v):
    hi = v.astype(bf16)
    rest = v - hi.astype(f32)
    mid = rest.astype(bf16)
    return hi, mid, (rest - mid.astype(f32)).astype(bf16)


def spread_matrix(heads, size):
    row = lax.broadcasted_iota(jnp.int32, (LANES, heads * size), 0)
    col = lax.broadcasted_iota(jnp.int32, (LANES, heads * size), 1)
    inside = (col >= row * size) & (col < (row + 1) * size)
    return jnp.where(inside, 1.0, 0.0).astype(bf16)


def spread(v, matrix):
    hi, lo = split2(v)
    return nn(hi, matrix) + nn(lo, matrix)


def collapse(v, matrix):
    hi, lo = split2(v)
    return nt(hi, matrix) + nt(lo, matrix)


def triangle(count, lower):
    row = lax.broadcasted_iota(jnp.int32, (count, count), 0)
    col = lax.broadcasted_iota(jnp.int32, (count, count), 1)
    keep = (row >= col) if lower else (row <= col)
    return jnp.where(keep, 1.0, 0.0).astype(bf16)


def exact_sums(matrix, v):
    hi, mid, lo = split3(v)
    return nn(matrix, hi) + nn(matrix, mid) + nn(matrix, lo)


def segments(positions, lens_ref, pack, count):
    total = jnp.zeros(positions.shape, jnp.int32)
    end = jnp.int32(0)
    for k in range(count):
        end = end + lens_ref[pack, k]
        total = total + jnp.where(positions >= end, 1, 0)
    return total


def column_segments(meta_ref, lens_ref, pack, count, nseq, before):
    rows = lax.broadcasted_iota(jnp.int32, (count + before, 1), 0)
    return segments(rows + (meta_ref[0] * count - before), lens_ref, pack, nseq)


def row_segments(meta_ref, lens_ref, pack, count, nseq):
    cols = lax.broadcasted_iota(jnp.int32, (1, count), 1)
    return segments(cols + meta_ref[0] * count, lens_ref, pack, nseq)


def carry_column(meta_ref, seg_ext, before):
    same = seg_ext[before:] == seg_ext[before - 1 : before]
    return jnp.where(same & (meta_ref[0] > 0), 1.0, 0.0)


def to_int16(v):
    return jnp.floor(v + 0.5).astype(jnp.int32).astype(jnp.int16)


def encode_state(out, p, state, decay, heads, size):
    lane = lax.broadcasted_iota(jnp.int32, (1, LANES), 1)
    powers = jnp.zeros((1, LANES), f32)
    for h in range(heads):
        part = state[h * size : (h + 1) * size]
        top = jnp.max(jnp.max(jnp.abs(part), axis=0, keepdims=True), axis=1, keepdims=True)
        power = jnp.ceil(jnp.log(jnp.maximum(top, 1e-30)) / LN2)
        powers = powers + jnp.where(lane == h, power, 0.0)
        codes = jnp.clip(part * (jnp.exp(-power * LN2) * STEPS), -32767.0, 32767.0)
        out[p, h * size : (h + 1) * size, :] = to_int16(codes)
    row = lax.broadcasted_iota(jnp.int32, (EDGE, LANES), 0)
    coarse = jnp.floor(decay * UNIT)
    fine = (decay * UNIT - coarse) * UNIT
    tail = jnp.where(row == 0, powers, jnp.where(row == 1, coarse, jnp.where(row == 2, fine, 0.0)))
    out[p, heads * size :, :] = to_int16(tail)


def decode_state(block, heads, size):
    values = block.astype(jnp.int32).astype(f32)
    tail = values[heads * size :]
    scale = jnp.exp(tail[0:1] * LN2) / STEPS
    decay = (tail[1:2] + tail[2:3] / UNIT) / UNIT
    return scaled_state(values[: heads * size], scale, heads, size), decay


def sigmoid(v):
    return 1.0 / (1.0 + jnp.exp(-v))


def scaled_state(state, decay, heads, size):
    return jnp.concatenate(
        [state[h * size : (h + 1) * size] * decay[:, h : h + 1] for h in range(heads)], axis=0
    )


def front_kernel(dims, meta, lens, *refs):
    packs, count, features, inner, bc, heads, size, width, nseq = dims
    tokens, edges, shared = refs[0:4], refs[4:8], refs[8:12]
    wz, wx, wdt, conv_x, small = refs[12:17]
    (
        normed_o, inv_o, edge_o, edge_inv_o, gate_o, rawx_o, rawbc_o, xbc_o, dsx_o, dsbc_o, dt_o,
        sig_o, cum_o, keep_o, send_o,
    ) = refs[17:32]
    stage, edge_stage, weights, raws, edge_raws, conv, gain = refs[32:]
    pack = pl.program_id(0)
    head = meta[1]
    part = features // 4
    wide = edge_stage.shape[2]

    def normalise(values):
        mean = jnp.sum(values * values, axis=0, keepdims=True) / features
        inv = lax.rsqrt(mean + EPSILON)
        return inv, ((values * inv) * gain[...]).astype(bf16)

    def raw_of(normed):
        wbc = weights[...].reshape(bc, weights.shape[2])[:, :features]
        return jnp.concatenate([nn(normed, wx[...]), nt(normed, wbc)], axis=1).astype(bf16)

    @pl.when(pack == 0)
    def _():
        for k in range(4):
            weights[head ^ k] = shared[k][...]
            edge_stage[head ^ k] = edges[k][...]
        extra = weights[...].reshape(bc, weights.shape[2])[:, features:].astype(f32)
        conv[:, :inner] = conv_x[...]
        conv[:, inner:] = jnp.transpose(extra)[0:8]
        bc_part = bc // 4
        pieces = part // bc_part
        for h in range(4):
            for c in range(pieces):
                gain[h * part + c * bc_part : h * part + (c + 1) * bc_part, :] = extra[
                    h * bc_part : (h + 1) * bc_part, width + 1 + c : width + 2 + c
                ]
        inv, normed = normalise(edge_stage[...].reshape(features, wide).astype(f32))
        edge_inv_o[...] = inv
        edge_o[...] = normed
        edge_raws[...] = raw_of(jnp.transpose(normed)).astype(f32)

    for k in range(4):
        stage[head ^ k] = tokens[k][0]
    inv, normed_t = normalise(stage[...].reshape(features, count).astype(f32))
    inv_o[0] = inv
    normed_o[0] = normed_t
    normed = jnp.transpose(normed_t)
    gate_o[0] = nn(normed, wz[...]).astype(bf16)
    raws[EDGE:, :] = raw_of(normed).astype(f32)
    raws[0:EDGE, :] = edge_raws[pl.ds(pl.multiple_of(pack * EDGE, EDGE), EDGE), :]

    def own_bc(values):
        bc_part = bc // 4
        parts = [values[:, inner + h * bc_part : inner + (h + 1) * bc_part] for h in range(4)]
        low = jnp.where((head & 1) == 0, parts[0], parts[1])
        high = jnp.where((head & 1) == 0, parts[2], parts[3])
        return jnp.where((head >> 1) == 0, low, high)

    rawx_o[0] = raws[:, :inner].astype(bf16)
    rawbc_o[0] = own_bc(raws[...]).astype(bf16)
    seg = column_segments(meta, lens, pack, count, nseq, EDGE)
    seg_main = seg[EDGE:]
    pre = jnp.broadcast_to(conv[width : width + 1, :], (count, inner + bc))
    for k in range(width):
        low = EDGE - (width - 1) + k
        mask = jnp.where(seg[low : low + count] == seg_main, 1.0, 0.0)
        pre = pre + conv[k : k + 1, :] * raws[low : low + count, :] * mask
    sig_pre = sigmoid(pre)
    xbc = (pre * sig_pre).astype(bf16)
    xbc_o[0] = xbc
    slope = sig_pre * (1.0 + pre * (1.0 - sig_pre))
    dsx_o[0] = slope[:, :inner]
    dsbc_o[0] = own_bc(slope)
    lane = lax.broadcasted_iota(jnp.int32, (1, LANES), 1)
    live = lane < heads
    v = nt(normed, wdt[...]).astype(bf16).astype(f32) + small[0:1, :]
    soft = jnp.maximum(v, 0.0) + jnp.log1p(jnp.exp(-jnp.abs(v)))
    dt = jnp.where(live, soft, 0.0)
    dt_o[0] = dt
    sig_o[0] = jnp.where(live, sigmoid(v), 0.0)
    rate = -dt * jnp.exp(small[1:2, :])
    cum = exact_sums(triangle(count, True), rate)
    cum_o[0] = cum
    cum_end = cum[count - 1 : count]
    weight = jnp.where(seg_main == seg[count + EDGE - 1 :], jnp.exp(cum_end - cum), 0.0) * dt
    matrix = spread_matrix(heads, size)
    scaled = (xbc[:, :inner].astype(f32) * spread(weight, matrix)).astype(bf16)
    state = tn(scaled, xbc[:, inner : inner + bc // 2])
    carry = carry_column(meta, seg, EDGE)
    store_state(
        meta, packs, pack, keep_o, send_o, state, carry[count - 1 :] * jnp.exp(cum_end), heads, size
    )


def store_state(meta, packs, pack, keep_o, send_o, state, decay, heads, size):
    mine = (pack // (packs // 2)) == (meta[0] & 1)

    @pl.when(mine)
    def _():
        encode_state(keep_o, 0, state, decay, heads, size)

    @pl.when(jnp.logical_not(mine))
    def _():
        encode_state(send_o, 0, state, decay, heads, size)


def load_state(meta, packs, pack, keep, recv, heads, size):
    mine = (pack // (packs // 2)) == (meta[0] & 1)
    block = jnp.where(mine, keep[0].astype(jnp.int32), recv[0].astype(jnp.int32))
    return decode_state(block, heads, size)[0]


def decay_parts(cum_col, cum_row, masked):
    return masked * jnp.exp(jnp.minimum(cum_col - cum_row, 0.0))


def block_mask(meta, lens, pack, count, nseq):
    col = column_segments(meta, lens, pack, count, nseq, 0)
    row = row_segments(meta, lens, pack, count, nseq)
    tri = lax.broadcasted_iota(jnp.int32, (count, count), 0) >= lax.broadcasted_iota(
        jnp.int32, (count, count), 1
    )
    return tri & (col == row)


def inner_kernel(dims, meta, lens, *refs):
    packs, count, features, inner, bc, heads, size, width, nseq = dims
    xbc, dt, cum, cot0, cot1, cot2, cot3, wout, inner_o, cot_o, gg_o, stage = refs
    pack = pl.program_id(0)
    head = meta[1]
    half = bc // 2
    b_vals, c_vals = xbc[0, :, inner : inner + half], xbc[0, :, inner + half :]
    scores = jnp.where(block_mask(meta, lens, pack, count, nseq), nt(c_vals, b_vals), 0.0)
    cum_col = cum[0]
    cum_row = jnp.transpose(cum_col)
    dt_row = jnp.transpose(dt[0])
    lane = lax.broadcasted_iota(jnp.int32, (count, 2 * size), 1)
    for pair in range(heads // 2):
        cols = slice(2 * pair * size, (2 * pair + 2) * size)
        x_pair = xbc[0, :, cols]
        parts = []
        for h in (2 * pair, 2 * pair + 1):
            weights = decay_parts(cum_col[:, h : h + 1], cum_row[h : h + 1], scores)
            parts.append(nn((weights * dt_row[h : h + 1]).astype(bf16), x_pair))
        inner_o[0, :, cols] = jnp.where(lane < size, parts[0], parts[1])
    for k, cot in enumerate((cot0, cot1, cot2, cot3)):
        stage[head ^ k] = cot[0]
    cotangent = stage[...].reshape(features, count)
    cot_o[0] = cotangent
    gg_o[0] = jnp.transpose(nn(wout[...], cotangent))


def compose(lower, upper, heads, size):
    return scaled_state(lower[0], upper[1], heads, size) + upper[0], lower[1] * upper[1]


def choose(flag, a, b):
    return jnp.where(flag, a[0], b[0]), jnp.where(flag, a[1], b[1])


def pair_kernel(dims, rev, meta, own, other, out):
    packs, heads, size = dims
    upper_is_own = ((meta[0] & 1) ^ rev) == 1
    for p in range(packs // 2):
        a, b = decode_state(own[p], heads, size), decode_state(other[p], heads, size)
        both = compose(choose(upper_is_own, b, a), choose(upper_is_own, a, b), heads, size)
        encode_state(out, p, *both, heads, size)


def entering_from(before, b, p, heads, size):
    if before is None:
        return (jnp.zeros_like(b[0]), jnp.ones_like(b[1])), b
    entering = decode_state(before[p], heads, size)
    return entering, compose(b, entering, heads, size)


def cube_kernel(dims, rev, bit, first, meta, *refs):
    packs, heads, size = dims
    total, other = refs[0], refs[1]
    before, next_o, before_o = (None, refs[2], refs[3]) if first else refs[2:5]
    upper_is_own = (((meta[0] >> bit) & 1) ^ rev) == 1
    for p in range(packs // 2):
        a, b = decode_state(total[p], heads, size), decode_state(other[p], heads, size)
        both = compose(choose(upper_is_own, b, a), choose(upper_is_own, a, b), heads, size)
        encode_state(next_o, p, *both, heads, size)
        entering, longer = entering_from(before, b, p, heads, size)
        encode_state(before_o, p, *choose(upper_is_own, longer, entering), heads, size)


def last_kernel(dims, rev, bit, first, meta, *refs):
    packs, heads, size = dims
    own, pair, other = refs[0:3]
    before, keep_o, send_o = (None, refs[3], refs[4]) if first else refs[3:6]
    add = (((meta[0] >> bit) & 1) ^ rev) == 1
    upper_is_own = ((meta[0] & 1) ^ rev) == 1
    for p in range(packs // 2):
        entering, longer = entering_from(
            before, decode_state(other[p], heads, size), p, heads, size
        )
        low = choose(add, longer, entering)
        lower = decode_state(jnp.where(upper_is_own, pair[p].astype(jnp.int32), own[p].astype(jnp.int32)), heads, size)
        high = compose(low, lower, heads, size)
        encode_state(keep_o, p, *choose(upper_is_own, high, low), heads, size)
        encode_state(send_o, p, *choose(upper_is_own, low, high), heads, size)


def gate_kernel(dims, meta, lens, *refs):
    packs, count, features, inner, bc, heads, size, width, nseq = dims
    xbc, cum, inner_in, keep, recv, gate, gg, gain, skip, y_o, mixed_o, stats_o = refs
    pack = pl.program_id(0)
    state_hi, state_lo = split2(load_state(meta, packs, pack, keep, recv, heads, size))
    carry = carry_column(meta, column_segments(meta, lens, pack, count, nseq, EDGE), EDGE)
    matrix = spread_matrix(heads, size)
    entering = spread(carry * jnp.exp(cum[0]), matrix)
    c_vals = xbc[0, :, inner + bc // 2 :]
    y = inner_in[0] + entering * (nt(c_vals, state_hi) + nt(c_vals, state_lo))
    y_o[0] = y
    gate_f = gate[0].astype(f32)
    ssd = y + xbc[0, :, :inner].astype(f32) * skip[...]
    mixed = ssd * (gate_f * sigmoid(gate_f))
    mixed_o[0] = mixed
    squares = jnp.sum(mixed * mixed, axis=1, keepdims=True)
    dots = jnp.sum(gain[...] * gg[0] * mixed, axis=1, keepdims=True)
    lane = lax.broadcasted_iota(jnp.int32, (count, LANES), 1)
    both = jnp.where(lane == 0, squares, 0.0) + jnp.where(lane == 1, dots, 0.0)
    stats_o[0] = jnp.transpose(both)[0:2]


def grad_kernel(dims, total_inner, meta, lens, *refs):
    packs, count, features, inner, bc, heads, size, width, nseq = dims
    (
        stats, xbc, cum, y, mixed, gate, gg, gain, skip,
        gy_o, ey_o, el_o, gated_o, ggate_o, keep_o, send_o, small_o,
    ) = refs
    pack = pl.program_id(0)
    sums = stats[0, 0] + stats[1, 0] + stats[2, 0] + stats[3, 0]
    row = lax.broadcasted_iota(jnp.int32, (LANES, count), 0)
    wide = jnp.where(row == 0, sums[0:1], 0.0) + jnp.where(row == 1, sums[1:2], 0.0)
    cols = jnp.transpose(wide)
    inv = lax.rsqrt(cols[:, 0:1] / total_inner + EPSILON)
    dot = cols[:, 1:2] / total_inner
    mixed_f, gg_f = mixed[0], gg[0]
    gated_o[0] = (mixed_f * inv * gain[...]).astype(bf16)
    grad_mixed = inv * gain[...] * gg_f - mixed_f * (inv * inv * inv * dot)
    gate_f = gate[0].astype(f32)
    sig = sigmoid(gate_f)
    gy_f = grad_mixed * (gate_f * sig)
    gy_o[0] = gy_f
    x_f = xbc[0, :, :inner].astype(f32)
    ssd = y[0] + x_f * skip[...]
    ggate_o[0] = (grad_mixed * ssd * sig * (1.0 + gate_f * (1.0 - sig))).astype(bf16)
    carry = carry_column(meta, column_segments(meta, lens, pack, count, nseq, EDGE), EDGE)
    matrix = spread_matrix(heads, size)
    ey_hi, ey_lo = split2(gy_f * spread(carry * jnp.exp(cum[0]), matrix))
    ey_o[0] = ey_hi
    el_o[0] = ey_lo
    c_vals = xbc[0, :, inner + bc // 2 :]
    state_grad = tn(ey_hi, c_vals) + tn(ey_lo, c_vals)
    decay = carry[count - 1 :] * jnp.exp(cum[0, count - 1 :])
    store_state(meta, packs, pack, keep_o, send_o, state_grad, decay, heads, size)

    @pl.when(pack == 0)
    def _():
        small_o[...] = jnp.zeros_like(small_o)

    small_o[0:1, :] += jnp.sum(gg_f * mixed_f * inv, axis=0, keepdims=True)
    small_o[1:2, :] += jnp.sum(gy_f * x_f, axis=0, keepdims=True)


def diag_kernel(dims, meta, lens, *refs):
    packs, count, features, inner, bc, heads, size, width, nseq = dims
    xbc, dt, cum, gy, ey, el, keep, recv, dx_o, dbc_o = refs
    pack = pl.program_id(0)
    half = bc // 2
    b_vals, c_vals = xbc[0, :, inner : inner + half], xbc[0, :, inner + half :]
    mask = block_mask(meta, lens, pack, count, nseq)
    scores = jnp.where(mask, nt(c_vals, b_vals), 0.0)
    cum_col = cum[0]
    cum_row = jnp.transpose(cum_col)
    dt_row = jnp.transpose(dt[0])
    lane = lax.broadcasted_iota(jnp.int32, (count, 2 * size), 1)
    grad_scores = jnp.zeros((count, count), f32)
    zero = jnp.zeros((), bf16)
    for pair in range(heads // 2):
        cols = slice(2 * pair * size, (2 * pair + 2) * size)
        x_pair = xbc[0, :, cols]
        gy_pair, gy_rest = split2(gy[0, :, cols])
        parts = []
        for h in (2 * pair, 2 * pair + 1):
            own = (lane < size) if h % 2 == 0 else (lane >= size)
            part = jnp.exp(jnp.minimum(cum_col[:, h : h + 1] - cum_row[h : h + 1], 0.0)) * dt_row[h : h + 1]
            weights = (scores * part).astype(bf16)
            parts.append(tn(weights, gy_pair))
            outer = nt(jnp.where(own, gy_pair, zero), x_pair) + nt(
                jnp.where(own, gy_rest, zero), x_pair
            )
            grad_scores = grad_scores + outer * part
        dx_o[0, :, cols] = jnp.where(lane < size, parts[0], parts[1])
    hi, lo = split2(jnp.where(mask, grad_scores, 0.0))
    state_hi, state_lo = split2(load_state(meta, packs, pack, keep, recv, heads, size))
    dbc_o[0, :, :half] = tn(hi, c_vals) + tn(lo, c_vals)
    dbc_o[0, :, half:] = (
        nn(hi, b_vals) + nn(lo, b_vals) + nn(ey[0], state_hi) + nn(ey[0], state_lo) + nn(el[0], state_hi)
    )


def scatter_pieces(head, stage, own_o, far_o, send_o):
    own_o[0] = stage[head]
    send_o[0, 0] = stage[head ^ 1].astype(bf16)
    far_o[0] = stage[head ^ 2]
    send_o[1, 0] = stage[head ^ 3].astype(bf16)


def side_kernel(dims, meta, lens, *refs):
    packs, count, features, inner, bc, heads, size, width, nseq = dims
    gated, cot, wout, normed, ggate, wz, own_o, far_o, send_o, terms_o, grads_o, stage, sums = refs
    pack = pl.program_id(0)
    out = tn(wout[...], jnp.transpose(gated[0]))
    stage[...] = out.reshape(stage.shape)
    scatter_pieces(meta[1], stage, own_o, far_o, send_o)
    terms_o[0] = nt(wz[...], ggate[0])

    @pl.when(pack == 0)
    def _():
        sums[...] = jnp.zeros_like(sums)

    sums[0:features, :] += nn(normed[0], ggate[0])
    sums[features:, :] += nn(cot[0], gated[0])

    @pl.when(pack == packs - 1)
    def _():
        grads_o[...] = sums[...].astype(bf16)


def end_weights(seg, seg_main, cum_col, dt_col, count):
    cum_end = cum_col[count - 1 :]
    end = seg[count + EDGE - 1 :]
    return jnp.where(seg_main == end, jnp.exp(cum_end - cum_col), 0.0) * dt_col


def share_kernel(dims, meta, lens, *refs):
    packs, count, features, inner, bc, heads, size, width, nseq = dims
    xbc, dt, cum, dbc, gkeep, grecv, own_o, near_o = refs
    pack = pl.program_id(0)
    half, quarter = bc // 2, bc // 4
    g_hi, g_lo = split2(load_state(meta, packs, pack, gkeep, grecv, heads, size))
    seg = column_segments(meta, lens, pack, count, nseq, EDGE)
    weight = end_weights(seg, seg[EDGE:], cum[0], dt[0], count)
    wide = spread(weight, spread_matrix(heads, size))
    hi, lo = split2(wide * xbc[0, :, :inner].astype(f32))
    grad_b = dbc[0, :, :half] + nn(hi, g_hi) + nn(lo, g_hi) + nn(hi, g_lo)
    grad_c = dbc[0, :, half:]
    even = jnp.concatenate([grad_b[:, :quarter], grad_c[:, :quarter]], axis=1)
    odd = jnp.concatenate([grad_b[:, quarter:], grad_c[:, quarter:]], axis=1)
    first = (meta[1] & 1) == 0
    own_o[0] = jnp.where(first, even, odd)
    near_o[0] = jnp.where(first, odd, even)


def middle_kernel(dims, meta, *refs):
    packs, quarter = dims
    own, near, keep_o, send_o = refs
    first = (meta[1] >> 1) == 0
    for p in range(packs // 2):
        a, b = own[p] + near[p], own[p + packs // 2] + near[p + packs // 2]
        low = jnp.concatenate([a[:, :quarter], b[:, :quarter]], axis=1)
        high = jnp.concatenate([a[:, quarter:], b[:, quarter:]], axis=1)
        keep_o[p] = jnp.where(first, low, high)
        send_o[p] = jnp.where(first, high, low)


def conv_back(grads, gpad, raws, conv, gconv_o, seg, dims):
    count, width = dims
    ext = count + EDGE
    seg_main = seg[EDGE:]
    seg_pad = jnp.concatenate([seg, jnp.full((8, 1), -1, jnp.int32)], axis=0)
    gpad[EDGE : EDGE + count, :] = grads
    total = jnp.zeros((ext, grads.shape[1]), f32)
    for k in range(width):
        low = EDGE - (width - 1) + k
        mask = jnp.where(seg[low : low + count] == seg_main, 1.0, 0.0)
        gconv_o[k : k + 1, :] += jnp.sum(
            grads * (raws[low : low + count, :] * mask), axis=0, keepdims=True
        )
        lag = width - 1 - k
        mask_back = jnp.where(seg_pad[lag : lag + ext] == seg, 1.0, 0.0)
        total = total + conv[k : k + 1, :] * (gpad[lag : lag + ext, :] * mask_back)
    gconv_o[width : width + 1, :] += jnp.sum(grads, axis=0, keepdims=True)
    return total.astype(bf16)


def xback_kernel(dims, meta, lens, *refs):
    packs, count, features, inner, bc, heads, size, width, nseq = dims
    (
        xbc, dt, sig, cum, gy, y, dx, keep, recv, gkeep, grecv, slope, raw, normed, edge, terms,
        wx, wdt, conv, small, skip,
        terms_o, edge_o, grads_o, gconv_o, gsmall_o, gdt_o,
        gpad, raws, sums, gdt_sums,
    ) = refs
    pack = pl.program_id(0)
    state = load_state(meta, packs, pack, keep, recv, heads, size)
    gstate = load_state(meta, packs, pack, gkeep, grecv, heads, size)
    g_hi, g_lo = split2(gstate)
    seg = column_segments(meta, lens, pack, count, nseq, EDGE)
    matrix = spread_matrix(heads, size)
    b_vals = xbc[0, :, inner : inner + bc // 2]
    x_f = xbc[0, :, :inner].astype(f32)
    gy_f = gy[0].astype(bf16).astype(f32)
    cum_col, dt_col = cum[0], dt[0]
    cum_end = cum_col[count - 1 :]
    wide = spread(end_weights(seg, seg[EDGE:], cum_col, dt_col, count), matrix)
    u_wide = wide * (nt(b_vals, g_hi) + nt(b_vals, g_lo))
    diag = dx[0]
    grad_x = (diag + u_wide + gy_f * skip[...]) * slope[0]
    row_sum = collapse(gy_f * y[0], matrix)
    col_sum = collapse(x_f * diag, matrix)
    state_sum = collapse(x_f * u_wide, matrix)
    carry = carry_column(meta, seg, EDGE)
    hi, lo = split2(gstate * state)
    ones = jnp.ones((8, LANES), bf16)
    by_head = collapse(nt(ones, hi) + nt(ones, lo), matrix)[0:1]
    last = by_head * carry[count - 1 :] * jnp.exp(cum_end) + jnp.sum(state_sum, axis=0, keepdims=True)
    rows = lax.broadcasted_iota(jnp.int32, (count, LANES), 0)
    grad_cum = row_sum - col_sum - state_sum + jnp.where(rows == count - 1, last, 0.0)
    grad_rate = exact_sums(triangle(count, False), grad_cum)
    decay_rate = -jnp.exp(small[1:2, :])
    ratio = jnp.where(dt_col > 1e-30, sig[0] / jnp.maximum(dt_col, 1e-30), 1.0)
    lane = lax.broadcasted_iota(jnp.int32, (1, LANES), 1)
    grad_dt = ratio * (col_sum + state_sum) + grad_rate * decay_rate * sig[0]
    grad_dt = jnp.where(lane < heads, grad_dt, 0.0)
    grad_dt_low = grad_dt.astype(bf16)

    @pl.when(pack == 0)
    def _():
        for ref in (sums, gdt_sums, gconv_o, gsmall_o, gpad, edge_o):
            ref[...] = jnp.zeros_like(ref)

    gsmall_o[0:1, :] += jnp.sum(grad_dt, axis=0, keepdims=True)
    gsmall_o[1:2, :] += jnp.sum(grad_rate * dt_col * decay_rate, axis=0, keepdims=True)
    raws[...] = raw[0].astype(f32)
    grad_raw = conv_back(grad_x, gpad, raws, conv, gconv_o, seg, (count, width))
    main = grad_raw[EDGE:]
    edge_o[pl.ds(pl.multiple_of(pack * EDGE, EDGE), EDGE), :] = grad_raw[:EDGE]
    terms_o[0] = terms[0] + nt(wx[...], main) + nt(wdt[...], grad_dt_low)
    sums[...] += nn(normed[0], main)
    gdt_sums[...] += nn(normed[0], grad_dt_low)

    @pl.when(pack == packs - 1)
    def _():
        grads_o[...] = (sums[...] + nn(edge[...], edge_o[...])).astype(bf16)
        gdt_o[...] = jnp.transpose(gdt_sums[...])[0:8]


def bcback_kernel(dims, meta, lens, *refs):
    packs, count, features, inner, bc, heads, size, width, nseq = dims
    (
        keep, recv, slope, raw, normed, edge, terms, wbc, wx, edge_x, conv,
        own_o, far_o, send_o, dots_o, grads_o, gconv_o,
        stage, gpad, raws, sums, edge_bc,
    ) = refs
    pack = pl.program_id(0)
    quarter = bc // 4
    wide = edge.shape[1]

    @pl.when(pack == 0)
    def _():
        for ref in (sums, gconv_o, gpad, edge_bc):
            ref[...] = jnp.zeros_like(ref)

    @pl.when(pack < packs)
    def _():
        both = keep[0] + recv[0]
        grad = jnp.where(pack < packs // 2, both[:, :quarter], both[:, quarter:]) * slope[0]
        seg = column_segments(meta, lens, pack, count, nseq, EDGE)
        raws[...] = raw[0].astype(f32)
        grad_raw = conv_back(grad, gpad, raws, conv, gconv_o, seg, (count, width))
        main = grad_raw[EDGE:]
        edge_bc[pl.ds(pl.multiple_of(pack * EDGE, EDGE), EDGE), :] = grad_raw[:EDGE]
        whole = terms[0] + nt(wbc[...], main)
        sums[...] += nn(normed[0], main)
        dots_o[0] = jnp.sum(whole * normed[0].astype(f32), axis=0, keepdims=True)
        stage[...] = whole.reshape(stage.shape)

    @pl.when(pack == packs)
    def _():
        whole = nt(wx[...], edge_x[...]) + nt(wbc[...], edge_bc[...])
        dots = jnp.sum(whole * edge[...].astype(f32), axis=0, keepdims=True)
        dots_o[0] = jnp.concatenate([dots, jnp.zeros((1, count - wide), f32)], axis=1)
        total = jnp.transpose(sums[...] + nn(edge[...], edge_bc[...]))
        grads_o[...] = jnp.concatenate(
            [total[:, :inner], total[:, inner:]], axis=0
        ).astype(bf16)
        padded = jnp.concatenate([whole, jnp.zeros((features, count - wide), f32)], axis=1)
        stage[...] = padded.reshape(stage.shape)

    scatter_pieces(meta[1], stage, own_o, far_o, send_o)


def final_kernel(dims, meta, *refs):
    packs, count, features = dims
    (
        own, near, far, dots, tokens, edge, inv, edge_inv, gain, out_grad,
        in_grad_o, edge_o, gain_o,
    ) = refs
    pack = pl.program_id(0)
    wide = edge.shape[1]
    grad = own[0] + near[0, 0].astype(f32) + far[0].astype(f32)
    mean = (dots[0, 0] + dots[1, 0] + dots[2, 0] + dots[3, 0]) / features

    @pl.when(pack == 0)
    def _():
        gain_o[...] = jnp.zeros_like(gain_o)

    @pl.when(pack < packs)
    def _():
        unit = tokens[0].astype(f32) * inv[0]
        grads = inv[0] * (gain[...] * grad - unit * mean)
        in_grad_o[0] = out_grad[0].astype(f32) + grads
        gain_o[...] += jnp.sum(grad * unit, axis=1, keepdims=True)

    @pl.when(pack == packs)
    def _():
        unit = edge[...].astype(f32) * edge_inv[...]
        edge_o[...] = edge_inv[...] * (gain[...] * grad[:, :wide] - unit * mean[:, :wide])
        gain_o[...] += jnp.sum(grad[:, :wide] * unit, axis=1, keepdims=True)


def total_kernel(parts, out):
    total = parts[0].astype(f32)
    for k in range(1, parts.shape[0]):
        total = total + parts[k].astype(f32)
    total = total.astype(bf16)
    for k in range(out.shape[0]):
        out[k] = total


def whole_spec(shape):
    return pl.BlockSpec(shape, lambda p, *_: (0,) * len(shape))


def pack_spec(shape):
    return pl.BlockSpec((1,) + shape, lambda p, *_: (p,) + (0,) * len(shape))


def half_spec(shape, half):
    return pl.BlockSpec((1,) + shape, lambda p, *_: (p % half,) + (0,) * len(shape))


def side_spec(shape, half, keep):
    def index(p, meta, *_):
        side = meta[0] & 1 if keep else 1 - (meta[0] & 1)
        group = p // half
        spot = jnp.where(group == side, p % half, jnp.where(group < side, 0, half - 1))
        return (spot,) + (0,) * len(shape)

    return pl.BlockSpec((1,) + shape, index)


def call(kernel, grid, in_specs, out_specs, out_shape, scratch, cost, prefetch, *args):
    return pl.pallas_call(
        kernel,
        grid_spec=pltpu.PrefetchScalarGridSpec(
            num_scalar_prefetch=len(prefetch),
            grid=grid,
            in_specs=in_specs,
            out_specs=out_specs,
            scratch_shapes=scratch,
        ),
        out_shape=out_shape,
        compiler_params=pltpu.CompilerParams(vmem_limit_bytes=VMEM_LIMIT),
        cost_estimate=pl.CostEstimate(flops=cost[0], bytes_accessed=cost[1], transcendentals=0),
    )(*prefetch, *args)


def shape(*dims_and_type):
    return jax.ShapeDtypeStruct(dims_and_type[:-1], dims_and_type[-1])


def scan_states(keep, send, meta, packs, heads, size, rev):
    dims = (packs, heads, size)
    rows = heads * size
    half = packs // 2
    pay = shape(half, rows + EDGE, LANES, jnp.int16)
    spec = whole_spec(pay.shape)
    cost = (1 << 20, 1 << 20)
    bits = (lax.axis_size("seq") - 1).bit_length()
    other = swap(send, "seq", 1)
    total = call(
        functools.partial(pair_kernel, dims, rev), (1,), [spec, spec], spec, pay, [], cost, (meta,),
        keep, other,
    )
    before = None
    for bit in range(1, bits):
        got = swap(total, "seq", 1 << bit)
        extra = () if before is None else (before,)
        if bit < bits - 1:
            total, before = call(
                functools.partial(cube_kernel, dims, rev, bit, before is None), (1,),
                [spec] * (2 + len(extra)), [spec, spec], [pay, pay], [], cost, (meta,),
                total, got, *extra,
            )
        else:
            own, back = call(
                functools.partial(last_kernel, dims, rev, bit, before is None), (1,),
                [spec] * (3 + len(extra)), [spec, spec], [pay, pay], [], cost,
                (meta,), keep, other, got, *extra,
            )
    return own, swap(back, "seq", 1)


def reduce_over_seq(parts, cost):
    n = lax.axis_size("seq")
    rows, cols = parts.shape
    pieces = lax.all_to_all(parts.reshape(n, rows // n, cols), "seq", 0, 0)
    spec = whole_spec(pieces.shape)
    shares = call(total_kernel, (1,), [spec], spec, shape(*pieces.shape, bf16), [], cost, (), pieces)
    return lax.all_to_all(shares, "seq", 0, 0).reshape(rows, cols)


def shards(
    tokens_in, out_grad, lengths, norm_gain, proj_z, proj_x, proj_bc, proj_dt, conv_x, conv_bc,
    bias_x, bias_bc, dt_bias, a_log, d_skip, gate_gain, proj_out,
):
    packs, count, part = tokens_in.shape
    features, inner = proj_x.shape
    heads = proj_dt.shape[1]
    size = inner // heads
    width = conv_x.shape[0]
    nseq = lengths.shape[1]
    bc_part = proj_bc.shape[1]
    bc = bc_part * lax.axis_size("head")
    half = packs // 2
    chans = inner + bc
    ext = count + EDGE
    rows = heads * size
    total_inner = inner * lax.axis_size("head")
    dims = (packs, count, features, inner, bc, heads, size, width, nseq)
    seq_place, head_place = lax.axis_index("seq"), lax.axis_index("head")
    meta = jnp.stack([seq_place, head_place]).astype(jnp.int32)
    pre = (meta, lengths)
    grid = (packs,)

    tokens = jnp.swapaxes(tokens_in, 1, 2)
    cotangent = jnp.swapaxes(out_grad, 1, 2)
    token_pieces = head_pieces(tokens)
    tail = jnp.concatenate([tokens[p, :, count - EDGE :] for p in range(packs)], axis=1)
    tail = jnp.pad(tail, ((0, 0), (0, LANES - packs * EDGE)))
    edge_pieces = head_pieces(shift(tail, "seq", 1))
    extra = jnp.concatenate(
        [conv_bc.T, bias_bc[:, None], norm_gain.reshape(-1, bc_part).T], axis=1
    )
    extra = jnp.pad(extra, ((0, 0), (0, LANES - extra.shape[1])))
    weight_pieces = head_pieces(jnp.concatenate([proj_bc.T, extra], axis=1))
    conv_own = jnp.pad(
        jnp.concatenate([conv_x, bias_x[None]], axis=0).astype(f32), ((0, 7 - width), (0, 0))
    )
    conv_bc_own = jnp.pad(
        jnp.concatenate([conv_bc, bias_bc[None]], axis=0).astype(f32), ((0, 7 - width), (0, 0))
    )
    w_dt = jnp.pad(proj_dt, ((0, 0), (0, LANES - heads)))
    small = jnp.pad(jnp.stack([dt_bias, a_log]).astype(f32), ((0, 6), (0, LANES - heads)))
    skip = jnp.repeat(d_skip.astype(f32), size)[None]
    gain_gate = gate_gain.astype(f32)[None]

    lane_spec = pack_spec((count, LANES))
    chan_spec = pack_spec((count, inner))
    xbc_spec = pack_spec((count, chans))
    model_spec = pack_spec((features, count))
    piece_spec = pack_spec((part, count))
    edge_spec = whole_spec((part, LANES))
    pay_shape = (rows + EDGE, LANES)
    pay_specs = [side_spec(pay_shape, half, k) for k in (True, False)]
    pay = shape(half, *pay_shape, jnp.int16)
    state_spec = half_spec(pay_shape, half)
    vec = whole_spec((1, inner))
    square = whole_spec((features, inner))

    (
        normed, inv, edge, edge_inv, gate, raw_x, raw_bc, xbc, slope_x, slope_bc, dt, sig, cum,
        keep, send,
    ) = call(
        functools.partial(front_kernel, dims),
        grid,
        [piece_spec] * 4
        + [edge_spec] * 4
        + [whole_spec((bc_part, features + LANES))] * 4
        + [square, square, whole_spec((LANES, features)), whole_spec((8, inner)),
           whole_spec((8, LANES))],
        [
            model_spec, pack_spec((1, count)), whole_spec((features, LANES)),
            whole_spec((1, LANES)), chan_spec, pack_spec((ext, inner)), pack_spec((ext, bc_part)),
            xbc_spec, chan_spec, pack_spec((count, bc_part)), lane_spec, lane_spec, lane_spec,
            *pay_specs,
        ],
        [
            shape(packs, features, count, bf16), shape(packs, 1, count, f32),
            shape(features, LANES, bf16), shape(1, LANES, f32), shape(packs, count, inner, bf16),
            shape(packs, ext, inner, bf16), shape(packs, ext, bc_part, bf16),
            shape(packs, count, chans, bf16), shape(packs, count, inner, f32),
            shape(packs, count, bc_part, f32), shape(packs, count, LANES, f32),
            shape(packs, count, LANES, f32), shape(packs, count, LANES, f32), pay, pay,
        ],
        [
            pltpu.VMEM((4, part, count), bf16), pltpu.VMEM((4, part, LANES), bf16),
            pltpu.VMEM((4, bc_part, features + LANES), bf16), pltpu.VMEM((ext, chans), f32),
            pltpu.VMEM((LANES, chans), f32), pltpu.VMEM((8, chans), f32),
            pltpu.VMEM((features, 1), f32),
        ],
        (2 * packs * ext * features * (inner * 2 + bc + LANES), 12 << 20),
        pre,
        *token_pieces, *edge_pieces, *weight_pieces, proj_z, proj_x, w_dt.T, conv_own, small,
    )

    inner_out, cot, gg = call(
        functools.partial(inner_kernel, dims),
        grid,
        [xbc_spec, lane_spec, lane_spec] + [piece_spec] * 4 + [whole_spec((inner, features))],
        [chan_spec, model_spec, chan_spec],
        [
            shape(packs, count, inner, f32), shape(packs, features, count, bf16),
            shape(packs, count, inner, f32),
        ],
        [pltpu.VMEM((4, part, count), bf16)],
        (2 * packs * count * (features * inner + heads * count * 256), 16 << 20),
        pre,
        xbc, dt, cum, *head_pieces(cotangent), proj_out,
    )

    state_keep, state_recv = scan_states(keep, send, meta, packs, heads, size, 0)

    y, mixed, stats = call(
        functools.partial(gate_kernel, dims),
        grid,
        [
            xbc_spec, lane_spec, chan_spec, state_spec, state_spec, chan_spec, chan_spec, vec, vec,
        ],
        [chan_spec, chan_spec, pack_spec((2, count))],
        [
            shape(packs, count, inner, f32), shape(packs, count, inner, f32),
            shape(packs, 2, count, f32),
        ],
        [],
        (2 * packs * count * inner * LANES, 12 << 20),
        pre,
        xbc, cum, inner_out, state_keep, state_recv, gate, gg, gain_gate, skip,
    )
    stats_all = lax.all_gather(stats, "head")

    gy, ey, el, gated, ggate, gkeep, gsend, gate_small = call(
        functools.partial(grad_kernel, dims, total_inner),
        grid,
        [
            pl.BlockSpec((4, 1, 2, count), lambda p, *_: (0, p, 0, 0)),
            xbc_spec, lane_spec, chan_spec, chan_spec, chan_spec, chan_spec, vec, vec,
        ],
        [chan_spec] * 5 + pay_specs + [whole_spec((8, inner))],
        [shape(packs, count, inner, f32)] + [shape(packs, count, inner, bf16)] * 4
        + [pay, pay, shape(8, inner, f32)],
        [],
        (2 * packs * count * inner * LANES, 16 << 20),
        pre,
        stats_all, xbc, cum, y, mixed, gate, gg, gain_gate, skip,
    )

    dx, dbc = call(
        functools.partial(diag_kernel, dims),
        grid,
        [xbc_spec, lane_spec, lane_spec, chan_spec, chan_spec, chan_spec, state_spec, state_spec],
        [chan_spec, pack_spec((count, bc))],
        [shape(packs, count, inner, f32), shape(packs, count, bc, f32)],
        [],
        (4 * packs * count * heads * count * 256, 12 << 20),
        pre,
        xbc, dt, cum, gy, ey, el, state_keep, state_recv,
    )

    def scatter_shapes(n):
        return (
            [piece_spec, piece_spec,
             pl.BlockSpec((2, 1, part, count), lambda p, *_: (0, p, 0, 0))],
            [shape(n, part, count, f32), shape(n, part, count, f32),
             shape(2, n, part, count, bf16)],
        )

    specs, shapes = scatter_shapes(packs)
    out_own, out_far, out_send, terms, grads_zo = call(
        functools.partial(side_kernel, dims),
        grid,
        [chan_spec, model_spec, whole_spec((inner, features)), model_spec, chan_spec, square],
        specs + [model_spec, whole_spec((2 * features, inner))],
        shapes + [shape(packs, features, count, f32), shape(2 * features, inner, bf16)],
        [pltpu.VMEM((4, part, count), f32), pltpu.VMEM((2 * features, inner), f32)],
        (8 * packs * count * features * inner, 20 << 20),
        pre,
        gated, cot, proj_out, normed, ggate, proj_z,
    )

    def to_far(far, near):
        return swap((far + near[1].astype(f32)).astype(bf16), "head", 2)

    near = swap(out_send, "head", 1)
    block_out = tokens.astype(f32) + out_own + near[0].astype(f32) + to_far(out_far, near).astype(f32)
    block_out = jnp.swapaxes(block_out.astype(bf16), 1, 2)

    gstate_keep, gstate_recv = scan_states(gkeep, gsend, meta, packs, heads, size, 1)

    share_own, share_near = call(
        functools.partial(share_kernel, dims),
        grid,
        [xbc_spec, lane_spec, lane_spec, pack_spec((count, bc)), state_spec, state_spec],
        [lane_spec, lane_spec],
        [shape(packs, count, LANES, f32)] * 2,
        [],
        (6 * packs * count * inner * LANES, 6 << 20),
        pre,
        xbc, dt, cum, dbc, gstate_keep, gstate_recv,
    )
    two = shape(half, count, LANES, f32)
    bc_keep, bc_send = call(
        functools.partial(middle_kernel, (packs, bc_part)),
        (1,),
        [whole_spec((packs, count, LANES))] * 2,
        [whole_spec(two.shape)] * 2,
        [two, two],
        [],
        (1 << 20, 2 << 20),
        (meta,),
        share_own, swap(share_near, "head", 1),
    )
    bc_recv = swap(bc_send, "head", 2)

    terms, edge_x, grads_x, grad_conv, grad_small, grad_dt = call(
        functools.partial(xback_kernel, dims),
        grid,
        [
            xbc_spec, lane_spec, lane_spec, lane_spec, chan_spec, chan_spec, chan_spec,
            state_spec, state_spec, state_spec, state_spec, chan_spec, pack_spec((ext, inner)),
            model_spec, whole_spec((features, LANES)), model_spec, square,
            whole_spec((features, LANES)), whole_spec((8, inner)), whole_spec((8, LANES)), vec,
        ],
        [
            model_spec, whole_spec((LANES, inner)), square, whole_spec((8, inner)),
            whole_spec((8, LANES)), whole_spec((8, features)),
        ],
        [
            shape(packs, features, count, f32), shape(LANES, inner, bf16),
            shape(features, inner, bf16), shape(8, inner, f32), shape(8, LANES, f32),
            shape(8, features, f32),
        ],
        [
            pltpu.VMEM((ext + EDGE, inner), f32), pltpu.VMEM((ext, inner), f32),
            pltpu.VMEM((features, inner), f32), pltpu.VMEM((features, LANES), f32),
        ],
        (4 * packs * ext * features * inner, 24 << 20),
        pre,
        xbc, dt, sig, cum, gy, y, dx, state_keep, state_recv, gstate_keep, gstate_recv, slope_x,
        raw_x, normed, edge, terms, proj_x, w_dt, conv_own, small, skip,
    )

    def late(spec_shape):
        return pl.BlockSpec(
            (1,) + spec_shape,
            lambda p, *_: (jnp.minimum(p, packs - 1),) + (0,) * len(spec_shape),
        )

    def late_half(spec_shape):
        return pl.BlockSpec(
            (1,) + spec_shape,
            lambda p, *_: (jnp.minimum(p, packs - 1) % half,) + (0,) * len(spec_shape),
        )

    specs, shapes = scatter_shapes(packs + 1)
    gn_own, gn_far, gn_send, dots, grads_bc, grad_conv_bc = call(
        functools.partial(bcback_kernel, dims),
        (packs + 1,),
        [
            late_half((count, LANES)), late_half((count, LANES)), late((count, bc_part)),
            late((ext, bc_part)), late((features, count)), whole_spec((features, LANES)),
            late((features, count)), whole_spec((features, bc_part)), square,
            whole_spec((LANES, inner)), whole_spec((8, bc_part)),
        ],
        specs + [
            pack_spec((1, count)), whole_spec((2 * bc_part, inner)), whole_spec((8, bc_part)),
        ],
        shapes + [
            shape(packs + 1, 1, count, f32), shape(2 * bc_part, inner, bf16),
            shape(8, bc_part, f32),
        ],
        [
            pltpu.VMEM((4, part, count), f32), pltpu.VMEM((ext + EDGE, bc_part), f32),
            pltpu.VMEM((ext, bc_part), f32), pltpu.VMEM((features, bc_part), f32),
            pltpu.VMEM((LANES, bc_part), bf16),
        ],
        (4 * packs * ext * features * bc_part, 20 << 20),
        pre,
        bc_keep, bc_recv, slope_bc, raw_bc, normed, edge, terms, proj_bc, proj_x, edge_x,
        conv_bc_own,
    )

    near = swap(gn_send, "head", 1)
    far = to_far(gn_far, near)
    dots_all = lax.all_gather(dots, "head")
    in_grad, edge_grad, grad_gain = call(
        functools.partial(final_kernel, (packs, count, features)),
        (packs + 1,),
        [
            piece_spec, pl.BlockSpec((1, 1, part, count), lambda p, *_: (0, p, 0, 0)), piece_spec,
            pl.BlockSpec((4, 1, 1, count), lambda p, *_: (0, p, 0, 0)), late((part, count)),
            edge_spec, late((1, count)), whole_spec((1, LANES)), whole_spec((part, 1)),
            late((part, count)),
        ],
        [late((part, count)), edge_spec, edge_spec],
        [shape(packs, part, count, f32), shape(part, LANES, f32), shape(part, LANES, f32)],
        [],
        (1 << 20, 6 << 20),
        (meta,),
        gn_own, near, far, dots_all, tokens, edge_pieces[0], inv, edge_inv,
        norm_gain.astype(f32)[:, None], cotangent,
    )
    from_next = shift(edge_grad, "seq", -1)[:, : packs * EDGE]
    from_next = from_next.reshape(part, packs, EDGE).transpose(1, 0, 2)
    in_grad = in_grad + jnp.pad(from_next, ((0, 0), (0, 0), (count - EDGE, 0)))
    in_grad = jnp.swapaxes(in_grad, 1, 2)

    cost = (1 << 20, 4 << 20)
    grads_zo = reduce_over_seq(grads_zo, cost)
    grads_x = reduce_over_seq(grads_x, cost)
    grads_bc = reduce_over_seq(grads_bc, cost)
    grad_bc = jnp.concatenate([grads_bc[:bc_part], grads_bc[bc_part:]], axis=1)
    smalls = [
        grad_gain[:, 0], grad_dt[:heads], grad_conv[: width + 1], grad_conv_bc[: width + 1],
        gate_small[0:2], grad_small[0:2],
    ]
    flat = jnp.concatenate([v.reshape(-1) for v in smalls])
    flat = jnp.pad(flat, (0, -flat.shape[0] % (8 * LANES))).reshape(-1, LANES)
    bit = 1
    while bit < lax.axis_size("seq"):
        flat = flat + swap(flat, "seq", bit)
        bit *= 2
    flat = flat.reshape(-1)
    sums, start = [], 0
    for v in smalls:
        sums.append(flat[start : start + v.size].reshape(v.shape))
        start += v.size
    grad_gain, grad_dt, grad_conv, grad_conv_bc, gate_small, grad_small = sums
    return (
        block_out,
        in_grad,
        grad_gain,
        grads_zo[:features].astype(f32),
        grads_x.astype(f32),
        grad_bc.T.astype(f32),
        grad_dt.T,
        grad_conv[:width],
        grad_conv_bc[:width],
        grad_conv[width],
        grad_conv_bc[width],
        grad_small[0, :heads],
        grad_small[1, :heads],
        jnp.sum(gate_small[1].reshape(heads, size), axis=1),
        gate_small[0],
        grads_zo[features:].astype(f32).T,
    )


def solution(mesh):
    token, column, vector = P(None, "seq", "head"), P(None, "head"), P("head")
    row = P("head", None)
    return jax.shard_map(
        shards,
        mesh=mesh,
        in_specs=(
            token, token, P(), vector, column, column, column, column, column, column, vector,
            vector, vector, vector, vector, vector, row,
        ),
        out_specs=(
            token, token, vector, column, column, column, column, column, column, vector, vector,
            vector, vector, vector, vector, row,
        ),
        check_vma=False,
    )
```

```python
import functools

import jax
import jax.numpy as jnp
from jax import lax
from jax.experimental import pallas as pl
from jax.experimental.pallas import tpu as pltpu
from jax.sharding import PartitionSpec as P

EPSILON = 1e-05
bf16 = jnp.bfloat16
f32 = jnp.float32
LANES = 128
EDGE = 16
MIB = 1024 * 1024
STEPS = 32000.0
UNIT = 16384.0
LN2 = 0.6931471805599453
GROUP = 16


def swap(x, axis, bit):
    return lax.ppermute(x, axis, [(i, i ^ bit) for i in range(lax.axis_size(axis))])


def shift(x, axis, distance):
    n = lax.axis_size(axis)
    return lax.ppermute(x, axis, [(i, i + distance) for i in range(n) if 0 <= i + distance < n])


def head_pieces(x):
    far = swap(x, "head", 2)
    near = swap(x, "head", 1)
    return x, near, far, swap(far, "head", 1)


def nn(a, b):
    return lax.dot_general(a, b, (((1,), (0,)), ((), ())), preferred_element_type=f32)


def nt(a, b):
    return lax.dot_general(a, b, (((1,), (1,)), ((), ())), preferred_element_type=f32)


def tn(a, b):
    return lax.dot_general(a, b, (((0,), (0,)), ((), ())), preferred_element_type=f32)


def split2(v):
    hi = v.astype(bf16)
    return hi, (v - hi.astype(f32)).astype(bf16)


def split3(v):
    hi = v.astype(bf16)
    rest = v - hi.astype(f32)
    mid = rest.astype(bf16)
    return hi, mid, (rest - mid.astype(f32)).astype(bf16)


def spread_matrix(heads, size):
    row = lax.broadcasted_iota(jnp.int32, (LANES, heads * size), 0)
    col = lax.broadcasted_iota(jnp.int32, (LANES, heads * size), 1)
    first = (col >= row * size) & (col < (row + 1) * size)
    again = (col >= (row - GROUP) * size) & (col < (row - GROUP + 1) * size)
    return jnp.where(first | again, 1.0, 0.0).astype(bf16)


def spread(v, matrix, heads):
    hi, lo = split2(head_lanes(v, heads))
    return nn((hi.astype(f32) + to_group(lo.astype(f32), 1)).astype(bf16), matrix)


def head_lanes(v, heads):
    return jnp.where(lax.broadcasted_iota(jnp.int32, v.shape, 1) < heads, v, 0.0)


def to_group(v, k):
    return pltpu.roll(v, k * GROUP, 1)


def from_group(v, k, heads):
    return head_lanes(pltpu.roll(v, LANES - k * GROUP, 1) if k else v, heads)


def collapse(v, matrix, heads):
    return head_lanes(nt(jnp.concatenate(split2(v), axis=1), jnp.concatenate([matrix] * 2, axis=1)), heads)


def triangle(count, lower):
    row = lax.broadcasted_iota(jnp.int32, (count, count), 0)
    col = lax.broadcasted_iota(jnp.int32, (count, count), 1)
    keep = (row >= col) if lower else (row <= col)
    return jnp.where(keep, 1.0, 0.0).astype(bf16)


def exact_sums(matrix, v, heads):
    hi, mid, lo = [piece.astype(f32) for piece in split3(v)]
    sums = nn(matrix, (hi + to_group(mid, 1) + to_group(lo, 2)).astype(bf16))
    return from_group(sums, 0, heads) + from_group(sums, 1, heads) + from_group(sums, 2, heads)


def step_sizes(v, heads):
    soft = jnp.maximum(v, 0.0) + jnp.log1p(jnp.exp(-jnp.abs(v)))
    return head_lanes(soft, heads)


def steps_of(block, heads):
    return step_sizes(block, heads), from_group(block, 1, heads)


def segments(positions, lens_ref, pack, count):
    total = jnp.zeros(positions.shape, jnp.int32)
    end = jnp.int32(0)
    for k in range(count):
        end = end + lens_ref[pack, k]
        total = total + jnp.where(positions >= end, 1, 0)
    return total


def column_segments(meta_ref, lens_ref, pack, count, nseq, before):
    rows = lax.broadcasted_iota(jnp.int32, (count + before, 1), 0)
    return segments(rows + (meta_ref[0] * count - before), lens_ref, pack, nseq)


def row_segments(meta_ref, lens_ref, pack, count, nseq):
    cols = lax.broadcasted_iota(jnp.int32, (1, count), 1)
    return segments(cols + meta_ref[0] * count, lens_ref, pack, nseq)


def carry_column(meta_ref, seg_ext, before):
    same = seg_ext[before:] == seg_ext[before - 1 : before]
    return jnp.where(same & (meta_ref[0] > 0), 1.0, 0.0)


def to_int16(v):
    return jnp.floor(v + 0.5).astype(jnp.int32).astype(jnp.int16)


def encode_state(out, p, state, decay, heads, size):
    lane = lax.broadcasted_iota(jnp.int32, (1, LANES), 1)
    powers = jnp.zeros((1, LANES), f32)
    for h in range(heads):
        part = state[h * size : (h + 1) * size]
        top = jnp.max(jnp.max(jnp.abs(part), axis=0, keepdims=True), axis=1, keepdims=True)
        power = jnp.ceil(jnp.log(jnp.maximum(top, 1e-30)) / LN2)
        powers = powers + jnp.where(lane == h, power, 0.0)
        codes = jnp.clip(part * (jnp.exp(-power * LN2) * STEPS), -32767.0, 32767.0)
        out[p, h * size : (h + 1) * size, :] = to_int16(codes)
    row = lax.broadcasted_iota(jnp.int32, (EDGE, LANES), 0)
    coarse = jnp.floor(decay * UNIT)
    fine = (decay * UNIT - coarse) * UNIT
    tail = jnp.where(row == 0, powers, jnp.where(row == 1, coarse, jnp.where(row == 2, fine, 0.0)))
    out[p, heads * size :, :] = to_int16(tail)


def decode_state(block, heads, size):
    values = block.astype(jnp.int32).astype(f32)
    tail = values[heads * size :]
    scale = jnp.exp(tail[0:1] * LN2) / STEPS
    decay = (tail[1:2] + tail[2:3] / UNIT) / UNIT
    return scaled_state(values[: heads * size], scale, heads, size), decay


def sigmoid(v):
    return 1.0 / (1.0 + jnp.exp(-v))


def scaled_state(state, decay, heads, size):
    return jnp.concatenate(
        [state[h * size : (h + 1) * size] * decay[:, h : h + 1] for h in range(heads)], axis=0
    )


def front_kernel(dims, meta, lens, *refs):
    packs, count, features, inner, bc, heads, size, width, nseq = dims
    tokens, edges, shared = refs[0:4], refs[4:8], refs[8:12]
    wx, wdt, conv_x, small = refs[12:16]
    normed_o, inv_o, edge_o, rawx_o, rawbc_o, xbc_o, steps_o, keep_o, send_o, gain_o = refs[16:26]
    stage, edge_stage, weights, raws, edge_raws, conv, gain = refs[26:]
    pack = pl.program_id(0)
    head = meta[1]
    part = features // 4
    wide = edge_stage.shape[2]

    def normalise(values):
        mean = jnp.sum(values * values, axis=0, keepdims=True) / features
        inv = lax.rsqrt(mean + EPSILON)
        return inv, ((values * inv) * gain[...]).astype(bf16)

    def raw_of(normed):
        wbc = weights[...].reshape(bc, weights.shape[2])[:, :features]
        return jnp.concatenate([nn(normed, wx[...]), nt(normed, wbc)], axis=1).astype(bf16)

    @pl.when(pack == 0)
    def _():
        for k in range(4):
            weights[head ^ k] = shared[k][...]
            edge_stage[head ^ k] = edges[k][...]
        extra = weights[...].reshape(bc, weights.shape[2])[:, features:].astype(f32)
        conv[:, :inner] = conv_x[...]
        conv[:, inner:] = jnp.transpose(extra)[0:8]
        bc_part = bc // 4
        pieces = part // bc_part
        for h in range(4):
            for c in range(pieces):
                gain[h * part + c * bc_part : h * part + (c + 1) * bc_part, :] = extra[
                    h * bc_part : (h + 1) * bc_part, width + 1 + c : width + 2 + c
                ]
        _, normed = normalise(edge_stage[...].reshape(features, wide).astype(f32))
        gain_o[...] = gain[...]
        edge_o[...] = normed
        edge_raws[...] = raw_of(jnp.transpose(normed)).astype(f32)

    for k in range(4):
        stage[head ^ k] = tokens[k][0]
    inv, normed_t = normalise(stage[...].reshape(features, count).astype(f32))
    inv_o[0] = inv
    normed_o[0] = normed_t
    normed = jnp.transpose(normed_t)
    raws[EDGE:, :] = raw_of(normed).astype(f32)
    raws[0:EDGE, :] = edge_raws[pl.ds(pl.multiple_of(pack * EDGE, EDGE), EDGE), :]

    def own_bc(values):
        bc_part = bc // 4
        parts = [values[:, inner + h * bc_part : inner + (h + 1) * bc_part] for h in range(4)]
        low = jnp.where((head & 1) == 0, parts[0], parts[1])
        high = jnp.where((head & 1) == 0, parts[2], parts[3])
        return jnp.where((head >> 1) == 0, low, high)

    rawx_o[0] = raws[:, :inner].astype(bf16)
    rawbc_o[0] = own_bc(raws[...]).astype(bf16)
    seg = column_segments(meta, lens, pack, count, nseq, EDGE)
    seg_main = seg[EDGE:]
    pre = convolved(raws, conv, seg, count, width)
    xbc = (pre * sigmoid(pre)).astype(bf16)
    xbc_o[0] = xbc
    v = head_lanes(nt(normed, wdt[...]).astype(bf16).astype(f32) + small[0:1, :], heads)
    dt = step_sizes(v, heads)
    rate = -dt * jnp.exp(small[1:2, :])
    cum = exact_sums(triangle(count, True), rate, heads)
    steps_o[0] = v + to_group(cum, 1)
    cum_end = cum[count - 1 : count]
    weight = jnp.where(seg_main == seg[count + EDGE - 1 :], jnp.exp(cum_end - cum), 0.0) * dt
    matrix = spread_matrix(heads, size)
    scaled = (xbc[:, :inner].astype(f32) * spread(weight, matrix, heads)).astype(bf16)
    state = tn(scaled, xbc[:, inner : inner + bc // 2])
    carry = carry_column(meta, seg, EDGE)
    store_state(
        meta, packs, pack, keep_o, send_o, state, carry[count - 1 :] * jnp.exp(cum_end), heads, size
    )


def convolved(raws, conv, seg, count, width):
    pre = jnp.broadcast_to(conv[width : width + 1, :], (count, raws.shape[1]))
    for k in range(width):
        low = EDGE - (width - 1) + k
        mask = jnp.where(seg[low : low + count] == seg[EDGE:], 1.0, 0.0)
        pre = pre + conv[k : k + 1, :] * raws[low : low + count, :] * mask
    return pre


def gate_slope_kernel(dims, meta, lens, *refs):
    packs, count, features, inner, bc, heads, size, width, nseq = dims
    normed, wz, raw_x, raw_bc, conv_x, conv_bc, gate_o, slope_x_o, slope_bc_o, raws, raws_bc = refs
    pack = pl.program_id(0)
    gate_o[0] = tn(normed[0], wz[...]).astype(bf16)
    seg = column_segments(meta, lens, pack, count, nseq, EDGE)
    for raw, wide, conv, out in ((raw_x, raws, conv_x, slope_x_o), (raw_bc, raws_bc, conv_bc, slope_bc_o)):
        wide[...] = raw[0].astype(f32)
        pre = convolved(wide, conv, seg, count, width)
        sig = sigmoid(pre)
        out[0] = sig * (1.0 + pre * (1.0 - sig))


def store_state(meta, packs, pack, keep_o, send_o, state, decay, heads, size):
    mine = (pack // (packs // 2)) == (meta[0] & 1)

    @pl.when(mine)
    def _():
        encode_state(keep_o, 0, state, decay, heads, size)

    @pl.when(jnp.logical_not(mine))
    def _():
        encode_state(send_o, 0, state, decay, heads, size)


def load_state(meta, packs, pack, keep, recv, heads, size):
    mine = (pack // (packs // 2)) == (meta[0] & 1)
    block = jnp.where(mine, keep[0].astype(jnp.int32), recv[0].astype(jnp.int32))
    return decode_state(block, heads, size)[0]


def decay_parts(cum_col, cum_row, masked):
    return masked * jnp.exp(jnp.minimum(cum_col - cum_row, 0.0))


def block_mask(meta, lens, pack, count, nseq):
    col = column_segments(meta, lens, pack, count, nseq, 0)
    row = row_segments(meta, lens, pack, count, nseq)
    tri = lax.broadcasted_iota(jnp.int32, (count, count), 0) >= lax.broadcasted_iota(
        jnp.int32, (count, count), 1
    )
    return tri & (col == row)


def inner_kernel(dims, meta, lens, *refs):
    packs, count, features, inner, bc, heads, size, width, nseq = dims
    xbc, steps, inner_o = refs
    pack = pl.program_id(0)
    half = bc // 2
    b_vals, c_vals = xbc[0, :, inner : inner + half], xbc[0, :, inner + half :]
    scores = jnp.where(block_mask(meta, lens, pack, count, nseq), nt(c_vals, b_vals), 0.0)
    dt, cum_col = steps_of(steps[0], heads)
    cum_row = jnp.transpose(cum_col)
    dt_row = jnp.transpose(dt)
    lane = lax.broadcasted_iota(jnp.int32, (count, 2 * size), 1)
    for pair in range(heads // 2):
        cols = slice(2 * pair * size, (2 * pair + 2) * size)
        x_pair = xbc[0, :, cols]
        parts = []
        for h in (2 * pair, 2 * pair + 1):
            weights = decay_parts(cum_col[:, h : h + 1], cum_row[h : h + 1], scores)
            parts.append(nn((weights * dt_row[h : h + 1]).astype(bf16), x_pair))
        inner_o[0, :, cols] = jnp.where(lane < size, parts[0], parts[1])


def cot_kernel(dims, meta, lens, *refs):
    packs, count, features, inner, bc, heads, size, width, nseq = dims
    pieces, (wout, cot_o, gg_o, stage) = refs[:4], refs[4:]
    for k in range(4):
        stage[meta[1] ^ k] = pieces[k][0]
    cotangent = stage[...].reshape(features, count)
    cot_o[0] = cotangent
    gg_o[0] = jnp.transpose(nn(wout[...], cotangent))


def compose(lower, upper, heads, size):
    return scaled_state(lower[0], upper[1], heads, size) + upper[0], lower[1] * upper[1]


def choose(flag, a, b):
    return jnp.where(flag, a[0], b[0]), jnp.where(flag, a[1], b[1])


def pair_kernel(dims, rev, meta, own, other, out):
    packs, heads, size = dims
    upper_is_own = ((meta[0] & 1) ^ rev) == 1
    for p in range(packs // 2):
        a, b = decode_state(own[p], heads, size), decode_state(other[p], heads, size)
        both = compose(choose(upper_is_own, b, a), choose(upper_is_own, a, b), heads, size)
        encode_state(out, p, *both, heads, size)


def entering_from(before, b, p, heads, size):
    if before is None:
        return (jnp.zeros_like(b[0]), jnp.ones_like(b[1])), b
    entering = decode_state(before[p], heads, size)
    return entering, compose(b, entering, heads, size)


def cube_kernel(dims, rev, bit, first, meta, *refs):
    packs, heads, size = dims
    total, other = refs[0], refs[1]
    before, next_o, before_o = (None, refs[2], refs[3]) if first else refs[2:5]
    upper_is_own = (((meta[0] >> bit) & 1) ^ rev) == 1
    for p in range(packs // 2):
        a, b = decode_state(total[p], heads, size), decode_state(other[p], heads, size)
        both = compose(choose(upper_is_own, b, a), choose(upper_is_own, a, b), heads, size)
        encode_state(next_o, p, *both, heads, size)
        entering, longer = entering_from(before, b, p, heads, size)
        encode_state(before_o, p, *choose(upper_is_own, longer, entering), heads, size)


def last_kernel(dims, rev, bit, first, meta, *refs):
    packs, heads, size = dims
    own, pair, other = refs[0:3]
    before, keep_o, send_o = (None, refs[3], refs[4]) if first else refs[3:6]
    add = (((meta[0] >> bit) & 1) ^ rev) == 1
    upper_is_own = ((meta[0] & 1) ^ rev) == 1
    for p in range(packs // 2):
        entering, longer = entering_from(
            before, decode_state(other[p], heads, size), p, heads, size
        )
        low = choose(add, longer, entering)
        lower = decode_state(jnp.where(upper_is_own, pair[p].astype(jnp.int32), own[p].astype(jnp.int32)), heads, size)
        high = compose(low, lower, heads, size)
        encode_state(keep_o, p, *choose(upper_is_own, high, low), heads, size)
        encode_state(send_o, p, *choose(upper_is_own, low, high), heads, size)


def gate_kernel(dims, meta, lens, *refs):
    packs, count, features, inner, bc, heads, size, width, nseq = dims
    xbc, steps, inner_in, keep, recv, gate, gg, gain, skip, y_o, stats_o = refs
    pack = pl.program_id(0)
    state = jnp.concatenate(
        split2(load_state(meta, packs, pack, keep, recv, heads, size)), axis=1
    )
    carry = carry_column(meta, column_segments(meta, lens, pack, count, nseq, EDGE), EDGE)
    matrix = spread_matrix(heads, size)
    entering = spread(carry * jnp.exp(from_group(steps[0], 1, heads)), matrix, heads)
    c_vals = xbc[0, :, inner + bc // 2 :]
    y = inner_in[0] + entering * nt(jnp.concatenate([c_vals, c_vals], axis=1), state)
    y_o[0] = y
    gate_f = gate[0].astype(f32)
    ssd = y + xbc[0, :, :inner].astype(f32) * skip[...]
    mixed = ssd * (gate_f * sigmoid(gate_f))
    squares = jnp.sum(mixed * mixed, axis=1, keepdims=True)
    dots = jnp.sum(gain[...] * gg[0] * mixed, axis=1, keepdims=True)
    lane = lax.broadcasted_iota(jnp.int32, (count, LANES), 1)
    both = jnp.where(lane == 0, squares, 0.0) + jnp.where(lane == 1, dots, 0.0)
    stats_o[0] = jnp.transpose(both)[0:2]


def grad_kernel(dims, total_inner, meta, lens, *refs):
    packs, count, features, inner, bc, heads, size, width, nseq = dims
    (
        stats, xbc, steps, y, gate, gg, gain, skip,
        gy_o, gated_o, ggate_o, keep_o, send_o, small_o,
    ) = refs
    pack = pl.program_id(0)
    sums = stats[0, 0] + stats[1, 0] + stats[2, 0] + stats[3, 0]
    row = lax.broadcasted_iota(jnp.int32, (LANES, count), 0)
    wide = jnp.where(row == 0, sums[0:1], 0.0) + jnp.where(row == 1, sums[1:2], 0.0)
    cols = jnp.transpose(wide)
    inv = lax.rsqrt(cols[:, 0:1] / total_inner + EPSILON)
    dot = cols[:, 1:2] / total_inner
    x_f, gg_f, gate_f = xbc[0, :, :inner].astype(f32), gg[0], gate[0].astype(f32)
    ssd = y[0] + x_f * skip[...]
    sig = sigmoid(gate_f)
    act = gate_f * sig
    mixed = ssd * act
    scaled = mixed * inv
    gated_o[0] = (scaled * gain[...]).astype(bf16)
    grad_mixed = inv * gain[...] * gg_f - mixed * (inv * inv * inv * dot)
    gy_f = grad_mixed * act
    gy_o[0] = gy_f
    ggate_o[0] = (grad_mixed * ssd * sig * (1.0 + gate_f * (1.0 - sig))).astype(bf16)
    carry = carry_column(meta, column_segments(meta, lens, pack, count, nseq, EDGE), EDGE)
    cum = from_group(steps[0], 1, heads)
    entering = carry * jnp.exp(cum)
    ey_hi, ey_lo = split2(gy_f * spread(entering, spread_matrix(heads, size), heads))
    c_vals = xbc[0, :, inner + bc // 2 :]
    state_grad = tn(ey_hi, c_vals) + tn(ey_lo, c_vals)
    store_state(
        meta, packs, pack, keep_o, send_o, state_grad, entering[count - 1 :], heads, size
    )

    @pl.when(pack == 0)
    def _():
        small_o[...] = jnp.zeros_like(small_o)

    small_o[0:1, :] += jnp.sum(gg_f * scaled, axis=0, keepdims=True)
    small_o[1:2, :] += jnp.sum(gy_f * x_f, axis=0, keepdims=True)


def diag_kernel(dims, meta, lens, *refs):
    packs, count, features, inner, bc, heads, size, width, nseq = dims
    xbc, steps, gy, y, keep, recv, dx_o, dbc_o, sums_o = refs
    pack = pl.program_id(0)
    half = bc // 2
    b_vals, c_vals = xbc[0, :, inner : inner + half], xbc[0, :, inner + half :]
    mask = block_mask(meta, lens, pack, count, nseq)
    scores = jnp.where(mask, nt(c_vals, b_vals), 0.0)
    dt, cum_col = steps_of(steps[0], heads)
    cum_row = jnp.transpose(cum_col)
    dt_row = jnp.transpose(dt)
    lane = lax.broadcasted_iota(jnp.int32, (count, 2 * size), 1)
    grad_scores = jnp.zeros((count, count), f32)
    zero = jnp.zeros((), bf16)
    for pair in range(heads // 2):
        cols = slice(2 * pair * size, (2 * pair + 2) * size)
        x_pair = xbc[0, :, cols]
        x_twice = jnp.concatenate([x_pair, x_pair], axis=1)
        gy_hi, gy_lo = split2(gy[0, :, cols])
        gy_wide = jnp.concatenate([gy_hi, gy_lo], axis=1)
        parts = []
        for h in (2 * pair, 2 * pair + 1):
            own = (lane < size) if h % 2 == 0 else (lane >= size)
            part = jnp.exp(jnp.minimum(cum_col[:, h : h + 1] - cum_row[h : h + 1], 0.0)) * dt_row[h : h + 1]
            parts.append(tn((scores * part).astype(bf16), gy_wide))
            both = jnp.concatenate([jnp.where(own, gy_hi, zero), jnp.where(own, gy_lo, zero)], axis=1)
            grad_scores = grad_scores + nt(both, x_twice) * part
        two = [part[:, : 2 * size] + part[:, 2 * size :] for part in parts]
        dx_o[0, :, cols] = jnp.where(lane < size, two[0], two[1])
    hi, lo = split2(jnp.where(mask, grad_scores, 0.0))
    state_hi, state_lo = split2(load_state(meta, packs, pack, keep, recv, heads, size))
    carry = carry_column(meta, column_segments(meta, lens, pack, count, nseq, EDGE), EDGE)
    matrix = spread_matrix(heads, size)
    ey_hi, ey_lo = split2(gy[0] * spread(carry * jnp.exp(cum_col), matrix, heads))
    dbc_o[0, :, :half] = tn(hi, c_vals) + tn(lo, c_vals)
    dbc_o[0, :, half:] = (
        nn(jnp.concatenate([hi, lo], axis=1), jnp.concatenate([b_vals, b_vals], axis=0))
        + nn(ey_hi, state_hi) + nn(ey_hi, state_lo) + nn(ey_lo, state_hi)
    )
    row_sum = collapse(gy[0] * y[0], matrix, heads)
    col_sum = collapse(xbc[0, :, :inner].astype(f32) * dx_o[0], matrix, heads)
    sums_o[0] = row_sum + to_group(col_sum, 1)


def scatter_pieces(head, stage, own_o, far_o, send_o):
    own_o[0] = stage[head]
    send_o[0, 0] = stage[head ^ 1].astype(bf16)
    far_o[0] = stage[head ^ 2]
    send_o[1, 0] = stage[head ^ 3].astype(bf16)


def accumulate(meta, pack, packs, sums, term, keep_o, send_o):
    wide = term.reshape(sums.shape)

    @pl.when(pack == 0)
    def _():
        sums[...] = wide

    @pl.when(pack > 0)
    def _():
        sums[...] += wide

    @pl.when(pack == packs - 1)
    def _():
        side = meta[0] & 1
        keep_o[...] = sums[side]
        send_o[...] = sums[1 - side].astype(bf16)


def out_kernel(dims, meta, lens, *refs):
    packs, count, features, inner, bc, heads, size, width, nseq = dims
    gated, cot, wout, own_o, far_o, send_o, keep_o, give_o, stage, sums = refs
    pack = pl.program_id(0)
    stage[...] = tn(wout[...], jnp.transpose(gated[0])).reshape(stage.shape)
    scatter_pieces(meta[1], stage, own_o, far_o, send_o)
    accumulate(meta, pack, packs, sums, nn(cot[0], gated[0]), keep_o, give_o)


def z_kernel(dims, meta, lens, *refs):
    normed, ggate, keep_o, give_o, sums = refs
    accumulate(
        meta, pl.program_id(0), dims[0], sums, nn(normed[0], ggate[0]), keep_o, give_o
    )


def end_weights(seg, seg_main, cum_col, dt_col, count):
    cum_end = cum_col[count - 1 :]
    end = seg[count + EDGE - 1 :]
    return jnp.where(seg_main == end, jnp.exp(cum_end - cum_col), 0.0) * dt_col


def share_kernel(dims, meta, lens, *refs):
    packs, count, features, inner, bc, heads, size, width, nseq = dims
    xbc, steps, dbc, gkeep, grecv, own_o, near_o = refs
    pack = pl.program_id(0)
    half, quarter = bc // 2, bc // 4
    g_hi, g_lo = split2(load_state(meta, packs, pack, gkeep, grecv, heads, size))
    seg = column_segments(meta, lens, pack, count, nseq, EDGE)
    dt, cum = steps_of(steps[0], heads)
    wide = spread(end_weights(seg, seg[EDGE:], cum, dt, count), spread_matrix(heads, size), heads)
    hi, lo = split2(wide * xbc[0, :, :inner].astype(f32))
    grad_b = dbc[0, :, :half] + nn(hi, g_hi) + nn(lo, g_hi) + nn(hi, g_lo)
    grad_c = dbc[0, :, half:]
    even = jnp.concatenate([grad_b[:, :quarter], grad_c[:, :quarter]], axis=1)
    odd = jnp.concatenate([grad_b[:, quarter:], grad_c[:, quarter:]], axis=1)
    first = (meta[1] & 1) == 0
    own_o[0] = jnp.where(first, even, odd)
    near_o[0] = jnp.where(first, odd, even)


def middle_kernel(dims, meta, *refs):
    packs, quarter = dims
    own, near, keep_o, send_o, edge_o = refs
    half = packs // 2
    first = (meta[1] >> 1) == 0
    for p in range(half):
        a, b = own[p] + near[p], own[p + half] + near[p + half]
        low = jnp.concatenate([a[:, :quarter], b[:, :quarter]], axis=1)
        high = jnp.concatenate([a[:, quarter:], b[:, quarter:]], axis=1)
        keep_o[p] = jnp.where(first, low, high)
        send_o[p] = jnp.where(first, high, low)
        edge_o[p] = keep_o[p, :EDGE, :]
        edge_o[half + p] = send_o[p, :EDGE, :]


def conv_taps(grads, raws, gconv_o, seg, count, width):
    seg_main = seg[EDGE : EDGE + count]
    for k in range(width):
        low = EDGE - (width - 1) + k
        mask = jnp.where(seg[low : low + count] == seg_main, 1.0, 0.0)
        gconv_o[k : k + 1, :] += jnp.sum(
            grads * (raws[low : low + count, :] * mask), axis=0, keepdims=True
        )
    gconv_o[width : width + 1, :] += jnp.sum(grads, axis=0, keepdims=True)


def conv_rows(gpad, conv, seg, rows, width):
    total = jnp.zeros((rows, gpad.shape[1]), f32)
    for lag in range(width):
        mask = jnp.where(seg[lag : lag + rows] == seg[:rows], 1.0, 0.0)
        k = width - 1 - lag
        total = total + conv[k : k + 1, :] * (gpad[lag : lag + rows, :] * mask)
    return total


def xback_kernel(dims, meta, lens, *refs):
    packs, count, features, inner, bc, heads, size, width, nseq = dims
    (
        xbc, steps, gy, dx, gkeep, grecv, slope, raw, normed, edge, conv, skip,
        main_o, edge_o, state_sum_o, keep_o, give_o, gconv_o,
        gpad, raws, sums,
    ) = refs
    pack = pl.program_id(0)
    gstate = jnp.concatenate(
        split2(load_state(meta, packs, pack, gkeep, grecv, heads, size)), axis=1
    )
    seg = column_segments(meta, lens, pack, count, nseq, EDGE)
    matrix = spread_matrix(heads, size)
    b_vals = xbc[0, :, inner : inner + bc // 2]
    dt, cum = steps_of(steps[0], heads)
    wide = spread(end_weights(seg, seg[EDGE:], cum, dt, count), matrix, heads)
    u_wide = wide * nt(jnp.concatenate([b_vals, b_vals], axis=1), gstate)
    state_sum_o[0] = collapse(xbc[0, :, :inner].astype(f32) * u_wide, matrix, heads)
    grad_x = (dx[0] + u_wide + gy[0] * skip[...]) * slope[0].astype(f32)

    @pl.when(pack == 0)
    def _():
        for ref in (gconv_o, gpad, edge_o):
            ref[...] = jnp.zeros_like(ref)

    raws[...] = raw[0].astype(f32)
    gpad[EDGE : EDGE + count, :] = grad_x
    conv_taps(grad_x, raws, gconv_o, seg, count, width)
    seg_pad = jnp.concatenate([seg, jnp.full((8, 1), -1, jnp.int32)], axis=0)
    grad_raw = conv_rows(gpad, conv, seg_pad, count + EDGE, width).astype(bf16)
    main_o[0] = grad_raw[EDGE:]
    edge_o[pl.ds(pl.multiple_of(pack * EDGE, EDGE), EDGE), :] = grad_raw[:EDGE]
    term = nn(normed[0], grad_raw[EDGE:]).reshape(sums.shape)

    @pl.when(pack == 0)
    def _():
        sums[...] = term

    @pl.when(pack > 0)
    def _():
        sums[...] += term

    @pl.when(pack == packs - 1)
    def _():
        sums[...] += nn(edge[...], edge_o[...]).reshape(sums.shape)
        side = meta[0] & 1
        keep_o[...] = sums[side]
        give_o[...] = sums[1 - side].astype(bf16)


def conv_bc_kernel(dims, meta, lens, *refs):
    packs, count, features, inner, bc, heads, size, width, nseq = dims
    (
        keep, recv, edge_keep, edge_recv, slope, slope_next, raw, normed, conv,
        rows_o, keep_o, give_o, gconv_o,
        gpad, raws, sums,
    ) = refs
    pack = pl.program_id(0)
    quarter = bc // 4
    early = pack < packs // 2

    @pl.when(pack == 0)
    def _():
        gconv_o[...] = jnp.zeros_like(gconv_o)

    def own_pack(values):
        return jnp.where(early, values[:, :quarter], values[:, quarter:])

    grad = own_pack(keep[0] + recv[0]) * slope[0]
    gpad[:count, :] = grad
    gpad[count:, :] = own_pack(edge_keep[0] + edge_recv[0]) * slope_next[0]
    rows = lax.broadcasted_iota(jnp.int32, (count + 2 * EDGE, 1), 0)
    seg = segments(rows + (meta[0] * count - EDGE), lens, pack, nseq)
    raws[...] = raw[0].astype(f32)
    conv_taps(grad, raws, gconv_o, seg, count, width)
    grad_bc = conv_rows(gpad, conv, seg[EDGE:], count, width).astype(bf16)
    rows_o[0] = grad_bc
    term = nn(normed[0], grad_bc)

    @pl.when(pack == 0)
    def _():
        sums[...] = term

    @pl.when(pack > 0)
    def _():
        sums[...] += term

    @pl.when(pack == packs - 1)
    def _():
        total = jnp.transpose(sums[...])
        first = (meta[0] & 1) == 0
        keep_o[...] = jnp.where(first, total[:, :inner], total[:, inner:])
        give_o[...] = jnp.where(first, total[:, inner:], total[:, :inner]).astype(bf16)


def step_kernel(dims, meta, lens, *refs):
    packs, count, features, inner, bc, heads, size, width, nseq = dims
    (
        steps, sums, state_sums, keep, recv, gkeep, grecv, small, normed, gconv_x, gconv_bc,
        gate_small,
        gdt_o, small_o,
        gdt_sums, gsmall,
    ) = refs
    pack = pl.program_id(0)
    state = load_state(meta, packs, pack, keep, recv, heads, size)
    gstate = load_state(meta, packs, pack, gkeep, grecv, heads, size)
    seg = column_segments(meta, lens, pack, count, nseq, EDGE)
    matrix = spread_matrix(heads, size)
    v = steps[0]
    dt, cum = steps_of(v, heads)
    sig = head_lanes(sigmoid(v), heads)
    row_sum, col_sum = from_group(sums[0], 0, heads), from_group(sums[0], 1, heads)
    state_sum = state_sums[0]
    carry = carry_column(meta, seg, EDGE)
    hi, lo = split2(gstate * state)
    ones = jnp.ones((8, LANES), bf16)
    by_head = collapse(nt(ones, hi) + nt(ones, lo), matrix, heads)[0:1]
    last = by_head * carry[count - 1 :] * jnp.exp(cum[count - 1 :]) + jnp.sum(
        state_sum, axis=0, keepdims=True
    )
    rows = lax.broadcasted_iota(jnp.int32, (count, LANES), 0)
    grad_cum = row_sum - col_sum - state_sum + jnp.where(rows == count - 1, last, 0.0)
    grad_rate = exact_sums(triangle(count, False), grad_cum, heads)
    decay_rate = -jnp.exp(small[1:2, :])
    ratio = jnp.where(dt > 1e-30, sig / jnp.maximum(dt, 1e-30), 1.0)
    grad_dt = head_lanes(ratio * (col_sum + state_sum) + grad_rate * decay_rate * sig, heads)
    low = grad_dt.astype(bf16)
    gdt_o[0] = low

    @pl.when(pack == 0)
    def _():
        for ref in (gsmall, gdt_sums):
            ref[...] = jnp.zeros_like(ref)

    gsmall[0:1, :] += jnp.sum(grad_dt, axis=0, keepdims=True)
    gsmall[1:2, :] += jnp.sum(grad_rate * dt * decay_rate, axis=0, keepdims=True)
    gdt_sums[...] += nn(normed[0], low)

    @pl.when(pack == packs - 1)
    def _():
        taps, quarter = width + 1, bc // 4
        small_o[...] = jnp.zeros_like(small_o)
        small_o[0:heads, :] = jnp.transpose(gdt_sums[...])[0:heads]
        small_o[8 : 8 + taps, :inner] = gconv_x[0:taps, :]
        small_o[8 : 8 + taps, inner : inner + quarter] = gconv_bc[0:taps, :]
        small_o[13:14, :inner] = gate_small[0:1, :]
        skips = collapse(gate_small[...], matrix, heads)
        start = 2 * inner - 3 * LANES
        small_o[13:14, start : start + LANES] = gsmall[0:1, :]
        small_o[13:14, start + LANES : start + 2 * LANES] = gsmall[1:2, :]
        small_o[13:14, start + 2 * LANES :] = skips[1:2, :]


def back_kernel(dims, meta, lens, *refs):
    packs, count, features, inner, bc, heads, size, width, nseq = dims
    (
        main, edge_x, ggate, gdt, gbc, normed, wz, wx, wbc, wdt, gain,
        own_o, far_o, send_o, extra_o,
        stage, gain_sums, gains,
    ) = refs
    pack = pl.program_id(0)
    head = meta[1]
    part = features // 4

    @pl.when(pack == 0)
    def _():
        gain_sums[...] = jnp.zeros_like(gain_sums)
        gains[...] = jnp.zeros_like(gains)

    late = main[0, count - EDGE :, :].astype(f32) + edge_x[...].astype(f32)
    grad_x = jnp.concatenate([main[0, : count - EDGE, :], late.astype(bf16)], axis=0)
    whole = nt(wz[...], ggate[0]) + nt(wx[...], grad_x) + nt(wbc[...], gbc[0]) + nt(wdt[...], gdt[0])
    product = whole * normed[0].astype(f32)
    gain_sums[...] += jnp.sum(product, axis=1, keepdims=True)
    dots = jnp.sum(product, axis=0, keepdims=True)
    stage[...] = whole.reshape(stage.shape)

    @pl.when(pack == packs - 1)
    def _():
        row = jnp.transpose(jnp.broadcast_to(gain_sums[...] / gain[...], (features, LANES)))
        for h in range(4):
            gains[h, 0:1, :part] = row[0:1, h * part : (h + 1) * part]

    own_o[0] = stage[head]
    far_o[0] = stage[head ^ 2]
    extra_o[0, 0:1, :] = dots
    extra_o[0, 1:2, :] = gains[head, 0:1, :]
    extra_o[0, 2:3, :] = gains[head ^ 2, 0:1, :]
    for k in range(2):
        send_o[k, 0, :part, :] = stage[head ^ (1 + 2 * k)].astype(bf16)
        send_o[k, 0, part:, :] = extra_rows(dots, gains[head ^ (1 + 2 * k), 0:1, :])


def extra_rows(*values):
    row = lax.broadcasted_iota(jnp.int32, (EDGE, values[0].shape[1]), 0)
    total = jnp.zeros(row.shape, f32)
    for i, value in enumerate(values):
        for k, piece in enumerate(split3(value)):
            total = total + jnp.where(row == 3 * i + k, piece.astype(f32), 0.0)
    return total.astype(bf16)


def read_extra(block, i):
    rows = block.astype(f32)
    return rows[3 * i : 3 * i + 1] + rows[3 * i + 1 : 3 * i + 2] + rows[3 * i + 2 : 3 * i + 3]


def gather_kernel(own, far, near, extra, own_o, far_o, extra_o):
    part = own.shape[1]
    own_o[0] = own[0] + near[0, 0, :part, :].astype(f32)
    far_o[0, :part, :] = (far[0] + near[1, 0, :part, :].astype(f32)).astype(bf16)
    mine, others = near[0, 0, part:, :], near[1, 0, part:, :]
    dots = extra[0, 0:1, :] + read_extra(mine, 0)
    extra_o[0, 0:1, :] = dots
    extra_o[0, 1:2, :] = extra[0, 1:2, :] + read_extra(mine, 1)
    far_o[0, part:, :] = extra_rows(dots, extra[0, 2:3, :] + read_extra(others, 1))


def final_kernel(dims, own, far, extra, tokens, inv, gain, out_grad, in_grad_o, gain_o):
    packs, count, features = dims
    part = own.shape[1]
    grad = own[0] + far[0, :part, :].astype(f32)
    mean = (extra[0, 0:1, :] + read_extra(far[0, part:, :], 0)) / features
    unit = tokens[0].astype(f32) * inv[0]
    in_grad_o[0] = out_grad[0].astype(f32) + inv[0] * (gain[...] * grad - unit * mean)

    @pl.when(pl.program_id(0) == packs - 1)
    def _():
        gain_o[...] = jnp.broadcast_to(
            extra[0, 1:2, :] + read_extra(far[0, part:, :], 1), gain_o.shape
        )


def add_kernel(bit, halve, segs, count, small, meta, *refs):
    keep, got, refs = refs[:count], refs[count : 2 * count], refs[2 * count :]
    if small:
        refs[-1][...] = refs[0][...] + refs[1][...]
        refs = refs[2:-1]
    read, write = 0, 0
    for i, rows in enumerate(segs):
        if count > 1:
            total = keep[i][...] + got[i][...].astype(f32)
        else:
            total = keep[0][read : read + rows, :].astype(f32) + got[0][read : read + rows, :].astype(f32)
        read += rows
        if halve:
            half = rows // 2
            first = ((meta[0] >> bit) & 1) == 0
            top, bottom = total[:half], total[half:]
            refs[0][write : write + half, :] = jnp.where(first, top, bottom)
            refs[1][write : write + half, :] = jnp.where(first, bottom, top).astype(bf16)
            write += half
        else:
            refs[0][write : write + rows, :] = total.astype(bf16)
            write += rows


def join_kernel(bit, segs, meta, mine, got, out):
    first = ((meta[0] >> bit) & 1) == 0
    read = 0
    for rows in segs:
        a = mine[read : read + rows, :].astype(f32)
        b = got[read : read + rows, :].astype(f32)
        out[2 * read : 2 * read + rows, :] = jnp.where(first, a, b).astype(bf16)
        out[2 * read + rows : 2 * read + 2 * rows, :] = jnp.where(first, b, a).astype(bf16)
        read += rows


def result_kernel(segs, ways, meta, mine, got, *outs):
    first = (meta[0] & 1) == 0
    read = 0
    for rows, way, out in zip(segs, ways, outs):
        a = mine[read : read + rows, :].astype(f32)
        b = got[read : read + rows, :].astype(f32)
        top, bottom = jnp.where(first, a, b), jnp.where(first, b, a)
        if way == "rows":
            out[:rows, :] = top
            out[rows:, :] = bottom
        elif way == "flip":
            out[:, :rows] = jnp.transpose(top)
            out[:, rows:] = jnp.transpose(bottom)
        else:
            out[...] = jnp.concatenate([top, bottom], axis=1)
        read += rows


def whole_spec(shape):
    return pl.BlockSpec(shape, lambda p, *_: (0,) * len(shape))


def pack_spec(shape):
    return pl.BlockSpec((1,) + shape, lambda p, *_: (p,) + (0,) * len(shape))


def half_spec(shape, half):
    return pl.BlockSpec((1,) + shape, lambda p, *_: (p % half,) + (0,) * len(shape))


def side_spec(shape, half, keep):
    def index(p, meta, *_):
        side = meta[0] & 1 if keep else 1 - (meta[0] & 1)
        group = p // half
        spot = jnp.where(group == side, p % half, jnp.where(group < side, 0, half - 1))
        return (spot,) + (0,) * len(shape)

    return pl.BlockSpec((1,) + shape, index)


class Order:
    def __init__(self):
        self.last = ()


order = Order()


def call(kernel, grid, in_specs, out_specs, out_shape, scratch, prefetch, *args, limit=60, wait=(), us=1):
    first = len(prefetch) + len(args)
    held = order.last + tuple(wait)
    late = len(held)

    def body(*refs):
        kernel(*refs[:first], *refs[first + late :])

    outs = pl.pallas_call(
        body,
        grid_spec=pltpu.PrefetchScalarGridSpec(
            num_scalar_prefetch=len(prefetch),
            grid=grid,
            in_specs=list(in_specs) + [pl.BlockSpec(memory_space=pl.ANY)] * late,
            out_specs=out_specs,
            scratch_shapes=scratch,
        ),
        out_shape=out_shape,
        compiler_params=pltpu.CompilerParams(vmem_limit_bytes=limit * MIB),
        cost_estimate=pl.CostEstimate(
            flops=int(us * 10e9), bytes_accessed=int(us * 3e6), transcendentals=0
        ),
    )(*prefetch, *args, *held)
    order.last = (min(jax.tree.leaves(outs), key=lambda x: x.size),)
    return outs


def shape(*dims_and_type):
    return jax.ShapeDtypeStruct(dims_and_type[:-1], dims_and_type[-1])


def scan_states(keep, send, meta, packs, heads, size, rev, beside, waits=lambda: ()):
    dims = (packs, heads, size)
    rows = heads * size
    half = packs // 2
    pay = shape(half, rows + EDGE, LANES, jnp.int16)
    spec = whole_spec(pay.shape)
    bits = (lax.axis_size("seq") - 1).bit_length()
    beside = list(beside)

    def work():
        if beside:
            beside.pop(0)()

    other = swap(send, "seq", 1)
    work()
    total = call(
        functools.partial(pair_kernel, dims, rev), (1,), [spec, spec], spec, pay, [], (meta,),
        keep, other, limit=8,
    )
    before = None
    for bit in range(1, bits):
        got = swap(total, "seq", 1 << bit)
        extra = () if before is None else (before,)
        work()
        if bit < bits - 1:
            total, before = call(
                functools.partial(cube_kernel, dims, rev, bit, before is None), (1,),
                [spec] * (2 + len(extra)), [spec, spec], [pay, pay], [], (meta,),
                total, got, *extra, limit=8,
            )
        else:
            own, back = call(
                functools.partial(last_kernel, dims, rev, bit, before is None), (1,),
                [spec] * (3 + len(extra)), [spec, spec], [pay, pay], [],
                (meta,), keep, other, got, *extra, limit=8, wait=waits(),
            )
    recv = swap(back, "seq", 1)
    while beside:
        work()
    return own, recv


class SeqSum:
    def __init__(self):
        self.keep, self.got, self.segs = [], [], []
        self.small = self.small_got = self.bit = None
        self.bits = list(range(1, (lax.axis_size("seq") - 1).bit_length()))
        self.halved = []

    def put(self, keep, give):
        self.keep.append(keep)
        self.got.append(swap(give, "seq", 1))
        self.segs.append(keep.shape[0])

    def put_small(self, small):
        self.small, self.small_got = small, swap(small, "seq", 1)

    def add(self, meta):
        bit = self.bits.pop(0) if self.bits else None
        halve = bit is not None and all(rows % (2 * EDGE) == 0 for rows in self.segs)
        cols = self.keep[0].shape[1]
        segs = [rows // 2 for rows in self.segs] if halve else self.segs
        rows = sum(segs)
        low = shape(rows, cols, bf16)
        out = [shape(rows, cols, f32), low] if halve else [low]
        small = [] if self.small is None else [self.small, self.small_got]
        if small:
            out.append(shape(*self.small.shape, f32))
        ins = [*self.keep, *self.got, *small]
        outs = call(
            functools.partial(add_kernel, bit, halve, self.segs, len(self.keep), bool(small)), (1,),
            [whole_spec(x.shape) for x in ins], [whole_spec(x.shape) for x in out], out, [],
            (meta,), *ins, limit=12,
        )
        if small:
            self.small = outs[-1]
        self.segs, self.keep = segs, [outs[0]]
        if bit is None:
            return True
        self.got = [swap(outs[1] if halve else outs[0], "seq", 1 << bit)]
        if small:
            self.small_got = swap(self.small, "seq", 1 << bit)
        if halve:
            self.halved.append(bit)
        return False

    def send_back(self):
        self.bit = self.halved.pop() if self.halved else 0
        self.got = [swap(self.keep[0], "seq", 1 << self.bit)]

    def join(self, meta):
        rows, cols = self.keep[0].shape
        both = shape(2 * rows, cols, bf16)
        spec = whole_spec((rows, cols))
        self.keep = [call(
            functools.partial(join_kernel, self.bit, self.segs), (1,), [spec, spec],
            whole_spec(both.shape), both, [], (meta,), self.keep[0], self.got[0], limit=12,
        )]
        self.segs = [2 * rows for rows in self.segs]

    def result(self, meta, ways):
        cols = self.keep[0].shape[1]
        shapes = {"rows": lambda r: (2 * r, cols), "flip": lambda r: (cols, 2 * r), "cols": lambda r: (r, 2 * cols)}
        out = [shape(*shapes[way](rows), f32) for way, rows in zip(ways, self.segs)]
        spec = whole_spec(self.keep[0].shape)
        return call(
            functools.partial(result_kernel, self.segs, ways), (1,), [spec, spec],
            [whole_spec(x.shape) for x in out], out, [], (meta,), self.keep[0], self.got[0],
            limit=16,
            us=2,
        )


def advance(total, meta):
    if total.bit is None:
        if total.add(meta):
            total.send_back()
    elif total.bit:
        total.join(meta)
        total.send_back()


def sum_over(x, axis):
    bit = 1
    while bit < lax.axis_size(axis):
        x = x + swap(x, axis, bit)
        bit *= 2
    return x


def shards(
    tokens_in, out_grad, lengths, norm_gain, proj_z, proj_x, proj_bc, proj_dt, conv_x, conv_bc,
    bias_x, bias_bc, dt_bias, a_log, d_skip, gate_gain, proj_out,
):
    packs, count, part = tokens_in.shape
    features, inner = proj_x.shape
    heads = proj_dt.shape[1]
    size = inner // heads
    width = conv_x.shape[0]
    nseq = lengths.shape[1]
    bc_part = proj_bc.shape[1]
    bc = bc_part * lax.axis_size("head")
    half = packs // 2
    chans = inner + bc
    ext = count + EDGE
    rows = heads * size
    total_inner = inner * lax.axis_size("head")
    dims = (packs, count, features, inner, bc, heads, size, width, nseq)
    seq_place, head_place = lax.axis_index("seq"), lax.axis_index("head")
    meta = jnp.stack([seq_place, head_place]).astype(jnp.int32)
    pre = (meta, lengths)
    grid = (packs,)

    order.last = ()
    tokens = jnp.swapaxes(tokens_in, 1, 2)
    cotangent = jnp.swapaxes(out_grad, 1, 2)
    token_pieces = head_pieces(tokens)
    tail = jnp.concatenate([tokens[p, :, count - EDGE :] for p in range(packs)], axis=1)
    tail = jnp.pad(tail, ((0, 0), (0, LANES - packs * EDGE)))
    edge_pieces = head_pieces(shift(tail, "seq", 1))
    extra = jnp.concatenate(
        [conv_bc.T, bias_bc[:, None], norm_gain.reshape(-1, bc_part).T], axis=1
    )
    extra = jnp.pad(extra, ((0, 0), (0, LANES - extra.shape[1])))
    weight_pieces = head_pieces(jnp.concatenate([proj_bc.T, extra], axis=1))
    conv_own = jnp.pad(
        jnp.concatenate([conv_x, bias_x[None]], axis=0).astype(f32), ((0, 7 - width), (0, 0))
    )
    conv_bc_own = jnp.pad(
        jnp.concatenate([conv_bc, bias_bc[None]], axis=0).astype(f32), ((0, 7 - width), (0, 0))
    )
    w_dt = jnp.pad(proj_dt, ((0, 0), (0, LANES - heads)))
    small = jnp.pad(jnp.stack([dt_bias, a_log]).astype(f32), ((0, 6), (0, LANES - heads)))
    skip = jnp.repeat(d_skip.astype(f32), size)[None]
    gain_gate = gate_gain.astype(f32)[None]

    lane_spec = pack_spec((count, LANES))
    chan_spec = pack_spec((count, inner))
    xbc_spec = pack_spec((count, chans))
    model_spec = pack_spec((features, count))
    piece_spec = pack_spec((part, count))
    edge_spec = whole_spec((part, LANES))
    pay_shape = (rows + EDGE, LANES)
    pay_specs = [side_spec(pay_shape, half, k) for k in (True, False)]
    pay = shape(half, *pay_shape, jnp.int16)
    state_spec = half_spec(pay_shape, half)
    vec = whole_spec((1, inner))
    square = whole_spec((features, inner))

    (
        normed, inv, edge, raw_x, raw_bc, xbc, steps, keep, send, gain_all,
    ) = call(
        functools.partial(front_kernel, dims),
        grid,
        [piece_spec] * 4
        + [edge_spec] * 4
        + [whole_spec((bc_part, features + LANES))] * 4
        + [square, whole_spec((LANES, features)), whole_spec((8, inner)),
           whole_spec((8, LANES))],
        [
            model_spec, pack_spec((1, count)), whole_spec((features, LANES)),
            pack_spec((ext, inner)), pack_spec((ext, bc_part)), xbc_spec, lane_spec, *pay_specs,
            whole_spec((features, 1)),
        ],
        [
            shape(packs, features, count, bf16), shape(packs, 1, count, f32),
            shape(features, LANES, bf16), shape(packs, ext, inner, bf16),
            shape(packs, ext, bc_part, bf16), shape(packs, count, chans, bf16),
            shape(packs, count, LANES, f32), pay, pay, shape(features, 1, f32),
        ],
        [
            pltpu.VMEM((4, part, count), bf16), pltpu.VMEM((4, part, LANES), bf16),
            pltpu.VMEM((4, bc_part, features + LANES), bf16), pltpu.VMEM((ext, chans), f32),
            pltpu.VMEM((LANES, chans), f32), pltpu.VMEM((8, chans), f32),
            pltpu.VMEM((features, 1), f32),
        ],
        pre,
        *token_pieces, *edge_pieces, *weight_pieces, proj_x, w_dt.T, conv_own, small,
        us=15,
    )

    cots = head_pieces(lax.optimization_barrier((cotangent, steps))[0])
    kept = {}

    def inner_work():
        kept["inner"] = call(
            functools.partial(inner_kernel, dims),
            grid,
            [xbc_spec, lane_spec],
            chan_spec,
            shape(packs, count, inner, f32),
            [],
            pre,
            xbc, steps,
            us=6,
        )

    def cot_work():
        kept["cot"], kept["gg"] = call(
            functools.partial(cot_kernel, dims),
            grid,
            [piece_spec] * 4 + [whole_spec((inner, features))],
            [model_spec, chan_spec],
            [shape(packs, features, count, bf16), shape(packs, count, inner, f32)],
            [pltpu.VMEM((4, part, count), bf16)],
            pre,
            *cots, proj_out,
            us=5.5,
        )

    def gate_slope_work():
        kept["slope"] = call(
            functools.partial(gate_slope_kernel, dims),
            grid,
            [model_spec, square, pack_spec((ext, inner)), pack_spec((ext, bc_part)),
             whole_spec((8, inner)), whole_spec((8, bc_part))],
            [chan_spec, chan_spec, pack_spec((count, bc_part))],
            [shape(packs, count, inner, bf16), shape(packs, count, inner, f32),
             shape(packs, count, bc_part, f32)],
            [pltpu.VMEM((ext, inner), f32), pltpu.VMEM((ext, bc_part), f32)],
            pre,
            normed, proj_z, raw_x, raw_bc, conv_own, conv_bc_own,
            us=7,
        )

    state_keep, state_recv = scan_states(
        keep, send, meta, packs, heads, size, 0, (inner_work, cot_work, gate_slope_work)
    )
    inner_out, cot, gg = kept["inner"], kept["cot"], kept["gg"]
    gate, slope_x, slope_bc = kept["slope"]
    slope_next = shift(slope_bc[:, :EDGE], "seq", -1)

    y, stats = call(
        functools.partial(gate_kernel, dims),
        grid,
        [
            xbc_spec, lane_spec, chan_spec, state_spec, state_spec, chan_spec, chan_spec, vec, vec,
        ],
        [chan_spec, pack_spec((2, count))],
        [shape(packs, count, inner, f32), shape(packs, 2, count, f32)],
        [],
        pre,
        xbc, steps, inner_out, state_keep, state_recv, gate, gg, gain_gate, skip,
        us=6.6,
    )
    stats_all = lax.all_gather(stats, "head")

    gy, gated, ggate, gkeep, gsend, gate_small = call(
        functools.partial(grad_kernel, dims, total_inner),
        grid,
        [
            pl.BlockSpec((4, 1, 2, count), lambda p, *_: (0, p, 0, 0)),
            xbc_spec, lane_spec, chan_spec, chan_spec, chan_spec, vec, vec,
        ],
        [chan_spec] * 3 + pay_specs + [whole_spec((8, inner))],
        [shape(packs, count, inner, f32)] + [shape(packs, count, inner, bf16)] * 2
        + [pay, pay, shape(8, inner, f32)],
        [],
        pre,
        stats_all, xbc, steps, y, gate, gg, gain_gate, skip,
        us=8.3,
    )

    piece_shape = shape(packs, part, count, f32)
    send_spec = pl.BlockSpec((2, 1, part, count), lambda p, *_: (0, p, 0, 0))
    rows_half = features // 2
    half_specs = [whole_spec((rows_half, inner))] * 2
    half_shapes = [shape(rows_half, inner, f32), shape(rows_half, inner, bf16)]
    half_sums = pltpu.VMEM((2, rows_half, inner), f32)

    early_sum, late_sum = SeqSum(), SeqSum()

    def out_work():
        *kept["out"], keep, give = call(
            functools.partial(out_kernel, dims),
            grid,
            [chan_spec, model_spec, whole_spec((inner, features))],
            [piece_spec, piece_spec, send_spec] + half_specs,
            [piece_shape, piece_shape, shape(2, packs, part, count, bf16)] + half_shapes,
            [pltpu.VMEM((4, part, count), f32), half_sums],
            pre,
            gated, cot, proj_out,
            us=6.8,
        )
        early_sum.put(keep, give)

    def z_work():
        keep, give = call(
            functools.partial(z_kernel, dims),
            grid,
            [model_spec, chan_spec],
            half_specs,
            half_shapes,
            [half_sums],
            pre,
            normed, ggate,
            us=5.3,
        )
        early_sum.put(keep, give)

    def diag_work():
        kept["diag"] = call(
            functools.partial(diag_kernel, dims),
            grid,
            [xbc_spec, lane_spec, chan_spec, chan_spec, state_spec, state_spec],
            [chan_spec, pack_spec((count, bc)), lane_spec],
            [
                shape(packs, count, inner, f32), shape(packs, count, bc, f32),
                shape(packs, count, LANES, f32),
            ],
            [],
            pre,
            xbc, steps, gy, y, state_keep, state_recv,
            us=12,
        )

    gstate_keep, gstate_recv = scan_states(
        gkeep, gsend, meta, packs, heads, size, 1, (out_work, z_work, diag_work, lambda: early_sum.add(meta)),
        lambda: early_sum.got,
    )
    out_own, out_far, out_send = kept["out"]
    dx, dbc, sums = kept["diag"]

    def to_far(far, near):
        return swap((far + near[1].astype(f32)).astype(bf16), "head", 2)

    near = swap(out_send, "head", 1)
    block_out = tokens.astype(f32) + out_own + near[0].astype(f32) + to_far(out_far, near).astype(f32)
    block_out = jnp.swapaxes(block_out.astype(bf16), 1, 2)

    share_own, share_near = call(
        functools.partial(share_kernel, dims),
        grid,
        [xbc_spec, lane_spec, pack_spec((count, bc)), state_spec, state_spec],
        [lane_spec, lane_spec],
        [shape(packs, count, LANES, f32)] * 2,
        [],
        pre,
        xbc, steps, dbc, gstate_keep, gstate_recv,
        us=6.4,
    )
    share_near = swap(share_near, "head", 1)
    advance(early_sum, meta)
    two = shape(half, count, LANES, f32)
    rows_out = shape(packs, EDGE, LANES, f32)
    bc_keep, bc_send, bc_edge = call(
        functools.partial(middle_kernel, (packs, bc_part)),
        (1,),
        [whole_spec((packs, count, LANES))] * 2,
        [whole_spec(two.shape)] * 2 + [whole_spec(rows_out.shape)],
        [two, two, rows_out],
        [],
        (meta,),
        share_own, share_near,
        limit=8,
    )
    bc_recv = swap(bc_send, "head", 2)
    bc_edge = shift(bc_edge, "seq", -1)
    bc_edge_recv = swap(bc_edge, "head", 2)


    main_x, edge_x, state_sums, keep, give, grad_conv = call(
        functools.partial(xback_kernel, dims),
        grid,
        [
            xbc_spec, lane_spec, chan_spec, chan_spec, state_spec, state_spec, chan_spec,
            pack_spec((ext, inner)), model_spec, whole_spec((features, LANES)),
            whole_spec((8, inner)), vec,
        ],
        [chan_spec, whole_spec((LANES, inner)), lane_spec] + half_specs + [whole_spec((8, inner))],
        [
            shape(packs, count, inner, bf16), shape(LANES, inner, bf16),
            shape(packs, count, LANES, f32), *half_shapes, shape(8, inner, f32),
        ],
        [
            pltpu.VMEM((ext + EDGE, inner), f32), pltpu.VMEM((ext, inner), f32), half_sums,
        ],
        pre,
        xbc, steps, gy, dx, gstate_keep, gstate_recv, slope_x, raw_x, normed, edge, conv_own, skip,
        us=12.5,
    )
    late_sum.put(keep, give)
    edge_x = shift(edge_x, "seq", -1)
    advance(early_sum, meta)

    def half_block(shape_of, first):
        return pl.BlockSpec(
            (1,) + shape_of, lambda p, *_: (p % half + first,) + (0,) * len(shape_of)
        )

    edge_rows = (EDGE, LANES)
    bc_half = (bc_part, inner)
    gbc, keep, give, grad_conv_bc = call(
        functools.partial(conv_bc_kernel, dims),
        grid,
        [
            half_block((count, LANES), 0), half_block((count, LANES), 0),
            half_block(edge_rows, 0), half_block(edge_rows, half),
            pack_spec((count, bc_part)), pack_spec((EDGE, bc_part)), pack_spec((ext, bc_part)),
            model_spec, whole_spec((8, bc_part)),
        ],
        [pack_spec((count, bc_part)), whole_spec(bc_half), whole_spec(bc_half),
         whole_spec((8, bc_part))],
        [
            shape(packs, count, bc_part, bf16), shape(*bc_half, f32), shape(*bc_half, bf16),
            shape(8, bc_part, f32),
        ],
        [
            pltpu.VMEM((count + EDGE, bc_part), f32), pltpu.VMEM((ext, bc_part), f32),
            pltpu.VMEM((features, bc_part), f32),
        ],
        pre,
        bc_keep, bc_recv, bc_edge, bc_edge_recv, slope_bc, slope_next, raw_bc, normed, conv_bc_own,
        us=6.3,
    )
    late_sum.put(keep, give)

    gdt, smalls = call(
        functools.partial(step_kernel, dims),
        grid,
        [
            lane_spec, lane_spec, lane_spec, state_spec, state_spec, state_spec, state_spec,
            whole_spec((8, LANES)), model_spec, whole_spec((8, inner)), whole_spec((8, bc_part)),
            whole_spec((8, inner)),
        ],
        [lane_spec, whole_spec((EDGE, features))],
        [shape(packs, count, LANES, bf16), shape(EDGE, features, f32)],
        [pltpu.VMEM((features, LANES), f32), pltpu.VMEM((8, LANES), f32)],
        pre,
        steps, sums, state_sums, state_keep, state_recv, gstate_keep, gstate_recv, small, normed,
        grad_conv, grad_conv_bc, gate_small,
        us=8,
    )
    late_sum.put_small(smalls)
    advance(early_sum, meta)

    tall = part + EDGE
    send_spec = pl.BlockSpec((2, 1, tall, count), lambda p, *_: (0, p, 0, 0))
    tall_spec = pack_spec((tall, count))
    extra_spec = pack_spec((8, count))
    extra_shape = shape(packs, 8, count, f32)
    gn_own, gn_far, gn_send, extra = call(
        functools.partial(back_kernel, dims),
        grid,
        [
            chan_spec, pl.BlockSpec((EDGE, inner), lambda p, *_: (p, 0)), chan_spec, lane_spec,
            pack_spec((count, bc_part)), model_spec, square, square,
            whole_spec((features, bc_part)), whole_spec((features, LANES)),
            whole_spec((features, 1)),
        ],
        [piece_spec, piece_spec, send_spec, extra_spec],
        [piece_shape, piece_shape, shape(2, packs, tall, count, bf16), extra_shape],
        [
            pltpu.VMEM((4, part, count), f32), pltpu.VMEM((features, 1), f32),
            pltpu.VMEM((4, 8, count), f32),
        ],
        pre,
        main_x, edge_x, ggate, gdt, gbc, normed, proj_z, proj_x, proj_bc, w_dt, gain_all,
        us=8.3,
    )
    near = swap(gn_send, "head", 1)
    advance(late_sum, meta)

    gn_own, gn_far, extra = call(
        gather_kernel,
        grid,
        [piece_spec, piece_spec, send_spec, extra_spec],
        [piece_spec, tall_spec, extra_spec],
        [piece_shape, shape(packs, tall, count, bf16), extra_shape],
        [],
        (),
        gn_own, gn_far, near, extra,
        us=3.8,
    )
    gn_far = swap(gn_far, "head", 2)
    advance(early_sum, meta)
    advance(late_sum, meta)
    while early_sum.bit != 0:
        advance(early_sum, meta)
    advance(late_sum, meta)
    in_grad, grad_gain = call(
        functools.partial(final_kernel, (packs, count, features)),
        grid,
        [
            piece_spec, tall_spec, extra_spec, piece_spec, pack_spec((1, count)),
            whole_spec((part, 1)), piece_spec,
        ],
        [piece_spec, whole_spec((8, count))],
        [piece_shape, shape(8, count, f32)],
        [],
        (),
        gn_own, gn_far, extra, tokens, inv, norm_gain.astype(f32)[:, None], cotangent,
        us=4,
    )
    in_grad = jnp.swapaxes(in_grad, 1, 2)
    advance(late_sum, meta)
    grads_out, grads_z = early_sum.result(meta, ("flip", "rows"))
    while late_sum.bit != 0:
        advance(late_sum, meta)
    grads_x, grad_bc = late_sum.result(meta, ("rows", "cols"))
    smalls = late_sum.small
    grad_gain = sum_over(grad_gain, "seq")[0, :part]
    grad_conv, grad_conv_bc = smalls[8:13, :inner], smalls[8:13, inner : inner + bc_part]
    start = 2 * inner - 3 * LANES
    per_head = [smalls[13, start + k * LANES : start + k * LANES + heads] for k in range(3)]
    return (
        block_out,
        in_grad,
        grad_gain,
        grads_z,
        grads_x,
        grad_bc.T,
        smalls[:heads].T,
        grad_conv[:width],
        grad_conv_bc[:width],
        grad_conv[width],
        grad_conv_bc[width],
        *per_head,
        smalls[13, :inner],
        grads_out,
    )


def solution(mesh):
    token, column, vector = P(None, "seq", "head"), P(None, "head"), P("head")
    row = P("head", None)
    return jax.shard_map(
        shards,
        mesh=mesh,
        in_specs=(
            token, token, P(), vector, column, column, column, column, column, column, vector,
            vector, vector, vector, vector, vector, row,
        ),
        out_specs=(
            token, token, vector, column, column, column, column, column, column, vector, vector,
            vector, vector, vector, vector, row,
        ),
        check_vma=False,
    )
```

```python
import functools

import jax
import jax.numpy as jnp
from jax import lax
from jax.experimental import pallas as pl
from jax.experimental.pallas import tpu as pltpu
from jax.sharding import PartitionSpec as P

EPSILON = 1e-05
bf16 = jnp.bfloat16
f32 = jnp.float32
LANES = 128
EDGE = 16
MIB = 1024 * 1024
STEPS = 32000.0
UNIT = 16384.0
LN2 = 0.6931471805599453
GROUP = 16


def permuted(x, axis, route):
    y = lax.ppermute(x, axis, route)
    order.near.append(y)
    return y


def swap(x, axis, bit):
    return permuted(x, axis, [(i, i ^ bit) for i in range(lax.axis_size(axis))])


def shift(x, axis, distance):
    n = lax.axis_size(axis)
    return permuted(x, axis, [(i, i + distance) for i in range(n) if 0 <= i + distance < n])


def head_pieces(x):
    far = swap(x, "head", 2)
    near = swap(x, "head", 1)
    return x, near, far, swap(far, "head", 1)


def nn(a, b):
    return lax.dot_general(a, b, (((1,), (0,)), ((), ())), preferred_element_type=f32)


def nt(a, b):
    return lax.dot_general(a, b, (((1,), (1,)), ((), ())), preferred_element_type=f32)


def tn(a, b):
    return lax.dot_general(a, b, (((0,), (0,)), ((), ())), preferred_element_type=f32)


def split2(v):
    hi = v.astype(bf16)
    return hi, (v - hi.astype(f32)).astype(bf16)


def split3(v):
    hi = v.astype(bf16)
    rest = v - hi.astype(f32)
    mid = rest.astype(bf16)
    return hi, mid, (rest - mid.astype(f32)).astype(bf16)


def spread_matrix(heads, size):
    row = lax.broadcasted_iota(jnp.int32, (LANES, heads * size), 0)
    col = lax.broadcasted_iota(jnp.int32, (LANES, heads * size), 1)
    first = (col >= row * size) & (col < (row + 1) * size)
    again = (col >= (row - GROUP) * size) & (col < (row - GROUP + 1) * size)
    return jnp.where(first | again, 1.0, 0.0).astype(bf16)


def spread(v, matrix, heads):
    hi, lo = split2(head_lanes(v, heads))
    return nn((hi.astype(f32) + to_group(lo.astype(f32), 1)).astype(bf16), matrix)


def head_lanes(v, heads):
    return jnp.where(lax.broadcasted_iota(jnp.int32, v.shape, 1) < heads, v, 0.0)


def to_group(v, k):
    return pltpu.roll(v, k * GROUP, 1)


def from_group(v, k, heads):
    return head_lanes(pltpu.roll(v, LANES - k * GROUP, 1) if k else v, heads)


def collapse(v, matrix, heads):
    return head_lanes(nt(jnp.concatenate(split2(v), axis=1), jnp.concatenate([matrix] * 2, axis=1)), heads)


def triangle(count, lower):
    row = lax.broadcasted_iota(jnp.int32, (count, count), 0)
    col = lax.broadcasted_iota(jnp.int32, (count, count), 1)
    keep = (row >= col) if lower else (row <= col)
    return jnp.where(keep, 1.0, 0.0).astype(bf16)


def exact_sums(matrix, v, heads):
    hi, mid, lo = [piece.astype(f32) for piece in split3(v)]
    sums = nn(matrix, (hi + to_group(mid, 1) + to_group(lo, 2)).astype(bf16))
    return from_group(sums, 0, heads) + from_group(sums, 1, heads) + from_group(sums, 2, heads)


def step_sizes(v, heads):
    soft = jnp.maximum(v, 0.0) + jnp.log1p(jnp.exp(-jnp.abs(v)))
    return head_lanes(soft, heads)


def steps_of(block, heads):
    return step_sizes(block, heads), from_group(block, 1, heads)


def segments(positions, lens_ref, pack, count):
    total = jnp.zeros(positions.shape, jnp.int32)
    end = jnp.int32(0)
    for k in range(count):
        end = end + lens_ref[pack, k]
        total = total + jnp.where(positions >= end, 1, 0)
    return total


def column_segments(meta_ref, lens_ref, pack, count, nseq, before):
    rows = lax.broadcasted_iota(jnp.int32, (count + before, 1), 0)
    return segments(rows + (meta_ref[0] * count - before), lens_ref, pack, nseq)


def row_segments(meta_ref, lens_ref, pack, count, nseq):
    cols = lax.broadcasted_iota(jnp.int32, (1, count), 1)
    return segments(cols + meta_ref[0] * count, lens_ref, pack, nseq)


def carry_column(meta_ref, seg_ext, before):
    same = seg_ext[before:] == seg_ext[before - 1 : before]
    return jnp.where(same & (meta_ref[0] > 0), 1.0, 0.0)


def to_int16(v):
    return jnp.floor(v + 0.5).astype(jnp.int32).astype(jnp.int16)


def encode_state(out, p, state, decay, heads, size):
    lane = lax.broadcasted_iota(jnp.int32, (1, LANES), 1)
    powers = jnp.zeros((1, LANES), f32)
    for h in range(heads):
        part = state[h * size : (h + 1) * size]
        top = jnp.max(jnp.max(jnp.abs(part), axis=0, keepdims=True), axis=1, keepdims=True)
        power = jnp.ceil(jnp.log(jnp.maximum(top, 1e-30)) / LN2)
        powers = powers + jnp.where(lane == h, power, 0.0)
        codes = jnp.clip(part * (jnp.exp(-power * LN2) * STEPS), -32767.0, 32767.0)
        out[p, h * size : (h + 1) * size, :] = to_int16(codes)
    row = lax.broadcasted_iota(jnp.int32, (EDGE, LANES), 0)
    coarse = jnp.floor(decay * UNIT)
    fine = (decay * UNIT - coarse) * UNIT
    tail = jnp.where(row == 0, powers, jnp.where(row == 1, coarse, jnp.where(row == 2, fine, 0.0)))
    out[p, heads * size :, :] = to_int16(tail)


def decode_state(block, heads, size):
    values = block.astype(jnp.int32).astype(f32)
    tail = values[heads * size :]
    scale = jnp.exp(tail[0:1] * LN2) / STEPS
    decay = (tail[1:2] + tail[2:3] / UNIT) / UNIT
    return scaled_state(values[: heads * size], scale, heads, size), decay


def sigmoid(v):
    return 1.0 / (1.0 + jnp.exp(-v))


def scaled_state(state, decay, heads, size):
    return jnp.concatenate(
        [state[h * size : (h + 1) * size] * decay[:, h : h + 1] for h in range(heads)], axis=0
    )


def front_kernel(dims, meta, lens, *refs):
    packs, count, features, inner, bc, heads, size, width, nseq = dims
    tokens, edges, shared = refs[0:4], refs[4:8], refs[8:12]
    wx, wdt, conv_x, small = refs[12:16]
    normed_o, inv_o, edge_o, rawx_o, rawbc_o, xbc_o, steps_o, keep_o, send_o, gain_o = refs[16:26]
    stage, edge_stage, weights, raws, edge_raws, conv, gain = refs[26:]
    pack = pl.program_id(0)
    head = meta[1]
    part = features // 4
    wide = edge_stage.shape[2]

    def normalise(values):
        mean = jnp.sum(values * values, axis=0, keepdims=True) / features
        inv = lax.rsqrt(mean + EPSILON)
        return inv, ((values * inv) * gain[...]).astype(bf16)

    def raw_of(normed):
        wbc = weights[...].reshape(bc, weights.shape[2])[:, :features]
        return jnp.concatenate([nn(normed, wx[...]), nt(normed, wbc)], axis=1).astype(bf16)

    @pl.when(pack == 0)
    def _():
        for k in range(4):
            weights[head ^ k] = shared[k][...]
            edge_stage[head ^ k] = edges[k][...]
        extra = weights[...].reshape(bc, weights.shape[2])[:, features:].astype(f32)
        conv[:, :inner] = conv_x[...]
        conv[:, inner:] = jnp.transpose(extra)[0:8]
        bc_part = bc // 4
        pieces = part // bc_part
        for h in range(4):
            for c in range(pieces):
                gain[h * part + c * bc_part : h * part + (c + 1) * bc_part, :] = extra[
                    h * bc_part : (h + 1) * bc_part, width + 1 + c : width + 2 + c
                ]
        _, normed = normalise(edge_stage[...].reshape(features, wide).astype(f32))
        gain_o[...] = gain[...]
        edge_o[...] = normed
        edge_raws[...] = raw_of(jnp.transpose(normed)).astype(f32)

    for k in range(4):
        stage[head ^ k] = tokens[k][0]
    inv, normed_t = normalise(stage[...].reshape(features, count).astype(f32))
    inv_o[0] = inv
    normed_o[0] = normed_t
    normed = jnp.transpose(normed_t)
    raws[EDGE:, :] = raw_of(normed).astype(f32)
    raws[0:EDGE, :] = edge_raws[pl.ds(pl.multiple_of(pack * EDGE, EDGE), EDGE), :]

    def own_bc(values):
        bc_part = bc // 4
        parts = [values[:, inner + h * bc_part : inner + (h + 1) * bc_part] for h in range(4)]
        low = jnp.where((head & 1) == 0, parts[0], parts[1])
        high = jnp.where((head & 1) == 0, parts[2], parts[3])
        return jnp.where((head >> 1) == 0, low, high)

    rawx_o[0] = raws[:, :inner].astype(bf16)
    rawbc_o[0] = own_bc(raws[...]).astype(bf16)
    seg = column_segments(meta, lens, pack, count, nseq, EDGE)
    seg_main = seg[EDGE:]
    pre = convolved(raws, conv, seg, count, width)
    xbc = (pre * sigmoid(pre)).astype(bf16)
    xbc_o[0] = xbc
    v = head_lanes(nt(normed, wdt[...]).astype(bf16).astype(f32) + small[0:1, :], heads)
    dt = step_sizes(v, heads)
    rate = -dt * jnp.exp(small[1:2, :])
    cum = exact_sums(triangle(count, True), rate, heads)
    steps_o[0] = v + to_group(cum, 1)
    cum_end = cum[count - 1 : count]
    weight = jnp.where(seg_main == seg[count + EDGE - 1 :], jnp.exp(cum_end - cum), 0.0) * dt
    matrix = spread_matrix(heads, size)
    scaled = (xbc[:, :inner].astype(f32) * spread(weight, matrix, heads)).astype(bf16)
    state = tn(scaled, xbc[:, inner : inner + bc // 2])
    carry = carry_column(meta, seg, EDGE)
    store_state(
        meta, packs, pack, keep_o, send_o, state, carry[count - 1 :] * jnp.exp(cum_end), heads, size
    )


def convolved(raws, conv, seg, count, width):
    pre = jnp.broadcast_to(conv[width : width + 1, :], (count, raws.shape[1]))
    for k in range(width):
        low = EDGE - (width - 1) + k
        mask = jnp.where(seg[low : low + count] == seg[EDGE:], 1.0, 0.0)
        pre = pre + conv[k : k + 1, :] * raws[low : low + count, :] * mask
    return pre


def gate_slope_kernel(dims, meta, lens, *refs):
    packs, count, features, inner, bc, heads, size, width, nseq = dims
    normed, wz, raw_x, raw_bc, conv_x, conv_bc, gate_o, slope_x_o, slope_bc_o, raws, raws_bc = refs
    pack = pl.program_id(0)
    gate_o[0] = tn(normed[0], wz[...]).astype(bf16)
    seg = column_segments(meta, lens, pack, count, nseq, EDGE)
    for raw, wide, conv, out in ((raw_x, raws, conv_x, slope_x_o), (raw_bc, raws_bc, conv_bc, slope_bc_o)):
        wide[...] = raw[0].astype(f32)
        pre = convolved(wide, conv, seg, count, width)
        sig = sigmoid(pre)
        out[0] = sig * (1.0 + pre * (1.0 - sig))


def store_state(meta, packs, pack, keep_o, send_o, state, decay, heads, size):
    mine = (pack // (packs // 2)) == (meta[0] & 1)

    @pl.when(mine)
    def _():
        encode_state(keep_o, 0, state, decay, heads, size)

    @pl.when(jnp.logical_not(mine))
    def _():
        encode_state(send_o, 0, state, decay, heads, size)


def load_state(meta, packs, pack, keep, recv, heads, size):
    mine = (pack // (packs // 2)) == (meta[0] & 1)
    block = jnp.where(mine, keep[0].astype(jnp.int32), recv[0].astype(jnp.int32))
    return decode_state(block, heads, size)[0]


def decay_parts(cum_col, cum_row, masked):
    return masked * jnp.exp(jnp.minimum(cum_col - cum_row, 0.0))


def block_mask(meta, lens, pack, count, nseq):
    col = column_segments(meta, lens, pack, count, nseq, 0)
    row = row_segments(meta, lens, pack, count, nseq)
    tri = lax.broadcasted_iota(jnp.int32, (count, count), 0) >= lax.broadcasted_iota(
        jnp.int32, (count, count), 1
    )
    return tri & (col == row)


def inner_kernel(dims, meta, lens, *refs):
    packs, count, features, inner, bc, heads, size, width, nseq = dims
    xbc, steps, inner_o = refs
    pack = pl.program_id(0)
    half = bc // 2
    b_vals, c_vals = xbc[0, :, inner : inner + half], xbc[0, :, inner + half :]
    scores = jnp.where(block_mask(meta, lens, pack, count, nseq), nt(c_vals, b_vals), 0.0)
    dt, cum_col = steps_of(steps[0], heads)
    cum_row = jnp.transpose(cum_col)
    dt_row = jnp.transpose(dt)
    lane = lax.broadcasted_iota(jnp.int32, (count, 2 * size), 1)
    for pair in range(heads // 2):
        cols = slice(2 * pair * size, (2 * pair + 2) * size)
        x_pair = xbc[0, :, cols]
        parts = []
        for h in (2 * pair, 2 * pair + 1):
            weights = decay_parts(cum_col[:, h : h + 1], cum_row[h : h + 1], scores)
            parts.append(nn((weights * dt_row[h : h + 1]).astype(bf16), x_pair))
        inner_o[0, :, cols] = jnp.where(lane < size, parts[0], parts[1])


def cot_kernel(dims, meta, lens, *refs):
    packs, count, features, inner, bc, heads, size, width, nseq = dims
    pieces, (wout, cot_o, gg_o, stage) = refs[:4], refs[4:]
    for k in range(4):
        stage[meta[1] ^ k] = pieces[k][0]
    cotangent = stage[...].reshape(features, count)
    cot_o[0] = cotangent
    gg_o[0] = jnp.transpose(nn(wout[...], cotangent))


def compose(lower, upper, heads, size):
    return scaled_state(lower[0], upper[1], heads, size) + upper[0], lower[1] * upper[1]


def choose(flag, a, b):
    return jnp.where(flag, a[0], b[0]), jnp.where(flag, a[1], b[1])


def pair_kernel(dims, rev, meta, own, other, out):
    packs, heads, size = dims
    upper_is_own = ((meta[0] & 1) ^ rev) == 1
    for p in range(packs // 2):
        a, b = decode_state(own[p], heads, size), decode_state(other[p], heads, size)
        both = compose(choose(upper_is_own, b, a), choose(upper_is_own, a, b), heads, size)
        encode_state(out, p, *both, heads, size)


def entering_from(before, b, p, heads, size):
    if before is None:
        return (jnp.zeros_like(b[0]), jnp.ones_like(b[1])), b
    entering = decode_state(before[p], heads, size)
    return entering, compose(b, entering, heads, size)


def cube_kernel(dims, rev, bit, first, meta, *refs):
    packs, heads, size = dims
    total, other = refs[0], refs[1]
    before, next_o, before_o = (None, refs[2], refs[3]) if first else refs[2:5]
    upper_is_own = (((meta[0] >> bit) & 1) ^ rev) == 1
    for p in range(packs // 2):
        a, b = decode_state(total[p], heads, size), decode_state(other[p], heads, size)
        both = compose(choose(upper_is_own, b, a), choose(upper_is_own, a, b), heads, size)
        encode_state(next_o, p, *both, heads, size)
        entering, longer = entering_from(before, b, p, heads, size)
        encode_state(before_o, p, *choose(upper_is_own, longer, entering), heads, size)


def last_kernel(dims, rev, bit, first, meta, *refs):
    packs, heads, size = dims
    own, pair, other = refs[0:3]
    before, keep_o, send_o = (None, refs[3], refs[4]) if first else refs[3:6]
    add = (((meta[0] >> bit) & 1) ^ rev) == 1
    upper_is_own = ((meta[0] & 1) ^ rev) == 1
    for p in range(packs // 2):
        entering, longer = entering_from(
            before, decode_state(other[p], heads, size), p, heads, size
        )
        low = choose(add, longer, entering)
        lower = decode_state(jnp.where(upper_is_own, pair[p].astype(jnp.int32), own[p].astype(jnp.int32)), heads, size)
        high = compose(low, lower, heads, size)
        encode_state(keep_o, p, *choose(upper_is_own, high, low), heads, size)
        encode_state(send_o, p, *choose(upper_is_own, low, high), heads, size)


def gate_kernel(dims, meta, lens, *refs):
    packs, count, features, inner, bc, heads, size, width, nseq = dims
    xbc, steps, inner_in, keep, recv, gate, gg, gain, skip, y_o, stats_o = refs
    pack = pl.program_id(0)
    state = jnp.concatenate(
        split2(load_state(meta, packs, pack, keep, recv, heads, size)), axis=1
    )
    carry = carry_column(meta, column_segments(meta, lens, pack, count, nseq, EDGE), EDGE)
    matrix = spread_matrix(heads, size)
    entering = spread(carry * jnp.exp(from_group(steps[0], 1, heads)), matrix, heads)
    c_vals = xbc[0, :, inner + bc // 2 :]
    y = inner_in[0] + entering * nt(jnp.concatenate([c_vals, c_vals], axis=1), state)
    y_o[0] = y
    gate_f = gate[0].astype(f32)
    ssd = y + xbc[0, :, :inner].astype(f32) * skip[...]
    mixed = ssd * (gate_f * sigmoid(gate_f))
    squares = jnp.sum(mixed * mixed, axis=1, keepdims=True)
    dots = jnp.sum(gain[...] * gg[0] * mixed, axis=1, keepdims=True)
    lane = lax.broadcasted_iota(jnp.int32, (count, LANES), 1)
    both = jnp.where(lane == 0, squares, 0.0) + jnp.where(lane == 1, dots, 0.0)
    stats_o[0] = jnp.transpose(both)[0:2]


def grad_kernel(dims, total_inner, meta, lens, *refs):
    packs, count, features, inner, bc, heads, size, width, nseq = dims
    (
        stats, xbc, steps, y, gate, gg, gain, skip,
        gy_o, gated_o, ggate_o, keep_o, send_o, small_o,
    ) = refs
    pack = pl.program_id(0)
    sums = stats[0, 0] + stats[1, 0] + stats[2, 0] + stats[3, 0]
    row = lax.broadcasted_iota(jnp.int32, (LANES, count), 0)
    wide = jnp.where(row == 0, sums[0:1], 0.0) + jnp.where(row == 1, sums[1:2], 0.0)
    cols = jnp.transpose(wide)
    inv = lax.rsqrt(cols[:, 0:1] / total_inner + EPSILON)
    dot = cols[:, 1:2] / total_inner
    x_f, gg_f, gate_f = xbc[0, :, :inner].astype(f32), gg[0], gate[0].astype(f32)
    ssd = y[0] + x_f * skip[...]
    sig = sigmoid(gate_f)
    act = gate_f * sig
    mixed = ssd * act
    scaled = mixed * inv
    gated_o[0] = (scaled * gain[...]).astype(bf16)
    grad_mixed = inv * gain[...] * gg_f - mixed * (inv * inv * inv * dot)
    gy_f = grad_mixed * act
    gy_o[0] = gy_f
    ggate_o[0] = (grad_mixed * ssd * sig * (1.0 + gate_f * (1.0 - sig))).astype(bf16)
    carry = carry_column(meta, column_segments(meta, lens, pack, count, nseq, EDGE), EDGE)
    cum = from_group(steps[0], 1, heads)
    entering = carry * jnp.exp(cum)
    ey_hi, ey_lo = split2(gy_f * spread(entering, spread_matrix(heads, size), heads))
    c_vals = xbc[0, :, inner + bc // 2 :]
    state_grad = tn(ey_hi, c_vals) + tn(ey_lo, c_vals)
    store_state(
        meta, packs, pack, keep_o, send_o, state_grad, entering[count - 1 :], heads, size
    )

    @pl.when(pack == 0)
    def _():
        small_o[...] = jnp.zeros_like(small_o)

    small_o[0:1, :] += jnp.sum(gg_f * scaled, axis=0, keepdims=True)
    small_o[1:2, :] += jnp.sum(gy_f * x_f, axis=0, keepdims=True)


def diag_kernel(dims, meta, lens, *refs):
    packs, count, features, inner, bc, heads, size, width, nseq = dims
    xbc, steps, gy, y, keep, recv, dx_o, dbc_o, sums_o = refs
    pack = pl.program_id(0)
    half = bc // 2
    b_vals, c_vals = xbc[0, :, inner : inner + half], xbc[0, :, inner + half :]
    mask = block_mask(meta, lens, pack, count, nseq)
    scores = jnp.where(mask, nt(c_vals, b_vals), 0.0)
    dt, cum_col = steps_of(steps[0], heads)
    cum_row = jnp.transpose(cum_col)
    dt_row = jnp.transpose(dt)
    lane = lax.broadcasted_iota(jnp.int32, (count, 2 * size), 1)
    grad_scores = jnp.zeros((count, count), f32)
    zero = jnp.zeros((), bf16)
    for pair in range(heads // 2):
        cols = slice(2 * pair * size, (2 * pair + 2) * size)
        x_pair = xbc[0, :, cols]
        x_twice = jnp.concatenate([x_pair, x_pair], axis=1)
        gy_hi, gy_lo = split2(gy[0, :, cols])
        gy_wide = jnp.concatenate([gy_hi, gy_lo], axis=1)
        parts = []
        for h in (2 * pair, 2 * pair + 1):
            own = (lane < size) if h % 2 == 0 else (lane >= size)
            part = jnp.exp(jnp.minimum(cum_col[:, h : h + 1] - cum_row[h : h + 1], 0.0)) * dt_row[h : h + 1]
            parts.append(tn((scores * part).astype(bf16), gy_wide))
            both = jnp.concatenate([jnp.where(own, gy_hi, zero), jnp.where(own, gy_lo, zero)], axis=1)
            grad_scores = grad_scores + nt(both, x_twice) * part
        two = [part[:, : 2 * size] + part[:, 2 * size :] for part in parts]
        dx_o[0, :, cols] = jnp.where(lane < size, two[0], two[1])
    hi, lo = split2(jnp.where(mask, grad_scores, 0.0))
    state_hi, state_lo = split2(load_state(meta, packs, pack, keep, recv, heads, size))
    carry = carry_column(meta, column_segments(meta, lens, pack, count, nseq, EDGE), EDGE)
    matrix = spread_matrix(heads, size)
    ey_hi, ey_lo = split2(gy[0] * spread(carry * jnp.exp(cum_col), matrix, heads))
    dbc_o[0, :, :half] = tn(hi, c_vals) + tn(lo, c_vals)
    dbc_o[0, :, half:] = (
        nn(jnp.concatenate([hi, lo], axis=1), jnp.concatenate([b_vals, b_vals], axis=0))
        + nn(ey_hi, state_hi) + nn(ey_hi, state_lo) + nn(ey_lo, state_hi)
    )
    row_sum = collapse(gy[0] * y[0], matrix, heads)
    col_sum = collapse(xbc[0, :, :inner].astype(f32) * dx_o[0], matrix, heads)
    sums_o[0] = row_sum + to_group(col_sum, 1)


def scatter_pieces(head, stage, own_o, far_o, send_o):
    own_o[0] = stage[head]
    send_o[0, 0] = stage[head ^ 1].astype(bf16)
    far_o[0] = stage[head ^ 2]
    send_o[1, 0] = stage[head ^ 3].astype(bf16)


def accumulate(meta, pack, packs, sums, term, keep_o, send_o):
    wide = term.reshape(sums.shape)

    @pl.when(pack == 0)
    def _():
        sums[...] = wide

    @pl.when(pack > 0)
    def _():
        sums[...] += wide

    @pl.when(pack == packs - 1)
    def _():
        side = meta[0] & 1
        keep_o[...] = sums[side]
        send_o[...] = sums[1 - side].astype(bf16)


def out_kernel(dims, meta, lens, *refs):
    packs, count, features, inner, bc, heads, size, width, nseq = dims
    gated, cot, wout, own_o, far_o, send_o, keep_o, give_o, stage, sums = refs
    pack = pl.program_id(0)
    stage[...] = tn(wout[...], jnp.transpose(gated[0])).reshape(stage.shape)
    scatter_pieces(meta[1], stage, own_o, far_o, send_o)
    accumulate(meta, pack, packs, sums, nn(cot[0], gated[0]), keep_o, give_o)


def z_kernel(dims, meta, lens, *refs):
    normed, ggate, keep_o, give_o, sums = refs
    accumulate(
        meta, pl.program_id(0), dims[0], sums, nn(normed[0], ggate[0]), keep_o, give_o
    )


def end_weights(seg, seg_main, cum_col, dt_col, count):
    cum_end = cum_col[count - 1 :]
    end = seg[count + EDGE - 1 :]
    return jnp.where(seg_main == end, jnp.exp(cum_end - cum_col), 0.0) * dt_col


def share_kernel(dims, meta, lens, *refs):
    packs, count, features, inner, bc, heads, size, width, nseq = dims
    xbc, steps, dbc, gkeep, grecv, own_o, near_o = refs
    pack = pl.program_id(0)
    half, quarter = bc // 2, bc // 4
    g_hi, g_lo = split2(load_state(meta, packs, pack, gkeep, grecv, heads, size))
    seg = column_segments(meta, lens, pack, count, nseq, EDGE)
    dt, cum = steps_of(steps[0], heads)
    wide = spread(end_weights(seg, seg[EDGE:], cum, dt, count), spread_matrix(heads, size), heads)
    hi, lo = split2(wide * xbc[0, :, :inner].astype(f32))
    grad_b = dbc[0, :, :half] + nn(hi, g_hi) + nn(lo, g_hi) + nn(hi, g_lo)
    grad_c = dbc[0, :, half:]
    even = jnp.concatenate([grad_b[:, :quarter], grad_c[:, :quarter]], axis=1)
    odd = jnp.concatenate([grad_b[:, quarter:], grad_c[:, quarter:]], axis=1)
    first = (meta[1] & 1) == 0
    own_o[0] = jnp.where(first, even, odd)
    near_o[0] = jnp.where(first, odd, even)


def middle_kernel(dims, meta, *refs):
    packs, quarter = dims
    own, near, keep_o, send_o, edge_o = refs
    half = packs // 2
    first = (meta[1] >> 1) == 0
    for p in range(half):
        a, b = own[p] + near[p], own[p + half] + near[p + half]
        low = jnp.concatenate([a[:, :quarter], b[:, :quarter]], axis=1)
        high = jnp.concatenate([a[:, quarter:], b[:, quarter:]], axis=1)
        keep_o[p] = jnp.where(first, low, high)
        send_o[p] = jnp.where(first, high, low)
        edge_o[p] = keep_o[p, :EDGE, :]
        edge_o[half + p] = send_o[p, :EDGE, :]


def conv_taps(grads, raws, gconv_o, seg, count, width):
    seg_main = seg[EDGE : EDGE + count]
    for k in range(width):
        low = EDGE - (width - 1) + k
        mask = jnp.where(seg[low : low + count] == seg_main, 1.0, 0.0)
        gconv_o[k : k + 1, :] += jnp.sum(
            grads * (raws[low : low + count, :] * mask), axis=0, keepdims=True
        )
    gconv_o[width : width + 1, :] += jnp.sum(grads, axis=0, keepdims=True)


def conv_rows(gpad, conv, seg, rows, width):
    total = jnp.zeros((rows, gpad.shape[1]), f32)
    for lag in range(width):
        mask = jnp.where(seg[lag : lag + rows] == seg[:rows], 1.0, 0.0)
        k = width - 1 - lag
        total = total + conv[k : k + 1, :] * (gpad[lag : lag + rows, :] * mask)
    return total


def xback_kernel(dims, meta, lens, *refs):
    packs, count, features, inner, bc, heads, size, width, nseq = dims
    (
        xbc, steps, gy, dx, gkeep, grecv, slope, raw, normed, edge, conv, skip,
        main_o, edge_o, state_sum_o, keep_o, give_o, gconv_o,
        gpad, raws, sums,
    ) = refs
    pack = pl.program_id(0)
    gstate = jnp.concatenate(
        split2(load_state(meta, packs, pack, gkeep, grecv, heads, size)), axis=1
    )
    seg = column_segments(meta, lens, pack, count, nseq, EDGE)
    matrix = spread_matrix(heads, size)
    b_vals = xbc[0, :, inner : inner + bc // 2]
    dt, cum = steps_of(steps[0], heads)
    wide = spread(end_weights(seg, seg[EDGE:], cum, dt, count), matrix, heads)
    u_wide = wide * nt(jnp.concatenate([b_vals, b_vals], axis=1), gstate)
    state_sum_o[0] = collapse(xbc[0, :, :inner].astype(f32) * u_wide, matrix, heads)
    grad_x = (dx[0] + u_wide + gy[0] * skip[...]) * slope[0].astype(f32)

    @pl.when(pack == 0)
    def _():
        for ref in (gconv_o, gpad, edge_o):
            ref[...] = jnp.zeros_like(ref)

    raws[...] = raw[0].astype(f32)
    gpad[EDGE : EDGE + count, :] = grad_x
    conv_taps(grad_x, raws, gconv_o, seg, count, width)
    seg_pad = jnp.concatenate([seg, jnp.full((8, 1), -1, jnp.int32)], axis=0)
    grad_raw = conv_rows(gpad, conv, seg_pad, count + EDGE, width).astype(bf16)
    main_o[0] = grad_raw[EDGE:]
    edge_o[pl.ds(pl.multiple_of(pack * EDGE, EDGE), EDGE), :] = grad_raw[:EDGE]
    term = nn(normed[0], grad_raw[EDGE:]).reshape(sums.shape)

    @pl.when(pack == 0)
    def _():
        sums[...] = term

    @pl.when(pack > 0)
    def _():
        sums[...] += term

    @pl.when(pack == packs - 1)
    def _():
        sums[...] += nn(edge[...], edge_o[...]).reshape(sums.shape)
        side = meta[0] & 1
        keep_o[...] = sums[side]
        give_o[...] = sums[1 - side].astype(bf16)


def conv_bc_kernel(dims, meta, lens, *refs):
    packs, count, features, inner, bc, heads, size, width, nseq = dims
    (
        keep, recv, edge_keep, edge_recv, slope, slope_next, raw, normed, conv,
        rows_o, keep_o, give_o, gconv_o,
        gpad, raws, sums,
    ) = refs
    pack = pl.program_id(0)
    quarter = bc // 4
    early = pack < packs // 2

    @pl.when(pack == 0)
    def _():
        gconv_o[...] = jnp.zeros_like(gconv_o)

    def own_pack(values):
        return jnp.where(early, values[:, :quarter], values[:, quarter:])

    grad = own_pack(keep[0] + recv[0]) * slope[0]
    gpad[:count, :] = grad
    gpad[count:, :] = own_pack(edge_keep[0] + edge_recv[0]) * slope_next[0]
    rows = lax.broadcasted_iota(jnp.int32, (count + 2 * EDGE, 1), 0)
    seg = segments(rows + (meta[0] * count - EDGE), lens, pack, nseq)
    raws[...] = raw[0].astype(f32)
    conv_taps(grad, raws, gconv_o, seg, count, width)
    grad_bc = conv_rows(gpad, conv, seg[EDGE:], count, width).astype(bf16)
    rows_o[0] = grad_bc
    term = nn(normed[0], grad_bc)

    @pl.when(pack == 0)
    def _():
        sums[...] = term

    @pl.when(pack > 0)
    def _():
        sums[...] += term

    @pl.when(pack == packs - 1)
    def _():
        total = jnp.transpose(sums[...])
        first = (meta[0] & 1) == 0
        keep_o[...] = jnp.where(first, total[:, :inner], total[:, inner:])
        give_o[...] = jnp.where(first, total[:, inner:], total[:, :inner]).astype(bf16)


def step_kernel(dims, meta, lens, *refs):
    packs, count, features, inner, bc, heads, size, width, nseq = dims
    (
        steps, sums, state_sums, keep, recv, gkeep, grecv, small, normed, gconv_x, gconv_bc,
        gate_small,
        gdt_o, small_o,
        gdt_sums, gsmall,
    ) = refs
    pack = pl.program_id(0)
    state = load_state(meta, packs, pack, keep, recv, heads, size)
    gstate = load_state(meta, packs, pack, gkeep, grecv, heads, size)
    seg = column_segments(meta, lens, pack, count, nseq, EDGE)
    matrix = spread_matrix(heads, size)
    v = steps[0]
    dt, cum = steps_of(v, heads)
    sig = head_lanes(sigmoid(v), heads)
    row_sum, col_sum = from_group(sums[0], 0, heads), from_group(sums[0], 1, heads)
    state_sum = state_sums[0]
    carry = carry_column(meta, seg, EDGE)
    hi, lo = split2(gstate * state)
    ones = jnp.ones((8, LANES), bf16)
    by_head = collapse(nt(ones, hi) + nt(ones, lo), matrix, heads)[0:1]
    last = by_head * carry[count - 1 :] * jnp.exp(cum[count - 1 :]) + jnp.sum(
        state_sum, axis=0, keepdims=True
    )
    rows = lax.broadcasted_iota(jnp.int32, (count, LANES), 0)
    grad_cum = row_sum - col_sum - state_sum + jnp.where(rows == count - 1, last, 0.0)
    grad_rate = exact_sums(triangle(count, False), grad_cum, heads)
    decay_rate = -jnp.exp(small[1:2, :])
    ratio = jnp.where(dt > 1e-30, sig / jnp.maximum(dt, 1e-30), 1.0)
    grad_dt = head_lanes(ratio * (col_sum + state_sum) + grad_rate * decay_rate * sig, heads)
    low = grad_dt.astype(bf16)
    gdt_o[0] = low

    @pl.when(pack == 0)
    def _():
        for ref in (gsmall, gdt_sums):
            ref[...] = jnp.zeros_like(ref)

    gsmall[0:1, :] += jnp.sum(grad_dt, axis=0, keepdims=True)
    gsmall[1:2, :] += jnp.sum(grad_rate * dt * decay_rate, axis=0, keepdims=True)
    gdt_sums[...] += nn(normed[0], low)

    @pl.when(pack == packs - 1)
    def _():
        taps, quarter = width + 1, bc // 4
        small_o[...] = jnp.zeros_like(small_o)
        small_o[0:heads, :] = jnp.transpose(gdt_sums[...])[0:heads]
        small_o[8 : 8 + taps, :inner] = gconv_x[0:taps, :]
        small_o[8 : 8 + taps, inner : inner + quarter] = gconv_bc[0:taps, :]
        small_o[13:14, :inner] = gate_small[0:1, :]
        skips = collapse(gate_small[...], matrix, heads)
        start = 2 * inner - 3 * LANES
        small_o[13:14, start : start + LANES] = gsmall[0:1, :]
        small_o[13:14, start + LANES : start + 2 * LANES] = gsmall[1:2, :]
        small_o[13:14, start + 2 * LANES :] = skips[1:2, :]


def back_kernel(dims, meta, lens, *refs):
    packs, count, features, inner, bc, heads, size, width, nseq = dims
    (
        main, edge_x, ggate, gdt, gbc, normed, wz, wx, wbc, wdt, gain,
        own_o, far_o, send_o, extra_o,
        stage, gain_sums, gains,
    ) = refs
    pack = pl.program_id(0)
    head = meta[1]
    part = features // 4

    @pl.when(pack == 0)
    def _():
        gain_sums[...] = jnp.zeros_like(gain_sums)
        gains[...] = jnp.zeros_like(gains)

    late = main[0, count - EDGE :, :].astype(f32) + edge_x[...].astype(f32)
    grad_x = jnp.concatenate([main[0, : count - EDGE, :], late.astype(bf16)], axis=0)
    whole = nt(wz[...], ggate[0]) + nt(wx[...], grad_x) + nt(wbc[...], gbc[0]) + nt(wdt[...], gdt[0])
    product = whole * normed[0].astype(f32)
    gain_sums[...] += jnp.sum(product, axis=1, keepdims=True)
    dots = jnp.sum(product, axis=0, keepdims=True)
    stage[...] = whole.reshape(stage.shape)

    @pl.when(pack == packs - 1)
    def _():
        row = jnp.transpose(jnp.broadcast_to(gain_sums[...] / gain[...], (features, LANES)))
        for h in range(4):
            gains[h, 0:1, :part] = row[0:1, h * part : (h + 1) * part]

    own_o[0] = stage[head]
    far_o[0] = stage[head ^ 2]
    extra_o[0, 0:1, :] = dots
    extra_o[0, 1:2, :] = gains[head, 0:1, :]
    extra_o[0, 2:3, :] = gains[head ^ 2, 0:1, :]
    for k in range(2):
        send_o[k, 0, :part, :] = stage[head ^ (1 + 2 * k)].astype(bf16)
        send_o[k, 0, part:, :] = extra_rows(dots, gains[head ^ (1 + 2 * k), 0:1, :])


def extra_rows(*values):
    row = lax.broadcasted_iota(jnp.int32, (EDGE, values[0].shape[1]), 0)
    total = jnp.zeros(row.shape, f32)
    for i, value in enumerate(values):
        for k, piece in enumerate(split3(value)):
            total = total + jnp.where(row == 3 * i + k, piece.astype(f32), 0.0)
    return total.astype(bf16)


def read_extra(block, i):
    rows = block.astype(f32)
    return rows[3 * i : 3 * i + 1] + rows[3 * i + 1 : 3 * i + 2] + rows[3 * i + 2 : 3 * i + 3]


def gather_kernel(own, far, near, extra, own_o, far_o, extra_o):
    part = own.shape[1]
    own_o[0] = own[0] + near[0, 0, :part, :].astype(f32)
    far_o[0, :part, :] = (far[0] + near[1, 0, :part, :].astype(f32)).astype(bf16)
    mine, others = near[0, 0, part:, :], near[1, 0, part:, :]
    dots = extra[0, 0:1, :] + read_extra(mine, 0)
    extra_o[0, 0:1, :] = dots
    extra_o[0, 1:2, :] = extra[0, 1:2, :] + read_extra(mine, 1)
    far_o[0, part:, :] = extra_rows(dots, extra[0, 2:3, :] + read_extra(others, 1))


def final_kernel(dims, own, far, extra, tokens, inv, gain, out_grad, in_grad_o, gain_o):
    packs, count, features = dims
    part = own.shape[1]
    grad = own[0] + far[0, :part, :].astype(f32)
    mean = (extra[0, 0:1, :] + read_extra(far[0, part:, :], 0)) / features
    unit = tokens[0].astype(f32) * inv[0]
    in_grad_o[0] = out_grad[0].astype(f32) + inv[0] * (gain[...] * grad - unit * mean)

    @pl.when(pl.program_id(0) == packs - 1)
    def _():
        gain_o[...] = jnp.broadcast_to(
            extra[0, 1:2, :] + read_extra(far[0, part:, :], 1), gain_o.shape
        )


def add_kernel(bit, halve, segs, count, small, meta, *refs):
    keep, got, refs = refs[:count], refs[count : 2 * count], refs[2 * count :]
    if small:
        refs[-1][...] = refs[0][...] + refs[1][...]
        refs = refs[2:-1]
    read, write = 0, 0
    for i, rows in enumerate(segs):
        if count > 1:
            total = keep[i][...] + got[i][...].astype(f32)
        else:
            total = keep[0][read : read + rows, :].astype(f32) + got[0][read : read + rows, :].astype(f32)
        read += rows
        if halve:
            half = rows // 2
            first = ((meta[0] >> bit) & 1) == 0
            top, bottom = total[:half], total[half:]
            refs[0][write : write + half, :] = jnp.where(first, top, bottom)
            refs[1][write : write + half, :] = jnp.where(first, bottom, top).astype(bf16)
            write += half
        else:
            refs[0][write : write + rows, :] = total.astype(bf16)
            write += rows


def join_kernel(bit, segs, meta, mine, got, out):
    first = ((meta[0] >> bit) & 1) == 0
    read = 0
    for rows in segs:
        a = mine[read : read + rows, :].astype(f32)
        b = got[read : read + rows, :].astype(f32)
        out[2 * read : 2 * read + rows, :] = jnp.where(first, a, b).astype(bf16)
        out[2 * read + rows : 2 * read + 2 * rows, :] = jnp.where(first, b, a).astype(bf16)
        read += rows


def result_kernel(segs, ways, meta, mine, got, *outs):
    first = (meta[0] & 1) == 0
    read = 0
    for rows, way, out in zip(segs, ways, outs):
        a = mine[read : read + rows, :].astype(f32)
        b = got[read : read + rows, :].astype(f32)
        top, bottom = jnp.where(first, a, b), jnp.where(first, b, a)
        if way == "rows":
            out[:rows, :] = top
            out[rows:, :] = bottom
        elif way == "flip":
            out[:, :rows] = jnp.transpose(top)
            out[:, rows:] = jnp.transpose(bottom)
        else:
            out[...] = jnp.concatenate([top, bottom], axis=1)
        read += rows


def whole_spec(shape):
    return pl.BlockSpec(shape, lambda p, *_: (0,) * len(shape))


def pack_spec(shape):
    return pl.BlockSpec((1,) + shape, lambda p, *_: (p,) + (0,) * len(shape))


def half_spec(shape, half):
    return pl.BlockSpec((1,) + shape, lambda p, *_: (p % half,) + (0,) * len(shape))


def side_spec(shape, half, keep):
    def index(p, meta, *_):
        side = meta[0] & 1 if keep else 1 - (meta[0] & 1)
        group = p // half
        spot = jnp.where(group == side, p % half, jnp.where(group < side, 0, half - 1))
        return (spot,) + (0,) * len(shape)

    return pl.BlockSpec((1,) + shape, index)


class Order:
    def __init__(self):
        self.clear()

    def clear(self):
        self.last, self.near = (), []

    def placed(self, x):
        return pltpu.with_memory_space_constraint(x, pltpu.VMEM) if self.holds(x) else x

    def holds(self, x):
        return any(x is y for y in self.near)


order = Order()


def call(
    kernel, grid, in_specs, out_specs, out_shape, scratch, prefetch, *args, limit=20, wait=(), us=1,
    out=False,
):
    first = len(prefetch) + len(args)
    held = order.last + tuple(wait)
    late = len(held)
    single = not isinstance(out_shape, (list, tuple))
    out_specs, out_shape = ([out_specs], [out_shape]) if single else (list(out_specs), list(out_shape))
    token = jax.ShapeDtypeStruct((8, LANES), f32)
    count = len(out_shape)

    def body(*refs):
        ins, rest = refs[:first], refs[first + late :]
        kernel(*ins, *rest[:count], *rest[count + 1 :])

    *outs, order_out = pl.pallas_call(
        body,
        grid_spec=pltpu.PrefetchScalarGridSpec(
            num_scalar_prefetch=len(prefetch),
            grid=grid,
            in_specs=list(in_specs) + [pl.BlockSpec(memory_space=pl.ANY)] * late,
            out_specs=out_specs + [whole_spec(token.shape)],
            scratch_shapes=scratch,
        ),
        out_shape=(out_shape if out else [pltpu.VMEM(x.shape, x.dtype) for x in out_shape])
        + [pltpu.VMEM(token.shape, token.dtype)],
        compiler_params=pltpu.CompilerParams(vmem_limit_bytes=limit * MIB),
        cost_estimate=pl.CostEstimate(
            flops=int(us * 10e9), bytes_accessed=int(us * 3e6), transcendentals=0
        ),
    )(*prefetch, *[order.placed(x) for x in args], *[order.placed(x) for x in held])
    order.last = (order_out,)
    order.near.append(order_out)
    if not out:
        order.near += outs
    return outs[0] if single else outs


def shape(*dims_and_type):
    return jax.ShapeDtypeStruct(dims_and_type[:-1], dims_and_type[-1])


def scan_states(keep, send, meta, packs, heads, size, rev, beside, waits=lambda: ()):
    dims = (packs, heads, size)
    rows = heads * size
    half = packs // 2
    pay = shape(half, rows + EDGE, LANES, jnp.int16)
    spec = whole_spec(pay.shape)
    bits = (lax.axis_size("seq") - 1).bit_length()
    beside = list(beside)

    def work():
        if beside:
            beside.pop(0)()

    other = swap(send, "seq", 1)
    work()
    total = call(
        functools.partial(pair_kernel, dims, rev), (1,), [spec, spec], spec, pay, [], (meta,),
        keep, other,
    )
    before = None
    for bit in range(1, bits):
        got = swap(total, "seq", 1 << bit)
        extra = () if before is None else (before,)
        work()
        if bit < bits - 1:
            total, before = call(
                functools.partial(cube_kernel, dims, rev, bit, before is None), (1,),
                [spec] * (2 + len(extra)), [spec, spec], [pay, pay], [], (meta,),
                total, got, *extra,
            )
        else:
            own, back = call(
                functools.partial(last_kernel, dims, rev, bit, before is None), (1,),
                [spec] * (3 + len(extra)), [spec, spec], [pay, pay], [],
                (meta,), keep, other, got, *extra, wait=waits(),
            )
    recv = swap(back, "seq", 1)
    while beside:
        work()
    return own, recv


class SeqSum:
    def __init__(self):
        self.keep, self.got, self.segs = [], [], []
        self.small = self.small_got = self.bit = None
        self.bits = list(range(1, (lax.axis_size("seq") - 1).bit_length()))
        self.halved = []

    def put(self, keep, give):
        self.keep.append(keep)
        self.got.append(swap(give, "seq", 1))
        self.segs.append(keep.shape[0])

    def put_small(self, small):
        self.small, self.small_got = small, swap(small, "seq", 1)

    def add(self, meta):
        bit = self.bits.pop(0) if self.bits else None
        halve = bit is not None and all(rows % (2 * EDGE) == 0 for rows in self.segs)
        cols = self.keep[0].shape[1]
        segs = [rows // 2 for rows in self.segs] if halve else self.segs
        rows = sum(segs)
        low = shape(rows, cols, bf16)
        out = [shape(rows, cols, f32), low] if halve else [low]
        small = [] if self.small is None else [self.small, self.small_got]
        if small:
            out.append(shape(*self.small.shape, f32))
        ins = [*self.keep, *self.got, *small]
        outs = call(
            functools.partial(add_kernel, bit, halve, self.segs, len(self.keep), bool(small)), (1,),
            [whole_spec(x.shape) for x in ins], [whole_spec(x.shape) for x in out], out, [],
            (meta,), *ins,
        )
        if small:
            self.small = outs[-1]
        self.segs, self.keep = segs, [outs[0]]
        if bit is None:
            return True
        self.got = [swap(outs[1] if halve else outs[0], "seq", 1 << bit)]
        if small:
            self.small_got = swap(self.small, "seq", 1 << bit)
        if halve:
            self.halved.append(bit)
        return False

    def send_back(self):
        self.bit = self.halved.pop() if self.halved else 0
        self.got = [swap(self.keep[0], "seq", 1 << self.bit)]

    def join(self, meta):
        rows, cols = self.keep[0].shape
        both = shape(2 * rows, cols, bf16)
        spec = whole_spec((rows, cols))
        self.keep = [call(
            functools.partial(join_kernel, self.bit, self.segs), (1,), [spec, spec],
            whole_spec(both.shape), both, [], (meta,), self.keep[0], self.got[0],
        )]
        self.segs = [2 * rows for rows in self.segs]

    def result(self, meta, ways):
        cols = self.keep[0].shape[1]
        shapes = {"rows": lambda r: (2 * r, cols), "flip": lambda r: (cols, 2 * r), "cols": lambda r: (r, 2 * cols)}
        out = [shape(*shapes[way](rows), f32) for way, rows in zip(ways, self.segs)]
        spec = whole_spec(self.keep[0].shape)
        return call(
            functools.partial(result_kernel, self.segs, ways), (1,), [spec, spec],
            [whole_spec(x.shape) for x in out], out, [], (meta,), self.keep[0], self.got[0],
            out=True, us=2,
        )


def advance(total, meta):
    if total.bit is None:
        if total.add(meta):
            total.send_back()
    elif total.bit:
        total.join(meta)
        total.send_back()


def sum_over(x, axis):
    bit = 1
    while bit < lax.axis_size(axis):
        x = x + swap(x, axis, bit)
        bit *= 2
    return x


def shards(
    tokens_in, out_grad, lengths, norm_gain, proj_z, proj_x, proj_bc, proj_dt, conv_x, conv_bc,
    bias_x, bias_bc, dt_bias, a_log, d_skip, gate_gain, proj_out,
):
    packs, count, part = tokens_in.shape
    features, inner = proj_x.shape
    heads = proj_dt.shape[1]
    size = inner // heads
    width = conv_x.shape[0]
    nseq = lengths.shape[1]
    bc_part = proj_bc.shape[1]
    bc = bc_part * lax.axis_size("head")
    half = packs // 2
    chans = inner + bc
    ext = count + EDGE
    rows = heads * size
    total_inner = inner * lax.axis_size("head")
    dims = (packs, count, features, inner, bc, heads, size, width, nseq)
    seq_place, head_place = lax.axis_index("seq"), lax.axis_index("head")
    meta = jnp.stack([seq_place, head_place]).astype(jnp.int32)
    pre = (meta, lengths)
    grid = (packs,)

    order.clear()
    tokens = jnp.swapaxes(tokens_in, 1, 2)
    cotangent = jnp.swapaxes(out_grad, 1, 2)
    token_pieces = head_pieces(tokens)
    tail = jnp.concatenate([tokens[p, :, count - EDGE :] for p in range(packs)], axis=1)
    tail = jnp.pad(tail, ((0, 0), (0, LANES - packs * EDGE)))
    edge_pieces = head_pieces(shift(tail, "seq", 1))
    extra = jnp.concatenate(
        [conv_bc.T, bias_bc[:, None], norm_gain.reshape(-1, bc_part).T], axis=1
    )
    extra = jnp.pad(extra, ((0, 0), (0, LANES - extra.shape[1])))
    weight_pieces = head_pieces(jnp.concatenate([proj_bc.T, extra], axis=1))
    conv_own = jnp.pad(
        jnp.concatenate([conv_x, bias_x[None]], axis=0).astype(f32), ((0, 7 - width), (0, 0))
    )
    conv_bc_own = jnp.pad(
        jnp.concatenate([conv_bc, bias_bc[None]], axis=0).astype(f32), ((0, 7 - width), (0, 0))
    )
    w_dt = jnp.pad(proj_dt, ((0, 0), (0, LANES - heads)))
    small = jnp.pad(jnp.stack([dt_bias, a_log]).astype(f32), ((0, 6), (0, LANES - heads)))
    skip = jnp.repeat(d_skip.astype(f32), size)[None]
    gain_gate = gate_gain.astype(f32)[None]

    lane_spec = pack_spec((count, LANES))
    chan_spec = pack_spec((count, inner))
    xbc_spec = pack_spec((count, chans))
    model_spec = pack_spec((features, count))
    piece_spec = pack_spec((part, count))
    edge_spec = whole_spec((part, LANES))
    pay_shape = (rows + EDGE, LANES)
    pay_specs = [side_spec(pay_shape, half, k) for k in (True, False)]
    pay = shape(half, *pay_shape, jnp.int16)
    state_spec = half_spec(pay_shape, half)
    vec = whole_spec((1, inner))
    square = whole_spec((features, inner))

    (
        normed, inv, edge, raw_x, raw_bc, xbc, steps, keep, send, gain_all,
    ) = call(
        functools.partial(front_kernel, dims),
        grid,
        [piece_spec] * 4
        + [edge_spec] * 4
        + [whole_spec((bc_part, features + LANES))] * 4
        + [square, whole_spec((LANES, features)), whole_spec((8, inner)),
           whole_spec((8, LANES))],
        [
            model_spec, pack_spec((1, count)), whole_spec((features, LANES)),
            pack_spec((ext, inner)), pack_spec((ext, bc_part)), xbc_spec, lane_spec, *pay_specs,
            whole_spec((features, 1)),
        ],
        [
            shape(packs, features, count, bf16), shape(packs, 1, count, f32),
            shape(features, LANES, bf16), shape(packs, ext, inner, bf16),
            shape(packs, ext, bc_part, bf16), shape(packs, count, chans, bf16),
            shape(packs, count, LANES, f32), pay, pay, shape(features, 1, f32),
        ],
        [
            pltpu.VMEM((4, part, count), bf16), pltpu.VMEM((4, part, LANES), bf16),
            pltpu.VMEM((4, bc_part, features + LANES), bf16), pltpu.VMEM((ext, chans), f32),
            pltpu.VMEM((LANES, chans), f32), pltpu.VMEM((8, chans), f32),
            pltpu.VMEM((features, 1), f32),
        ],
        pre,
        *token_pieces, *edge_pieces, *weight_pieces, proj_x, w_dt.T, conv_own, small,
        us=15,
    )

    cots = head_pieces(lax.optimization_barrier((cotangent, steps))[0])
    kept = {}

    def inner_work():
        kept["inner"] = call(
            functools.partial(inner_kernel, dims),
            grid,
            [xbc_spec, lane_spec],
            chan_spec,
            shape(packs, count, inner, f32),
            [],
            pre,
            xbc, steps,
            us=6,
        )

    def cot_work():
        kept["cot"], kept["gg"] = call(
            functools.partial(cot_kernel, dims),
            grid,
            [piece_spec] * 4 + [whole_spec((inner, features))],
            [model_spec, chan_spec],
            [shape(packs, features, count, bf16), shape(packs, count, inner, f32)],
            [pltpu.VMEM((4, part, count), bf16)],
            pre,
            *cots, proj_out,
            us=5.5,
        )

    def gate_slope_work():
        kept["slope"] = call(
            functools.partial(gate_slope_kernel, dims),
            grid,
            [model_spec, square, pack_spec((ext, inner)), pack_spec((ext, bc_part)),
             whole_spec((8, inner)), whole_spec((8, bc_part))],
            [chan_spec, chan_spec, pack_spec((count, bc_part))],
            [shape(packs, count, inner, bf16), shape(packs, count, inner, f32),
             shape(packs, count, bc_part, f32)],
            [pltpu.VMEM((ext, inner), f32), pltpu.VMEM((ext, bc_part), f32)],
            pre,
            normed, proj_z, raw_x, raw_bc, conv_own, conv_bc_own,
            us=7,
        )

    state_keep, state_recv = scan_states(
        keep, send, meta, packs, heads, size, 0, (inner_work, cot_work, gate_slope_work)
    )
    inner_out, cot, gg = kept["inner"], kept["cot"], kept["gg"]
    gate, slope_x, slope_bc = kept["slope"]
    slope_next = shift(slope_bc[:, :EDGE], "seq", -1)

    y, stats = call(
        functools.partial(gate_kernel, dims),
        grid,
        [
            xbc_spec, lane_spec, chan_spec, state_spec, state_spec, chan_spec, chan_spec, vec, vec,
        ],
        [chan_spec, pack_spec((2, count))],
        [shape(packs, count, inner, f32), shape(packs, 2, count, f32)],
        [],
        pre,
        xbc, steps, inner_out, state_keep, state_recv, gate, gg, gain_gate, skip,
        us=6.6,
    )
    stats_all = lax.all_gather(stats, "head")

    gy, gated, ggate, gkeep, gsend, gate_small = call(
        functools.partial(grad_kernel, dims, total_inner),
        grid,
        [
            pl.BlockSpec((4, 1, 2, count), lambda p, *_: (0, p, 0, 0)),
            xbc_spec, lane_spec, chan_spec, chan_spec, chan_spec, vec, vec,
        ],
        [chan_spec] * 3 + pay_specs + [whole_spec((8, inner))],
        [shape(packs, count, inner, f32)] + [shape(packs, count, inner, bf16)] * 2
        + [pay, pay, shape(8, inner, f32)],
        [],
        pre,
        stats_all, xbc, steps, y, gate, gg, gain_gate, skip,
        us=8.3,
    )

    piece_shape = shape(packs, part, count, f32)
    send_spec = pl.BlockSpec((2, 1, part, count), lambda p, *_: (0, p, 0, 0))
    rows_half = features // 2
    half_specs = [whole_spec((rows_half, inner))] * 2
    half_shapes = [shape(rows_half, inner, f32), shape(rows_half, inner, bf16)]
    half_sums = pltpu.VMEM((2, rows_half, inner), f32)

    early_sum, late_sum = SeqSum(), SeqSum()

    def out_work():
        *kept["out"], keep, give = call(
            functools.partial(out_kernel, dims),
            grid,
            [chan_spec, model_spec, whole_spec((inner, features))],
            [piece_spec, piece_spec, send_spec] + half_specs,
            [piece_shape, piece_shape, shape(2, packs, part, count, bf16)] + half_shapes,
            [pltpu.VMEM((4, part, count), f32), half_sums],
            pre,
            gated, cot, proj_out,
            us=6.8,
        )
        early_sum.put(keep, give)

    def z_work():
        keep, give = call(
            functools.partial(z_kernel, dims),
            grid,
            [model_spec, chan_spec],
            half_specs,
            half_shapes,
            [half_sums],
            pre,
            normed, ggate,
            us=5.3,
        )
        early_sum.put(keep, give)

    def diag_work():
        kept["diag"] = call(
            functools.partial(diag_kernel, dims),
            grid,
            [xbc_spec, lane_spec, chan_spec, chan_spec, state_spec, state_spec],
            [chan_spec, pack_spec((count, bc)), lane_spec],
            [
                shape(packs, count, inner, f32), shape(packs, count, bc, f32),
                shape(packs, count, LANES, f32),
            ],
            [],
            pre,
            xbc, steps, gy, y, state_keep, state_recv,
            us=12,
        )

    gstate_keep, gstate_recv = scan_states(
        gkeep, gsend, meta, packs, heads, size, 1, (out_work, z_work, diag_work, lambda: early_sum.add(meta)),
        lambda: early_sum.got,
    )
    out_own, out_far, out_send = kept["out"]
    dx, dbc, sums = kept["diag"]

    def to_far(far, near):
        return swap((far + near[1].astype(f32)).astype(bf16), "head", 2)

    near = swap(out_send, "head", 1)
    block_out = tokens.astype(f32) + out_own + near[0].astype(f32) + to_far(out_far, near).astype(f32)
    block_out = jnp.swapaxes(block_out.astype(bf16), 1, 2)

    share_own, share_near = call(
        functools.partial(share_kernel, dims),
        grid,
        [xbc_spec, lane_spec, pack_spec((count, bc)), state_spec, state_spec],
        [lane_spec, lane_spec],
        [shape(packs, count, LANES, f32)] * 2,
        [],
        pre,
        xbc, steps, dbc, gstate_keep, gstate_recv,
        us=6.4,
    )
    share_near = swap(share_near, "head", 1)
    advance(early_sum, meta)
    two = shape(half, count, LANES, f32)
    rows_out = shape(packs, EDGE, LANES, f32)
    bc_keep, bc_send, bc_edge = call(
        functools.partial(middle_kernel, (packs, bc_part)),
        (1,),
        [whole_spec((packs, count, LANES))] * 2,
        [whole_spec(two.shape)] * 2 + [whole_spec(rows_out.shape)],
        [two, two, rows_out],
        [],
        (meta,),
        share_own, share_near,
    )
    bc_recv = swap(bc_send, "head", 2)
    bc_edge = shift(bc_edge, "seq", -1)
    bc_edge_recv = swap(bc_edge, "head", 2)


    main_x, edge_x, state_sums, keep, give, grad_conv = call(
        functools.partial(xback_kernel, dims),
        grid,
        [
            xbc_spec, lane_spec, chan_spec, chan_spec, state_spec, state_spec, chan_spec,
            pack_spec((ext, inner)), model_spec, whole_spec((features, LANES)),
            whole_spec((8, inner)), vec,
        ],
        [chan_spec, whole_spec((LANES, inner)), lane_spec] + half_specs + [whole_spec((8, inner))],
        [
            shape(packs, count, inner, bf16), shape(LANES, inner, bf16),
            shape(packs, count, LANES, f32), *half_shapes, shape(8, inner, f32),
        ],
        [
            pltpu.VMEM((ext + EDGE, inner), f32), pltpu.VMEM((ext, inner), f32), half_sums,
        ],
        pre,
        xbc, steps, gy, dx, gstate_keep, gstate_recv, slope_x, raw_x, normed, edge, conv_own, skip,
        us=12.5,
    )
    late_sum.put(keep, give)
    edge_x = shift(edge_x, "seq", -1)
    advance(early_sum, meta)

    def half_block(shape_of, first):
        return pl.BlockSpec(
            (1,) + shape_of, lambda p, *_: (p % half + first,) + (0,) * len(shape_of)
        )

    edge_rows = (EDGE, LANES)
    bc_half = (bc_part, inner)
    gbc, keep, give, grad_conv_bc = call(
        functools.partial(conv_bc_kernel, dims),
        grid,
        [
            half_block((count, LANES), 0), half_block((count, LANES), 0),
            half_block(edge_rows, 0), half_block(edge_rows, half),
            pack_spec((count, bc_part)), pack_spec((EDGE, bc_part)), pack_spec((ext, bc_part)),
            model_spec, whole_spec((8, bc_part)),
        ],
        [pack_spec((count, bc_part)), whole_spec(bc_half), whole_spec(bc_half),
         whole_spec((8, bc_part))],
        [
            shape(packs, count, bc_part, bf16), shape(*bc_half, f32), shape(*bc_half, bf16),
            shape(8, bc_part, f32),
        ],
        [
            pltpu.VMEM((count + EDGE, bc_part), f32), pltpu.VMEM((ext, bc_part), f32),
            pltpu.VMEM((features, bc_part), f32),
        ],
        pre,
        bc_keep, bc_recv, bc_edge, bc_edge_recv, slope_bc, slope_next, raw_bc, normed, conv_bc_own,
        us=6.3,
    )
    late_sum.put(keep, give)

    gdt, smalls = call(
        functools.partial(step_kernel, dims),
        grid,
        [
            lane_spec, lane_spec, lane_spec, state_spec, state_spec, state_spec, state_spec,
            whole_spec((8, LANES)), model_spec, whole_spec((8, inner)), whole_spec((8, bc_part)),
            whole_spec((8, inner)),
        ],
        [lane_spec, whole_spec((EDGE, features))],
        [shape(packs, count, LANES, bf16), shape(EDGE, features, f32)],
        [pltpu.VMEM((features, LANES), f32), pltpu.VMEM((8, LANES), f32)],
        pre,
        steps, sums, state_sums, state_keep, state_recv, gstate_keep, gstate_recv, small, normed,
        grad_conv, grad_conv_bc, gate_small,
        us=8,
    )
    late_sum.put_small(smalls)
    advance(early_sum, meta)

    tall = part + EDGE
    send_spec = pl.BlockSpec((2, 1, tall, count), lambda p, *_: (0, p, 0, 0))
    tall_spec = pack_spec((tall, count))
    extra_spec = pack_spec((8, count))
    extra_shape = shape(packs, 8, count, f32)
    gn_own, gn_far, gn_send, extra = call(
        functools.partial(back_kernel, dims),
        grid,
        [
            chan_spec, pl.BlockSpec((EDGE, inner), lambda p, *_: (p, 0)), chan_spec, lane_spec,
            pack_spec((count, bc_part)), model_spec, square, square,
            whole_spec((features, bc_part)), whole_spec((features, LANES)),
            whole_spec((features, 1)),
        ],
        [piece_spec, piece_spec, send_spec, extra_spec],
        [piece_shape, piece_shape, shape(2, packs, tall, count, bf16), extra_shape],
        [
            pltpu.VMEM((4, part, count), f32), pltpu.VMEM((features, 1), f32),
            pltpu.VMEM((4, 8, count), f32),
        ],
        pre,
        main_x, edge_x, ggate, gdt, gbc, normed, proj_z, proj_x, proj_bc, w_dt, gain_all,
        us=8.3,
    )
    near = swap(gn_send, "head", 1)
    advance(late_sum, meta)

    gn_own, gn_far, extra = call(
        gather_kernel,
        grid,
        [piece_spec, piece_spec, send_spec, extra_spec],
        [piece_spec, tall_spec, extra_spec],
        [piece_shape, shape(packs, tall, count, bf16), extra_shape],
        [],
        (),
        gn_own, gn_far, near, extra,
        us=3.8,
    )
    gn_far = swap(gn_far, "head", 2)
    advance(early_sum, meta)
    advance(late_sum, meta)
    while early_sum.bit != 0:
        advance(early_sum, meta)
    advance(late_sum, meta)
    in_grad, grad_gain = call(
        functools.partial(final_kernel, (packs, count, features)),
        grid,
        [
            piece_spec, tall_spec, extra_spec, piece_spec, pack_spec((1, count)),
            whole_spec((part, 1)), piece_spec,
        ],
        [piece_spec, whole_spec((8, count))],
        [piece_shape, shape(8, count, f32)],
        [],
        (),
        gn_own, gn_far, extra, tokens, inv, norm_gain.astype(f32)[:, None], cotangent,
        us=4, out=True,
    )
    in_grad = jnp.swapaxes(in_grad, 1, 2)
    advance(late_sum, meta)
    grads_out, grads_z = early_sum.result(meta, ("flip", "rows"))
    while late_sum.bit != 0:
        advance(late_sum, meta)
    grads_x, grad_bc = late_sum.result(meta, ("rows", "cols"))
    smalls = late_sum.small
    grad_gain = sum_over(grad_gain, "seq")[0, :part]
    grad_conv, grad_conv_bc = smalls[8:13, :inner], smalls[8:13, inner : inner + bc_part]
    start = 2 * inner - 3 * LANES
    per_head = [smalls[13, start + k * LANES : start + k * LANES + heads] for k in range(3)]
    return (
        block_out,
        in_grad,
        grad_gain,
        grads_z,
        grads_x,
        grad_bc.T,
        smalls[:heads].T,
        grad_conv[:width],
        grad_conv_bc[:width],
        grad_conv[width],
        grad_conv_bc[width],
        *per_head,
        smalls[13, :inner],
        grads_out,
    )


def solution(mesh):
    token, column, vector = P(None, "seq", "head"), P(None, "head"), P("head")
    row = P("head", None)
    return jax.shard_map(
        shards,
        mesh=mesh,
        in_specs=(
            token, token, P(), vector, column, column, column, column, column, column, vector,
            vector, vector, vector, vector, vector, row,
        ),
        out_specs=(
            token, token, vector, column, column, column, column, column, column, vector, vector,
            vector, vector, vector, vector, row,
        ),
        check_vma=False,
    )
```

```python
import functools

import jax
import jax.numpy as jnp
from jax import lax
from jax.experimental import pallas as pl
from jax.experimental.pallas import tpu as pltpu
from jax.sharding import PartitionSpec as P

EPSILON = 1e-05
bf16 = jnp.bfloat16
f32 = jnp.float32
LANES = 128
EDGE = 16
MIB = 1024 * 1024
STEPS = 32000.0
UNIT = 16384.0
LN2 = 0.6931471805599453
GROUP = 16
SMALL = 32


def permuted(x, axis, route):
    y = lax.ppermute(x, axis, route)
    order.near.append(y)
    return y


def swap(x, axis, bit):
    return permuted(x, axis, [(i, i ^ bit) for i in range(lax.axis_size(axis))])


def shift(x, axis, distance):
    n = lax.axis_size(axis)
    return permuted(x, axis, [(i, i + distance) for i in range(n) if 0 <= i + distance < n])


def head_pieces(x):
    far = swap(x, "head", 2)
    near = swap(x, "head", 1)
    return x, near, far, swap(far, "head", 1)


def nn(a, b):
    return lax.dot_general(a, b, (((1,), (0,)), ((), ())), preferred_element_type=f32)


def nt(a, b):
    return lax.dot_general(a, b, (((1,), (1,)), ((), ())), preferred_element_type=f32)


def tn(a, b):
    return lax.dot_general(a, b, (((0,), (0,)), ((), ())), preferred_element_type=f32)


def split2(v):
    hi = v.astype(bf16)
    return hi, (v - hi.astype(f32)).astype(bf16)


def split3(v):
    hi = v.astype(bf16)
    rest = v - hi.astype(f32)
    mid = rest.astype(bf16)
    return hi, mid, (rest - mid.astype(f32)).astype(bf16)


def spread_matrix(heads, size):
    row = lax.broadcasted_iota(jnp.int32, (LANES, heads * size), 0)
    col = lax.broadcasted_iota(jnp.int32, (LANES, heads * size), 1)
    first = (col >= row * size) & (col < (row + 1) * size)
    again = (col >= (row - GROUP) * size) & (col < (row - GROUP + 1) * size)
    return jnp.where(first | again, 1.0, 0.0).astype(bf16)


def spread(v, matrix, heads):
    hi, lo = split2(head_lanes(v, heads))
    return nn((hi.astype(f32) + to_group(lo.astype(f32), 1)).astype(bf16), matrix)


def head_lanes(v, heads):
    return jnp.where(lax.broadcasted_iota(jnp.int32, v.shape, 1) < heads, v, 0.0)


def to_group(v, k):
    return pltpu.roll(v, k * GROUP, 1)


def from_group(v, k, heads):
    return head_lanes(pltpu.roll(v, LANES - k * GROUP, 1) if k else v, heads)


def collapse(v, matrix, heads):
    return head_lanes(nt(jnp.concatenate(split2(v), axis=1), jnp.concatenate([matrix] * 2, axis=1)), heads)


def triangle(count, lower):
    row = lax.broadcasted_iota(jnp.int32, (count, count), 0)
    col = lax.broadcasted_iota(jnp.int32, (count, count), 1)
    keep = (row >= col) if lower else (row <= col)
    return jnp.where(keep, 1.0, 0.0).astype(bf16)


def exact_sums(matrix, v, heads):
    hi, mid, lo = [piece.astype(f32) for piece in split3(v)]
    sums = nn(matrix, (hi + to_group(mid, 1) + to_group(lo, 2)).astype(bf16))
    return from_group(sums, 0, heads) + from_group(sums, 1, heads) + from_group(sums, 2, heads)


def step_sizes(v, heads):
    soft = jnp.maximum(v, 0.0) + jnp.log1p(jnp.exp(-jnp.abs(v)))
    return head_lanes(soft, heads)


def steps_of(block, heads):
    return step_sizes(block, heads), from_group(block, 1, heads)


def segments(positions, lens_ref, pack, count):
    total = jnp.zeros(positions.shape, jnp.int32)
    end = jnp.int32(0)
    for k in range(count):
        end = end + lens_ref[pack, k]
        total = total + jnp.where(positions >= end, 1, 0)
    return total


def column_segments(meta_ref, lens_ref, pack, count, nseq, before):
    rows = lax.broadcasted_iota(jnp.int32, (count + before, 1), 0)
    return segments(rows + (meta_ref[0] * count - before), lens_ref, pack, nseq)


def row_segments(meta_ref, lens_ref, pack, count, nseq):
    cols = lax.broadcasted_iota(jnp.int32, (1, count), 1)
    return segments(cols + meta_ref[0] * count, lens_ref, pack, nseq)


def carry_column(meta_ref, seg_ext, before):
    same = seg_ext[before:] == seg_ext[before - 1 : before]
    return jnp.where(same & (meta_ref[0] > 0), 1.0, 0.0)


def to_int16(v):
    return jnp.floor(v + 0.5).astype(jnp.int32).astype(jnp.int16)


def encode_state(out, p, state, decay, heads, size):
    lane = lax.broadcasted_iota(jnp.int32, (1, LANES), 1)
    powers = jnp.zeros((1, LANES), f32)
    for h in range(heads):
        part = state[h * size : (h + 1) * size]
        top = jnp.max(jnp.max(jnp.abs(part), axis=0, keepdims=True), axis=1, keepdims=True)
        power = jnp.ceil(jnp.log(jnp.maximum(top, 1e-30)) / LN2)
        powers = powers + jnp.where(lane == h, power, 0.0)
        codes = jnp.clip(part * (jnp.exp(-power * LN2) * STEPS), -32767.0, 32767.0)
        out[p, h * size : (h + 1) * size, :] = to_int16(codes)
    row = lax.broadcasted_iota(jnp.int32, (EDGE, LANES), 0)
    coarse = jnp.floor(decay * UNIT)
    fine = (decay * UNIT - coarse) * UNIT
    tail = jnp.where(row == 0, powers, jnp.where(row == 1, coarse, jnp.where(row == 2, fine, 0.0)))
    out[p, heads * size :, :] = to_int16(tail)


def decode_state(block, heads, size):
    values = block.astype(jnp.int32).astype(f32)
    tail = values[heads * size :]
    scale = jnp.exp(tail[0:1] * LN2) / STEPS
    decay = (tail[1:2] + tail[2:3] / UNIT) / UNIT
    return scaled_state(values[: heads * size], scale, heads, size), decay


def sigmoid(v):
    return 1.0 / (1.0 + jnp.exp(-v))


def scaled_state(state, decay, heads, size):
    return jnp.concatenate(
        [state[h * size : (h + 1) * size] * decay[:, h : h + 1] for h in range(heads)], axis=0
    )


def tail_kernel(tokens, out):
    lane = lax.broadcasted_iota(jnp.int32, out.shape, 1)
    total = jnp.zeros(out.shape, f32)
    for p in range(tokens.shape[0]):
        moved = pltpu.roll(tokens[p].astype(f32), (p + 1) * EDGE, 1)
        total = jnp.where((lane >= p * EDGE) & (lane < (p + 1) * EDGE), moved, total)
    out[...] = total.astype(bf16)


def wide_row(ref, lanes=LANES):
    row = ref[...].astype(f32)[None, :]
    blank = lanes - row.shape[1]
    return jnp.concatenate([row, jnp.zeros((1, blank), f32)], axis=1) if blank else row


def prepare_kernel(dims, *refs):
    packs, count, features, inner, bc, heads, size, width, nseq = dims
    (
        wbc, conv_bc, bias_bc, norm_gain, wdt, conv_x, bias_x, dt_bias, a_log, d_skip, gate_gain,
        shared_o, wbc_o, wdt_o, wdt_rows_o, conv_x_o, conv_bc_o, small_o, skip_o, gate_gain_o, gain_o,
    ) = refs
    bc_part, part = bc // 4, features // 4
    taps = conv_bc[...].astype(f32)
    bias = wide_row(bias_bc, bc_part)
    gain = wide_row(norm_gain, part)
    pieces = [gain[:, c * bc_part : (c + 1) * bc_part] for c in range(part // bc_part)]
    rows = jnp.concatenate([taps, bias] + pieces, axis=0)
    rows = jnp.concatenate([rows, jnp.zeros((LANES - rows.shape[0], bc_part), f32)], axis=0)
    rows = jnp.concatenate([rows, jnp.zeros((LANES, LANES - bc_part), f32)], axis=1)
    extra = jnp.transpose(rows)[:bc_part].astype(bf16)
    shared_o[:, :features] = wbc[...]
    shared_o[:, features:] = extra
    wbc_o[...] = jnp.transpose(wbc[...].astype(f32)).astype(bf16)
    dt_rows = jnp.concatenate(
        [wdt[...].astype(f32), jnp.zeros((LANES - heads, features), f32)], axis=0
    )
    wdt_rows_o[...] = dt_rows.astype(bf16)
    wdt_o[...] = jnp.transpose(dt_rows).astype(bf16)
    blank = jnp.zeros((7 - width, inner), f32)
    conv_x_o[...] = jnp.concatenate(
        [conv_x[...].astype(f32), wide_row(bias_x, inner), blank], axis=0
    )
    conv_bc_o[...] = jnp.concatenate([taps, bias, blank[:, :bc_part]], axis=0)
    small_o[...] = jnp.concatenate(
        [wide_row(dt_bias), wide_row(a_log), jnp.zeros((6, LANES), f32)], axis=0
    )
    skips = jnp.concatenate([wide_row(d_skip), jnp.zeros((7, LANES), f32)], axis=0)
    matrix = spread_matrix(heads, size)
    skip_o[...] = sum(nn(piece, matrix) for piece in split3(skips))[0:1]
    gate_gain_o[...] = wide_row(gate_gain, inner)
    column = jnp.concatenate([gain, jnp.zeros((LANES - 1, part), f32)], axis=0)
    column = jnp.concatenate([column, jnp.zeros((LANES, 2 * LANES - part), f32)], axis=1)
    gain_o[...] = jnp.transpose(column)[:part, 0:1]


def front_kernel(dims, meta, lens, *refs):
    packs, count, features, inner, bc, heads, size, width, nseq = dims
    tokens, edges, shared = refs[0:4], refs[4:8], refs[8:12]
    wx, wdt, conv_x, small = refs[12:16]
    normed_o, inv_o, edge_o, rawx_o, rawbc_o, xbc_o, steps_o, keep_o, send_o, gain_o = refs[16:26]
    stage, edge_stage, weights, raws, edge_raws, conv, gain = refs[26:]
    pack = pl.program_id(0)
    head = meta[1]
    part = features // 4
    wide = edge_stage.shape[2]

    def normalise(values):
        mean = jnp.sum(values * values, axis=0, keepdims=True) / features
        inv = lax.rsqrt(mean + EPSILON)
        return inv, ((values * inv) * gain[...]).astype(bf16)

    def raw_of(normed):
        wbc = weights[...].reshape(bc, weights.shape[2])[:, :features]
        return jnp.concatenate([nn(normed, wx[...]), nt(normed, wbc)], axis=1).astype(bf16)

    @pl.when(pack == 0)
    def _():
        for k in range(4):
            weights[head ^ k] = shared[k][...]
            edge_stage[head ^ k] = edges[k][...]
        extra = weights[...].reshape(bc, weights.shape[2])[:, features:].astype(f32)
        conv[:, :inner] = conv_x[...]
        conv[:, inner:] = jnp.transpose(extra)[0:8]
        bc_part = bc // 4
        pieces = part // bc_part
        for h in range(4):
            for c in range(pieces):
                gain[h * part + c * bc_part : h * part + (c + 1) * bc_part, :] = extra[
                    h * bc_part : (h + 1) * bc_part, width + 1 + c : width + 2 + c
                ]
        _, normed = normalise(edge_stage[...].reshape(features, wide).astype(f32))
        gain_o[...] = gain[...]
        edge_o[...] = normed
        edge_raws[...] = raw_of(jnp.transpose(normed)).astype(f32)

    for k in range(4):
        stage[head ^ k] = tokens[k][0]
    inv, normed_t = normalise(stage[...].reshape(features, count).astype(f32))
    inv_o[0] = inv
    normed_o[0] = normed_t
    normed = jnp.transpose(normed_t)
    raws[EDGE:, :] = raw_of(normed).astype(f32)
    raws[0:EDGE, :] = edge_raws[pl.ds(pl.multiple_of(pack * EDGE, EDGE), EDGE), :]

    def own_bc(values):
        bc_part = bc // 4
        parts = [values[:, inner + h * bc_part : inner + (h + 1) * bc_part] for h in range(4)]
        low = jnp.where((head & 1) == 0, parts[0], parts[1])
        high = jnp.where((head & 1) == 0, parts[2], parts[3])
        return jnp.where((head >> 1) == 0, low, high)

    rawx_o[0] = raws[:, :inner].astype(bf16)
    rawbc_o[0] = own_bc(raws[...]).astype(bf16)
    seg = column_segments(meta, lens, pack, count, nseq, EDGE)
    seg_main = seg[EDGE:]
    pre = convolved(raws, conv, seg, count, width)
    xbc = (pre * sigmoid(pre)).astype(bf16)
    xbc_o[0] = xbc
    v = head_lanes(nt(normed, wdt[...]).astype(bf16).astype(f32) + small[0:1, :], heads)
    dt = step_sizes(v, heads)
    rate = -dt * jnp.exp(small[1:2, :])
    cum = exact_sums(triangle(count, True), rate, heads)
    steps_o[0] = v + to_group(cum, 1)
    cum_end = cum[count - 1 : count]
    weight = jnp.where(seg_main == seg[count + EDGE - 1 :], jnp.exp(cum_end - cum), 0.0) * dt
    matrix = spread_matrix(heads, size)
    scaled = (xbc[:, :inner].astype(f32) * spread(weight, matrix, heads)).astype(bf16)
    state = tn(scaled, xbc[:, inner : inner + bc // 2])
    carry = carry_column(meta, seg, EDGE)
    store_state(
        meta, packs, pack, keep_o, send_o, state, carry[count - 1 :] * jnp.exp(cum_end), heads, size
    )


def convolved(raws, conv, seg, count, width):
    pre = jnp.broadcast_to(conv[width : width + 1, :], (count, raws.shape[1]))
    for k in range(width):
        low = EDGE - (width - 1) + k
        mask = jnp.where(seg[low : low + count] == seg[EDGE:], 1.0, 0.0)
        pre = pre + conv[k : k + 1, :] * raws[low : low + count, :] * mask
    return pre


def gate_slope_kernel(dims, meta, lens, *refs):
    packs, count, features, inner, bc, heads, size, width, nseq = dims
    normed, wz, raw_x, raw_bc, conv_x, conv_bc, gate_o, slope_x_o, slope_bc_o, raws, raws_bc = refs
    pack = pl.program_id(0)
    gate_o[0] = tn(normed[0], wz[...]).astype(bf16)
    seg = column_segments(meta, lens, pack, count, nseq, EDGE)
    for raw, wide, conv, out in ((raw_x, raws, conv_x, slope_x_o), (raw_bc, raws_bc, conv_bc, slope_bc_o)):
        wide[...] = raw[0].astype(f32)
        pre = convolved(wide, conv, seg, count, width)
        sig = sigmoid(pre)
        out[0] = sig * (1.0 + pre * (1.0 - sig))


def store_state(meta, packs, pack, keep_o, send_o, state, decay, heads, size):
    mine = (pack // (packs // 2)) == (meta[0] & 1)

    @pl.when(mine)
    def _():
        encode_state(keep_o, 0, state, decay, heads, size)

    @pl.when(jnp.logical_not(mine))
    def _():
        encode_state(send_o, 0, state, decay, heads, size)


def load_state(meta, packs, pack, keep, recv, heads, size):
    mine = (pack // (packs // 2)) == (meta[0] & 1)
    block = jnp.where(mine, keep[0].astype(jnp.int32), recv[0].astype(jnp.int32))
    return decode_state(block, heads, size)[0]


def decay_parts(cum_col, cum_row, masked):
    return masked * jnp.exp(jnp.minimum(cum_col - cum_row, 0.0))


def block_mask(meta, lens, pack, count, nseq):
    col = column_segments(meta, lens, pack, count, nseq, 0)
    row = row_segments(meta, lens, pack, count, nseq)
    tri = lax.broadcasted_iota(jnp.int32, (count, count), 0) >= lax.broadcasted_iota(
        jnp.int32, (count, count), 1
    )
    return tri & (col == row)


def inner_kernel(dims, meta, lens, *refs):
    packs, count, features, inner, bc, heads, size, width, nseq = dims
    xbc, steps, inner_o = refs
    pack = pl.program_id(0)
    half = bc // 2
    b_vals, c_vals = xbc[0, :, inner : inner + half], xbc[0, :, inner + half :]
    scores = jnp.where(block_mask(meta, lens, pack, count, nseq), nt(c_vals, b_vals), 0.0)
    dt, cum_col = steps_of(steps[0], heads)
    cum_row = jnp.transpose(cum_col)
    dt_row = jnp.transpose(dt)
    lane = lax.broadcasted_iota(jnp.int32, (count, 2 * size), 1)
    for pair in range(heads // 2):
        cols = slice(2 * pair * size, (2 * pair + 2) * size)
        x_pair = xbc[0, :, cols]
        parts = []
        for h in (2 * pair, 2 * pair + 1):
            weights = decay_parts(cum_col[:, h : h + 1], cum_row[h : h + 1], scores)
            parts.append(nn((weights * dt_row[h : h + 1]).astype(bf16), x_pair))
        inner_o[0, :, cols] = jnp.where(lane < size, parts[0], parts[1])


def cot_kernel(dims, meta, lens, *refs):
    packs, count, features, inner, bc, heads, size, width, nseq = dims
    pieces, (wout, cot_o, gg_o, stage) = refs[:4], refs[4:]
    for k in range(4):
        stage[meta[1] ^ k] = pieces[k][0]
    cotangent = stage[...].reshape(features, count)
    cot_o[0] = cotangent
    gg_o[0] = jnp.transpose(nn(wout[...], cotangent))


def compose(lower, upper, heads, size):
    return scaled_state(lower[0], upper[1], heads, size) + upper[0], lower[1] * upper[1]


def choose(flag, a, b):
    return jnp.where(flag, a[0], b[0]), jnp.where(flag, a[1], b[1])


def pair_kernel(dims, rev, meta, own, other, out):
    packs, heads, size = dims
    upper_is_own = ((meta[0] & 1) ^ rev) == 1
    for p in range(packs // 2):
        a, b = decode_state(own[p], heads, size), decode_state(other[p], heads, size)
        both = compose(choose(upper_is_own, b, a), choose(upper_is_own, a, b), heads, size)
        encode_state(out, p, *both, heads, size)


def entering_from(before, b, p, heads, size):
    if before is None:
        return (jnp.zeros_like(b[0]), jnp.ones_like(b[1])), b
    entering = decode_state(before[p], heads, size)
    return entering, compose(b, entering, heads, size)


def cube_kernel(dims, rev, bit, first, meta, *refs):
    packs, heads, size = dims
    total, other = refs[0], refs[1]
    before, next_o, before_o = (None, refs[2], refs[3]) if first else refs[2:5]
    upper_is_own = (((meta[0] >> bit) & 1) ^ rev) == 1
    for p in range(packs // 2):
        a, b = decode_state(total[p], heads, size), decode_state(other[p], heads, size)
        both = compose(choose(upper_is_own, b, a), choose(upper_is_own, a, b), heads, size)
        encode_state(next_o, p, *both, heads, size)
        entering, longer = entering_from(before, b, p, heads, size)
        encode_state(before_o, p, *choose(upper_is_own, longer, entering), heads, size)


def last_kernel(dims, rev, bit, first, meta, *refs):
    packs, heads, size = dims
    own, pair, other = refs[0:3]
    before, keep_o, send_o = (None, refs[3], refs[4]) if first else refs[3:6]
    add = (((meta[0] >> bit) & 1) ^ rev) == 1
    upper_is_own = ((meta[0] & 1) ^ rev) == 1
    for p in range(packs // 2):
        entering, longer = entering_from(
            before, decode_state(other[p], heads, size), p, heads, size
        )
        low = choose(add, longer, entering)
        lower = decode_state(jnp.where(upper_is_own, pair[p].astype(jnp.int32), own[p].astype(jnp.int32)), heads, size)
        high = compose(low, lower, heads, size)
        encode_state(keep_o, p, *choose(upper_is_own, high, low), heads, size)
        encode_state(send_o, p, *choose(upper_is_own, low, high), heads, size)


def gate_kernel(dims, meta, lens, *refs):
    packs, count, features, inner, bc, heads, size, width, nseq = dims
    xbc, steps, inner_in, keep, recv, gate, gg, gain, skip, y_o, stats_o = refs
    pack = pl.program_id(0)
    state = jnp.concatenate(
        split2(load_state(meta, packs, pack, keep, recv, heads, size)), axis=1
    )
    carry = carry_column(meta, column_segments(meta, lens, pack, count, nseq, EDGE), EDGE)
    matrix = spread_matrix(heads, size)
    entering = spread(carry * jnp.exp(from_group(steps[0], 1, heads)), matrix, heads)
    c_vals = xbc[0, :, inner + bc // 2 :]
    y = inner_in[0] + entering * nt(jnp.concatenate([c_vals, c_vals], axis=1), state)
    y_o[0] = y
    gate_f = gate[0].astype(f32)
    ssd = y + xbc[0, :, :inner].astype(f32) * skip[...]
    mixed = ssd * (gate_f * sigmoid(gate_f))
    squares = jnp.sum(mixed * mixed, axis=1, keepdims=True)
    dots = jnp.sum(gain[...] * gg[0] * mixed, axis=1, keepdims=True)
    lane = lax.broadcasted_iota(jnp.int32, (count, LANES), 1)
    both = jnp.where(lane == 0, squares, 0.0) + jnp.where(lane == 1, dots, 0.0)
    stats_o[0] = jnp.transpose(both)[0:2]


def grad_kernel(dims, total_inner, meta, lens, *refs):
    packs, count, features, inner, bc, heads, size, width, nseq = dims
    (
        stats, near, far, diagonal, xbc, steps, y, gate, gg, gain, skip,
        gy_o, gated_o, ggate_o, keep_o, send_o, small_o,
    ) = refs
    pack = pl.program_id(0)
    sums = (stats[0] + near[0]) + (far[0] + diagonal[0])
    row = lax.broadcasted_iota(jnp.int32, (LANES, count), 0)
    wide = jnp.where(row == 0, sums[0:1], 0.0) + jnp.where(row == 1, sums[1:2], 0.0)
    cols = jnp.transpose(wide)
    inv = lax.rsqrt(cols[:, 0:1] / total_inner + EPSILON)
    dot = cols[:, 1:2] / total_inner
    x_f, gg_f, gate_f = xbc[0, :, :inner].astype(f32), gg[0], gate[0].astype(f32)
    ssd = y[0] + x_f * skip[...]
    sig = sigmoid(gate_f)
    act = gate_f * sig
    mixed = ssd * act
    scaled = mixed * inv
    gated_o[0] = (scaled * gain[...]).astype(bf16)
    grad_mixed = inv * gain[...] * gg_f - mixed * (inv * inv * inv * dot)
    gy_f = grad_mixed * act
    gy_o[0] = gy_f
    ggate_o[0] = (grad_mixed * ssd * sig * (1.0 + gate_f * (1.0 - sig))).astype(bf16)
    carry = carry_column(meta, column_segments(meta, lens, pack, count, nseq, EDGE), EDGE)
    cum = from_group(steps[0], 1, heads)
    entering = carry * jnp.exp(cum)
    ey_hi, ey_lo = split2(gy_f * spread(entering, spread_matrix(heads, size), heads))
    c_vals = xbc[0, :, inner + bc // 2 :]
    state_grad = tn(ey_hi, c_vals) + tn(ey_lo, c_vals)
    store_state(
        meta, packs, pack, keep_o, send_o, state_grad, entering[count - 1 :], heads, size
    )

    @pl.when(pack == 0)
    def _():
        small_o[...] = jnp.zeros_like(small_o)

    small_o[0:1, :] += jnp.sum(gg_f * scaled, axis=0, keepdims=True)
    small_o[1:2, :] += jnp.sum(gy_f * x_f, axis=0, keepdims=True)


def diag_kernel(dims, meta, lens, *refs):
    packs, count, features, inner, bc, heads, size, width, nseq = dims
    xbc, steps, gy, y, keep, recv, dx_o, dbc_o, sums_o = refs
    pack = pl.program_id(0)
    half = bc // 2
    b_vals, c_vals = xbc[0, :, inner : inner + half], xbc[0, :, inner + half :]
    mask = block_mask(meta, lens, pack, count, nseq)
    scores = jnp.where(mask, nt(c_vals, b_vals), 0.0)
    dt, cum_col = steps_of(steps[0], heads)
    cum_row = jnp.transpose(cum_col)
    dt_row = jnp.transpose(dt)
    lane = lax.broadcasted_iota(jnp.int32, (count, 2 * size), 1)
    grad_scores = jnp.zeros((count, count), f32)
    zero = jnp.zeros((), bf16)
    for pair in range(heads // 2):
        cols = slice(2 * pair * size, (2 * pair + 2) * size)
        x_pair = xbc[0, :, cols]
        x_twice = jnp.concatenate([x_pair, x_pair], axis=1)
        gy_hi, gy_lo = split2(gy[0, :, cols])
        gy_wide = jnp.concatenate([gy_hi, gy_lo], axis=1)
        parts = []
        for h in (2 * pair, 2 * pair + 1):
            own = (lane < size) if h % 2 == 0 else (lane >= size)
            part = jnp.exp(jnp.minimum(cum_col[:, h : h + 1] - cum_row[h : h + 1], 0.0)) * dt_row[h : h + 1]
            parts.append(tn((scores * part).astype(bf16), gy_wide))
            both = jnp.concatenate([jnp.where(own, gy_hi, zero), jnp.where(own, gy_lo, zero)], axis=1)
            grad_scores = grad_scores + nt(both, x_twice) * part
        two = [part[:, : 2 * size] + part[:, 2 * size :] for part in parts]
        dx_o[0, :, cols] = jnp.where(lane < size, two[0], two[1])
    hi, lo = split2(jnp.where(mask, grad_scores, 0.0))
    state_hi, state_lo = split2(load_state(meta, packs, pack, keep, recv, heads, size))
    carry = carry_column(meta, column_segments(meta, lens, pack, count, nseq, EDGE), EDGE)
    matrix = spread_matrix(heads, size)
    ey_hi, ey_lo = split2(gy[0] * spread(carry * jnp.exp(cum_col), matrix, heads))
    dbc_o[0, :, :half] = tn(hi, c_vals) + tn(lo, c_vals)
    dbc_o[0, :, half:] = (
        nn(jnp.concatenate([hi, lo], axis=1), jnp.concatenate([b_vals, b_vals], axis=0))
        + nn(ey_hi, state_hi) + nn(ey_hi, state_lo) + nn(ey_lo, state_hi)
    )
    row_sum = collapse(gy[0] * y[0], matrix, heads)
    col_sum = collapse(xbc[0, :, :inner].astype(f32) * dx_o[0], matrix, heads)
    sums_o[0] = row_sum + to_group(col_sum, 1)


def scatter_pieces(head, stage, own_o, far_o, send_o):
    own_o[0] = stage[head]
    send_o[0, 0] = stage[head ^ 1].astype(bf16)
    far_o[0] = stage[head ^ 2]
    send_o[1, 0] = stage[head ^ 3].astype(bf16)


def accumulate(meta, pack, packs, sums, term, keep_o, send_o):
    wide = term.reshape(sums.shape)

    @pl.when(pack == 0)
    def _():
        sums[...] = wide

    @pl.when(pack > 0)
    def _():
        sums[...] += wide

    @pl.when(pack == packs - 1)
    def _():
        side = meta[0] & 1
        keep_o[...] = sums[side]
        send_o[...] = sums[1 - side].astype(bf16)


def out_kernel(dims, meta, lens, *refs):
    packs, count, features, inner, bc, heads, size, width, nseq = dims
    gated, cot, wout, own_o, far_o, send_o, keep_o, give_o, stage, sums = refs
    pack = pl.program_id(0)
    stage[...] = tn(wout[...], jnp.transpose(gated[0])).reshape(stage.shape)
    scatter_pieces(meta[1], stage, own_o, far_o, send_o)
    accumulate(meta, pack, packs, sums, nn(cot[0], gated[0]), keep_o, give_o)


def gain_row(weights, grads):
    part = jnp.sum(weights.astype(f32) * grads, axis=1, keepdims=True)
    return jnp.transpose(jnp.broadcast_to(part, (part.shape[0], LANES)))[0:8]


def z_kernel(dims, meta, lens, *refs):
    normed, ggate, wz, keep_o, give_o, gain_o, sums = refs
    pack = pl.program_id(0)
    accumulate(meta, pack, dims[0], sums, nn(normed[0], ggate[0]), keep_o, give_o)

    @pl.when(pack == dims[0] - 1)
    def _():
        gain_o[...] = gain_row(wz[...], sums[...].reshape(wz.shape))


def end_weights(seg, seg_main, cum_col, dt_col, count):
    cum_end = cum_col[count - 1 :]
    end = seg[count + EDGE - 1 :]
    return jnp.where(seg_main == end, jnp.exp(cum_end - cum_col), 0.0) * dt_col


def share_kernel(dims, meta, lens, *refs):
    packs, count, features, inner, bc, heads, size, width, nseq = dims
    (
        xbc, steps, dbc, gkeep, grecv, gy, dx, slope, conv, skip,
        own_o, near_o, grad_o, state_sum_o, edge_o,
        gpad,
    ) = refs
    pack = pl.program_id(0)
    half, quarter = bc // 2, bc // 4
    g_hi, g_lo = split2(load_state(meta, packs, pack, gkeep, grecv, heads, size))
    seg = column_segments(meta, lens, pack, count, nseq, EDGE)
    dt, cum = steps_of(steps[0], heads)
    matrix = spread_matrix(heads, size)
    wide = spread(end_weights(seg, seg[EDGE:], cum, dt, count), matrix, heads)
    x_f = xbc[0, :, :inner].astype(f32)
    hi, lo = split2(wide * x_f)
    grad_b = dbc[0, :, :half] + nn(hi, g_hi) + nn(lo, g_hi) + nn(hi, g_lo)
    grad_c = dbc[0, :, half:]
    even = jnp.concatenate([grad_b[:, :quarter], grad_c[:, :quarter]], axis=1)
    odd = jnp.concatenate([grad_b[:, quarter:], grad_c[:, quarter:]], axis=1)
    first = (meta[1] & 1) == 0
    own_o[0] = jnp.where(first, even, odd)
    near_o[0] = jnp.where(first, odd, even)
    b_vals = xbc[0, :, inner : inner + half]
    u_wide = wide * nt(
        jnp.concatenate([b_vals, b_vals], axis=1), jnp.concatenate([g_hi, g_lo], axis=1)
    )
    state_sum_o[0] = collapse(x_f * u_wide, matrix, heads)
    grad_x = (dx[0] + u_wide + gy[0] * skip[...]) * slope[0]
    grad_o[0] = grad_x
    gpad[:EDGE, :] = jnp.zeros((EDGE, inner), f32)
    gpad[EDGE:, :] = grad_x[:EDGE]
    edge_o[0] = conv_rows(gpad, conv, seg, EDGE, width).astype(bf16)


def middle_kernel(dims, meta, *refs):
    packs, quarter = dims
    own, near, keep_o, send_o = refs
    half = packs // 2
    first = (meta[1] >> 1) == 0
    for p in range(half):
        a, b = own[p] + near[p], own[p + half] + near[p + half]
        low = jnp.concatenate([a[:, :quarter], b[:, :quarter]], axis=1)
        high = jnp.concatenate([a[:, quarter:], b[:, quarter:]], axis=1)
        keep_o[p] = jnp.where(first, low, high)
        send_o[p] = jnp.where(first, high, low)


def conv_taps(grads, raws, gconv_o, seg, count, width):
    seg_main = seg[EDGE : EDGE + count]
    for k in range(width):
        low = EDGE - (width - 1) + k
        mask = jnp.where(seg[low : low + count] == seg_main, 1.0, 0.0)
        gconv_o[k : k + 1, :] += jnp.sum(
            grads * (raws[low : low + count, :] * mask), axis=0, keepdims=True
        )
    gconv_o[width : width + 1, :] += jnp.sum(grads, axis=0, keepdims=True)


def conv_rows(gpad, conv, seg, rows, width):
    total = jnp.zeros((rows, gpad.shape[1]), f32)
    for lag in range(width):
        mask = jnp.where(seg[lag : lag + rows] == seg[:rows], 1.0, 0.0)
        k = width - 1 - lag
        total = total + conv[k : k + 1, :] * (gpad[lag : lag + rows, :] * mask)
    return total


def step_kernel(dims, meta, lens, *refs):
    packs, count, features, inner, bc, heads, size, width, nseq = dims
    (
        steps, sums, state_sums, keep, recv, gkeep, grecv, small, normed, wdt,
        gdt_o, gdt_rows_o, gsmall_o, gain_o,
        gdt_sums,
    ) = refs
    pack = pl.program_id(0)
    state = load_state(meta, packs, pack, keep, recv, heads, size)
    gstate = load_state(meta, packs, pack, gkeep, grecv, heads, size)
    seg = column_segments(meta, lens, pack, count, nseq, EDGE)
    matrix = spread_matrix(heads, size)
    v = steps[0]
    dt, cum = steps_of(v, heads)
    sig = head_lanes(sigmoid(v), heads)
    row_sum, col_sum = from_group(sums[0], 0, heads), from_group(sums[0], 1, heads)
    state_sum = state_sums[0]
    carry = carry_column(meta, seg, EDGE)
    hi, lo = split2(gstate * state)
    ones = jnp.ones((8, LANES), bf16)
    by_head = collapse(nt(ones, hi) + nt(ones, lo), matrix, heads)[0:1]
    last = by_head * carry[count - 1 :] * jnp.exp(cum[count - 1 :]) + jnp.sum(
        state_sum, axis=0, keepdims=True
    )
    rows = lax.broadcasted_iota(jnp.int32, (count, LANES), 0)
    grad_cum = row_sum - col_sum - state_sum + jnp.where(rows == count - 1, last, 0.0)
    grad_rate = exact_sums(triangle(count, False), grad_cum, heads)
    decay_rate = -jnp.exp(small[1:2, :])
    ratio = jnp.where(dt > 1e-30, sig / jnp.maximum(dt, 1e-30), 1.0)
    grad_dt = head_lanes(ratio * (col_sum + state_sum) + grad_rate * decay_rate * sig, heads)
    low = grad_dt.astype(bf16)
    gdt_o[0] = low

    @pl.when(pack == 0)
    def _():
        for ref in (gsmall_o, gdt_sums):
            ref[...] = jnp.zeros_like(ref)

    gsmall_o[0:1, :] += jnp.sum(grad_dt, axis=0, keepdims=True)
    gsmall_o[1:2, :] += jnp.sum(grad_rate * dt * decay_rate, axis=0, keepdims=True)
    gdt_sums[...] += nn(normed[0], low)

    @pl.when(pack == packs - 1)
    def _():
        gdt_rows_o[...] = jnp.transpose(gdt_sums[...])[0:8]
        gain_o[...] = gain_row(wdt[...], gdt_sums[...])


def xback_kernel(dims, meta, lens, *refs):
    packs, count, features, inner, bc, heads, size, width, nseq = dims
    (
        grads, raw, normed, edge, edge_x, conv, wx,
        main_o, keep_o, give_o, gconv_o, gain_o,
        gpad, raws, sums, rows_x,
    ) = refs
    pack = pl.program_id(0)
    seg = column_segments(meta, lens, pack, count, nseq, EDGE)

    @pl.when(pack == 0)
    def _():
        for ref in (gconv_o, gpad, rows_x):
            ref[...] = jnp.zeros_like(ref)

    raws[...] = raw[0].astype(f32)
    gpad[:count, :] = grads[0]
    conv_taps(grads[0], raws, gconv_o, seg, count, width)
    seg_pad = jnp.concatenate([seg[EDGE:], jnp.full((8, 1), -1, jnp.int32)], axis=0)
    main = conv_rows(gpad, conv, seg_pad, count, width).astype(bf16)
    main_o[0] = main
    rows_x[pl.ds(pl.multiple_of(pack * EDGE, EDGE), EDGE), :] = edge_x[0]
    term = nn(normed[0], main).reshape(sums.shape)

    @pl.when(pack == 0)
    def _():
        sums[...] = term

    @pl.when(pack > 0)
    def _():
        sums[...] += term

    @pl.when(pack == packs - 1)
    def _():
        sums[...] += nn(edge[...], rows_x[...]).reshape(sums.shape)
        side = meta[0] & 1
        keep_o[...] = sums[side]
        give_o[...] = sums[1 - side].astype(bf16)
        gain_o[...] = gain_row(wx[...], sums[...].reshape(wx.shape))


def conv_bc_kernel(dims, meta, lens, *refs):
    packs, count, features, inner, bc, heads, size, width, nseq = dims
    (
        keep, recv, slope, raw, normed, edge, wbc, conv, edge_x,
        gconv_x, gdt_rows, gsmall, gate_small, gain_z, gain_x, gain_dt, gain,
        rows_o, edges_o, keep_o, give_o, small_o,
        gpad, raws, sums, edge_bc, gconv,
    ) = refs
    pack = pl.program_id(0)
    quarter = bc // 4

    @pl.when(pack == 0)
    def _():
        for ref in (gconv, gpad, edge_bc, sums):
            ref[...] = jnp.zeros_like(ref)

    both = keep[0] + recv[0]
    grad = jnp.where(pack < packs // 2, both[:, :quarter], both[:, quarter:]) * slope[0]
    seg = column_segments(meta, lens, pack, count, nseq, EDGE)
    raws[...] = raw[0].astype(f32)
    gpad[EDGE : EDGE + count, :] = grad
    conv_taps(grad, raws, gconv, seg, count, width)
    seg_pad = jnp.concatenate([seg, jnp.full((8, 1), -1, jnp.int32)], axis=0)
    grad_raw = conv_rows(gpad, conv, seg_pad, count + EDGE, width).astype(bf16)
    rows_o[0] = grad_raw[EDGE:]
    edge_bc[pl.ds(pl.multiple_of(pack * EDGE, EDGE), EDGE), :] = grad_raw[:EDGE]
    edges_o[0, :, :inner] = edge_x[0]
    blank = jnp.zeros((EDGE, LANES - quarter), bf16)
    edges_o[0, :, inner:] = jnp.concatenate([grad_raw[:EDGE], blank], axis=1)
    sums[...] += nn(normed[0], grad_raw[EDGE:])

    @pl.when(pack == packs - 1)
    def _():
        total = sums[...] + nn(edge[...], edge_bc[...])
        rows = jnp.transpose(total)
        left, right = rows[:, :inner], rows[:, inner:]
        first = (meta[0] & 1) == 0
        taps = width + 1
        keep_o[...] = jnp.where(first, left, right)
        give_o[:quarter, :] = jnp.where(first, right, left).astype(bf16)
        small_o[...] = jnp.zeros_like(small_o)
        for h in range(heads):
            small_o[2 * h : 2 * h + 1, :] = gdt_rows[h : h + 1, :inner]
            small_o[2 * h + 1 : 2 * h + 2, :] = gdt_rows[h : h + 1, inner:]
        row = 2 * heads
        small_o[row : row + taps, :] = gconv_x[:taps, :]
        row += taps
        small_o[row : row + 1, :] = gate_small[0:1, :]
        skips = collapse(gate_small[...], spread_matrix(heads, size), heads)
        small_o[row + 1 : row + 2, :] = jnp.concatenate(
            [gsmall[0:1, :], gsmall[1:2, :], skips[1:2, :]], axis=1
        )
        blank_row = jnp.zeros((1, inner - taps * quarter), f32)
        small_o[row + 2 : row + 3, :] = jnp.concatenate(
            [gconv[k : k + 1, :] for k in range(taps)] + [blank_row], axis=1
        )
        gains = gain_row(wbc[...], total)[0:1] + gain_z[0:1, :] + gain_x[0:1, :] + gain_dt[0:1, :]
        gains = gains / jnp.transpose(jnp.broadcast_to(gain[...], (features, LANES)))[0:1]
        small_o[row + 3 : row + 4, :] = gains[:, :inner]
        small_o[row + 4 : row + 5, :] = gains[:, inner:]
        hi, lo = split2(small_o[...])
        give_o[quarter : quarter + SMALL, :] = hi
        give_o[quarter + SMALL :, :] = lo


def back_kernel(dims, meta, lens, *refs):
    packs, count, features, inner, bc, heads, size, width, nseq = dims
    (
        main, edges, ggate, gdt, gbc, normed, wz, wx, wbc, wdt,
        own_o, far_o, send_o, dots_o,
        stage,
    ) = refs
    head = meta[1]
    part, quarter = features // 4, bc // 4
    late = count - EDGE

    def with_edge(rows, edge):
        low = (rows[late:].astype(f32) + edge.astype(f32)).astype(bf16)
        return jnp.concatenate([rows[:late], low], axis=0)

    grad_x = with_edge(main[0], edges[0, :, :inner])
    grad_bc = with_edge(gbc[0], edges[0, :, inner : inner + quarter])
    whole = nt(wz[...], ggate[0]) + nt(wx[...], grad_x) + nt(wbc[...], grad_bc) + nt(wdt[...], gdt[0])
    dots = jnp.sum(whole * normed[0].astype(f32), axis=0, keepdims=True)
    stage[...] = whole.reshape(stage.shape)
    dots_o[0] = dots
    own_o[0] = stage[head]
    far_o[0] = stage[head ^ 2]
    for k in range(2):
        send_o[k, 0, :part, :] = stage[head ^ (1 + 2 * k)].astype(bf16)
        send_o[k, 0, part:, :] = extra_rows(dots)


def extra_rows(*values):
    row = lax.broadcasted_iota(jnp.int32, (EDGE, values[0].shape[1]), 0)
    total = jnp.zeros(row.shape, f32)
    for i, value in enumerate(values):
        for k, piece in enumerate(split3(value)):
            total = total + jnp.where(row == 3 * i + k, piece.astype(f32), 0.0)
    return total.astype(bf16)


def read_extra(block, i):
    rows = block.astype(f32)
    return rows[3 * i : 3 * i + 1] + rows[3 * i + 1 : 3 * i + 2] + rows[3 * i + 2 : 3 * i + 3]


def gather_kernel(own, far, near, dots, own_o, far_o, dots_o):
    part = own.shape[1]
    own_o[0] = own[0] + near[0, 0, :part, :].astype(f32)
    far_o[0, :part, :] = (far[0] + near[1, 0, :part, :].astype(f32)).astype(bf16)
    both = dots[0] + read_extra(near[0, 0, part:, :], 0)
    dots_o[0] = both
    far_o[0, part:, :] = extra_rows(both)


def final_kernel(dims, own, far, dots, tokens, inv, gain, out_grad, in_grad_o):
    packs, count, features = dims
    part = own.shape[1]
    grad = own[0] + far[0, :part, :].astype(f32)
    mean = (dots[0] + read_extra(far[0, part:, :], 0)) / features
    unit = tokens[0].astype(f32) * inv[0]
    in_grad_o[0] = out_grad[0].astype(f32) + inv[0] * (gain[...] * grad - unit * mean)


def out_gather_kernel(own, far, near, own_o, far_o):
    own_o[0] = own[0] + near[0, 0].astype(f32)
    far_o[0] = (far[0] + near[1, 0].astype(f32)).astype(bf16)


def out_final_kernel(own, far, tokens, out):
    out[0] = (tokens[0].astype(f32) + (own[0] + far[0].astype(f32))).astype(bf16)


def add_kernel(bit, halve, segs, count, small, meta, *refs):
    keep, got, refs = refs[:count], refs[count : 2 * count], refs[2 * count :]
    end = segs[-1] if count > 1 else sum(segs)
    write = 0
    if small:
        small_in, *refs, small_o = refs
        hi, lo = split2(small_in[...])
        mine = hi.astype(f32) + lo.astype(f32)
        theirs = got[-1][end : end + SMALL, :].astype(f32) + got[-1][end + SMALL :, :].astype(f32)
        total = mine + theirs
        small_o[...] = total
        if bit is not None:
            send_o = refs[-1]
            behind = send_o.shape[0] - 2 * SMALL
            hi, lo = split2(total)
            send_o[behind : behind + SMALL, :] = hi
            send_o[behind + SMALL :, :] = lo
    read = 0
    for i, rows in enumerate(segs):
        if count > 1:
            total = keep[i][...] + got[i][:rows, :].astype(f32)
        else:
            total = keep[0][read : read + rows, :].astype(f32) + got[0][read : read + rows, :].astype(f32)
        read += rows
        if halve:
            half = rows // 2
            first = ((meta[0] >> bit) & 1) == 0
            top, bottom = total[:half], total[half:]
            refs[0][write : write + half, :] = jnp.where(first, top, bottom)
            refs[1][write : write + half, :] = jnp.where(first, bottom, top).astype(bf16)
            write += half
        else:
            refs[0][write : write + rows, :] = total.astype(bf16)
            write += rows


def join_kernel(bit, segs, meta, mine, got, out):
    first = ((meta[0] >> bit) & 1) == 0
    read = 0
    for rows in segs:
        a = mine[read : read + rows, :].astype(f32)
        b = got[read : read + rows, :].astype(f32)
        out[2 * read : 2 * read + rows, :] = jnp.where(first, a, b).astype(bf16)
        out[2 * read + rows : 2 * read + 2 * rows, :] = jnp.where(first, b, a).astype(bf16)
        read += rows


def result_kernel(segs, ways, meta, mine, got, *outs):
    first = (meta[0] & 1) == 0
    read = 0
    for rows, way, out in zip(segs, ways, outs):
        a = mine[read : read + rows, :].astype(f32)
        b = got[read : read + rows, :].astype(f32)
        top, bottom = jnp.where(first, a, b), jnp.where(first, b, a)
        if way == "rows":
            out[:rows, :] = top
            out[rows:, :] = bottom
        elif way == "flip":
            out[:, :rows] = jnp.transpose(top)
            out[:, rows:] = jnp.transpose(bottom)
        else:
            out[...] = jnp.concatenate([top, bottom], axis=1)
        read += rows


def plus_kernel(a, b, out):
    out[...] = a[...] + b[...]


def unpack_kernel(dims, meta, *refs):
    heads, features, bc_part, width = dims
    smalls, gains, dt_o, taps_x_o, taps_bc_o, bias_x_o, bias_bc_o, dt_bias_o, a_log_o, skip_o, gate_o, gain_o = refs
    for h in range(heads):
        dt_o[h : h + 1, :] = jnp.concatenate(
            [smalls[2 * h : 2 * h + 1, :], smalls[2 * h + 1 : 2 * h + 2, :]], axis=1
        )
    row = 2 * heads
    taps_x_o[...] = smalls[row : row + width, :]
    bias_x_o[...] = smalls[row + width, :]
    row += width + 1
    gate_o[...] = smalls[row, :]
    for k, out in enumerate((dt_bias_o, a_log_o, skip_o)):
        out[...] = smalls[row + 1, k * LANES : k * LANES + heads]
    taps = smalls[row + 2 : row + 3, :]
    for k in range(width):
        taps_bc_o[k : k + 1, :] = taps[:, k * bc_part : (k + 1) * bc_part]
    bias_bc_o[...] = taps[0, width * bc_part : (width + 1) * bc_part]
    both = jnp.concatenate([gains[row + 3 : row + 4, :], gains[row + 4 : row + 5, :]], axis=1)
    part = features // 4
    parts = [both[:, h * part : (h + 1) * part] for h in range(4)]
    low = jnp.where((meta[1] & 1) == 0, parts[0], parts[1])
    high = jnp.where((meta[1] & 1) == 0, parts[2], parts[3])
    gain_o[...] = jnp.where((meta[1] >> 1) == 0, low, high)[0]


def whole_spec(shape):
    return pl.BlockSpec(shape, lambda p, *_: (0,) * len(shape))


def pack_spec(shape):
    return pl.BlockSpec((1,) + shape, lambda p, *_: (p,) + (0,) * len(shape))


def half_spec(shape, half):
    return pl.BlockSpec((1,) + shape, lambda p, *_: (p % half,) + (0,) * len(shape))


def side_spec(shape, half, keep):
    def index(p, meta, *_):
        side = meta[0] & 1 if keep else 1 - (meta[0] & 1)
        group = p // half
        spot = jnp.where(group == side, p % half, jnp.where(group < side, 0, half - 1))
        return (spot,) + (0,) * len(shape)

    return pl.BlockSpec((1,) + shape, index)


class Order:
    def __init__(self):
        self.clear()

    def clear(self):
        self.last, self.near, self.held = (), [], []

    def hold(self, *arrays):
        self.held += arrays

    def drop(self, *arrays):
        self.held = [x for x in self.held if not any(x is y for y in arrays)]

    def placed(self, x):
        return pltpu.with_memory_space_constraint(x, pltpu.VMEM) if self.holds(x) else x

    def holds(self, x):
        return any(x is y for y in self.near)


order = Order()


def call(
    kernel, grid, in_specs, out_specs, out_shape, scratch, prefetch, *args, limit=20, wait=(), us=1,
    out=False,
):
    first = len(prefetch) + len(args)
    held = order.last + tuple(wait)
    held += tuple(x for x in order.held if not any(x is y for y in args + held))
    late = len(held)
    single = not isinstance(out_shape, (list, tuple))
    out_specs, out_shape = ([out_specs], [out_shape]) if single else (list(out_specs), list(out_shape))
    token = jax.ShapeDtypeStruct((8, LANES), f32)
    count = len(out_shape)

    def body(*refs):
        ins, rest = refs[:first], refs[first + late :]
        kernel(*ins, *rest[:count], *rest[count + 1 :])

    *outs, order_out = pl.pallas_call(
        body,
        grid_spec=pltpu.PrefetchScalarGridSpec(
            num_scalar_prefetch=len(prefetch),
            grid=grid,
            in_specs=list(in_specs) + [pl.BlockSpec(memory_space=pl.ANY)] * late,
            out_specs=out_specs + [whole_spec(token.shape)],
            scratch_shapes=scratch,
        ),
        out_shape=(out_shape if out else [pltpu.VMEM(x.shape, x.dtype) for x in out_shape])
        + [pltpu.VMEM(token.shape, token.dtype)],
        compiler_params=pltpu.CompilerParams(vmem_limit_bytes=limit * MIB),
        cost_estimate=pl.CostEstimate(
            flops=int(us * 10e9), bytes_accessed=int(us * 3e6), transcendentals=0
        ),
    )(*[pltpu.with_memory_space_constraint(x, pltpu.VMEM) for x in prefetch], *[order.placed(x) for x in args], *[order.placed(x) for x in held])
    order.last = (order_out,)
    order.near.append(order_out)
    if not out:
        order.near += outs
    return outs[0] if single else outs


def shape(*dims_and_type):
    return jax.ShapeDtypeStruct(dims_and_type[:-1], dims_and_type[-1])


def scan_states(keep, send, meta, packs, heads, size, rev, beside, waits=lambda: ()):
    dims = (packs, heads, size)
    rows = heads * size
    half = packs // 2
    pay = shape(half, rows + EDGE, LANES, jnp.int16)
    spec = whole_spec(pay.shape)
    bits = (lax.axis_size("seq") - 1).bit_length()
    beside = list(beside)

    def work(newest):
        if beside:
            beside.pop(0)(newest)

    other = swap(send, "seq", 1)
    work(send)
    total = call(
        functools.partial(pair_kernel, dims, rev), (1,), [spec, spec], spec, pay, [], (meta,),
        keep, other,
    )
    before = None
    for bit in range(1, bits):
        got = swap(total, "seq", 1 << bit)
        extra = () if before is None else (before,)
        work(total)
        if bit < bits - 1:
            total, before = call(
                functools.partial(cube_kernel, dims, rev, bit, before is None), (1,),
                [spec] * (2 + len(extra)), [spec, spec], [pay, pay], [], (meta,),
                total, got, *extra,
            )
        else:
            own, back = call(
                functools.partial(last_kernel, dims, rev, bit, before is None), (1,),
                [spec] * (3 + len(extra)), [spec, spec], [pay, pay], [],
                (meta,), keep, other, got, *extra, wait=waits(),
            )
    recv = swap(back, "seq", 1)
    while beside:
        work(back)
    return own, recv


class SeqSum:
    def __init__(self):
        self.keep, self.got, self.segs = [], [], []
        self.small = self.bit = None
        self.bits = list(range(1, (lax.axis_size("seq") - 1).bit_length()))
        self.halved = []

    def put(self, keep, give, segs=None, small=None):
        self.keep.append(keep)
        self.got.append(swap(give, "seq", 1))
        self.segs += segs or [keep.shape[0]]
        self.small = small

    def add(self, meta, us=1, wait=()):
        bit = self.bits.pop(0) if self.bits else None
        halve = bit is not None and all(rows % (2 * EDGE) == 0 for rows in self.segs)
        cols = self.keep[0].shape[1]
        segs = [rows // 2 for rows in self.segs] if halve else self.segs
        rows = sum(segs)
        small = self.small is not None
        behind = 2 * SMALL if small and bit is not None else 0
        low = shape(rows + behind, cols, bf16)
        out = [shape(rows, cols, f32), low] if halve else [low]
        ins = [*self.keep, *self.got]
        if small:
            ins.append(self.small)
            out.append(shape(*self.small.shape, f32))
        outs = call(
            functools.partial(add_kernel, bit, halve, self.segs, len(self.keep), small), (1,),
            [whole_spec(x.shape) for x in ins], [whole_spec(x.shape) for x in out], out, [],
            (meta,), *ins, us=us, wait=wait,
        )
        if small:
            self.small = outs[-1]
        self.segs, self.keep = segs, [outs[0]]
        if bit is None:
            return True
        self.got = [swap(outs[1] if halve else outs[0], "seq", 1 << bit)]
        if halve:
            self.halved.append(bit)
        return False

    def send_back(self):
        self.bit = self.halved.pop() if self.halved else 0
        self.got = [swap(self.keep[0], "seq", 1 << self.bit)]

    def join(self, meta, us=1):
        rows, cols = self.keep[0].shape
        both = shape(2 * rows, cols, bf16)
        spec = whole_spec((rows, cols))
        self.keep = [call(
            functools.partial(join_kernel, self.bit, self.segs), (1,), [spec, spec],
            whole_spec(both.shape), both, [], (meta,), self.keep[0], self.got[0], us=us,
        )]
        self.segs = [2 * rows for rows in self.segs]

    def result(self, meta, ways):
        cols = self.keep[0].shape[1]
        shapes = {"rows": lambda r: (2 * r, cols), "flip": lambda r: (cols, 2 * r), "cols": lambda r: (r, 2 * cols)}
        out = [shape(*shapes[way](rows), f32) for way, rows in zip(ways, self.segs)]
        spec = whole_spec(self.keep[0].shape)
        return call(
            functools.partial(result_kernel, self.segs, ways), (1,), [spec, spec],
            [whole_spec(x.shape) for x in out], out, [], (meta,), self.keep[0], self.got[0],
            out=True, us=0.1,
        )


def advance(total, meta, us=1, wait=()):
    if total.bit is None:
        if total.add(meta, us, wait):
            total.send_back()
    elif total.bit:
        total.join(meta, us)
        total.send_back()


def shards(
    tokens_in, out_grad, lengths, norm_gain, proj_z, proj_x, proj_bc, proj_dt, conv_x, conv_bc,
    bias_x, bias_bc, dt_bias, a_log, d_skip, gate_gain, proj_out,
):
    packs, count, part = tokens_in.shape
    features, inner = proj_x.shape
    heads = proj_dt.shape[1]
    size = inner // heads
    width = conv_x.shape[0]
    nseq = lengths.shape[1]
    bc_part = proj_bc.shape[1]
    bc = bc_part * lax.axis_size("head")
    half = packs // 2
    chans = inner + bc
    ext = count + EDGE
    rows = heads * size
    total_inner = inner * lax.axis_size("head")
    dims = (packs, count, features, inner, bc, heads, size, width, nseq)
    seq_place, head_place = lax.axis_index("seq"), lax.axis_index("head")
    meta = jnp.stack([seq_place, head_place]).astype(jnp.int32)
    pre = (meta, lengths)
    grid = (packs,)

    order.clear()
    tokens = jnp.swapaxes(tokens_in, 1, 2)
    cotangent = jnp.swapaxes(out_grad, 1, 2)
    far = swap(tokens, "head", 2)
    near = swap(tokens, "head", 1)
    tail = call(
        tail_kernel, (1,),
        [pl.BlockSpec((packs, part, LANES), lambda p: (0, 0, count // LANES - 1))],
        whole_spec((part, LANES)), shape(part, LANES, bf16), [], (), tokens, us=0.05,
    )
    tail = shift(tail, "seq", 1)
    ins = [
        proj_bc.T, conv_bc, bias_bc, norm_gain, proj_dt.T, conv_x, bias_x, dt_bias, a_log, d_skip,
        gate_gain,
    ]
    outs = [
        shape(bc_part, features + LANES, bf16), shape(features, bc_part, bf16),
        shape(features, LANES, bf16), shape(LANES, features, bf16), shape(8, inner, f32),
        shape(8, bc_part, f32), shape(8, LANES, f32), shape(1, inner, f32), shape(1, inner, f32),
        shape(part, 1, f32),
    ]
    (
        shared, w_bc, w_dt, w_dt_rows, conv_own, conv_bc_own, small, skip, gain_gate, norm_gain_own,
    ) = call(
        functools.partial(prepare_kernel, dims), (1,), [whole_spec(x.shape) for x in ins],
        [whole_spec(x.shape) for x in outs], outs, [], (), *ins, wait=(tail,),
        us=0.05,
    )
    edge_pieces = head_pieces(tail)
    weight_pieces = head_pieces(shared)
    behind = (far, edge_pieces[2], weight_pieces[2])
    diagonal = swap(lax.optimization_barrier(behind)[0], "head", 1)
    token_pieces = tokens, near, far, diagonal

    lane_spec = pack_spec((count, LANES))
    chan_spec = pack_spec((count, inner))
    xbc_spec = pack_spec((count, chans))
    model_spec = pack_spec((features, count))
    piece_spec = pack_spec((part, count))
    edge_spec = whole_spec((part, LANES))
    pay_shape = (rows + EDGE, LANES)
    pay_specs = [side_spec(pay_shape, half, k) for k in (True, False)]
    pay = shape(half, *pay_shape, jnp.int16)
    state_spec = half_spec(pay_shape, half)
    vec = whole_spec((1, inner))
    square = whole_spec((features, inner))

    (
        normed, inv, edge, raw_x, raw_bc, xbc, steps, keep, send, gain_all,
    ) = call(
        functools.partial(front_kernel, dims),
        grid,
        [piece_spec] * 4
        + [edge_spec] * 4
        + [whole_spec((bc_part, features + LANES))] * 4
        + [square, whole_spec((LANES, features)), whole_spec((8, inner)),
           whole_spec((8, LANES))],
        [
            model_spec, pack_spec((1, count)), whole_spec((features, LANES)),
            pack_spec((ext, inner)), pack_spec((ext, bc_part)), xbc_spec, lane_spec, *pay_specs,
            whole_spec((features, 1)),
        ],
        [
            shape(packs, features, count, bf16), shape(packs, 1, count, f32),
            shape(features, LANES, bf16), shape(packs, ext, inner, bf16),
            shape(packs, ext, bc_part, bf16), shape(packs, count, chans, bf16),
            shape(packs, count, LANES, f32), pay, pay, shape(features, 1, f32),
        ],
        [
            pltpu.VMEM((4, part, count), bf16), pltpu.VMEM((4, part, LANES), bf16),
            pltpu.VMEM((4, bc_part, features + LANES), bf16), pltpu.VMEM((ext, chans), f32),
            pltpu.VMEM((LANES, chans), f32), pltpu.VMEM((8, chans), f32),
            pltpu.VMEM((features, 1), f32),
        ],
        pre,
        *token_pieces, *edge_pieces, *weight_pieces, proj_x, w_dt_rows, conv_own, small,
        us=15,
    )

    kept = {}
    order.hold(xbc, steps, normed)

    def inner_work(_):
        kept["inner"] = call(
            functools.partial(inner_kernel, dims),
            grid,
            [xbc_spec, lane_spec],
            chan_spec,
            shape(packs, count, inner, f32),
            [],
            pre,
            xbc, steps,
            us=6,
        )
        own = lax.optimization_barrier((cotangent, kept["inner"]))[0]
        kept["cots"] = own, swap(own, "head", 2)
        order.hold(kept["inner"])

    def cot_work(newest):
        own, far = kept["cots"]
        near = swap(own, "head", 1)
        cots = own, near, far, swap(lax.optimization_barrier((far, newest))[0], "head", 1)
        kept["cot"], kept["gg"] = call(
            functools.partial(cot_kernel, dims),
            grid,
            [piece_spec] * 4 + [whole_spec((inner, features))],
            [model_spec, chan_spec],
            [shape(packs, features, count, bf16), shape(packs, count, inner, f32)],
            [pltpu.VMEM((4, part, count), bf16)],
            pre,
            *cots, proj_out,
            us=5.5,
        )

    def gate_slope_work(_):
        kept["slope"] = call(
            functools.partial(gate_slope_kernel, dims),
            grid,
            [model_spec, square, pack_spec((ext, inner)), pack_spec((ext, bc_part)),
             whole_spec((8, inner)), whole_spec((8, bc_part))],
            [chan_spec, chan_spec, pack_spec((count, bc_part))],
            [shape(packs, count, inner, bf16), shape(packs, count, inner, f32),
             shape(packs, count, bc_part, f32)],
            [pltpu.VMEM((ext, inner), f32), pltpu.VMEM((ext, bc_part), f32)],
            pre,
            normed, proj_z, raw_x, raw_bc, conv_own, conv_bc_own,
            us=7,
        )

    state_keep, state_recv = scan_states(
        keep, send, meta, packs, heads, size, 0, (inner_work, gate_slope_work, cot_work)
    )
    inner_out, cot, gg = kept["inner"], kept["cot"], kept["gg"]
    gate, slope_x, slope_bc = kept["slope"]
    order.drop(inner_out)

    y, stats = call(
        functools.partial(gate_kernel, dims),
        grid,
        [
            xbc_spec, lane_spec, chan_spec, state_spec, state_spec, chan_spec, chan_spec, vec, vec,
        ],
        [chan_spec, pack_spec((2, count))],
        [shape(packs, count, inner, f32), shape(packs, 2, count, f32)],
        [],
        pre,
        xbc, steps, inner_out, state_keep, state_recv, gate, gg, gain_gate, skip,
        us=6.6,
    )
    stats = head_pieces(stats)

    gy, gated, ggate, gkeep, gsend, gate_small = call(
        functools.partial(grad_kernel, dims, total_inner),
        grid,
        [
            *[pack_spec((2, count))] * 4, xbc_spec, lane_spec, chan_spec, chan_spec, chan_spec, vec,
            vec,
        ],
        [chan_spec] * 3 + pay_specs + [whole_spec((8, inner))],
        [shape(packs, count, inner, f32)] + [shape(packs, count, inner, bf16)] * 2
        + [pay, pay, shape(8, inner, f32)],
        [],
        pre,
        *stats, xbc, steps, y, gate, gg, gain_gate, skip,
        us=8.3,
    )

    piece_shape = shape(packs, part, count, f32)
    send_spec = pl.BlockSpec((2, 1, part, count), lambda p, *_: (0, p, 0, 0))
    rows_half = features // 2
    half_specs = [whole_spec((rows_half, inner))] * 2
    half_shapes = [shape(rows_half, inner, f32), shape(rows_half, inner, bf16)]
    half_sums = pltpu.VMEM((2, rows_half, inner), f32)
    row8, row8_shape = whole_spec((8, features)), shape(8, features, f32)

    early_sum, late_sum = SeqSum(), SeqSum()

    def out_work(_):
        *kept["out"], keep, give = call(
            functools.partial(out_kernel, dims),
            grid,
            [chan_spec, model_spec, whole_spec((inner, features))],
            [piece_spec, piece_spec, send_spec] + half_specs,
            [piece_shape, piece_shape, shape(2, packs, part, count, bf16)] + half_shapes,
            [pltpu.VMEM((4, part, count), f32), half_sums],
            pre,
            gated, cot, proj_out,
            us=6.8,
        )
        early_sum.put(keep, give)

    def z_work(_):
        keep, give, kept["gain"] = call(
            functools.partial(z_kernel, dims),
            grid,
            [model_spec, chan_spec, square],
            half_specs + [row8],
            half_shapes + [row8_shape],
            [half_sums],
            pre,
            normed, ggate, proj_z,
            us=5.3,
        )
        early_sum.put(keep, give)

    def diag_work(_):
        kept["diag"] = call(
            functools.partial(diag_kernel, dims),
            grid,
            [xbc_spec, lane_spec, chan_spec, chan_spec, state_spec, state_spec],
            [chan_spec, pack_spec((count, bc)), lane_spec],
            [
                shape(packs, count, inner, f32), shape(packs, count, bc, f32),
                shape(packs, count, LANES, f32),
            ],
            [],
            pre,
            xbc, steps, gy, y, state_keep, state_recv,
            us=12,
        )

    def early_work(_):
        early_sum.add(meta)
        own, far, send = kept["out"]
        own, far = call(
            out_gather_kernel, grid, [piece_spec, piece_spec, send_spec], [piece_spec, piece_spec],
            [piece_shape, shape(packs, part, count, bf16)], [], (), own, far, swap(send, "head", 1),
        )
        kept["out"] = own, swap(far, "head", 2)

    gstate_keep, gstate_recv = scan_states(
        gkeep, gsend, meta, packs, heads, size, 1, (out_work, z_work, diag_work, early_work),
        lambda: early_sum.got,
    )
    out_own, out_far = kept["out"]
    dx, dbc, sums = kept["diag"]

    edge_tile = (EDGE, inner)
    share_own, share_near, grad_x, state_sums, edge_x = call(
        functools.partial(share_kernel, dims),
        grid,
        [xbc_spec, lane_spec, pack_spec((count, bc)), state_spec, state_spec, chan_spec, chan_spec,
         chan_spec, whole_spec((8, inner)), vec],
        [lane_spec, lane_spec, chan_spec, lane_spec, pack_spec(edge_tile)],
        [shape(packs, count, LANES, f32)] * 2
        + [shape(packs, count, inner, f32), shape(packs, count, LANES, f32),
           shape(packs, *edge_tile, bf16)],
        [pltpu.VMEM((2 * EDGE, inner), f32)],
        pre,
        xbc, steps, dbc, gstate_keep, gstate_recv, gy, dx, slope_x, conv_own, skip,
        us=6.4,
    )
    share_near = swap(share_near, "head", 1)
    advance(early_sum, meta)
    two = shape(half, count, LANES, f32)
    bc_keep, bc_send = call(
        functools.partial(middle_kernel, (packs, bc_part)),
        (1,),
        [whole_spec((packs, count, LANES))] * 2,
        [whole_spec(two.shape)] * 2,
        [two, two],
        [],
        (meta,),
        share_own, share_near,
    )
    bc_recv = swap(bc_send, "head", 2)

    main_x, keep, give, grad_conv, gain_x = call(
        functools.partial(xback_kernel, dims),
        grid,
        [
            chan_spec, pack_spec((ext, inner)), model_spec, whole_spec((features, LANES)),
            pack_spec(edge_tile), whole_spec((8, inner)), square,
        ],
        [chan_spec, *half_specs, whole_spec((8, inner)), row8],
        [shape(packs, count, inner, bf16), *half_shapes, shape(8, inner, f32), row8_shape],
        [
            pltpu.VMEM((count + EDGE, inner), f32), pltpu.VMEM((ext, inner), f32), half_sums,
            pltpu.VMEM((LANES, inner), bf16),
        ],
        pre,
        grad_x, raw_x, normed, edge, edge_x, conv_own, proj_x,
        us=7, wait=(out_far,),
    )
    late_sum.put(keep, give)
    advance(early_sum, meta)

    gdt, gdt_rows, grad_small, gain_dt = call(
        functools.partial(step_kernel, dims),
        grid,
        [
            lane_spec, lane_spec, lane_spec, state_spec, state_spec, state_spec, state_spec,
            whole_spec((8, LANES)), model_spec, whole_spec((features, LANES)),
        ],
        [lane_spec, row8, whole_spec((8, LANES)), row8],
        [shape(packs, count, LANES, bf16), row8_shape, shape(8, LANES, f32), row8_shape],
        [pltpu.VMEM((features, LANES), f32)],
        pre,
        steps, sums, state_sums, state_keep, state_recv, gstate_keep, gstate_recv, small, normed,
        w_dt,
        us=6,
    )
    advance(early_sum, meta)
    give_rows = bc_part + 2 * SMALL
    gbc, edges, keep, give, smalls = call(
        functools.partial(conv_bc_kernel, dims),
        grid,
        [
            half_spec((count, LANES), half), half_spec((count, LANES), half),
            pack_spec((count, bc_part)), pack_spec((ext, bc_part)), model_spec,
            whole_spec((features, LANES)), whole_spec((features, bc_part)),
            whole_spec((8, bc_part)), pack_spec(edge_tile), whole_spec((8, inner)), row8,
            whole_spec((8, LANES)), whole_spec((8, inner)), row8, row8, row8,
            whole_spec((features, 1)),
        ],
        [
            pack_spec((count, bc_part)), pack_spec((EDGE, inner + LANES)),
            whole_spec((bc_part, inner)), whole_spec((give_rows, inner)),
            whole_spec((SMALL, inner)),
        ],
        [
            shape(packs, count, bc_part, bf16), shape(packs, EDGE, inner + LANES, bf16),
            shape(bc_part, inner, f32), shape(give_rows, inner, bf16), shape(SMALL, inner, f32),
        ],
        [
            pltpu.VMEM((ext + EDGE, bc_part), f32), pltpu.VMEM((ext, bc_part), f32),
            pltpu.VMEM((features, bc_part), f32), pltpu.VMEM((LANES, bc_part), bf16),
            pltpu.VMEM((8, bc_part), f32),
        ],
        pre,
        bc_keep, bc_recv, slope_bc, raw_bc, normed, edge, w_bc, conv_bc_own, edge_x, grad_conv,
        gdt_rows, grad_small, gate_small, kept["gain"], gain_x, gain_dt, gain_all,
        us=5,
    )
    edges = shift(edges, "seq", -1)
    late_sum.put(keep, give, small=smalls)
    advance(late_sum, meta, wait=early_sum.got)
    advance(early_sum, meta)

    tall = part + EDGE
    tall_send = pl.BlockSpec((2, 1, tall, count), lambda p, *_: (0, p, 0, 0))
    tall_spec = pack_spec((tall, count))
    row_spec, row_shape = pack_spec((1, count)), shape(packs, 1, count, f32)
    gn_own, gn_far, gn_send, dots = call(
        functools.partial(back_kernel, dims),
        grid,
        [
            chan_spec, pack_spec((EDGE, inner + LANES)), chan_spec, lane_spec,
            pack_spec((count, bc_part)), model_spec, square, square,
            whole_spec((features, bc_part)), whole_spec((features, LANES)),
        ],
        [piece_spec, piece_spec, tall_send, row_spec],
        [piece_shape, piece_shape, shape(2, packs, tall, count, bf16), row_shape],
        [pltpu.VMEM((4, part, count), f32)],
        pre,
        main_x, edges, ggate, gdt, gbc, normed, proj_z, proj_x, w_bc, w_dt,
        us=6,
    )
    near = swap(gn_send, "head", 1)
    order.drop(xbc, steps, normed)
    advance(late_sum, meta, 0.1)

    block_out = call(
        out_final_kernel, grid, [piece_spec] * 3, piece_spec, shape(packs, part, count, bf16), [],
        (), out_own, out_far, tokens, out=True, us=2,
    )
    block_out = jnp.swapaxes(block_out, 1, 2)
    while early_sum.bit != 0:
        advance(early_sum, meta)
    advance(late_sum, meta, 0.1)

    gn_own, gn_far, dots = call(
        gather_kernel,
        grid,
        [piece_spec, piece_spec, tall_send, row_spec],
        [piece_spec, tall_spec, row_spec],
        [piece_shape, shape(packs, tall, count, bf16), row_shape],
        [],
        (),
        gn_own, gn_far, near, dots,
        us=0.1,
    )
    gn_far = swap(gn_far, "head", 2)
    order.hold(gn_own)
    grads_out, grads_z = early_sum.result(meta, ("flip", "rows"))
    advance(late_sum, meta, 0.1)
    smalls = gains = late_sum.small
    small_spec = whole_spec(smalls.shape)

    def head_step(x, bit):
        return call(
            plus_kernel, (1,), [small_spec, small_spec], small_spec, shape(*x.shape, f32), [], (),
            x, swap(x, "head", bit), us=1,
        )

    gains = head_step(gains, 1)
    advance(late_sum, meta)
    gains = head_step(gains, 2)
    while late_sum.bit != 0:
        advance(late_sum, meta)
    in_grad = call(
        functools.partial(final_kernel, (packs, count, features)),
        grid,
        [piece_spec, tall_spec, row_spec, piece_spec, row_spec, whole_spec((part, 1)), piece_spec],
        piece_spec,
        piece_shape,
        [],
        (),
        gn_own, gn_far, dots, tokens, inv, norm_gain_own, cotangent,
        us=2, out=True,
    )
    in_grad = jnp.swapaxes(in_grad, 1, 2)
    order.drop(gn_own)
    vectors = [(inner,), (bc_part,), (heads,), (heads,), (heads,), (inner,), (part,)]
    tables = [(heads, features), (width, inner), (width, bc_part)]
    outs = call(
        functools.partial(unpack_kernel, (heads, features, bc_part, width)), (1,),
        [small_spec, small_spec], [whole_spec(x) for x in tables + vectors],
        [shape(*x, f32) for x in tables + vectors], [], (meta,), smalls, gains, out=True,
    )
    grad_dt, grad_conv, grad_conv_bc = outs[:3]
    bias_x_grad, bias_bc_grad, dt_bias_grad, a_log_grad, skip_grad, gate_grad, grad_gain = outs[3:]
    grads_x, grad_bc = late_sum.result(meta, ("rows", "cols"))
    return (
        block_out,
        in_grad,
        grad_gain,
        grads_z,
        grads_x,
        grad_bc.T,
        grad_dt.T,
        grad_conv,
        grad_conv_bc,
        bias_x_grad,
        bias_bc_grad,
        dt_bias_grad,
        a_log_grad,
        skip_grad,
        gate_grad,
        grads_out,
    )


def solution(mesh):
    token, column, vector = P(None, "seq", "head"), P(None, "head"), P("head")
    row = P("head", None)
    return jax.shard_map(
        shards,
        mesh=mesh,
        in_specs=(
            token, token, P(), vector, column, column, column, column, column, column, vector,
            vector, vector, vector, vector, vector, row,
        ),
        out_specs=(
            token, token, vector, column, column, column, column, column, column, vector, vector,
            vector, vector, vector, vector, row,
        ),
        check_vma=False,
    )
```

```python
import functools

import jax
import jax.numpy as jnp
from jax import lax
from jax.experimental import pallas as pl
from jax.experimental.pallas import tpu as pltpu
from jax.sharding import PartitionSpec as P

EPSILON = 1e-05
bf16 = jnp.bfloat16
f32 = jnp.float32
LANES = 128
EDGE = 16
MIB = 1024 * 1024
STEPS = 32000.0
UNIT = 16384.0
LN2 = 0.6931471805599453
GROUP = 16
SMALL = 32


def permuted(x, axis, route):
    y = lax.ppermute(x, axis, route)
    order.near.append(y)
    return y


def swap(x, axis, bit):
    return permuted(x, axis, [(i, i ^ bit) for i in range(lax.axis_size(axis))])


def shift(x, axis, distance):
    n = lax.axis_size(axis)
    return permuted(x, axis, [(i, i + distance) for i in range(n) if 0 <= i + distance < n])


def head_pieces(x):
    far = swap(x, "head", 2)
    near = swap(x, "head", 1)
    return x, near, far, swap(far, "head", 1)


def nn(a, b):
    return lax.dot_general(a, b, (((1,), (0,)), ((), ())), preferred_element_type=f32)


def nt(a, b):
    return lax.dot_general(a, b, (((1,), (1,)), ((), ())), preferred_element_type=f32)


def tn(a, b):
    return lax.dot_general(a, b, (((0,), (0,)), ((), ())), preferred_element_type=f32)


def split2(v):
    hi = v.astype(bf16)
    return hi, (v - hi.astype(f32)).astype(bf16)


def split3(v):
    hi = v.astype(bf16)
    rest = v - hi.astype(f32)
    mid = rest.astype(bf16)
    return hi, mid, (rest - mid.astype(f32)).astype(bf16)


def spread_matrix(heads, size):
    row = lax.broadcasted_iota(jnp.int32, (LANES, heads * size), 0)
    col = lax.broadcasted_iota(jnp.int32, (LANES, heads * size), 1)
    first = (col >= row * size) & (col < (row + 1) * size)
    again = (col >= (row - GROUP) * size) & (col < (row - GROUP + 1) * size)
    return jnp.where(first | again, 1.0, 0.0).astype(bf16)


def spread(v, matrix, heads):
    hi, lo = split2(head_lanes(v, heads))
    return nn((hi.astype(f32) + to_group(lo.astype(f32), 1)).astype(bf16), matrix)


def head_lanes(v, heads):
    return jnp.where(lax.broadcasted_iota(jnp.int32, v.shape, 1) < heads, v, 0.0)


def to_group(v, k):
    return pltpu.roll(v, k * GROUP, 1)


def from_group(v, k, heads):
    return head_lanes(pltpu.roll(v, LANES - k * GROUP, 1) if k else v, heads)


def collapse(v, matrix, heads):
    return head_lanes(nt(jnp.concatenate(split2(v), axis=1), jnp.concatenate([matrix] * 2, axis=1)), heads)


def triangle(count, lower):
    row = lax.broadcasted_iota(jnp.int32, (count, count), 0)
    col = lax.broadcasted_iota(jnp.int32, (count, count), 1)
    keep = (row >= col) if lower else (row <= col)
    return jnp.where(keep, 1.0, 0.0).astype(bf16)


def exact_sums(matrix, v, heads):
    hi, mid, lo = [piece.astype(f32) for piece in split3(v)]
    sums = nn(matrix, (hi + to_group(mid, 1) + to_group(lo, 2)).astype(bf16))
    return from_group(sums, 0, heads) + from_group(sums, 1, heads) + from_group(sums, 2, heads)


def step_sizes(v, heads):
    soft = jnp.maximum(v, 0.0) + jnp.log1p(jnp.exp(-jnp.abs(v)))
    return head_lanes(soft, heads)


def steps_of(block, heads):
    return step_sizes(block, heads), from_group(block, 1, heads)


def segments(positions, lens_ref, pack, count):
    total = jnp.zeros(positions.shape, jnp.int32)
    end = jnp.int32(0)
    for k in range(count):
        end = end + lens_ref[pack, k]
        total = total + jnp.where(positions >= end, 1, 0)
    return total


def column_segments(meta_ref, lens_ref, pack, count, nseq, before):
    rows = lax.broadcasted_iota(jnp.int32, (count + before, 1), 0)
    return segments(rows + (meta_ref[0] * count - before), lens_ref, pack, nseq)


def row_segments(meta_ref, lens_ref, pack, count, nseq):
    cols = lax.broadcasted_iota(jnp.int32, (1, count), 1)
    return segments(cols + meta_ref[0] * count, lens_ref, pack, nseq)


def carry_column(meta_ref, seg_ext, before):
    same = seg_ext[before:] == seg_ext[before - 1 : before]
    return jnp.where(same & (meta_ref[0] > 0), 1.0, 0.0)


def to_int16(v):
    return jnp.floor(v + 0.5).astype(jnp.int32).astype(jnp.int16)


def encode_state(out, p, state, decay, heads, size):
    lane = lax.broadcasted_iota(jnp.int32, (1, LANES), 1)
    powers = jnp.zeros((1, LANES), f32)
    for h in range(heads):
        part = state[h * size : (h + 1) * size]
        top = jnp.max(jnp.max(jnp.abs(part), axis=0, keepdims=True), axis=1, keepdims=True)
        power = jnp.ceil(jnp.log(jnp.maximum(top, 1e-30)) / LN2)
        powers = powers + jnp.where(lane == h, power, 0.0)
        codes = jnp.clip(part * (jnp.exp(-power * LN2) * STEPS), -32767.0, 32767.0)
        out[p, h * size : (h + 1) * size, :] = to_int16(codes)
    row = lax.broadcasted_iota(jnp.int32, (EDGE, LANES), 0)
    coarse = jnp.floor(decay * UNIT)
    fine = (decay * UNIT - coarse) * UNIT
    tail = jnp.where(row == 0, powers, jnp.where(row == 1, coarse, jnp.where(row == 2, fine, 0.0)))
    out[p, heads * size :, :] = to_int16(tail)


def decode_state(block, heads, size):
    values = block.astype(jnp.int32).astype(f32)
    tail = values[heads * size :]
    scale = jnp.exp(tail[0:1] * LN2) / STEPS
    decay = (tail[1:2] + tail[2:3] / UNIT) / UNIT
    return scaled_state(values[: heads * size], scale, heads, size), decay


def sigmoid(v):
    return 1.0 / (1.0 + jnp.exp(-v))


def scaled_state(state, decay, heads, size):
    return jnp.concatenate(
        [state[h * size : (h + 1) * size] * decay[:, h : h + 1] for h in range(heads)], axis=0
    )


def tail_kernel(meta, tokens, out):
    lane = lax.broadcasted_iota(jnp.int32, out.shape, 1)
    total = jnp.zeros(out.shape, f32)
    for p in range(tokens.shape[0]):
        moved = pltpu.roll(tokens[p].astype(f32), (p + 1) * EDGE, 1)
        total = jnp.where((lane >= p * EDGE) & (lane < (p + 1) * EDGE), moved, total)
    out[...] = total.astype(bf16)


def wide_row(ref, lanes=LANES):
    row = ref[...].astype(f32)[None, :]
    blank = lanes - row.shape[1]
    return jnp.concatenate([row, jnp.zeros((1, blank), f32)], axis=1) if blank else row


def prepare_kernel(dims, *refs):
    packs, count, features, inner, bc, heads, size, width, nseq = dims
    (
        wbc, conv_bc, bias_bc, norm_gain, wdt, conv_x, bias_x, dt_bias, a_log, d_skip, gate_gain, wout,
        wout_o, shared_o, wbc_o, wdt_o, wdt_rows_o, conv_x_o, conv_bc_o, small_o, skip_o, gate_gain_o, gain_o,
    ) = refs
    bc_part, part = bc // 4, features // 4
    wout_o[...] = jnp.transpose(wout[...])
    taps = conv_bc[...].astype(f32)
    bias = wide_row(bias_bc, bc_part)
    gain = wide_row(norm_gain, part)
    pieces = [gain[:, c * bc_part : (c + 1) * bc_part] for c in range(part // bc_part)]
    rows = jnp.concatenate([taps, bias] + pieces, axis=0)
    rows = jnp.concatenate([rows, jnp.zeros((LANES - rows.shape[0], bc_part), f32)], axis=0)
    rows = jnp.concatenate([rows, jnp.zeros((LANES, LANES - bc_part), f32)], axis=1)
    extra = jnp.transpose(rows)[:bc_part].astype(bf16)
    shared_o[:, :features] = wbc[...]
    shared_o[:, features:] = extra
    wbc_o[...] = jnp.transpose(wbc[...].astype(f32)).astype(bf16)
    dt_rows = jnp.concatenate(
        [wdt[...].astype(f32), jnp.zeros((LANES - heads, features), f32)], axis=0
    )
    wdt_rows_o[...] = dt_rows.astype(bf16)
    wdt_o[...] = jnp.transpose(dt_rows).astype(bf16)
    blank = jnp.zeros((7 - width, inner), f32)
    conv_x_o[...] = jnp.concatenate(
        [conv_x[...].astype(f32), wide_row(bias_x, inner), blank], axis=0
    )
    conv_bc_o[...] = jnp.concatenate([taps, bias, blank[:, :bc_part]], axis=0)
    small_o[...] = jnp.concatenate(
        [wide_row(dt_bias), wide_row(a_log), jnp.zeros((6, LANES), f32)], axis=0
    )
    skips = jnp.concatenate([wide_row(d_skip), jnp.zeros((7, LANES), f32)], axis=0)
    matrix = spread_matrix(heads, size)
    skip_o[...] = sum(nn(piece, matrix) for piece in split3(skips))[0:1]
    gate_gain_o[...] = wide_row(gate_gain, inner)
    column = jnp.concatenate([gain, jnp.zeros((LANES - 1, part), f32)], axis=0)
    column = jnp.concatenate([column, jnp.zeros((LANES, 2 * LANES - part), f32)], axis=1)
    gain_o[...] = jnp.transpose(column)[:part, 0:1]


def normalise(values, gain, features):
    mean = jnp.sum(values * values, axis=0, keepdims=True) / features
    inv = lax.rsqrt(mean + EPSILON)
    return inv, ((values * inv) * gain).astype(bf16)


def raw_rows(normed, wx, wbc):
    return jnp.concatenate([nn(normed, wx), nt(normed, wbc)], axis=1).astype(bf16)


def border_kernel(dims, meta, *refs):
    packs, count, features, inner, bc, heads, size, width, nseq = dims
    edges, shared = refs[0:4], refs[4:8]
    wx, conv_x, wbc_o, conv_o, gain_o, edge_o, raws_o, stage, weights = refs[8:]
    head = meta[1]
    part, bc_part = features // 4, bc // 4
    for k in range(4):
        weights[head ^ k] = shared[k][...]
        stage[head ^ k] = edges[k][...]
    whole = weights[...].reshape(bc, weights.shape[2])
    wbc_o[...] = whole[:, :features]
    extra = whole[:, features:].astype(f32)
    conv_o[:, :inner] = conv_x[...]
    conv_o[:, inner:] = jnp.transpose(extra)[0:8]
    for h in range(4):
        for c in range(part // bc_part):
            gain_o[h * part + c * bc_part : h * part + (c + 1) * bc_part, :] = extra[
                h * bc_part : (h + 1) * bc_part, width + 1 + c : width + 2 + c
            ]
    _, normed = normalise(stage[...].reshape(features, stage.shape[2]).astype(f32), gain_o[...], features)
    edge_o[...] = normed
    raws_o[...] = raw_rows(jnp.transpose(normed), wx[...], wbc_o[...]).astype(f32)


def front_kernel(dims, keep, meta, lens, *refs):
    packs, count, features, inner, bc, heads, size, width, nseq = dims
    tokens, refs = refs[0:4], refs[4:]
    wx, wbc, wdt, conv, small, gain, edge_raws, *refs = refs
    normed_o, inv_o, rawx_o, rawbc_o, xbc_o, steps_o, state_o, stage, raws = refs[-9:]
    side = meta[0] & 1 if keep else 1 - (meta[0] & 1)
    pack = order.pack + (packs // 2) * side
    head = meta[1]
    for k in range(4):
        stage[head ^ k] = tokens[k][0]
    inv, normed_t = normalise(stage[...].reshape(features, count).astype(f32), gain[...], features)
    inv_o[0] = inv
    normed_o[0] = normed_t
    normed = jnp.transpose(normed_t)
    raws[EDGE:, :] = raw_rows(normed, wx[...], wbc[...]).astype(f32)
    raws[0:EDGE, :] = edge_raws[pl.ds(pl.multiple_of(pack * EDGE, EDGE), EDGE), :]

    def own_bc(values):
        bc_part = bc // 4
        parts = [values[:, inner + h * bc_part : inner + (h + 1) * bc_part] for h in range(4)]
        low = jnp.where((head & 1) == 0, parts[0], parts[1])
        high = jnp.where((head & 1) == 0, parts[2], parts[3])
        return jnp.where((head >> 1) == 0, low, high)

    rawx_o[0] = raws[:, :inner].astype(bf16)
    rawbc_o[0] = own_bc(raws[...]).astype(bf16)
    seg = column_segments(meta, lens, pack, count, nseq, EDGE)
    seg_main = seg[EDGE:]
    pre = convolved(raws, conv, seg, count, width)
    xbc = (pre * sigmoid(pre)).astype(bf16)
    xbc_o[0] = xbc
    v = head_lanes(nt(normed, wdt[...]).astype(bf16).astype(f32) + small[0:1, :], heads)
    dt = step_sizes(v, heads)
    rate = -dt * jnp.exp(small[1:2, :])
    cum = exact_sums(triangle(count, True), rate, heads)
    steps_o[0] = v + to_group(cum, 1)
    cum_end = cum[count - 1 : count]
    weight = jnp.where(seg_main == seg[count + EDGE - 1 :], jnp.exp(cum_end - cum), 0.0) * dt
    matrix = spread_matrix(heads, size)
    scaled = (xbc[:, :inner].astype(f32) * spread(weight, matrix, heads)).astype(bf16)
    state = jnp.transpose(nn(jnp.transpose(xbc[:, inner : inner + bc // 2]), scaled))
    carry = carry_column(meta, seg, EDGE)
    encode_state(state_o, 0, state, carry[count - 1 :] * jnp.exp(cum_end), heads, size)


def convolved(raws, conv, seg, count, width):
    pre = jnp.broadcast_to(conv[width : width + 1, :], (count, raws.shape[1]))
    for k in range(width):
        low = EDGE - (width - 1) + k
        mask = jnp.where(seg[low : low + count] == seg[EDGE:], 1.0, 0.0)
        pre = pre + conv[k : k + 1, :] * raws[low : low + count, :] * mask
    return pre


def gate_slope_kernel(dims, meta, lens, *refs):
    packs, count, features, inner, bc, heads, size, width, nseq = dims
    normed, wz, raw_x, raw_bc, conv_x, conv_bc, gate_o, slope_x_o, slope_bc_o, raws, raws_bc = refs
    pack = order.pack
    gate_o[0] = tn(normed[0], wz[...]).astype(bf16)
    seg = column_segments(meta, lens, pack, count, nseq, EDGE)
    for raw, wide, conv, out in ((raw_x, raws, conv_x, slope_x_o), (raw_bc, raws_bc, conv_bc, slope_bc_o)):
        wide[...] = raw[0].astype(f32)
        pre = convolved(wide, conv, seg, count, width)
        sig = sigmoid(pre)
        out[0] = sig * (1.0 + pre * (1.0 - sig))


def store_state(meta, packs, pack, keep_o, send_o, state, decay, heads, size):
    mine = (pack // (packs // 2)) == (meta[0] & 1)

    @pl.when(mine)
    def _():
        encode_state(keep_o, 0, state, decay, heads, size)

    @pl.when(jnp.logical_not(mine))
    def _():
        encode_state(send_o, 0, state, decay, heads, size)


def load_state(meta, packs, pack, keep, recv, heads, size):
    mine = (pack // (packs // 2)) == (meta[0] & 1)
    block = jnp.where(mine, keep[0].astype(jnp.int32), recv[0].astype(jnp.int32))
    return decode_state(block, heads, size)[0]


def decay_parts(cum_col, cum_row, masked):
    return masked * jnp.exp(jnp.minimum(cum_col - cum_row, 0.0))


def block_mask(meta, lens, pack, count, nseq):
    col = column_segments(meta, lens, pack, count, nseq, 0)
    row = row_segments(meta, lens, pack, count, nseq)
    tri = lax.broadcasted_iota(jnp.int32, (count, count), 0) >= lax.broadcasted_iota(
        jnp.int32, (count, count), 1
    )
    return tri & (col == row)


def inner_kernel(dims, meta, lens, *refs):
    packs, count, features, inner, bc, heads, size, width, nseq = dims
    xbc, steps, inner_o = refs
    pack = order.pack
    half = bc // 2
    b_vals, c_vals = xbc[0, :, inner : inner + half], xbc[0, :, inner + half :]
    scores = jnp.where(block_mask(meta, lens, pack, count, nseq), nt(c_vals, b_vals), 0.0)
    dt, cum_col = steps_of(steps[0], heads)
    cum_row = jnp.transpose(cum_col)
    dt_row = jnp.transpose(dt)
    lane = lax.broadcasted_iota(jnp.int32, (count, 2 * size), 1)
    for pair in range(heads // 2):
        cols = slice(2 * pair * size, (2 * pair + 2) * size)
        x_pair = xbc[0, :, cols]
        parts = []
        for h in (2 * pair, 2 * pair + 1):
            weights = decay_parts(cum_col[:, h : h + 1], cum_row[h : h + 1], scores)
            parts.append(nn((weights * dt_row[h : h + 1]).astype(bf16), x_pair))
        inner_o[0, :, cols] = jnp.where(lane < size, parts[0], parts[1])


def cot_kernel(dims, meta, lens, *refs):
    packs, count, features, inner, bc, heads, size, width, nseq = dims
    pieces, (wout, cot_o, gg_o, stage) = refs[:4], refs[4:]
    for k in range(4):
        stage[meta[1] ^ k] = pieces[k][0]
    cotangent = stage[...].reshape(features, count)
    cot_o[0] = cotangent
    gg_o[0] = jnp.transpose(nn(wout[...], cotangent))


def compose(lower, upper, heads, size):
    return scaled_state(lower[0], upper[1], heads, size) + upper[0], lower[1] * upper[1]


def choose(flag, a, b):
    return jnp.where(flag, a[0], b[0]), jnp.where(flag, a[1], b[1])


def pair_kernel(dims, rev, meta, own, other, out):
    packs, heads, size = dims
    upper_is_own = ((meta[0] & 1) ^ rev) == 1
    for p in range(packs // 2):
        a, b = decode_state(own[p], heads, size), decode_state(other[p], heads, size)
        both = compose(choose(upper_is_own, b, a), choose(upper_is_own, a, b), heads, size)
        encode_state(out, p, *both, heads, size)


def entering_from(before, b, p, heads, size):
    if before is None:
        return (jnp.zeros_like(b[0]), jnp.ones_like(b[1])), b
    entering = decode_state(before[p], heads, size)
    return entering, compose(b, entering, heads, size)


def cube_kernel(dims, rev, bit, first, meta, *refs):
    packs, heads, size = dims
    total, other = refs[0], refs[1]
    before, next_o, before_o = (None, refs[2], refs[3]) if first else refs[2:5]
    upper_is_own = (((meta[0] >> bit) & 1) ^ rev) == 1
    for p in range(packs // 2):
        a, b = decode_state(total[p], heads, size), decode_state(other[p], heads, size)
        both = compose(choose(upper_is_own, b, a), choose(upper_is_own, a, b), heads, size)
        encode_state(next_o, p, *both, heads, size)
        entering, longer = entering_from(before, b, p, heads, size)
        encode_state(before_o, p, *choose(upper_is_own, longer, entering), heads, size)


def last_kernel(dims, rev, bit, first, meta, *refs):
    packs, heads, size = dims
    own, pair, other = refs[0:3]
    before, keep_o, send_o = (None, refs[3], refs[4]) if first else refs[3:6]
    add = (((meta[0] >> bit) & 1) ^ rev) == 1
    upper_is_own = ((meta[0] & 1) ^ rev) == 1
    for p in range(packs // 2):
        entering, longer = entering_from(
            before, decode_state(other[p], heads, size), p, heads, size
        )
        low = choose(add, longer, entering)
        lower = decode_state(jnp.where(upper_is_own, pair[p].astype(jnp.int32), own[p].astype(jnp.int32)), heads, size)
        high = compose(low, lower, heads, size)
        encode_state(keep_o, p, *choose(upper_is_own, high, low), heads, size)
        encode_state(send_o, p, *choose(upper_is_own, low, high), heads, size)


def gate_kernel(dims, meta, lens, *refs):
    packs, count, features, inner, bc, heads, size, width, nseq = dims
    xbc, steps, inner_in, keep, recv, gate, gg, gain, skip, y_o, stats_o = refs
    pack = order.pack
    state = jnp.concatenate(
        split2(load_state(meta, packs, pack, keep, recv, heads, size)), axis=1
    )
    carry = carry_column(meta, column_segments(meta, lens, pack, count, nseq, EDGE), EDGE)
    matrix = spread_matrix(heads, size)
    entering = spread(carry * jnp.exp(from_group(steps[0], 1, heads)), matrix, heads)
    c_vals = xbc[0, :, inner + bc // 2 :]
    y = inner_in[0] + entering * nt(jnp.concatenate([c_vals, c_vals], axis=1), state)
    y_o[0] = y
    gate_f = gate[0].astype(f32)
    ssd = y + xbc[0, :, :inner].astype(f32) * skip[...]
    mixed = ssd * (gate_f * sigmoid(gate_f))
    squares = jnp.sum(mixed * mixed, axis=1, keepdims=True)
    dots = jnp.sum(gain[...] * gg[0] * mixed, axis=1, keepdims=True)
    lane = lax.broadcasted_iota(jnp.int32, (count, LANES), 1)
    both = jnp.where(lane == 0, squares, 0.0) + jnp.where(lane == 1, dots, 0.0)
    stats_o[0] = jnp.transpose(both)[0:2]


def grad_kernel(dims, total_inner, meta, lens, *refs):
    packs, count, features, inner, bc, heads, size, width, nseq = dims
    (
        stats, near, far, diagonal, xbc, steps, y, gate, gg, gain, skip,
        gy_o, gated_o, ggate_o, keep_o, send_o, small_o,
    ) = refs
    pack = order.pack

    @order.first
    def _():
        small_o[...] = jnp.zeros_like(small_o)

    sums = (stats[0] + near[0]) + (far[0] + diagonal[0])
    row = lax.broadcasted_iota(jnp.int32, (LANES, count), 0)
    wide = jnp.where(row == 0, sums[0:1], 0.0) + jnp.where(row == 1, sums[1:2], 0.0)
    cols = jnp.transpose(wide)
    inv = lax.rsqrt(cols[:, 0:1] / total_inner + EPSILON)
    dot = cols[:, 1:2] / total_inner
    x_f, gg_f, gate_f = xbc[0, :, :inner].astype(f32), gg[0], gate[0].astype(f32)
    ssd = y[0] + x_f * skip[...]
    sig = sigmoid(gate_f)
    act = gate_f * sig
    mixed = ssd * act
    scaled = mixed * inv
    gated_o[0] = (scaled * gain[...]).astype(bf16)
    grad_mixed = inv * gain[...] * gg_f - mixed * (inv * inv * inv * dot)
    gy_f = grad_mixed * act
    gy_o[0] = gy_f
    ggate_o[0] = (grad_mixed * ssd * sig * (1.0 + gate_f * (1.0 - sig))).astype(bf16)
    carry = carry_column(meta, column_segments(meta, lens, pack, count, nseq, EDGE), EDGE)
    cum = from_group(steps[0], 1, heads)
    entering = carry * jnp.exp(cum)
    ey_hi, ey_lo = split2(gy_f * spread(entering, spread_matrix(heads, size), heads))
    c_rows = jnp.transpose(xbc[0, :, inner + bc // 2 :])
    state_grad = jnp.transpose(nn(c_rows, ey_hi) + nn(c_rows, ey_lo))
    small_o[0:1, :] += jnp.sum(gg_f * scaled, axis=0, keepdims=True)
    small_o[1:2, :] += jnp.sum(gy_f * x_f, axis=0, keepdims=True)
    return lambda: store_state(
        meta, packs, pack, keep_o, send_o, state_grad, entering[count - 1 :], heads, size
    )


def diag_kernel(dims, meta, lens, *refs):
    packs, count, features, inner, bc, heads, size, width, nseq = dims
    xbc, steps, gy, y, keep, recv, dx_o, dbc_o, sums_o = refs
    pack = order.pack
    half = bc // 2
    b_vals, c_vals = xbc[0, :, inner : inner + half], xbc[0, :, inner + half :]
    col = column_segments(meta, lens, pack, count, nseq, 0)
    row = row_segments(meta, lens, pack, count, nseq)
    mask = (col == row) & (
        lax.broadcasted_iota(jnp.int32, (count, count), 0)
        <= lax.broadcasted_iota(jnp.int32, (count, count), 1)
    )
    scores = jnp.where(mask, nt(b_vals, c_vals), 0.0)
    dt, cum_col = steps_of(steps[0], heads)
    cum_row = jnp.transpose(cum_col)
    lane = lax.broadcasted_iota(jnp.int32, (count, 2 * size), 1)
    grad_scores = jnp.zeros((count, count), f32)
    zero = jnp.zeros((), bf16)
    for pair in range(heads // 2):
        cols = slice(2 * pair * size, (2 * pair + 2) * size)
        x_pair = xbc[0, :, cols]
        x_twice = jnp.concatenate([x_pair, x_pair], axis=1)
        gy_hi, gy_lo = split2(gy[0, :, cols])
        gy_wide = jnp.concatenate([gy_hi, gy_lo], axis=1)
        parts = []
        for h in (2 * pair, 2 * pair + 1):
            own = (lane < size) if h % 2 == 0 else (lane >= size)
            part = jnp.exp(jnp.minimum(cum_row[h : h + 1] - cum_col[:, h : h + 1], 0.0)) * dt[:, h : h + 1]
            parts.append(nn((scores * part).astype(bf16), gy_wide))
            both = jnp.concatenate([jnp.where(own, gy_hi, zero), jnp.where(own, gy_lo, zero)], axis=1)
            grad_scores = grad_scores + nt(x_twice, both) * part
        two = [part[:, : 2 * size] + part[:, 2 * size :] for part in parts]
        dx_o[0, :, cols] = jnp.where(lane < size, two[0], two[1])
    hi, lo = split2(jnp.where(mask, grad_scores, 0.0))
    state_hi, state_lo = split2(load_state(meta, packs, pack, keep, recv, heads, size))
    carry = carry_column(meta, column_segments(meta, lens, pack, count, nseq, EDGE), EDGE)
    matrix = spread_matrix(heads, size)
    ey_hi, ey_lo = split2(gy[0] * spread(carry * jnp.exp(cum_col), matrix, heads))
    dbc_o[0, :, :half] = nn(
        jnp.concatenate([hi, lo], axis=1), jnp.concatenate([c_vals, c_vals], axis=0)
    )
    b_rows = jnp.transpose(b_vals)
    dbc_o[0, :, half:] = (
        jnp.transpose(nn(b_rows, hi) + nn(b_rows, lo))
        + nn(ey_hi, state_hi) + nn(ey_hi, state_lo) + nn(ey_lo, state_hi)
    )
    row_sum = collapse(gy[0] * y[0], matrix, heads)
    col_sum = collapse(xbc[0, :, :inner].astype(f32) * dx_o[0], matrix, heads)
    sums_o[0] = row_sum + to_group(col_sum, 1)


def scatter_pieces(head, stage, own_o, far_o, send_o):
    own_o[0] = stage[head]
    send_o[0, 0] = stage[head ^ 1].astype(bf16)
    far_o[0] = stage[head ^ 2]
    send_o[0, 1] = stage[head ^ 3].astype(bf16)


def accumulate(meta, pack, packs, sums, term, keep_o, send_o):
    sums[...] += term.reshape(sums.shape)

    def finish():
        @last_pack(pack, packs)
        def _():
            side = meta[0] & 1
            keep_o[...] = sums[side]
            send_o[...] = sums[1 - side].astype(bf16)

    return finish


def last_pack(pack, packs):
    return lambda work: pl.when(pack == packs - 1)(work)


def cleared(*refs):
    @order.first
    def _():
        for ref in refs:
            ref[...] = jnp.zeros_like(ref)


def out_kernel(dims, meta, lens, *refs):
    packs, count, features, inner, bc, heads, size, width, nseq = dims
    gated, cot, wout, own_o, far_o, send_o, keep_o, give_o, stage, sums = refs
    pack = order.pack
    cleared(sums)
    stage[...] = nt(wout[...], gated[0]).reshape(stage.shape)
    scatter_pieces(meta[1], stage, own_o, far_o, send_o)
    return accumulate(meta, pack, packs, sums, nn(cot[0], gated[0]), keep_o, give_o)


def gain_row(weights, grads):
    part = jnp.sum(weights.astype(f32) * grads, axis=1, keepdims=True)
    return jnp.transpose(jnp.broadcast_to(part, (part.shape[0], LANES)))[0:8]


def z_kernel(dims, meta, lens, *refs):
    normed, ggate, wz, keep_o, give_o, gain_o, sums = refs
    pack = order.pack
    cleared(sums)
    store = accumulate(meta, pack, dims[0], sums, nn(normed[0], ggate[0]), keep_o, give_o)

    def finish():
        store()

        @last_pack(pack, dims[0])
        def _():
            gain_o[...] = gain_row(wz[...], sums[...].reshape(wz.shape))

    return finish


def end_weights(seg, seg_main, cum_col, dt_col, count):
    cum_end = cum_col[count - 1 :]
    end = seg[count + EDGE - 1 :]
    return jnp.where(seg_main == end, jnp.exp(cum_end - cum_col), 0.0) * dt_col


def share_kernel(dims, meta, lens, *refs):
    packs, count, features, inner, bc, heads, size, width, nseq = dims
    (
        xbc, steps, dbc, gkeep, grecv, gy, dx, slope, conv, skip,
        own_o, near_o, grad_o, state_sum_o, edge_o,
        gpad,
    ) = refs
    pack = order.pack
    half, quarter = bc // 2, bc // 4
    g_hi, g_lo = split2(load_state(meta, packs, pack, gkeep, grecv, heads, size))
    seg = column_segments(meta, lens, pack, count, nseq, EDGE)
    dt, cum = steps_of(steps[0], heads)
    matrix = spread_matrix(heads, size)
    wide = spread(end_weights(seg, seg[EDGE:], cum, dt, count), matrix, heads)
    x_f = xbc[0, :, :inner].astype(f32)
    hi, lo = split2(wide * x_f)
    grad_b = dbc[0, :, :half] + nn(hi, g_hi) + nn(lo, g_hi) + nn(hi, g_lo)
    grad_c = dbc[0, :, half:]
    even = jnp.concatenate([grad_b[:, :quarter], grad_c[:, :quarter]], axis=1)
    odd = jnp.concatenate([grad_b[:, quarter:], grad_c[:, quarter:]], axis=1)
    first = (meta[1] & 1) == 0
    own_o[0] = jnp.where(first, even, odd)
    near_o[0] = jnp.where(first, odd, even)
    b_vals = xbc[0, :, inner : inner + half]
    u_wide = wide * nt(
        jnp.concatenate([b_vals, b_vals], axis=1), jnp.concatenate([g_hi, g_lo], axis=1)
    )
    state_sum_o[0] = collapse(x_f * u_wide, matrix, heads)
    grad_x = (dx[0] + u_wide + gy[0] * skip[...]) * slope[0]
    grad_o[0] = grad_x
    gpad[:EDGE, :] = jnp.zeros((EDGE, inner), f32)
    gpad[EDGE:, :] = grad_x[:EDGE]
    edge_o[0] = conv_rows(gpad, conv, seg, EDGE, width).astype(bf16)


def middle_kernel(dims, meta, *refs):
    packs, quarter = dims
    own, near, keep_o, send_o = refs
    half = packs // 2
    first = (meta[1] >> 1) == 0
    for p in range(half):
        a, b = own[p] + near[p], own[p + half] + near[p + half]
        low = jnp.concatenate([a[:, :quarter], b[:, :quarter]], axis=1)
        high = jnp.concatenate([a[:, quarter:], b[:, quarter:]], axis=1)
        keep_o[p] = jnp.where(first, low, high)
        send_o[p] = jnp.where(first, high, low)


def conv_taps(grads, raws, gconv_o, seg, count, width):
    seg_main = seg[EDGE : EDGE + count]
    for k in range(width):
        low = EDGE - (width - 1) + k
        mask = jnp.where(seg[low : low + count] == seg_main, 1.0, 0.0)
        gconv_o[k : k + 1, :] += jnp.sum(
            grads * (raws[low : low + count, :] * mask), axis=0, keepdims=True
        )
    gconv_o[width : width + 1, :] += jnp.sum(grads, axis=0, keepdims=True)


def conv_rows(gpad, conv, seg, rows, width):
    total = jnp.zeros((rows, gpad.shape[1]), f32)
    for lag in range(width):
        mask = jnp.where(seg[lag : lag + rows] == seg[:rows], 1.0, 0.0)
        k = width - 1 - lag
        total = total + conv[k : k + 1, :] * (gpad[lag : lag + rows, :] * mask)
    return total


def step_kernel(dims, meta, lens, *refs):
    packs, count, features, inner, bc, heads, size, width, nseq = dims
    (
        steps, sums, state_sums, keep, recv, gkeep, grecv, small, normed, wdt,
        gdt_o, gdt_rows_o, gsmall_o, gain_o,
        gdt_sums,
    ) = refs
    group, half = pl.program_id(0), packs // 2
    matrix = spread_matrix(heads, size)
    ones = jnp.ones((8, LANES), bf16)
    decay_rate = -jnp.exp(small[1:2, :])
    upper = triangle(count, False)
    rows = lax.broadcasted_iota(jnp.int32, (count, LANES), 0)
    mine = group == (meta[0] & 1)
    bias_sum, rate_sum = jnp.zeros((1, LANES), f32), jnp.zeros((1, LANES), f32)
    term = jnp.zeros((features, LANES), f32)
    for j in range(half):
        pick = lambda a, b: jnp.where(mine, a[j].astype(jnp.int32), b[j].astype(jnp.int32))
        state = decode_state(pick(keep, recv), heads, size)[0]
        gstate = decode_state(pick(gkeep, grecv), heads, size)[0]
        seg = column_segments(meta, lens, group * half + j, count, nseq, EDGE)
        v = steps[j]
        dt, cum = steps_of(v, heads)
        sig = head_lanes(sigmoid(v), heads)
        row_sum, col_sum = from_group(sums[j], 0, heads), from_group(sums[j], 1, heads)
        state_sum = state_sums[j]
        carry = carry_column(meta, seg, EDGE)
        hi, lo = split2(gstate * state)
        by_head = collapse(nt(ones, hi) + nt(ones, lo), matrix, heads)[0:1]
        last = by_head * carry[count - 1 :] * jnp.exp(cum[count - 1 :]) + jnp.sum(
            state_sum, axis=0, keepdims=True
        )
        grad_cum = row_sum - col_sum - state_sum + jnp.where(rows == count - 1, last, 0.0)
        grad_rate = exact_sums(upper, grad_cum, heads)
        ratio = jnp.where(dt > 1e-30, sig / jnp.maximum(dt, 1e-30), 1.0)
        grad_dt = head_lanes(ratio * (col_sum + state_sum) + grad_rate * decay_rate * sig, heads)
        low = grad_dt.astype(bf16)
        gdt_o[j] = low
        bias_sum = bias_sum + jnp.sum(grad_dt, axis=0, keepdims=True)
        rate_sum = rate_sum + jnp.sum(grad_rate * dt * decay_rate, axis=0, keepdims=True)
        term = term + nn(normed[j], low)

    @pl.when(group == 0)
    def _():
        gsmall_o[...] = jnp.zeros_like(gsmall_o)
        gdt_sums[...] = jnp.zeros_like(gdt_sums)

    gsmall_o[0:1, :] += bias_sum
    gsmall_o[1:2, :] += rate_sum
    gdt_sums[...] += term

    @pl.when(group == packs // half - 1)
    def _():
        gdt_rows_o[...] = jnp.transpose(gdt_sums[...])[0:8]
        gain_o[...] = gain_row(wdt[...], gdt_sums[...])


def xback_kernel(dims, meta, lens, *refs):
    packs, count, features, inner, bc, heads, size, width, nseq = dims
    (
        grads, raw, normed, edge, edge_x, conv, wx,
        main_o, keep_o, give_o, gconv_o, gain_o,
        gpad, raws, sums, rows_x,
    ) = refs
    pack = order.pack
    seg = column_segments(meta, lens, pack, count, nseq, EDGE)

    cleared(gconv_o, rows_x, sums)
    raws[...] = raw[0].astype(f32)
    gpad[:count, :] = grads[0]
    gpad[count:, :] = jnp.zeros((EDGE, inner), f32)
    conv_taps(grads[0], raws, gconv_o, seg, count, width)
    seg_pad = jnp.concatenate([seg[EDGE:], jnp.full((8, 1), -1, jnp.int32)], axis=0)
    main = conv_rows(gpad, conv, seg_pad, count, width).astype(bf16)
    main_o[0] = main
    rows_x[pl.ds(pl.multiple_of(pack * EDGE, EDGE), EDGE), :] = edge_x[0]
    sums[...] += nn(normed[0], main).reshape(sums.shape)

    def finish():
        @last_pack(pack, packs)
        def _():
            sums[...] += nn(edge[...], rows_x[...]).reshape(sums.shape)
            side = meta[0] & 1
            keep_o[...] = sums[side]
            give_o[...] = sums[1 - side].astype(bf16)
            gain_o[...] = gain_row(wx[...], sums[...].reshape(wx.shape))

    return finish


def conv_bc_kernel(dims, meta, lens, *refs):
    packs, count, features, inner, bc, heads, size, width, nseq = dims
    (
        keep, recv, slope, raw, normed, edge, wbc, conv, edge_x,
        gconv_x, gdt_rows, gsmall, gate_small, gain_z, gain_x, gain_dt, gain,
        rows_o, edges_o, give_o, small_o,
        gpad, raws, sums, edge_bc, gconv,
    ) = refs
    pack = order.pack
    quarter = bc // 4

    cleared(gconv, edge_bc, sums)
    gpad[:EDGE, :] = jnp.zeros((EDGE, quarter), f32)
    gpad[EDGE + count :, :] = jnp.zeros((EDGE, quarter), f32)
    both = keep[0] + recv[0]
    grad = jnp.where(pack < packs // 2, both[:, :quarter], both[:, quarter:]) * slope[0]
    seg = column_segments(meta, lens, pack, count, nseq, EDGE)
    raws[...] = raw[0].astype(f32)
    gpad[EDGE : EDGE + count, :] = grad
    conv_taps(grad, raws, gconv, seg, count, width)
    seg_pad = jnp.concatenate([seg, jnp.full((8, 1), -1, jnp.int32)], axis=0)
    grad_raw = conv_rows(gpad, conv, seg_pad, count + EDGE, width).astype(bf16)
    rows_o[0] = grad_raw[EDGE:]
    edge_bc[pl.ds(pl.multiple_of(pack * EDGE, EDGE), EDGE), :] = grad_raw[:EDGE]
    edges_o[0, :, :inner] = edge_x[0]
    blank = jnp.zeros((EDGE, LANES - quarter), bf16)
    edges_o[0, :, inner:] = jnp.concatenate([grad_raw[:EDGE], blank], axis=1)
    sums[...] += nn(normed[0], grad_raw[EDGE:])

    def finish():
        @last_pack(pack, packs)
        def _():
            total = sums[...] + nn(edge[...], edge_bc[...])
            rows = jnp.transpose(total)
            taps = width + 1
            give_o[:quarter, :] = rows[:, :inner].astype(bf16)
            give_o[quarter : 2 * quarter, :] = rows[:, inner:].astype(bf16)
            small_o[...] = jnp.zeros_like(small_o)
            for h in range(heads):
                small_o[2 * h : 2 * h + 1, :] = gdt_rows[h : h + 1, :inner]
                small_o[2 * h + 1 : 2 * h + 2, :] = gdt_rows[h : h + 1, inner:]
            row = 2 * heads
            small_o[row : row + taps, :] = gconv_x[:taps, :]
            row += taps
            small_o[row : row + 1, :] = gate_small[0:1, :]
            skips = collapse(gate_small[...], spread_matrix(heads, size), heads)
            small_o[row + 1 : row + 2, :] = jnp.concatenate(
                [gsmall[0:1, :], gsmall[1:2, :], skips[1:2, :]], axis=1
            )
            blank_row = jnp.zeros((1, inner - taps * quarter), f32)
            small_o[row + 2 : row + 3, :] = jnp.concatenate(
                [gconv[k : k + 1, :] for k in range(taps)] + [blank_row], axis=1
            )
            gains = gain_row(wbc[...], total)[0:1] + gain_z[0:1, :] + gain_x[0:1, :] + gain_dt[0:1, :]
            gains = gains / jnp.transpose(jnp.broadcast_to(gain[...], (features, LANES)))[0:1]
            small_o[row + 3 : row + 4, :] = gains[:, :inner]
            small_o[row + 4 : row + 5, :] = gains[:, inner:]
            hi, lo = split2(small_o[...])
            give_o[2 * quarter : 2 * quarter + SMALL, :] = hi
            give_o[2 * quarter + SMALL :, :] = lo

    return finish


def back_kernel(dims, meta, lens, *refs):
    packs, count, features, inner, bc, heads, size, width, nseq = dims
    (
        main, edges, ggate, gdt, gbc, normed, wz, wx, wbc, wdt,
        own_o, far_o, send_o, dots_o,
        stage,
    ) = refs
    head = meta[1]
    part, quarter = features // 4, bc // 4
    late = count - EDGE

    def with_edge(rows, edge):
        low = (rows[late:].astype(f32) + edge.astype(f32)).astype(bf16)
        return jnp.concatenate([rows[:late], low], axis=0)

    grad_x = with_edge(main[0], edges[0, :, :inner])
    grad_bc = with_edge(gbc[0], edges[0, :, inner : inner + quarter])
    whole = nt(wz[...], ggate[0]) + nt(wx[...], grad_x) + nt(wbc[...], grad_bc) + nt(wdt[...], gdt[0])
    dots = jnp.sum(whole * normed[0].astype(f32), axis=0, keepdims=True)
    stage[...] = whole.reshape(stage.shape)
    dots_o[0] = dots
    own_o[0] = stage[head]
    far_o[0] = stage[head ^ 2]
    for k in range(2):
        send_o[0, k, :part, :] = stage[head ^ (1 + 2 * k)].astype(bf16)
        send_o[0, k, part:, :] = extra_rows(dots)


def extra_rows(*values):
    row = lax.broadcasted_iota(jnp.int32, (EDGE, values[0].shape[1]), 0)
    total = jnp.zeros(row.shape, f32)
    for i, value in enumerate(values):
        for k, piece in enumerate(split3(value)):
            total = total + jnp.where(row == 3 * i + k, piece.astype(f32), 0.0)
    return total.astype(bf16)


def read_extra(block, i):
    rows = block.astype(f32)
    return rows[3 * i : 3 * i + 1] + rows[3 * i + 1 : 3 * i + 2] + rows[3 * i + 2 : 3 * i + 3]


def gather_kernel(own, far, near, dots, own_o, far_o, dots_o):
    part = own.shape[1]
    own_o[0] = own[0] + near[0, 0, :part, :].astype(f32)
    far_o[0, :part, :] = (far[0] + near[0, 1, :part, :].astype(f32)).astype(bf16)
    both = dots[0] + read_extra(near[0, 0, part:, :], 0)
    dots_o[0] = both
    far_o[0, part:, :] = extra_rows(both)


def final_kernel(dims, own, far, dots, tokens, inv, gain, out_grad, in_grad_o):
    packs, count, features = dims
    part = own.shape[1]
    grad = own[0] + far[0, :part, :].astype(f32)
    mean = (dots[0] + read_extra(far[0, part:, :], 0)) / features
    unit = tokens[0].astype(f32) * inv[0]
    in_grad_o[0] = out_grad[0].astype(f32) + inv[0] * (gain[...] * grad - unit * mean)


def out_gather_kernel(own, far, near, own_o, far_o):
    own_o[0] = own[0] + near[0, 0].astype(f32)
    far_o[0] = (far[0] + near[0, 1].astype(f32)).astype(bf16)


def out_final_kernel(own, far, tokens, out):
    out[0] = (tokens[0].astype(f32) + (own[0] + far[0].astype(f32))).astype(bf16)


def add_kernel(bit, halve, segs, count, small, meta, *refs):
    keep, got, refs = refs[:count], refs[count : 2 * count], refs[2 * count :]
    end = segs[-1] if count > 1 else sum(segs)
    write = 0
    if small:
        small_in, *refs, small_o = refs
        hi, lo = split2(small_in[...])
        mine = hi.astype(f32) + lo.astype(f32)
        theirs = got[-1][end : end + SMALL, :].astype(f32) + got[-1][end + SMALL :, :].astype(f32)
        total = mine + theirs
        small_o[...] = total
        if bit is not None:
            send_o = refs[-1]
            behind = send_o.shape[0] - 2 * SMALL
            hi, lo = split2(total)
            send_o[behind : behind + SMALL, :] = hi
            send_o[behind + SMALL :, :] = lo
    read = 0
    for i, rows in enumerate(segs):
        if count > 1:
            total = keep[i][...] + got[i][:rows, :].astype(f32)
        else:
            total = keep[0][read : read + rows, :].astype(f32) + got[0][read : read + rows, :].astype(f32)
        read += rows
        if halve:
            half = rows // 2
            first = ((meta[0] >> bit) & 1) == 0
            top, bottom = total[:half], total[half:]
            refs[0][write : write + half, :] = jnp.where(first, top, bottom)
            refs[1][write : write + half, :] = jnp.where(first, bottom, top).astype(bf16)
            write += half
        else:
            refs[0][write : write + rows, :] = total.astype(bf16)
            write += rows


def whole_kernel(quarter, keep, got, small, out, small_o):
    total = keep[: 2 * quarter, :].astype(f32) + got[: 2 * quarter, :].astype(f32)
    out[...] = jnp.concatenate([total[:quarter], total[quarter:]], axis=1)
    hi, lo = split2(small[...])
    end = 2 * quarter
    theirs = got[end : end + SMALL, :].astype(f32) + got[end + SMALL :, :].astype(f32)
    small_o[...] = (hi.astype(f32) + lo.astype(f32)) + theirs


def join_kernel(bit, segs, meta, mine, got, out):
    first = ((meta[0] >> bit) & 1) == 0
    read = 0
    for rows in segs:
        a = mine[read : read + rows, :].astype(f32)
        b = got[read : read + rows, :].astype(f32)
        out[2 * read : 2 * read + rows, :] = jnp.where(first, a, b).astype(bf16)
        out[2 * read + rows : 2 * read + 2 * rows, :] = jnp.where(first, b, a).astype(bf16)
        read += rows


def result_kernel(segs, ways, meta, mine, got, *outs):
    first = (meta[0] & 1) == 0
    read = 0
    for rows, way, out in zip(segs, ways, outs):
        a = mine[read : read + rows, :].astype(f32)
        b = got[read : read + rows, :].astype(f32)
        top, bottom = jnp.where(first, a, b), jnp.where(first, b, a)
        if way == "rows":
            out[:rows, :] = top
            out[rows:, :] = bottom
        elif way == "flip":
            out[:, :rows] = jnp.transpose(top)
            out[:, rows:] = jnp.transpose(bottom)
        else:
            out[...] = jnp.concatenate([top, bottom], axis=1)
        read += rows


def plus_kernel(a, b, out):
    out[...] = a[...] + b[...]


def unpack_kernel(dims, meta, *refs):
    heads, features, bc_part, width = dims
    smalls, gains, dt_o, taps_x_o, taps_bc_o, bias_x_o, bias_bc_o, dt_bias_o, a_log_o, skip_o, gate_o, gain_o = refs
    for h in range(heads):
        dt_o[h : h + 1, :] = jnp.concatenate(
            [smalls[2 * h : 2 * h + 1, :], smalls[2 * h + 1 : 2 * h + 2, :]], axis=1
        )
    row = 2 * heads
    taps_x_o[...] = smalls[row : row + width, :]
    bias_x_o[...] = smalls[row + width, :]
    row += width + 1
    gate_o[...] = smalls[row, :]
    for k, out in enumerate((dt_bias_o, a_log_o, skip_o)):
        out[...] = smalls[row + 1, k * LANES : k * LANES + heads]
    taps = smalls[row + 2 : row + 3, :]
    for k in range(width):
        taps_bc_o[k : k + 1, :] = taps[:, k * bc_part : (k + 1) * bc_part]
    bias_bc_o[...] = taps[0, width * bc_part : (width + 1) * bc_part]
    both = jnp.concatenate([gains[row + 3 : row + 4, :], gains[row + 4 : row + 5, :]], axis=1)
    part = features // 4
    parts = [both[:, h * part : (h + 1) * part] for h in range(4)]
    low = jnp.where((meta[1] & 1) == 0, parts[0], parts[1])
    high = jnp.where((meta[1] & 1) == 0, parts[2], parts[3])
    gain_o[...] = jnp.where((meta[1] >> 1) == 0, low, high)[0]


class Spec:
    def __init__(self, shape, index, each=True):
        self.shape, self.index, self.each = tuple(shape), index, each

    def block(self, group):
        zeros = (0,) * len(self.shape)
        if not self.each:
            return pl.BlockSpec(self.shape, lambda p, *_: zeros)
        size = group or 1
        return pl.BlockSpec(
            (size,) + self.shape, lambda p, *pre: (self.index(p, pre, bool(group)),) + zeros
        )


def whole_spec(shape):
    return Spec(shape, None, False)


def pack_spec(shape):
    return Spec(shape, lambda p, pre, grouped: p)


def half_spec(shape, half):
    return Spec(shape, lambda p, pre, grouped: 0 if grouped else p % half)


def sided_spec(shape, half, keep):
    def index(p, pre, grouped):
        side = pre[0][0] & 1 if keep else 1 - (pre[0][0] & 1)
        return side if grouped else p + half * side

    return Spec(shape, index)


def side_spec(shape, half, keep):
    def index(p, pre, grouped):
        if grouped:
            return 0
        side = pre[0][0] & 1 if keep else 1 - (pre[0][0] & 1)
        group = p // half
        return jnp.where(group == side, p % half, jnp.where(group < side, 0, half - 1))

    return Spec(shape, index)


class Each:
    def __init__(self, shape, dtype):
        self.shape, self.dtype = tuple(shape), dtype

    def scratch(self, group):
        return pltpu.VMEM(((group,) if group else ()) + self.shape, self.dtype)


class Order:
    def __init__(self):
        self.clear()

    def clear(self):
        self.last, self.near, self.held = (), [], []
        self.pack, self.lane, self.lanes = None, 0, 1

    def first(self, work):
        if self.lane == 0:
            pl.when(self.pack == 0)(work)

    def hold(self, *arrays):
        self.held += arrays

    def drop(self, *arrays):
        self.held = [x for x in self.held if not any(x is y for y in arrays)]

    def placed(self, x):
        return pltpu.with_memory_space_constraint(x, pltpu.VMEM) if self.holds(x) else x

    def holds(self, x):
        return any(x is y for y in self.near)


order = Order()


def call(
    kernel, grid, in_specs, out_specs, out_shape, scratch, prefetch, *args, limit=28, wait=(), us=1,
    out=False, onto=(), group=0,
):
    first = len(prefetch) + len(args)
    args = args + tuple(onto)
    in_specs = list(in_specs) + [pl.BlockSpec(memory_space=pl.ANY)] * len(onto)
    given = len(prefetch) + len(args)
    held = order.last + tuple(wait)
    held += tuple(x for x in order.held if not any(x is y for y in args + held))
    late = len(held)
    single = not isinstance(out_shape, (list, tuple))
    out_specs, out_shape = ([out_specs], [out_shape]) if single else (list(out_specs), list(out_shape))
    token = jax.ShapeDtypeStruct((8, LANES), f32)
    count = len(out_shape)

    specs = list(in_specs[: len(in_specs) - len(onto)]) + out_specs
    blocks = lambda items: [x.block(group) if isinstance(x, Spec) else x for x in items]

    def body(*refs):
        ins, rest = refs[:first], refs[given + late :]
        fixed, blocked = ins[: len(prefetch)], (*ins[len(prefetch) :], *rest[:count])
        own = rest[count + 1 :]
        finish = []
        for lane in range(group or 1):
            order.pack, order.lane, order.lanes = pl.program_id(0), lane, group or 1
            views, scratches = blocked, own
            if group:
                order.pack = order.pack * group + lane
                views = [
                    ref.at[pl.ds(lane, 1)] if isinstance(spec, Spec) and spec.each else ref
                    for ref, spec in zip(blocked, specs)
                ]
                scratches = [
                    ref.at[lane] if isinstance(item, Each) else ref for ref, item in zip(own, scratch)
                ]
            finish.append(kernel(*fixed, *views, *scratches))
        for work in finish:
            if work is not None:
                work()

    *outs, order_out = pl.pallas_call(
        body,
        grid_spec=pltpu.PrefetchScalarGridSpec(
            num_scalar_prefetch=len(prefetch),
            grid=grid,
            in_specs=blocks(in_specs) + [pl.BlockSpec(memory_space=pl.ANY)] * late,
            out_specs=blocks(out_specs + [whole_spec(token.shape)]),
            scratch_shapes=[x.scratch(group) if isinstance(x, Each) else x for x in scratch],
        ),
        input_output_aliases={first + i: i for i in range(len(onto))},
        out_shape=(out_shape if out else [pltpu.VMEM(x.shape, x.dtype) for x in out_shape])
        + [pltpu.VMEM(token.shape, token.dtype)],
        compiler_params=pltpu.CompilerParams(vmem_limit_bytes=limit * MIB),
        cost_estimate=pl.CostEstimate(
            flops=int(us * 10e9), bytes_accessed=int(us * 3e6), transcendentals=0
        ),
    )(*[pltpu.with_memory_space_constraint(x, pltpu.VMEM) for x in prefetch], *[order.placed(x) for x in args], *[order.placed(x) for x in held])
    order.last = (order_out,)
    order.near.append(order_out)
    if not out:
        order.near += outs
    return outs[0] if single else outs


def shape(*dims_and_type):
    return jax.ShapeDtypeStruct(dims_and_type[:-1], dims_and_type[-1])


def scan_states(keep, send, meta, packs, heads, size, rev, beside, waits=lambda: ()):
    dims = (packs, heads, size)
    rows = heads * size
    half = packs // 2
    pay = shape(half, rows + EDGE, LANES, jnp.int16)
    spec = whole_spec(pay.shape)
    bits = (lax.axis_size("seq") - 1).bit_length()
    beside = list(beside)

    def work(newest):
        if beside:
            beside.pop(0)(newest)

    other = swap(send, "seq", 1)
    work(send)
    keep = keep() if callable(keep) else keep
    total = call(
        functools.partial(pair_kernel, dims, rev), (1,), [spec, spec], spec, pay, [], (meta,),
        keep, other,
    )
    before = None
    for bit in range(1, bits):
        got = swap(total, "seq", 1 << bit)
        extra = () if before is None else (before,)
        work(total)
        if bit < bits - 1:
            total, before = call(
                functools.partial(cube_kernel, dims, rev, bit, before is None), (1,),
                [spec] * (2 + len(extra)), [spec, spec], [pay, pay], [], (meta,),
                total, got, *extra,
            )
        else:
            own, back = call(
                functools.partial(last_kernel, dims, rev, bit, before is None), (1,),
                [spec] * (3 + len(extra)), [spec, spec], [pay, pay], [],
                (meta,), keep, other, got, *extra, wait=waits(),
            )
    recv = swap(back, "seq", 1)
    while beside:
        work(back)
    return own, recv


class SeqSum:
    def __init__(self):
        self.keep, self.got, self.segs = [], [], []
        self.small = self.bit = None
        self.bits = list(range(1, (lax.axis_size("seq") - 1).bit_length()))
        self.halved = []

    def put(self, keep, give, segs=None, small=None):
        self.keep.append(keep)
        self.got.append(swap(give, "seq", 1))
        self.segs += segs or [keep.shape[0]]
        self.small = small

    def add(self, meta, us=1, wait=()):
        bit = self.bits.pop(0) if self.bits else None
        halve = bit is not None and all(rows % (2 * EDGE) == 0 for rows in self.segs)
        cols = self.keep[0].shape[1]
        segs = [rows // 2 for rows in self.segs] if halve else self.segs
        rows = sum(segs)
        small = self.small is not None
        behind = 2 * SMALL if small and bit is not None else 0
        low = shape(rows + behind, cols, bf16)
        out = [shape(rows, cols, f32), low] if halve else [low]
        ins = [*self.keep, *self.got]
        if small:
            ins.append(self.small)
            out.append(shape(*self.small.shape, f32))
        outs = call(
            functools.partial(add_kernel, bit, halve, self.segs, len(self.keep), small), (1,),
            [whole_spec(x.shape) for x in ins], [whole_spec(x.shape) for x in out], out, [],
            (meta,), *ins, us=us, wait=wait,
        )
        if small:
            self.small = outs[-1]
        self.segs, self.keep = segs, [outs[0]]
        if bit is None:
            return True
        self.got = [swap(outs[1] if halve else outs[0], "seq", 1 << bit)]
        if halve:
            self.halved.append(bit)
        return False

    def send_back(self):
        self.bit = self.halved.pop() if self.halved else 0
        self.got = [swap(self.keep[0], "seq", 1 << self.bit)]

    def join(self, meta, us=1):
        rows, cols = self.keep[0].shape
        both = shape(2 * rows, cols, bf16)
        spec = whole_spec((rows, cols))
        self.keep = [call(
            functools.partial(join_kernel, self.bit, self.segs), (1,), [spec, spec],
            whole_spec(both.shape), both, [], (meta,), self.keep[0], self.got[0], us=us,
        )]
        self.segs = [2 * rows for rows in self.segs]

    def result(self, meta, ways):
        cols = self.keep[0].shape[1]
        shapes = {"rows": lambda r: (2 * r, cols), "flip": lambda r: (cols, 2 * r), "cols": lambda r: (r, 2 * cols)}
        out = [shape(*shapes[way](rows), f32) for way, rows in zip(ways, self.segs)]
        spec = whole_spec(self.keep[0].shape)
        return call(
            functools.partial(result_kernel, self.segs, ways), (1,), [spec, spec],
            [whole_spec(x.shape) for x in out], out, [], (meta,), self.keep[0], self.got[0],
            out=True, us=0.1,
        )


def advance(total, meta, us=1, wait=()):
    if total.bit is None:
        if total.add(meta, us, wait):
            total.send_back()
    elif total.bit:
        total.join(meta, us)
        total.send_back()


def shards(
    tokens_in, out_grad, lengths, norm_gain, proj_z, proj_x, proj_bc, proj_dt, conv_x, conv_bc,
    bias_x, bias_bc, dt_bias, a_log, d_skip, gate_gain, proj_out,
):
    packs, count, part = tokens_in.shape
    features, inner = proj_x.shape
    heads = proj_dt.shape[1]
    size = inner // heads
    width = conv_x.shape[0]
    nseq = lengths.shape[1]
    bc_part = proj_bc.shape[1]
    bc = bc_part * lax.axis_size("head")
    half = packs // 2
    chans = inner + bc
    ext = count + EDGE
    rows = heads * size
    total_inner = inner * lax.axis_size("head")
    dims = (packs, count, features, inner, bc, heads, size, width, nseq)
    seq_place, head_place = lax.axis_index("seq"), lax.axis_index("head")
    meta = jnp.stack([seq_place, head_place]).astype(jnp.int32)
    pre = (meta, lengths)
    grid = (packs,)

    order.clear()
    tokens = jnp.swapaxes(tokens_in, 1, 2)
    cotangent = jnp.swapaxes(out_grad, 1, 2)
    far = swap(tokens, "head", 2)
    near = swap(tokens, "head", 1)
    tail = call(
        tail_kernel, (1,),
        [pl.BlockSpec((packs, part, LANES), lambda p, _: (0, 0, count // LANES - 1))],
        whole_spec((part, LANES)), shape(part, LANES, bf16), [], (meta,),
        pltpu.with_memory_space_constraint(tokens, pltpu.HBM), us=0.05,
    )
    tail = shift(tail, "seq", 1)
    ins = [
        proj_bc.T, conv_bc, bias_bc, norm_gain, proj_dt.T, conv_x, bias_x, dt_bias, a_log, d_skip,
        gate_gain, proj_out,
    ]
    outs = [
        shape(features, inner, bf16),
        shape(bc_part, features + LANES, bf16), shape(features, bc_part, bf16),
        shape(features, LANES, bf16), shape(LANES, features, bf16), shape(8, inner, f32),
        shape(8, bc_part, f32), shape(8, LANES, f32), shape(1, inner, f32), shape(1, inner, f32),
        shape(part, 1, f32),
    ]
    (
        w_out, shared, w_bc, w_dt, w_dt_rows, conv_own, conv_bc_own, small, skip, gain_gate, norm_gain_own,
    ) = call(
        functools.partial(prepare_kernel, dims), (1,), [whole_spec(x.shape) for x in ins],
        [whole_spec(x.shape) for x in outs], outs, [], (), *ins, wait=(tail,),
        us=0.05,
    )
    edge_far, shared_far = swap(tail, "head", 2), swap(shared, "head", 2)
    far, edge_far, shared_far = lax.optimization_barrier((far, edge_far, shared_far))
    edge_pieces = tail, swap(tail, "head", 1), edge_far, swap(edge_far, "head", 1)
    weight_pieces = shared, swap(shared, "head", 1), shared_far, swap(shared_far, "head", 1)
    diagonal = swap(far, "head", 1)
    token_pieces = tokens, near, far, diagonal

    lane_spec = pack_spec((count, LANES))
    chan_spec = pack_spec((count, inner))
    xbc_spec = pack_spec((count, chans))
    model_spec = pack_spec((features, count))
    piece_spec = pack_spec((part, count))
    edge_spec = whole_spec((part, LANES))
    pay_shape = (rows + EDGE, LANES)
    pay_specs = [side_spec(pay_shape, half, k) for k in (True, False)]
    pay = shape(half, *pay_shape, jnp.int16)
    state_spec = half_spec(pay_shape, half)
    vec = whole_spec((1, inner))
    square = whole_spec((features, inner))

    w_bc_rows, conv_all, gain_all, edge, edge_raws = call(
        functools.partial(border_kernel, dims),
        (1,),
        [edge_spec] * 4 + [whole_spec((bc_part, features + LANES))] * 4
        + [square, whole_spec((8, inner))],
        [
            whole_spec((bc, features)), whole_spec((8, chans)), whole_spec((features, 1)),
            whole_spec((features, LANES)), whole_spec((LANES, chans)),
        ],
        [
            shape(bc, features, bf16), shape(8, chans, f32), shape(features, 1, f32),
            shape(features, LANES, bf16), shape(LANES, chans, f32),
        ],
        [pltpu.VMEM((4, part, LANES), bf16), pltpu.VMEM((4, bc_part, features + LANES), bf16)],
        (meta,),
        *edge_pieces, *weight_pieces, proj_x, conv_own,
    )

    def front(keep, onto):
        spec = lambda shape_of: sided_spec(shape_of, half, keep)
        return call(
            functools.partial(front_kernel, dims, keep),
            (1,),
            [spec((part, count))] * 4
            + [
                square, whole_spec((bc, features)), whole_spec((LANES, features)),
                whole_spec((8, chans)), whole_spec((8, LANES)), whole_spec((features, 1)),
                whole_spec((LANES, chans)),
            ],
            [
                spec((features, count)), spec((1, count)), spec((ext, inner)), spec((ext, bc_part)),
                spec((count, chans)), spec((count, LANES)), pack_spec(pay_shape),
            ],
            [
                shape(packs, features, count, bf16), shape(packs, 1, count, f32),
                shape(packs, ext, inner, bf16), shape(packs, ext, bc_part, bf16),
                shape(packs, count, chans, bf16), shape(packs, count, LANES, f32), pay,
            ],
            [Each((4, part, count), bf16), Each((ext, chans), f32)],
            pre,
            *token_pieces, proj_x, w_bc_rows, w_dt_rows, conv_all, small, gain_all, edge_raws,
            us=6, onto=onto, group=half,
        )

    *early, send = front(False, ())
    kept = {}

    def keep_work(_):
        *kept["front"], kept["keep"] = front(True, early)
        order.hold(*(kept["front"][i] for i in (0, 4, 5)))

    def inner_work(_):
        *_, xbc, steps = kept["front"]
        kept["inner"] = call(
            functools.partial(inner_kernel, dims),
            (packs // half,),
            [xbc_spec, lane_spec],
            chan_spec,
            shape(packs, count, inner, f32),
            [],
            pre,
            xbc, steps,
            us=6, group=half,
        )
        order.hold(kept["inner"])

    def cot_work(newest):
        own, far = kept["cots"]
        near = swap(own, "head", 1)
        cots = own, near, far, swap(lax.optimization_barrier((far, newest))[0], "head", 1)
        kept["cot"], kept["gg"] = call(
            functools.partial(cot_kernel, dims),
            (packs // half,),
            [piece_spec] * 4 + [whole_spec((inner, features))],
            [model_spec, chan_spec],
            [shape(packs, features, count, bf16), shape(packs, count, inner, f32)],
            [Each((4, part, count), bf16)],
            pre,
            *cots, proj_out,
            us=5.5, group=half,
        )

    def gate_slope_work(_):
        normed, _, raw_x, raw_bc, *_ = kept["front"]
        own = lax.optimization_barrier((cotangent, normed))[0]
        kept["cots"] = own, swap(own, "head", 2)
        kept["slope"] = call(
            functools.partial(gate_slope_kernel, dims),
            (packs // half,),
            [model_spec, square, pack_spec((ext, inner)), pack_spec((ext, bc_part)),
             whole_spec((8, inner)), whole_spec((8, bc_part))],
            [chan_spec, chan_spec, pack_spec((count, bc_part))],
            [shape(packs, count, inner, bf16), shape(packs, count, inner, f32),
             shape(packs, count, bc_part, f32)],
            [Each((ext, inner), f32), Each((ext, bc_part), f32)],
            pre,
            normed, proj_z, raw_x, raw_bc, conv_own, conv_bc_own,
            us=7, group=half,
        )

    state_keep, state_recv = scan_states(
        lambda: kept["keep"], send, meta, packs, heads, size, 0,
        (keep_work, gate_slope_work, inner_work, cot_work),
    )
    normed, inv, raw_x, raw_bc, xbc, steps = kept["front"]
    inner_out, cot, gg = kept["inner"], kept["cot"], kept["gg"]
    gate, slope_x, slope_bc = kept["slope"]
    order.drop(inner_out)

    y, stats = call(
        functools.partial(gate_kernel, dims),
        (packs // half,),
        [
            xbc_spec, lane_spec, chan_spec, state_spec, state_spec, chan_spec, chan_spec, vec, vec,
        ],
        [chan_spec, pack_spec((2, count))],
        [shape(packs, count, inner, f32), shape(packs, 2, count, f32)],
        [],
        pre,
        xbc, steps, inner_out, state_keep, state_recv, gate, gg, gain_gate, skip,
        us=6.6, group=half,
    )
    stats = head_pieces(stats)

    gy, gated, ggate, gkeep, gsend, gate_small = call(
        functools.partial(grad_kernel, dims, total_inner),
        (packs // half,),
        [
            *[pack_spec((2, count))] * 4, xbc_spec, lane_spec, chan_spec, chan_spec, chan_spec, vec,
            vec,
        ],
        [chan_spec] * 3 + pay_specs + [whole_spec((8, inner))],
        [shape(packs, count, inner, f32)] + [shape(packs, count, inner, bf16)] * 2
        + [pay, pay, shape(8, inner, f32)],
        [],
        pre,
        *stats, xbc, steps, y, gate, gg, gain_gate, skip,
        us=8.3, group=half,
    )

    piece_shape = shape(packs, part, count, f32)
    send_spec = pack_spec((2, part, count))
    rows_half = features // 2
    half_specs = [whole_spec((rows_half, inner))] * 2
    half_shapes = [shape(rows_half, inner, f32), shape(rows_half, inner, bf16)]
    half_sums = pltpu.VMEM((2, rows_half, inner), f32)
    row8, row8_shape = whole_spec((8, features)), shape(8, features, f32)

    early_sum, late_sum = SeqSum(), SeqSum()

    def out_work(_):
        *kept["out"], keep, give = call(
            functools.partial(out_kernel, dims),
            (packs // half,),
            [chan_spec, model_spec, square],
            [piece_spec, piece_spec, send_spec] + half_specs,
            [piece_shape, piece_shape, shape(packs, 2, part, count, bf16)] + half_shapes,
            [Each((4, part, count), f32), half_sums],
            pre,
            gated, cot, w_out,
            us=6.8, group=half,
        )
        early_sum.put(keep, give)

    def z_work(_):
        keep, give, kept["gain"] = call(
            functools.partial(z_kernel, dims),
            (packs // half,),
            [model_spec, chan_spec, square],
            half_specs + [row8],
            half_shapes + [row8_shape],
            [half_sums],
            pre,
            normed, ggate, proj_z,
            us=5.3, group=half,
        )
        early_sum.put(keep, give)

    def diag_work(_):
        kept["diag"] = call(
            functools.partial(diag_kernel, dims),
            (packs // half,),
            [xbc_spec, lane_spec, chan_spec, chan_spec, state_spec, state_spec],
            [chan_spec, pack_spec((count, bc)), lane_spec],
            [
                shape(packs, count, inner, f32), shape(packs, count, bc, f32),
                shape(packs, count, LANES, f32),
            ],
            [],
            pre,
            xbc, steps, gy, y, state_keep, state_recv,
            us=12, group=half,
        )

    def early_work(_):
        early_sum.add(meta)
        own, far, send = kept["out"]
        own, far = call(
            out_gather_kernel, grid, [piece_spec, piece_spec, send_spec], [piece_spec, piece_spec],
            [piece_shape, shape(packs, part, count, bf16)], [], (), own, far, swap(send, "head", 1),
        )
        kept["out"] = own, swap(far, "head", 2)

    gstate_keep, gstate_recv = scan_states(
        gkeep, gsend, meta, packs, heads, size, 1, (out_work, z_work, diag_work, early_work),
        lambda: early_sum.got,
    )
    out_own, out_far = kept["out"]
    dx, dbc, sums = kept["diag"]

    edge_tile = (EDGE, inner)

    def pair_spec(shape_of):
        return pl.BlockSpec((half,) + shape_of, lambda p, *_: (p,) + (0,) * len(shape_of))

    pair_lane = pair_spec((count, LANES))
    share_own, share_near, grad_x, state_sums, edge_x = call(
        functools.partial(share_kernel, dims),
        (packs // half,),
        [xbc_spec, lane_spec, pack_spec((count, bc)), state_spec, state_spec, chan_spec, chan_spec,
         chan_spec, whole_spec((8, inner)), vec],
        [lane_spec, lane_spec, chan_spec, lane_spec, pack_spec(edge_tile)],
        [shape(packs, count, LANES, f32)] * 2
        + [shape(packs, count, inner, f32), shape(packs, count, LANES, f32),
           shape(packs, *edge_tile, bf16)],
        [Each((2 * EDGE, inner), f32)],
        pre,
        xbc, steps, dbc, gstate_keep, gstate_recv, gy, dx, slope_x, conv_own, skip,
        us=6.4, group=half,
    )
    share_near = swap(share_near, "head", 1)
    advance(early_sum, meta)
    two = shape(half, count, LANES, f32)
    bc_keep, bc_send = call(
        functools.partial(middle_kernel, (packs, bc_part)),
        (1,),
        [whole_spec((packs, count, LANES))] * 2,
        [whole_spec(two.shape)] * 2,
        [two, two],
        [],
        (meta,),
        share_own, share_near,
    )
    bc_recv = swap(bc_send, "head", 2)

    main_x, keep, give, grad_conv, gain_x = call(
        functools.partial(xback_kernel, dims),
        (packs // half,),
        [
            chan_spec, pack_spec((ext, inner)), model_spec, whole_spec((features, LANES)),
            pack_spec(edge_tile), whole_spec((8, inner)), square,
        ],
        [chan_spec, *half_specs, whole_spec((8, inner)), row8],
        [shape(packs, count, inner, bf16), *half_shapes, shape(8, inner, f32), row8_shape],
        [
            Each((count + EDGE, inner), f32), Each((ext, inner), f32), half_sums,
            pltpu.VMEM((LANES, inner), bf16),
        ],
        pre,
        grad_x, raw_x, normed, edge, edge_x, conv_own, proj_x,
        us=7, group=half, wait=(out_far,),
    )
    late_sum.put(keep, give)
    advance(early_sum, meta)

    gdt, gdt_rows, grad_small, gain_dt = call(
        functools.partial(step_kernel, dims),
        (packs // half,),
        [
            pair_lane, pair_lane, pair_lane, *[whole_spec((half,) + pay_shape)] * 4,
            whole_spec((8, LANES)), pair_spec((features, count)), whole_spec((features, LANES)),
        ],
        [pair_lane, row8, whole_spec((8, LANES)), row8],
        [shape(packs, count, LANES, bf16), row8_shape, shape(8, LANES, f32), row8_shape],
        [pltpu.VMEM((features, LANES), f32)],
        pre,
        steps, sums, state_sums, state_keep, state_recv, gstate_keep, gstate_recv, small, normed,
        w_dt,
        us=6,
    )
    advance(early_sum, meta)
    advance(late_sum, meta)
    give_rows = 2 * bc_part + 2 * SMALL
    gbc, edges, bc_sum, smalls = call(
        functools.partial(conv_bc_kernel, dims),
        (packs // half,),
        [
            half_spec((count, LANES), half), half_spec((count, LANES), half),
            pack_spec((count, bc_part)), pack_spec((ext, bc_part)), model_spec,
            whole_spec((features, LANES)), whole_spec((features, bc_part)),
            whole_spec((8, bc_part)), pack_spec(edge_tile), whole_spec((8, inner)), row8,
            whole_spec((8, LANES)), whole_spec((8, inner)), row8, row8, row8,
            whole_spec((features, 1)),
        ],
        [
            pack_spec((count, bc_part)), pack_spec((EDGE, inner + LANES)),
            whole_spec((give_rows, inner)), whole_spec((SMALL, inner)),
        ],
        [
            shape(packs, count, bc_part, bf16), shape(packs, EDGE, inner + LANES, bf16),
            shape(give_rows, inner, bf16), shape(SMALL, inner, f32),
        ],
        [
            Each((ext + EDGE, bc_part), f32), Each((ext, bc_part), f32),
            pltpu.VMEM((features, bc_part), f32), pltpu.VMEM((LANES, bc_part), bf16),
            pltpu.VMEM((8, bc_part), f32),
        ],
        pre,
        bc_keep, bc_recv, slope_bc, raw_bc, normed, edge, w_bc, conv_bc_own, edge_x, grad_conv,
        gdt_rows, grad_small, gate_small, kept["gain"], gain_x, gain_dt, gain_all,
        us=5, group=half,
    )
    edges = shift(edges, "seq", -1)
    bc_bits = [1 << k for k in range((lax.axis_size("seq") - 1).bit_length())]
    bc_got = swap(bc_sum, "seq", 1)
    advance(late_sum, meta)

    def bc_step(bit):
        nonlocal bc_sum, smalls, bc_got
        spec, small_spec = whole_spec(bc_sum.shape), whole_spec(smalls.shape)
        bc_sum, smalls = call(
            functools.partial(add_kernel, 1, False, [2 * bc_part], 1, True), (1,),
            [spec, spec, small_spec], [spec, small_spec],
            [shape(*bc_sum.shape, bf16), shape(*smalls.shape, f32)], [], (meta,),
            bc_sum, bc_got, smalls, us=0.1,
        )
        bc_got = swap(bc_sum, "seq", bit)

    bc_step(bc_bits[1])
    advance(early_sum, meta)

    tall = part + EDGE
    tall_send = pack_spec((2, tall, count))
    tall_spec = pack_spec((tall, count))
    row_spec, row_shape = pack_spec((1, count)), shape(packs, 1, count, f32)
    gn_own, gn_far, gn_send, dots = call(
        functools.partial(back_kernel, dims),
        (packs // half,),
        [
            chan_spec, pack_spec((EDGE, inner + LANES)), chan_spec, lane_spec,
            pack_spec((count, bc_part)), model_spec, square, square,
            whole_spec((features, bc_part)), whole_spec((features, LANES)),
        ],
        [piece_spec, piece_spec, tall_send, row_spec],
        [piece_shape, piece_shape, shape(packs, 2, tall, count, bf16), row_shape],
        [Each((4, part, count), f32)],
        pre,
        main_x, edges, ggate, gdt, gbc, normed, proj_z, proj_x, w_bc, w_dt,
        us=6, group=half,
    )
    near = swap(gn_send, "head", 1)
    order.drop(xbc, steps, normed)
    advance(late_sum, meta, 0.1)
    for bit in bc_bits[2:]:
        bc_step(bit)
    block_out = call(
        out_final_kernel, grid, [piece_spec] * 3, piece_spec, shape(packs, part, count, bf16), [],
        (), out_own, out_far, tokens, out=True, us=2,
    )
    block_out = jnp.swapaxes(block_out, 1, 2)

    gn_own, gn_far, dots = call(
        gather_kernel,
        grid,
        [piece_spec, piece_spec, tall_send, row_spec],
        [piece_spec, tall_spec, row_spec],
        [piece_shape, shape(packs, tall, count, bf16), row_shape],
        [],
        (),
        gn_own, gn_far, near, dots,
        us=0.1,
    )
    gn_far = swap(gn_far, "head", 2)
    order.hold(gn_own)
    while early_sum.bit != 0:
        advance(early_sum, meta)
    advance(late_sum, meta, 0.1)
    small_spec, give_spec = whole_spec(smalls.shape), whole_spec(bc_sum.shape)
    grad_bc, smalls = call(
        functools.partial(whole_kernel, bc_part), (1,), [give_spec, give_spec, small_spec],
        [whole_spec((bc_part, features)), small_spec],
        [shape(bc_part, features, f32), shape(*smalls.shape, f32)], [], (), bc_sum, bc_got, smalls,
        us=0.1,
    )

    def head_step(x, bit):
        return call(
            plus_kernel, (1,), [small_spec, small_spec], small_spec, shape(*x.shape, f32), [], (),
            x, swap(x, "head", bit), us=0.1,
        )

    gains = head_step(smalls, 1)
    grads_out, grads_z = early_sum.result(meta, ("flip", "rows"))
    while late_sum.bit != 0:
        advance(late_sum, meta, 0.1)
    gains = head_step(gains, 2)
    in_grad = call(
        functools.partial(final_kernel, (packs, count, features)),
        grid,
        [piece_spec, tall_spec, row_spec, piece_spec, row_spec, whole_spec((part, 1)), piece_spec],
        piece_spec,
        piece_shape,
        [],
        (),
        gn_own, gn_far, dots, tokens, inv, norm_gain_own, cotangent,
        us=2, out=True,
    )
    in_grad = jnp.swapaxes(in_grad, 1, 2)
    order.drop(gn_own)
    vectors = [(inner,), (bc_part,), (heads,), (heads,), (heads,), (inner,), (part,)]
    tables = [(heads, features), (width, inner), (width, bc_part)]
    outs = call(
        functools.partial(unpack_kernel, (heads, features, bc_part, width)), (1,),
        [small_spec, small_spec], [whole_spec(x) for x in tables + vectors],
        [shape(*x, f32) for x in tables + vectors], [], (meta,), smalls, gains, out=True,
    )
    grad_dt, grad_conv, grad_conv_bc = outs[:3]
    bias_x_grad, bias_bc_grad, dt_bias_grad, a_log_grad, skip_grad, gate_grad, grad_gain = outs[3:]
    grads_x, = late_sum.result(meta, ("rows",))
    return (
        block_out,
        in_grad,
        grad_gain,
        grads_z,
        grads_x,
        grad_bc.T,
        grad_dt.T,
        grad_conv,
        grad_conv_bc,
        bias_x_grad,
        bias_bc_grad,
        dt_bias_grad,
        a_log_grad,
        skip_grad,
        gate_grad,
        grads_out,
    )


def solution(mesh):
    token, column, vector = P(None, "seq", "head"), P(None, "head"), P("head")
    row = P("head", None)
    return jax.shard_map(
        shards,
        mesh=mesh,
        in_specs=(
            token, token, P(), vector, column, column, column, column, column, column, vector,
            vector, vector, vector, vector, vector, row,
        ),
        out_specs=(
            token, token, vector, column, column, column, column, column, column, vector, vector,
            vector, vector, vector, vector, row,
        ),
        check_vma=False,
    )
```

```python
import functools

import jax
import jax.numpy as jnp
from jax import lax
from jax.experimental import pallas as pl
from jax.experimental.pallas import tpu as pltpu
from jax.sharding import PartitionSpec as P

EPSILON = 1e-05
bf16 = jnp.bfloat16
f32 = jnp.float32
LANES = 128
EDGE = 16
MIB = 1024 * 1024
STEPS = 32000.0
UNIT = 16384.0
LN2 = 0.6931471805599453
GROUP = 16
SMALL = 32


def permuted(x, axis, route):
    y = lax.ppermute(x, axis, route)
    order.near.append(y)
    return y


def swap(x, axis, bit):
    return permuted(x, axis, [(i, i ^ bit) for i in range(lax.axis_size(axis))])


def shift(x, axis, distance):
    n = lax.axis_size(axis)
    return permuted(x, axis, [(i, i + distance) for i in range(n) if 0 <= i + distance < n])


def head_pieces(x):
    far = swap(x, "head", 2)
    near = swap(x, "head", 1)
    return x, near, far, swap(far, "head", 1)


def nn(a, b):
    return lax.dot_general(a, b, (((1,), (0,)), ((), ())), preferred_element_type=f32)


def nt(a, b):
    return lax.dot_general(a, b, (((1,), (1,)), ((), ())), preferred_element_type=f32)


def tn(a, b):
    return lax.dot_general(a, b, (((0,), (0,)), ((), ())), preferred_element_type=f32)


def split2(v):
    hi = v.astype(bf16)
    return hi, (v - hi.astype(f32)).astype(bf16)


def split3(v):
    hi = v.astype(bf16)
    rest = v - hi.astype(f32)
    mid = rest.astype(bf16)
    return hi, mid, (rest - mid.astype(f32)).astype(bf16)


def spread_matrix(heads, size):
    row = lax.broadcasted_iota(jnp.int32, (LANES, heads * size), 0)
    col = lax.broadcasted_iota(jnp.int32, (LANES, heads * size), 1)
    first = (col >= row * size) & (col < (row + 1) * size)
    again = (col >= (row - GROUP) * size) & (col < (row - GROUP + 1) * size)
    return jnp.where(first | again, 1.0, 0.0).astype(bf16)


def spread(v, matrix, heads):
    hi, lo = split2(head_lanes(v, heads))
    return nn((hi.astype(f32) + to_group(lo.astype(f32), 1)).astype(bf16), matrix)


def head_lanes(v, heads):
    return jnp.where(lax.broadcasted_iota(jnp.int32, v.shape, 1) < heads, v, 0.0)


def to_group(v, k):
    return pltpu.roll(v, k * GROUP, 1)


def from_group(v, k, heads):
    return head_lanes(pltpu.roll(v, LANES - k * GROUP, 1) if k else v, heads)


def collapse(v, matrix, heads):
    return head_lanes(nt(jnp.concatenate(split2(v), axis=1), jnp.concatenate([matrix] * 2, axis=1)), heads)


def triangle(count, lower):
    row = lax.broadcasted_iota(jnp.int32, (count, count), 0)
    col = lax.broadcasted_iota(jnp.int32, (count, count), 1)
    keep = (row >= col) if lower else (row <= col)
    return jnp.where(keep, 1.0, 0.0).astype(bf16)


def exact_sums(matrix, v, heads):
    hi, mid, lo = [piece.astype(f32) for piece in split3(v)]
    sums = nn(matrix, (hi + to_group(mid, 1) + to_group(lo, 2)).astype(bf16))
    return from_group(sums, 0, heads) + from_group(sums, 1, heads) + from_group(sums, 2, heads)


def step_sizes(v, heads):
    soft = jnp.maximum(v, 0.0) + jnp.log1p(jnp.exp(-jnp.abs(v)))
    return head_lanes(soft, heads)


def steps_of(block, heads):
    return step_sizes(block, heads), from_group(block, 1, heads)


def segments(positions, lens_ref, pack, count):
    total = jnp.zeros(positions.shape, jnp.int32)
    end = jnp.int32(0)
    for k in range(count):
        end = end + lens_ref[pack, k]
        total = total + jnp.where(positions >= end, 1, 0)
    return total


def column_segments(meta_ref, lens_ref, pack, count, nseq, before):
    rows = lax.broadcasted_iota(jnp.int32, (count + before, 1), 0)
    return segments(rows + (meta_ref[0] * count - before), lens_ref, pack, nseq)


def row_segments(meta_ref, lens_ref, pack, count, nseq):
    cols = lax.broadcasted_iota(jnp.int32, (1, count), 1)
    return segments(cols + meta_ref[0] * count, lens_ref, pack, nseq)


def carry_column(meta_ref, seg_ext, before):
    same = seg_ext[before:] == seg_ext[before - 1 : before]
    return jnp.where(same & (meta_ref[0] > 0), 1.0, 0.0)


def to_int16(v):
    return jnp.floor(v + 0.5).astype(jnp.int32).astype(jnp.int16)


def encode_state(out, p, state, decay, heads, size):
    lane = lax.broadcasted_iota(jnp.int32, (1, LANES), 1)
    powers = jnp.zeros((1, LANES), f32)
    for h in range(heads):
        part = state[h * size : (h + 1) * size]
        top = jnp.max(jnp.max(jnp.abs(part), axis=0, keepdims=True), axis=1, keepdims=True)
        power = jnp.ceil(jnp.log(jnp.maximum(top, 1e-30)) / LN2)
        powers = powers + jnp.where(lane == h, power, 0.0)
        codes = jnp.clip(part * (jnp.exp(-power * LN2) * STEPS), -32767.0, 32767.0)
        out[p, h * size : (h + 1) * size, :] = to_int16(codes)
    row = lax.broadcasted_iota(jnp.int32, (EDGE, LANES), 0)
    coarse = jnp.floor(decay * UNIT)
    fine = (decay * UNIT - coarse) * UNIT
    tail = jnp.where(row == 0, powers, jnp.where(row == 1, coarse, jnp.where(row == 2, fine, 0.0)))
    out[p, heads * size :, :] = to_int16(tail)


def decode_state(block, heads, size):
    values = block.astype(jnp.int32).astype(f32)
    tail = values[heads * size :]
    scale = jnp.exp(tail[0:1] * LN2) / STEPS
    decay = (tail[1:2] + tail[2:3] / UNIT) / UNIT
    return scaled_state(values[: heads * size], scale, heads, size), decay


def sigmoid(v):
    return 1.0 / (1.0 + jnp.exp(-v))


def scaled_state(state, decay, heads, size):
    return jnp.concatenate(
        [state[h * size : (h + 1) * size] * decay[:, h : h + 1] for h in range(heads)], axis=0
    )


def tail_kernel(meta, tokens, out):
    lane = lax.broadcasted_iota(jnp.int32, out.shape, 1)
    total = jnp.zeros(out.shape, f32)
    for p in range(tokens.shape[0]):
        moved = pltpu.roll(tokens[p].astype(f32), (p + 1) * EDGE, 1)
        total = jnp.where((lane >= p * EDGE) & (lane < (p + 1) * EDGE), moved, total)
    out[...] = total.astype(bf16)


def wide_row(ref, lanes=LANES):
    row = ref[...].astype(f32)[None, :]
    blank = lanes - row.shape[1]
    return jnp.concatenate([row, jnp.zeros((1, blank), f32)], axis=1) if blank else row


def prepare_kernel(dims, *refs):
    packs, count, features, inner, bc, heads, size, width, nseq = dims
    (
        wbc, conv_bc, bias_bc, norm_gain, wdt, conv_x, bias_x, dt_bias, a_log, d_skip, gate_gain, wout,
        wout_o, shared_o, wbc_o, wdt_o, wdt_rows_o, conv_x_o, conv_bc_o, small_o, skip_o, gate_gain_o, gain_o,
    ) = refs
    bc_part, part = bc // 4, features // 4
    wout_o[...] = jnp.transpose(wout[...])
    taps = conv_bc[...].astype(f32)
    bias = wide_row(bias_bc, bc_part)
    gain = wide_row(norm_gain, part)
    pieces = [gain[:, c * bc_part : (c + 1) * bc_part] for c in range(part // bc_part)]
    rows = jnp.concatenate([taps, bias] + pieces, axis=0)
    rows = jnp.concatenate([rows, jnp.zeros((LANES - rows.shape[0], bc_part), f32)], axis=0)
    rows = jnp.concatenate([rows, jnp.zeros((LANES, LANES - bc_part), f32)], axis=1)
    extra = jnp.transpose(rows)[:bc_part].astype(bf16)
    shared_o[:, :features] = wbc[...]
    shared_o[:, features:] = extra
    wbc_o[...] = jnp.transpose(wbc[...].astype(f32)).astype(bf16)
    dt_rows = jnp.concatenate(
        [wdt[...].astype(f32), jnp.zeros((LANES - heads, features), f32)], axis=0
    )
    wdt_rows_o[...] = dt_rows.astype(bf16)
    wdt_o[...] = jnp.transpose(dt_rows).astype(bf16)
    blank = jnp.zeros((7 - width, inner), f32)
    conv_x_o[...] = jnp.concatenate(
        [conv_x[...].astype(f32), wide_row(bias_x, inner), blank], axis=0
    )
    conv_bc_o[...] = jnp.concatenate([taps, bias, blank[:, :bc_part]], axis=0)
    small_o[...] = jnp.concatenate(
        [wide_row(dt_bias), wide_row(a_log), jnp.zeros((6, LANES), f32)], axis=0
    )
    skips = jnp.concatenate([wide_row(d_skip), jnp.zeros((7, LANES), f32)], axis=0)
    matrix = spread_matrix(heads, size)
    skip_o[...] = sum(nn(piece, matrix) for piece in split3(skips))[0:1]
    gate_gain_o[...] = wide_row(gate_gain, inner)
    column = jnp.concatenate([gain, jnp.zeros((LANES - 1, part), f32)], axis=0)
    column = jnp.concatenate([column, jnp.zeros((LANES, 2 * LANES - part), f32)], axis=1)
    gain_o[...] = jnp.transpose(column)[:part, 0:1]


def normalise(values, gain, features):
    mean = jnp.sum(values * values, axis=0, keepdims=True) / features
    inv = lax.rsqrt(mean + EPSILON)
    return inv, ((values * inv) * gain).astype(bf16)


def raw_rows(normed, wx, wbc):
    return jnp.concatenate([nn(normed, wx), nt(normed, wbc)], axis=1).astype(bf16)


def border_kernel(dims, meta, *refs):
    packs, count, features, inner, bc, heads, size, width, nseq = dims
    edges, shared = refs[0:4], refs[4:8]
    wx, conv_x, wbc_o, conv_o, gain_o, edge_o, raws_o, stage, weights = refs[8:]
    head = meta[1]
    part, bc_part = features // 4, bc // 4
    for k in range(4):
        weights[head ^ k] = shared[k][...]
        stage[head ^ k] = edges[k][...]
    whole = weights[...].reshape(bc, weights.shape[2])
    wbc_o[...] = whole[:, :features]
    extra = whole[:, features:].astype(f32)
    conv_o[:, :inner] = conv_x[...]
    conv_o[:, inner:] = jnp.transpose(extra)[0:8]
    for h in range(4):
        for c in range(part // bc_part):
            gain_o[h * part + c * bc_part : h * part + (c + 1) * bc_part, :] = extra[
                h * bc_part : (h + 1) * bc_part, width + 1 + c : width + 2 + c
            ]
    _, normed = normalise(stage[...].reshape(features, stage.shape[2]).astype(f32), gain_o[...], features)
    edge_o[...] = normed
    raws_o[...] = raw_rows(jnp.transpose(normed), wx[...], wbc_o[...]).astype(f32)


def front_kernel(dims, keep, meta, lens, *refs):
    packs, count, features, inner, bc, heads, size, width, nseq = dims
    tokens, refs = refs[0:4], refs[4:]
    wx, wbc, wdt, conv, small, gain, edge_raws, *refs = refs
    normed_o, inv_o, rawx_o, rawbc_o, xbc_o, steps_o, state_o, stage, raws = refs[-9:]
    side = meta[0] & 1 if keep else 1 - (meta[0] & 1)
    pack = order.pack + (packs // 2) * side
    head = meta[1]
    for k in range(4):
        stage[head ^ k] = tokens[k][0]
    inv, normed_t = normalise(stage[...].reshape(features, count).astype(f32), gain[...], features)
    inv_o[0] = inv
    normed_o[0] = normed_t
    normed = jnp.transpose(normed_t)
    raws[EDGE:, :] = raw_rows(normed, wx[...], wbc[...]).astype(f32)
    raws[0:EDGE, :] = edge_raws[pl.ds(pl.multiple_of(pack * EDGE, EDGE), EDGE), :]

    def own_bc(values):
        bc_part = bc // 4
        parts = [values[:, inner + h * bc_part : inner + (h + 1) * bc_part] for h in range(4)]
        low = jnp.where((head & 1) == 0, parts[0], parts[1])
        high = jnp.where((head & 1) == 0, parts[2], parts[3])
        return jnp.where((head >> 1) == 0, low, high)

    rawx_o[0] = raws[:, :inner].astype(bf16)
    rawbc_o[0] = own_bc(raws[...]).astype(bf16)
    seg = column_segments(meta, lens, pack, count, nseq, EDGE)
    seg_main = seg[EDGE:]
    pre = convolved(raws, conv, seg, count, width)
    xbc = (pre * sigmoid(pre)).astype(bf16)
    xbc_o[0] = xbc
    v = head_lanes(nt(normed, wdt[...]).astype(bf16).astype(f32) + small[0:1, :], heads)
    dt = step_sizes(v, heads)
    rate = -dt * jnp.exp(small[1:2, :])
    cum = exact_sums(triangle(count, True), rate, heads)
    steps_o[0] = v + to_group(cum, 1)
    cum_end = cum[count - 1 : count]
    weight = jnp.where(seg_main == seg[count + EDGE - 1 :], jnp.exp(cum_end - cum), 0.0) * dt
    matrix = spread_matrix(heads, size)
    scaled = (xbc[:, :inner].astype(f32) * spread(weight, matrix, heads)).astype(bf16)
    state = jnp.transpose(nn(jnp.transpose(xbc[:, inner : inner + bc // 2]), scaled))
    carry = carry_column(meta, seg, EDGE)
    encode_state(state_o, 0, state, carry[count - 1 :] * jnp.exp(cum_end), heads, size)


def convolved(raws, conv, seg, count, width):
    pre = jnp.broadcast_to(conv[width : width + 1, :], (count, raws.shape[1]))
    for k in range(width):
        low = EDGE - (width - 1) + k
        mask = jnp.where(seg[low : low + count] == seg[EDGE:], 1.0, 0.0)
        pre = pre + conv[k : k + 1, :] * raws[low : low + count, :] * mask
    return pre


def gate_slope_kernel(dims, meta, lens, *refs):
    packs, count, features, inner, bc, heads, size, width, nseq = dims
    normed, wz, raw_x, raw_bc, conv_x, conv_bc, gate_o, slope_x_o, slope_bc_o, raws, raws_bc = refs
    pack = order.pack
    gate_o[0] = tn(normed[0], wz[...]).astype(bf16)
    seg = column_segments(meta, lens, pack, count, nseq, EDGE)
    for raw, wide, conv, out in ((raw_x, raws, conv_x, slope_x_o), (raw_bc, raws_bc, conv_bc, slope_bc_o)):
        wide[...] = raw[0].astype(f32)
        pre = convolved(wide, conv, seg, count, width)
        sig = sigmoid(pre)
        out[0] = sig * (1.0 + pre * (1.0 - sig))


def store_state(meta, packs, pack, keep_o, send_o, state, decay, heads, size):
    mine = (pack // (packs // 2)) == (meta[0] & 1)

    @pl.when(mine)
    def _():
        encode_state(keep_o, 0, state, decay, heads, size)

    @pl.when(jnp.logical_not(mine))
    def _():
        encode_state(send_o, 0, state, decay, heads, size)


def load_state(meta, packs, pack, keep, recv, heads, size):
    mine = (pack // (packs // 2)) == (meta[0] & 1)
    block = jnp.where(mine, keep[0].astype(jnp.int32), recv[0].astype(jnp.int32))
    return decode_state(block, heads, size)[0]


def decay_parts(cum_col, cum_row, masked):
    return masked * jnp.exp(jnp.minimum(cum_col - cum_row, 0.0))


def block_mask(meta, lens, pack, count, nseq):
    col = column_segments(meta, lens, pack, count, nseq, 0)
    row = row_segments(meta, lens, pack, count, nseq)
    tri = lax.broadcasted_iota(jnp.int32, (count, count), 0) >= lax.broadcasted_iota(
        jnp.int32, (count, count), 1
    )
    return tri & (col == row)


def inner_kernel(dims, meta, lens, *refs):
    packs, count, features, inner, bc, heads, size, width, nseq = dims
    xbc, steps, inner_o = refs
    pack = order.pack
    half = bc // 2
    b_vals, c_vals = xbc[0, :, inner : inner + half], xbc[0, :, inner + half :]
    scores = jnp.where(block_mask(meta, lens, pack, count, nseq), nt(c_vals, b_vals), 0.0)
    dt, cum_col = steps_of(steps[0], heads)
    cum_row = jnp.transpose(cum_col)
    dt_row = jnp.transpose(dt)
    lane = lax.broadcasted_iota(jnp.int32, (count, 2 * size), 1)
    for pair in range(heads // 2):
        cols = slice(2 * pair * size, (2 * pair + 2) * size)
        x_pair = xbc[0, :, cols]
        parts = []
        for h in (2 * pair, 2 * pair + 1):
            weights = decay_parts(cum_col[:, h : h + 1], cum_row[h : h + 1], scores)
            parts.append(nn((weights * dt_row[h : h + 1]).astype(bf16), x_pair))
        inner_o[0, :, cols] = jnp.where(lane < size, parts[0], parts[1])


def cot_kernel(dims, meta, lens, *refs):
    packs, count, features, inner, bc, heads, size, width, nseq = dims
    pieces, (wout, cot_o, gg_o, stage) = refs[:4], refs[4:]
    for k in range(4):
        stage[meta[1] ^ k] = pieces[k][0]
    cotangent = stage[...].reshape(features, count)
    cot_o[0] = cotangent
    gg_o[0] = jnp.transpose(nn(wout[...], cotangent))


def compose(lower, upper, heads, size):
    return scaled_state(lower[0], upper[1], heads, size) + upper[0], lower[1] * upper[1]


def choose(flag, a, b):
    return jnp.where(flag, a[0], b[0]), jnp.where(flag, a[1], b[1])


def pair_kernel(dims, rev, meta, own, other, out):
    packs, heads, size = dims
    upper_is_own = ((meta[0] & 1) ^ rev) == 1
    for p in range(packs // 2):
        a, b = decode_state(own[p], heads, size), decode_state(other[p], heads, size)
        both = compose(choose(upper_is_own, b, a), choose(upper_is_own, a, b), heads, size)
        encode_state(out, p, *both, heads, size)


def entering_from(before, b, p, heads, size):
    if before is None:
        return (jnp.zeros_like(b[0]), jnp.ones_like(b[1])), b
    entering = decode_state(before[p], heads, size)
    return entering, compose(b, entering, heads, size)


def cube_kernel(dims, rev, bit, first, meta, *refs):
    packs, heads, size = dims
    total, other = refs[0], refs[1]
    before, next_o, before_o = (None, refs[2], refs[3]) if first else refs[2:5]
    upper_is_own = (((meta[0] >> bit) & 1) ^ rev) == 1
    for p in range(packs // 2):
        a, b = decode_state(total[p], heads, size), decode_state(other[p], heads, size)
        both = compose(choose(upper_is_own, b, a), choose(upper_is_own, a, b), heads, size)
        encode_state(next_o, p, *both, heads, size)
        entering, longer = entering_from(before, b, p, heads, size)
        encode_state(before_o, p, *choose(upper_is_own, longer, entering), heads, size)


def last_kernel(dims, rev, bit, first, meta, *refs):
    packs, heads, size = dims
    own, pair, other = refs[0:3]
    before, keep_o, send_o = (None, refs[3], refs[4]) if first else refs[3:6]
    add = (((meta[0] >> bit) & 1) ^ rev) == 1
    upper_is_own = ((meta[0] & 1) ^ rev) == 1
    for p in range(packs // 2):
        entering, longer = entering_from(
            before, decode_state(other[p], heads, size), p, heads, size
        )
        low = choose(add, longer, entering)
        lower = decode_state(jnp.where(upper_is_own, pair[p].astype(jnp.int32), own[p].astype(jnp.int32)), heads, size)
        high = compose(low, lower, heads, size)
        encode_state(keep_o, p, *choose(upper_is_own, high, low), heads, size)
        encode_state(send_o, p, *choose(upper_is_own, low, high), heads, size)


def gate_kernel(dims, meta, lens, *refs):
    packs, count, features, inner, bc, heads, size, width, nseq = dims
    xbc, steps, inner_in, keep, recv, gate, gg, gain, skip, y_o, stats_o = refs
    pack = order.pack
    state = jnp.concatenate(
        split2(load_state(meta, packs, pack, keep, recv, heads, size)), axis=1
    )
    carry = carry_column(meta, column_segments(meta, lens, pack, count, nseq, EDGE), EDGE)
    matrix = spread_matrix(heads, size)
    entering = spread(carry * jnp.exp(from_group(steps[0], 1, heads)), matrix, heads)
    c_vals = xbc[0, :, inner + bc // 2 :]
    y = inner_in[0] + entering * nt(jnp.concatenate([c_vals, c_vals], axis=1), state)
    y_o[0] = y
    gate_f = gate[0].astype(f32)
    ssd = y + xbc[0, :, :inner].astype(f32) * skip[...]
    mixed = ssd * (gate_f * sigmoid(gate_f))
    squares = jnp.sum(mixed * mixed, axis=1, keepdims=True)
    dots = jnp.sum(gain[...] * gg[0] * mixed, axis=1, keepdims=True)
    lane = lax.broadcasted_iota(jnp.int32, (count, LANES), 1)
    both = jnp.where(lane == 0, squares, 0.0) + jnp.where(lane == 1, dots, 0.0)
    stats_o[0] = jnp.transpose(both)[0:2]


def grad_kernel(dims, total_inner, meta, lens, *refs):
    packs, count, features, inner, bc, heads, size, width, nseq = dims
    (
        stats, near, far, diagonal, xbc, steps, y, gate, gg, gain, skip,
        gy_o, gated_o, ggate_o, keep_o, send_o, small_o,
    ) = refs
    pack = order.pack

    @order.first
    def _():
        small_o[...] = jnp.zeros_like(small_o)

    sums = (stats[0] + near[0]) + (far[0] + diagonal[0])
    row = lax.broadcasted_iota(jnp.int32, (LANES, count), 0)
    wide = jnp.where(row == 0, sums[0:1], 0.0) + jnp.where(row == 1, sums[1:2], 0.0)
    cols = jnp.transpose(wide)
    inv = lax.rsqrt(cols[:, 0:1] / total_inner + EPSILON)
    dot = cols[:, 1:2] / total_inner
    x_f, gg_f, gate_f = xbc[0, :, :inner].astype(f32), gg[0], gate[0].astype(f32)
    ssd = y[0] + x_f * skip[...]
    sig = sigmoid(gate_f)
    act = gate_f * sig
    mixed = ssd * act
    scaled = mixed * inv
    gated_o[0] = (scaled * gain[...]).astype(bf16)
    grad_mixed = inv * gain[...] * gg_f - mixed * (inv * inv * inv * dot)
    gy_f = grad_mixed * act
    gy_o[0] = gy_f
    ggate_o[0] = (grad_mixed * ssd * sig * (1.0 + gate_f * (1.0 - sig))).astype(bf16)
    carry = carry_column(meta, column_segments(meta, lens, pack, count, nseq, EDGE), EDGE)
    cum = from_group(steps[0], 1, heads)
    entering = carry * jnp.exp(cum)
    ey_hi, ey_lo = split2(gy_f * spread(entering, spread_matrix(heads, size), heads))
    c_rows = jnp.transpose(xbc[0, :, inner + bc // 2 :])
    state_grad = jnp.transpose(nn(c_rows, ey_hi) + nn(c_rows, ey_lo))
    small_o[0:1, :] += jnp.sum(gg_f * scaled, axis=0, keepdims=True)
    small_o[1:2, :] += jnp.sum(gy_f * x_f, axis=0, keepdims=True)
    return lambda: store_state(
        meta, packs, pack, keep_o, send_o, state_grad, entering[count - 1 :], heads, size
    )


def diag_kernel(dims, meta, lens, *refs):
    packs, count, features, inner, bc, heads, size, width, nseq = dims
    xbc, steps, gy, y, keep, recv, dx_o, dbc_o, sums_o = refs
    pack = order.pack
    half = bc // 2
    b_vals, c_vals = xbc[0, :, inner : inner + half], xbc[0, :, inner + half :]
    col = column_segments(meta, lens, pack, count, nseq, 0)
    row = row_segments(meta, lens, pack, count, nseq)
    mask = (col == row) & (
        lax.broadcasted_iota(jnp.int32, (count, count), 0)
        <= lax.broadcasted_iota(jnp.int32, (count, count), 1)
    )
    scores = jnp.where(mask, nt(b_vals, c_vals), 0.0)
    dt, cum_col = steps_of(steps[0], heads)
    cum_row = jnp.transpose(cum_col)
    lane = lax.broadcasted_iota(jnp.int32, (count, 2 * size), 1)
    grad_scores = jnp.zeros((count, count), f32)
    zero = jnp.zeros((), bf16)
    for pair in range(heads // 2):
        cols = slice(2 * pair * size, (2 * pair + 2) * size)
        x_pair = xbc[0, :, cols]
        x_twice = jnp.concatenate([x_pair, x_pair], axis=1)
        gy_hi, gy_lo = split2(gy[0, :, cols])
        gy_wide = jnp.concatenate([gy_hi, gy_lo], axis=1)
        parts = []
        for h in (2 * pair, 2 * pair + 1):
            own = (lane < size) if h % 2 == 0 else (lane >= size)
            part = jnp.exp(jnp.minimum(cum_row[h : h + 1] - cum_col[:, h : h + 1], 0.0)) * dt[:, h : h + 1]
            parts.append(nn((scores * part).astype(bf16), gy_wide))
            both = jnp.concatenate([jnp.where(own, gy_hi, zero), jnp.where(own, gy_lo, zero)], axis=1)
            grad_scores = grad_scores + nt(x_twice, both) * part
        two = [part[:, : 2 * size] + part[:, 2 * size :] for part in parts]
        dx_o[0, :, cols] = jnp.where(lane < size, two[0], two[1])
    hi, lo = split2(jnp.where(mask, grad_scores, 0.0))
    state_hi, state_lo = split2(load_state(meta, packs, pack, keep, recv, heads, size))
    carry = carry_column(meta, column_segments(meta, lens, pack, count, nseq, EDGE), EDGE)
    matrix = spread_matrix(heads, size)
    ey_hi, ey_lo = split2(gy[0] * spread(carry * jnp.exp(cum_col), matrix, heads))
    dbc_o[0, :, :half] = nn(
        jnp.concatenate([hi, lo], axis=1), jnp.concatenate([c_vals, c_vals], axis=0)
    )
    b_rows = jnp.transpose(b_vals)
    dbc_o[0, :, half:] = (
        jnp.transpose(nn(b_rows, hi) + nn(b_rows, lo))
        + nn(ey_hi, state_hi) + nn(ey_hi, state_lo) + nn(ey_lo, state_hi)
    )
    row_sum = collapse(gy[0] * y[0], matrix, heads)
    col_sum = collapse(xbc[0, :, :inner].astype(f32) * dx_o[0], matrix, heads)
    sums_o[0] = row_sum + to_group(col_sum, 1)


def scatter_pieces(head, stage, own_o, far_o, send_o):
    own_o[0] = stage[head]
    send_o[0, 0] = stage[head ^ 1].astype(bf16)
    far_o[0] = stage[head ^ 2]
    send_o[0, 1] = stage[head ^ 3].astype(bf16)


def accumulate(meta, pack, packs, sums, term, keep_o, send_o):
    sums[...] += term.reshape(sums.shape)

    def finish():
        @last_pack(pack, packs)
        def _():
            side = meta[0] & 1
            keep_o[...] = sums[side]
            send_o[...] = sums[1 - side].astype(bf16)

    return finish


def last_pack(pack, packs):
    return lambda work: pl.when(pack == packs - 1)(work)


def cleared(*refs):
    @order.first
    def _():
        for ref in refs:
            ref[...] = jnp.zeros_like(ref)


def out_kernel(dims, meta, lens, *refs):
    packs, count, features, inner, bc, heads, size, width, nseq = dims
    gated, cot, wout, own_o, far_o, send_o, keep_o, give_o, stage, sums = refs
    pack = order.pack
    cleared(sums)
    stage[...] = nt(wout[...], gated[0]).reshape(stage.shape)
    scatter_pieces(meta[1], stage, own_o, far_o, send_o)
    return accumulate(meta, pack, packs, sums, nn(cot[0], gated[0]), keep_o, give_o)


def gain_row(weights, grads):
    part = jnp.sum(weights.astype(f32) * grads, axis=1, keepdims=True)
    return jnp.transpose(jnp.broadcast_to(part, (part.shape[0], LANES)))[0:8]


def z_kernel(dims, meta, lens, *refs):
    normed, ggate, wz, keep_o, give_o, gain_o, sums = refs
    pack = order.pack
    cleared(sums)
    store = accumulate(meta, pack, dims[0], sums, nn(normed[0], ggate[0]), keep_o, give_o)

    def finish():
        store()

        @last_pack(pack, dims[0])
        def _():
            gain_o[...] = gain_row(wz[...], sums[...].reshape(wz.shape))

    return finish


def end_weights(seg, seg_main, cum_col, dt_col, count):
    cum_end = cum_col[count - 1 :]
    end = seg[count + EDGE - 1 :]
    return jnp.where(seg_main == end, jnp.exp(cum_end - cum_col), 0.0) * dt_col


def share_kernel(dims, meta, lens, *refs):
    packs, count, features, inner, bc, heads, size, width, nseq = dims
    (
        xbc, steps, dbc, gkeep, grecv, gy, dx, slope, conv, skip,
        own_o, near_o, grad_o, state_sum_o, edge_o,
        gpad,
    ) = refs
    pack = order.pack
    half, quarter = bc // 2, bc // 4
    g_hi, g_lo = split2(load_state(meta, packs, pack, gkeep, grecv, heads, size))
    seg = column_segments(meta, lens, pack, count, nseq, EDGE)
    dt, cum = steps_of(steps[0], heads)
    matrix = spread_matrix(heads, size)
    wide = spread(end_weights(seg, seg[EDGE:], cum, dt, count), matrix, heads)
    x_f = xbc[0, :, :inner].astype(f32)
    hi, lo = split2(wide * x_f)
    grad_b = dbc[0, :, :half] + nn(hi, g_hi) + nn(lo, g_hi) + nn(hi, g_lo)
    grad_c = dbc[0, :, half:]
    even = jnp.concatenate([grad_b[:, :quarter], grad_c[:, :quarter]], axis=1)
    odd = jnp.concatenate([grad_b[:, quarter:], grad_c[:, quarter:]], axis=1)
    first = (meta[1] & 1) == 0
    own_o[0] = jnp.where(first, even, odd)
    near_o[0] = jnp.where(first, odd, even)
    b_vals = xbc[0, :, inner : inner + half]
    u_wide = wide * nt(
        jnp.concatenate([b_vals, b_vals], axis=1), jnp.concatenate([g_hi, g_lo], axis=1)
    )
    state_sum_o[0] = collapse(x_f * u_wide, matrix, heads)
    grad_x = (dx[0] + u_wide + gy[0] * skip[...]) * slope[0]
    grad_o[0] = grad_x
    gpad[:EDGE, :] = jnp.zeros((EDGE, inner), f32)
    gpad[EDGE:, :] = grad_x[:EDGE]
    edge_o[0] = conv_rows(gpad, conv, seg, EDGE, width).astype(bf16)


def middle_kernel(dims, meta, *refs):
    packs, quarter = dims
    own, near, keep_o, send_o = refs
    half = packs // 2
    first = (meta[1] >> 1) == 0
    for p in range(half):
        a, b = own[p] + near[p], own[p + half] + near[p + half]
        low = jnp.concatenate([a[:, :quarter], b[:, :quarter]], axis=1)
        high = jnp.concatenate([a[:, quarter:], b[:, quarter:]], axis=1)
        keep_o[p] = jnp.where(first, low, high)
        send_o[p] = jnp.where(first, high, low)


def conv_taps(grads, raws, gconv_o, seg, count, width):
    seg_main = seg[EDGE : EDGE + count]
    for k in range(width):
        low = EDGE - (width - 1) + k
        mask = jnp.where(seg[low : low + count] == seg_main, 1.0, 0.0)
        gconv_o[k : k + 1, :] += jnp.sum(
            grads * (raws[low : low + count, :] * mask), axis=0, keepdims=True
        )
    gconv_o[width : width + 1, :] += jnp.sum(grads, axis=0, keepdims=True)


def conv_rows(gpad, conv, seg, rows, width):
    total = jnp.zeros((rows, gpad.shape[1]), f32)
    for lag in range(width):
        mask = jnp.where(seg[lag : lag + rows] == seg[:rows], 1.0, 0.0)
        k = width - 1 - lag
        total = total + conv[k : k + 1, :] * (gpad[lag : lag + rows, :] * mask)
    return total


def step_kernel(dims, meta, lens, *refs):
    packs, count, features, inner, bc, heads, size, width, nseq = dims
    (
        steps, sums, state_sums, keep, recv, gkeep, grecv, small, normed, wdt,
        gdt_o, gdt_rows_o, gsmall_o, gain_o,
        gdt_sums,
    ) = refs
    group, half = pl.program_id(0), packs // 2
    matrix = spread_matrix(heads, size)
    ones = jnp.ones((8, LANES), bf16)
    decay_rate = -jnp.exp(small[1:2, :])
    upper = triangle(count, False)
    rows = lax.broadcasted_iota(jnp.int32, (count, LANES), 0)
    mine = group == (meta[0] & 1)
    bias_sum, rate_sum = jnp.zeros((1, LANES), f32), jnp.zeros((1, LANES), f32)
    term = jnp.zeros((features, LANES), f32)
    for j in range(half):
        pick = lambda a, b: jnp.where(mine, a[j].astype(jnp.int32), b[j].astype(jnp.int32))
        state = decode_state(pick(keep, recv), heads, size)[0]
        gstate = decode_state(pick(gkeep, grecv), heads, size)[0]
        seg = column_segments(meta, lens, group * half + j, count, nseq, EDGE)
        v = steps[j]
        dt, cum = steps_of(v, heads)
        sig = head_lanes(sigmoid(v), heads)
        row_sum, col_sum = from_group(sums[j], 0, heads), from_group(sums[j], 1, heads)
        state_sum = state_sums[j]
        carry = carry_column(meta, seg, EDGE)
        hi, lo = split2(gstate * state)
        by_head = collapse(nt(ones, hi) + nt(ones, lo), matrix, heads)[0:1]
        last = by_head * carry[count - 1 :] * jnp.exp(cum[count - 1 :]) + jnp.sum(
            state_sum, axis=0, keepdims=True
        )
        grad_cum = row_sum - col_sum - state_sum + jnp.where(rows == count - 1, last, 0.0)
        grad_rate = exact_sums(upper, grad_cum, heads)
        ratio = jnp.where(dt > 1e-30, sig / jnp.maximum(dt, 1e-30), 1.0)
        grad_dt = head_lanes(ratio * (col_sum + state_sum) + grad_rate * decay_rate * sig, heads)
        low = grad_dt.astype(bf16)
        gdt_o[j] = low
        bias_sum = bias_sum + jnp.sum(grad_dt, axis=0, keepdims=True)
        rate_sum = rate_sum + jnp.sum(grad_rate * dt * decay_rate, axis=0, keepdims=True)
        term = term + nn(normed[j], low)

    @pl.when(group == 0)
    def _():
        gsmall_o[...] = jnp.zeros_like(gsmall_o)
        gdt_sums[...] = jnp.zeros_like(gdt_sums)

    gsmall_o[0:1, :] += bias_sum
    gsmall_o[1:2, :] += rate_sum
    gdt_sums[...] += term

    @pl.when(group == packs // half - 1)
    def _():
        gdt_rows_o[...] = jnp.transpose(gdt_sums[...])[0:8]
        gain_o[...] = gain_row(wdt[...], gdt_sums[...])


def xback_kernel(dims, meta, lens, *refs):
    packs, count, features, inner, bc, heads, size, width, nseq = dims
    (
        grads, raw, normed, edge, edge_x, conv, wx,
        main_o, keep_o, give_o, gconv_o, gain_o,
        gpad, raws, sums, rows_x,
    ) = refs
    pack = order.pack
    seg = column_segments(meta, lens, pack, count, nseq, EDGE)

    cleared(gconv_o, rows_x, sums)
    raws[...] = raw[0].astype(f32)
    gpad[:count, :] = grads[0]
    gpad[count:, :] = jnp.zeros((EDGE, inner), f32)
    conv_taps(grads[0], raws, gconv_o, seg, count, width)
    seg_pad = jnp.concatenate([seg[EDGE:], jnp.full((8, 1), -1, jnp.int32)], axis=0)
    main = conv_rows(gpad, conv, seg_pad, count, width).astype(bf16)
    main_o[0] = main
    rows_x[pl.ds(pl.multiple_of(pack * EDGE, EDGE), EDGE), :] = edge_x[0]
    sums[...] += nn(normed[0], main).reshape(sums.shape)

    def finish():
        @last_pack(pack, packs)
        def _():
            sums[...] += nn(edge[...], rows_x[...]).reshape(sums.shape)
            side = meta[0] & 1
            keep_o[...] = sums[side]
            give_o[...] = sums[1 - side].astype(bf16)
            gain_o[...] = gain_row(wx[...], sums[...].reshape(wx.shape))

    return finish


def conv_bc_kernel(dims, meta, lens, *refs):
    packs, count, features, inner, bc, heads, size, width, nseq = dims
    (
        keep, recv, slope, raw, normed, edge, wbc, conv, edge_x,
        gconv_x, gdt_rows, gsmall, gate_small, gain_z, gain_x, gain_dt, gain,
        rows_o, edges_o, give_o, small_o,
        gpad, raws, sums, edge_bc, gconv,
    ) = refs
    pack = order.pack
    quarter = bc // 4

    cleared(gconv, edge_bc, sums)
    gpad[:EDGE, :] = jnp.zeros((EDGE, quarter), f32)
    gpad[EDGE + count :, :] = jnp.zeros((EDGE, quarter), f32)
    both = keep[0] + recv[0]
    grad = jnp.where(pack < packs // 2, both[:, :quarter], both[:, quarter:]) * slope[0]
    seg = column_segments(meta, lens, pack, count, nseq, EDGE)
    raws[...] = raw[0].astype(f32)
    gpad[EDGE : EDGE + count, :] = grad
    conv_taps(grad, raws, gconv, seg, count, width)
    seg_pad = jnp.concatenate([seg, jnp.full((8, 1), -1, jnp.int32)], axis=0)
    grad_raw = conv_rows(gpad, conv, seg_pad, count + EDGE, width).astype(bf16)
    rows_o[0] = grad_raw[EDGE:]
    edge_bc[pl.ds(pl.multiple_of(pack * EDGE, EDGE), EDGE), :] = grad_raw[:EDGE]
    edges_o[0, :, :inner] = edge_x[0]
    blank = jnp.zeros((EDGE, LANES - quarter), bf16)
    edges_o[0, :, inner:] = jnp.concatenate([grad_raw[:EDGE], blank], axis=1)
    sums[...] += nn(normed[0], grad_raw[EDGE:])

    def finish():
        @last_pack(pack, packs)
        def _():
            total = sums[...] + nn(edge[...], edge_bc[...])
            rows = jnp.transpose(total)
            taps = width + 1
            give_o[:quarter, :] = rows[:, :inner].astype(bf16)
            give_o[quarter : 2 * quarter, :] = rows[:, inner:].astype(bf16)
            small_o[...] = jnp.zeros_like(small_o)
            for h in range(heads):
                small_o[2 * h : 2 * h + 1, :] = gdt_rows[h : h + 1, :inner]
                small_o[2 * h + 1 : 2 * h + 2, :] = gdt_rows[h : h + 1, inner:]
            row = 2 * heads
            small_o[row : row + taps, :] = gconv_x[:taps, :]
            row += taps
            small_o[row : row + 1, :] = gate_small[0:1, :]
            skips = collapse(gate_small[...], spread_matrix(heads, size), heads)
            small_o[row + 1 : row + 2, :] = jnp.concatenate(
                [gsmall[0:1, :], gsmall[1:2, :], skips[1:2, :]], axis=1
            )
            blank_row = jnp.zeros((1, inner - taps * quarter), f32)
            small_o[row + 2 : row + 3, :] = jnp.concatenate(
                [gconv[k : k + 1, :] for k in range(taps)] + [blank_row], axis=1
            )
            gains = gain_row(wbc[...], total)[0:1] + gain_z[0:1, :] + gain_x[0:1, :] + gain_dt[0:1, :]
            gains = gains / jnp.transpose(jnp.broadcast_to(gain[...], (features, LANES)))[0:1]
            small_o[row + 3 : row + 4, :] = gains[:, :inner]
            small_o[row + 4 : row + 5, :] = gains[:, inner:]
            hi, lo = split2(small_o[...])
            give_o[2 * quarter : 2 * quarter + SMALL, :] = hi
            give_o[2 * quarter + SMALL :, :] = lo

    return finish


def back_kernel(dims, meta, lens, *refs):
    packs, count, features, inner, bc, heads, size, width, nseq = dims
    (
        main, edges, ggate, gdt, gbc, normed, wz, wx, wbc, wdt,
        own_o, far_o, send_o, dots_o,
        stage,
    ) = refs
    head = meta[1]
    part, quarter = features // 4, bc // 4
    late = count - EDGE

    def with_edge(rows, edge):
        low = (rows[late:].astype(f32) + edge.astype(f32)).astype(bf16)
        return jnp.concatenate([rows[:late], low], axis=0)

    grad_x = with_edge(main[0], edges[0, :, :inner])
    grad_bc = with_edge(gbc[0], edges[0, :, inner : inner + quarter])
    whole = nt(wz[...], ggate[0]) + nt(wx[...], grad_x) + nt(wbc[...], grad_bc) + nt(wdt[...], gdt[0])
    dots = jnp.sum(whole * normed[0].astype(f32), axis=0, keepdims=True)
    stage[...] = whole.reshape(stage.shape)
    dots_o[0] = dots
    own_o[0] = stage[head]
    far_o[0] = stage[head ^ 2]
    for k in range(2):
        send_o[0, k, :part, :] = stage[head ^ (1 + 2 * k)].astype(bf16)
        send_o[0, k, part:, :] = extra_rows(dots)


def extra_rows(*values):
    row = lax.broadcasted_iota(jnp.int32, (EDGE, values[0].shape[1]), 0)
    total = jnp.zeros(row.shape, f32)
    for i, value in enumerate(values):
        for k, piece in enumerate(split3(value)):
            total = total + jnp.where(row == 3 * i + k, piece.astype(f32), 0.0)
    return total.astype(bf16)


def read_extra(block, i):
    rows = block.astype(f32)
    return rows[3 * i : 3 * i + 1] + rows[3 * i + 1 : 3 * i + 2] + rows[3 * i + 2 : 3 * i + 3]


def gather_kernel(own, far, near, dots, own_o, far_o, dots_o):
    part = own.shape[1]
    own_o[0] = own[0] + near[0, 0, :part, :].astype(f32)
    far_o[0, :part, :] = (far[0] + near[0, 1, :part, :].astype(f32)).astype(bf16)
    both = dots[0] + read_extra(near[0, 0, part:, :], 0)
    dots_o[0] = both
    far_o[0, part:, :] = extra_rows(both)


def final_kernel(dims, own, far, dots, tokens, inv, gain, out_grad, in_grad_o):
    packs, count, features = dims
    part = own.shape[1]
    grad = own[0] + far[0, :part, :].astype(f32)
    mean = (dots[0] + read_extra(far[0, part:, :], 0)) / features
    unit = tokens[0].astype(f32) * inv[0]
    in_grad_o[0] = out_grad[0].astype(f32) + inv[0] * (gain[...] * grad - unit * mean)


def out_gather_kernel(own, far, near, own_o, far_o):
    own_o[0] = own[0] + near[0, 0].astype(f32)
    far_o[0] = (far[0] + near[0, 1].astype(f32)).astype(bf16)


def out_final_kernel(own, far, tokens, out):
    out[0] = (tokens[0].astype(f32) + (own[0] + far[0].astype(f32))).astype(bf16)


def add_kernel(bit, halve, segs, count, small, meta, *refs):
    keep, got, refs = refs[:count], refs[count : 2 * count], refs[2 * count :]
    end = segs[-1] if count > 1 else sum(segs)
    write = 0
    if small:
        small_in, *refs, small_o = refs
        hi, lo = split2(small_in[...])
        mine = hi.astype(f32) + lo.astype(f32)
        theirs = got[-1][end : end + SMALL, :].astype(f32) + got[-1][end + SMALL :, :].astype(f32)
        total = mine + theirs
        small_o[...] = total
        if bit is not None:
            send_o = refs[-1]
            behind = send_o.shape[0] - 2 * SMALL
            hi, lo = split2(total)
            send_o[behind : behind + SMALL, :] = hi
            send_o[behind + SMALL :, :] = lo
    read = 0
    for i, rows in enumerate(segs):
        if count > 1:
            total = keep[i][...] + got[i][:rows, :].astype(f32)
        else:
            total = keep[0][read : read + rows, :].astype(f32) + got[0][read : read + rows, :].astype(f32)
        read += rows
        if halve:
            half = rows // 2
            first = ((meta[0] >> bit) & 1) == 0
            top, bottom = total[:half], total[half:]
            refs[0][write : write + half, :] = jnp.where(first, top, bottom)
            refs[1][write : write + half, :] = jnp.where(first, bottom, top).astype(bf16)
            write += half
        else:
            refs[0][write : write + rows, :] = total.astype(bf16)
            write += rows


def whole_kernel(quarter, keep, got, small, out, small_o):
    total = keep[: 2 * quarter, :].astype(f32) + got[: 2 * quarter, :].astype(f32)
    out[...] = jnp.concatenate([total[:quarter], total[quarter:]], axis=1)
    hi, lo = split2(small[...])
    end = 2 * quarter
    theirs = got[end : end + SMALL, :].astype(f32) + got[end + SMALL :, :].astype(f32)
    small_o[...] = (hi.astype(f32) + lo.astype(f32)) + theirs


def join_kernel(bit, segs, meta, mine, got, out):
    first = ((meta[0] >> bit) & 1) == 0
    read = 0
    for rows in segs:
        a = mine[read : read + rows, :].astype(f32)
        b = got[read : read + rows, :].astype(f32)
        out[2 * read : 2 * read + rows, :] = jnp.where(first, a, b).astype(bf16)
        out[2 * read + rows : 2 * read + 2 * rows, :] = jnp.where(first, b, a).astype(bf16)
        read += rows


def result_kernel(segs, ways, meta, mine, got, *outs):
    first = (meta[0] & 1) == 0
    read = 0
    for rows, way, out in zip(segs, ways, outs):
        a = mine[read : read + rows, :].astype(f32)
        b = got[read : read + rows, :].astype(f32)
        top, bottom = jnp.where(first, a, b), jnp.where(first, b, a)
        if way == "rows":
            out[:rows, :] = top
            out[rows:, :] = bottom
        elif way == "flip":
            out[:, :rows] = jnp.transpose(top)
            out[:, rows:] = jnp.transpose(bottom)
        else:
            out[...] = jnp.concatenate([top, bottom], axis=1)
        read += rows


def plus_kernel(a, b, out):
    out[...] = a[...] + b[...]


def unpack_kernel(dims, meta, *refs):
    heads, features, bc_part, width = dims
    smalls, gains, dt_o, taps_x_o, taps_bc_o, bias_x_o, bias_bc_o, dt_bias_o, a_log_o, skip_o, gate_o, gain_o = refs
    for h in range(heads):
        dt_o[h : h + 1, :] = jnp.concatenate(
            [smalls[2 * h : 2 * h + 1, :], smalls[2 * h + 1 : 2 * h + 2, :]], axis=1
        )
    row = 2 * heads
    taps_x_o[...] = smalls[row : row + width, :]
    bias_x_o[...] = smalls[row + width, :]
    row += width + 1
    gate_o[...] = smalls[row, :]
    for k, out in enumerate((dt_bias_o, a_log_o, skip_o)):
        out[...] = smalls[row + 1, k * LANES : k * LANES + heads]
    taps = smalls[row + 2 : row + 3, :]
    for k in range(width):
        taps_bc_o[k : k + 1, :] = taps[:, k * bc_part : (k + 1) * bc_part]
    bias_bc_o[...] = taps[0, width * bc_part : (width + 1) * bc_part]
    both = jnp.concatenate([gains[row + 3 : row + 4, :], gains[row + 4 : row + 5, :]], axis=1)
    part = features // 4
    parts = [both[:, h * part : (h + 1) * part] for h in range(4)]
    low = jnp.where((meta[1] & 1) == 0, parts[0], parts[1])
    high = jnp.where((meta[1] & 1) == 0, parts[2], parts[3])
    gain_o[...] = jnp.where((meta[1] >> 1) == 0, low, high)[0]


class Spec:
    def __init__(self, shape, index, each=True):
        self.shape, self.index, self.each = tuple(shape), index, each

    def block(self, group):
        zeros = (0,) * len(self.shape)
        if not self.each:
            return pl.BlockSpec(self.shape, lambda p, *_: zeros)
        size = group or 1
        return pl.BlockSpec(
            (size,) + self.shape, lambda p, *pre: (self.index(p, pre, bool(group)),) + zeros
        )


def whole_spec(shape):
    return Spec(shape, None, False)


def pack_spec(shape):
    return Spec(shape, lambda p, pre, grouped: p)


def half_spec(shape, half):
    return Spec(shape, lambda p, pre, grouped: 0 if grouped else p % half)


def sided_spec(shape, half, keep):
    def index(p, pre, grouped):
        side = pre[0][0] & 1 if keep else 1 - (pre[0][0] & 1)
        return side if grouped else p + half * side

    return Spec(shape, index)


def side_spec(shape, half, keep):
    def index(p, pre, grouped):
        if grouped:
            return 0
        side = pre[0][0] & 1 if keep else 1 - (pre[0][0] & 1)
        group = p // half
        return jnp.where(group == side, p % half, jnp.where(group < side, 0, half - 1))

    return Spec(shape, index)


class Each:
    def __init__(self, shape, dtype):
        self.shape, self.dtype = tuple(shape), dtype

    def scratch(self, group):
        return pltpu.VMEM(((group,) if group else ()) + self.shape, self.dtype)


class Order:
    def __init__(self):
        self.clear()

    def clear(self):
        self.last, self.near, self.held = (), [], []
        self.pack, self.lane, self.lanes = None, 0, 1

    def first(self, work):
        if self.lane == 0:
            pl.when(self.pack == 0)(work)

    def hold(self, *arrays):
        self.held += arrays

    def drop(self, *arrays):
        self.held = [x for x in self.held if not any(x is y for y in arrays)]

    def placed(self, x):
        return pltpu.with_memory_space_constraint(x, pltpu.VMEM) if self.holds(x) else x

    def holds(self, x):
        return any(x is y for y in self.near)


order = Order()


def call(
    kernel, grid, in_specs, out_specs, out_shape, scratch, prefetch, *args, limit=28, wait=(), us=1,
    out=False, onto=(), group=0,
):
    first = len(prefetch) + len(args)
    args = args + tuple(onto)
    in_specs = list(in_specs) + [pl.BlockSpec(memory_space=pl.ANY)] * len(onto)
    given = len(prefetch) + len(args)
    held = order.last + tuple(wait)
    held += tuple(x for x in order.held if not any(x is y for y in args + held))
    late = len(held)
    single = not isinstance(out_shape, (list, tuple))
    out_specs, out_shape = ([out_specs], [out_shape]) if single else (list(out_specs), list(out_shape))
    token = jax.ShapeDtypeStruct((8, LANES), f32)
    count = len(out_shape)
    results = count if out is True else int(out)

    specs = list(in_specs[: len(in_specs) - len(onto)]) + out_specs
    blocks = lambda items: [x.block(group) if isinstance(x, Spec) else x for x in items]

    def body(*refs):
        ins, rest = refs[:first], refs[given + late :]
        fixed, blocked = ins[: len(prefetch)], (*ins[len(prefetch) :], *rest[:count])
        own = rest[count + 1 :]
        finish = []
        for lane in range(group or 1):
            order.pack, order.lane, order.lanes = pl.program_id(0), lane, group or 1
            views, scratches = blocked, own
            if group:
                order.pack = order.pack * group + lane
                views = [
                    ref.at[pl.ds(lane, 1)] if isinstance(spec, Spec) and spec.each else ref
                    for ref, spec in zip(blocked, specs)
                ]
                scratches = [
                    ref.at[lane] if isinstance(item, Each) else ref for ref, item in zip(own, scratch)
                ]
            finish.append(kernel(*fixed, *views, *scratches))
        for work in finish:
            if work is not None:
                work()

    *outs, order_out = pl.pallas_call(
        body,
        grid_spec=pltpu.PrefetchScalarGridSpec(
            num_scalar_prefetch=len(prefetch),
            grid=grid,
            in_specs=blocks(in_specs) + [pl.BlockSpec(memory_space=pl.ANY)] * late,
            out_specs=blocks(out_specs + [whole_spec(token.shape)]),
            scratch_shapes=[x.scratch(group) if isinstance(x, Each) else x for x in scratch],
        ),
        input_output_aliases={first + i: i for i in range(len(onto))},
        out_shape=[
            x if i < results else pltpu.VMEM(x.shape, x.dtype) for i, x in enumerate(out_shape + [token])
        ],
        compiler_params=pltpu.CompilerParams(vmem_limit_bytes=limit * MIB),
        cost_estimate=pl.CostEstimate(
            flops=int(us * 10e9), bytes_accessed=int(us * 3e6), transcendentals=0
        ),
    )(*[pltpu.with_memory_space_constraint(x, pltpu.VMEM) for x in prefetch], *[order.placed(x) for x in args], *[order.placed(x) for x in held])
    order.last = (order_out,)
    order.near.append(order_out)
    order.near += outs[results:]
    return outs[0] if single else outs


def shape(*dims_and_type):
    return jax.ShapeDtypeStruct(dims_and_type[:-1], dims_and_type[-1])


def scan_states(keep, send, meta, packs, heads, size, rev, beside, waits=lambda: ()):
    dims = (packs, heads, size)
    rows = heads * size
    half = packs // 2
    pay = shape(half, rows + EDGE, LANES, jnp.int16)
    spec = whole_spec(pay.shape)
    bits = (lax.axis_size("seq") - 1).bit_length()
    beside = list(beside)

    def work(newest):
        if beside:
            beside.pop(0)(newest)

    other = swap(send, "seq", 1)
    work(send)
    keep = keep() if callable(keep) else keep
    total = call(
        functools.partial(pair_kernel, dims, rev), (1,), [spec, spec], spec, pay, [], (meta,),
        keep, other,
    )
    before = None
    for bit in range(1, bits):
        got = swap(total, "seq", 1 << bit)
        extra = () if before is None else (before,)
        work(total)
        if bit < bits - 1:
            total, before = call(
                functools.partial(cube_kernel, dims, rev, bit, before is None), (1,),
                [spec] * (2 + len(extra)), [spec, spec], [pay, pay], [], (meta,),
                total, got, *extra,
            )
        else:
            own, back = call(
                functools.partial(last_kernel, dims, rev, bit, before is None), (1,),
                [spec] * (3 + len(extra)), [spec, spec], [pay, pay], [],
                (meta,), keep, other, got, *extra, wait=waits(),
            )
    recv = swap(back, "seq", 1)
    while beside:
        work(back)
    return own, recv


class SeqSum:
    def __init__(self):
        self.keep, self.got, self.segs = [], [], []
        self.small = self.bit = None
        self.bits = list(range(1, (lax.axis_size("seq") - 1).bit_length()))
        self.halved = []

    def put(self, keep, give, segs=None, small=None):
        self.keep.append(keep)
        self.got.append(swap(give, "seq", 1))
        self.segs += segs or [keep.shape[0]]
        self.small = small

    def add(self, meta, us=1, wait=()):
        bit = self.bits.pop(0) if self.bits else None
        halve = bit is not None and all(rows % (2 * EDGE) == 0 for rows in self.segs)
        cols = self.keep[0].shape[1]
        segs = [rows // 2 for rows in self.segs] if halve else self.segs
        rows = sum(segs)
        small = self.small is not None
        behind = 2 * SMALL if small and bit is not None else 0
        low = shape(rows + behind, cols, bf16)
        out = [shape(rows, cols, f32), low] if halve else [low]
        ins = [*self.keep, *self.got]
        if small:
            ins.append(self.small)
            out.append(shape(*self.small.shape, f32))
        outs = call(
            functools.partial(add_kernel, bit, halve, self.segs, len(self.keep), small), (1,),
            [whole_spec(x.shape) for x in ins], [whole_spec(x.shape) for x in out], out, [],
            (meta,), *ins, us=us, wait=wait,
        )
        if small:
            self.small = outs[-1]
        self.segs, self.keep = segs, [outs[0]]
        if bit is None:
            return True
        self.got = [swap(outs[1] if halve else outs[0], "seq", 1 << bit)]
        if halve:
            self.halved.append(bit)
        return False

    def send_back(self):
        self.bit = self.halved.pop() if self.halved else 0
        self.got = [swap(self.keep[0], "seq", 1 << self.bit)]

    def join(self, meta, us=1):
        rows, cols = self.keep[0].shape
        both = shape(2 * rows, cols, bf16)
        spec = whole_spec((rows, cols))
        self.keep = [call(
            functools.partial(join_kernel, self.bit, self.segs), (1,), [spec, spec],
            whole_spec(both.shape), both, [], (meta,), self.keep[0], self.got[0], us=us,
        )]
        self.segs = [2 * rows for rows in self.segs]

    def result(self, meta, ways, us=0.01):
        cols = self.keep[0].shape[1]
        shapes = {"rows": lambda r: (2 * r, cols), "flip": lambda r: (cols, 2 * r), "cols": lambda r: (r, 2 * cols)}
        out = [shape(*shapes[way](rows), f32) for way, rows in zip(ways, self.segs)]
        spec = whole_spec(self.keep[0].shape)
        return call(
            functools.partial(result_kernel, self.segs, ways), (1,), [spec, spec],
            [whole_spec(x.shape) for x in out], out, [], (meta,), self.keep[0], self.got[0],
            out=True, us=us,
        )


def advance(total, meta, us=1, wait=()):
    if total.bit is None:
        if total.add(meta, us, wait):
            total.send_back()
    elif total.bit:
        total.join(meta, us)
        total.send_back()


def shards(
    tokens_in, out_grad, lengths, norm_gain, proj_z, proj_x, proj_bc, proj_dt, conv_x, conv_bc,
    bias_x, bias_bc, dt_bias, a_log, d_skip, gate_gain, proj_out,
):
    packs, count, part = tokens_in.shape
    features, inner = proj_x.shape
    heads = proj_dt.shape[1]
    size = inner // heads
    width = conv_x.shape[0]
    nseq = lengths.shape[1]
    bc_part = proj_bc.shape[1]
    bc = bc_part * lax.axis_size("head")
    half = packs // 2
    chans = inner + bc
    ext = count + EDGE
    rows = heads * size
    total_inner = inner * lax.axis_size("head")
    dims = (packs, count, features, inner, bc, heads, size, width, nseq)
    seq_place, head_place = lax.axis_index("seq"), lax.axis_index("head")
    meta = jnp.stack([seq_place, head_place]).astype(jnp.int32)
    pre = (meta, lengths)
    grid = (packs,)

    order.clear()
    tokens = jnp.swapaxes(tokens_in, 1, 2)
    cotangent = jnp.swapaxes(out_grad, 1, 2)
    far = swap(tokens, "head", 2)
    near = swap(tokens, "head", 1)
    tail = call(
        tail_kernel, (1,),
        [pl.BlockSpec((packs, part, LANES), lambda p, _: (0, 0, count // LANES - 1))],
        whole_spec((part, LANES)), shape(part, LANES, bf16), [], (meta,),
        pltpu.with_memory_space_constraint(tokens, pltpu.HBM), us=0.05,
    )
    tail = shift(tail, "seq", 1)
    ins = [
        proj_bc.T, conv_bc, bias_bc, norm_gain, proj_dt.T, conv_x, bias_x, dt_bias, a_log, d_skip,
        gate_gain, proj_out,
    ]
    outs = [
        shape(features, inner, bf16),
        shape(bc_part, features + LANES, bf16), shape(features, bc_part, bf16),
        shape(features, LANES, bf16), shape(LANES, features, bf16), shape(8, inner, f32),
        shape(8, bc_part, f32), shape(8, LANES, f32), shape(1, inner, f32), shape(1, inner, f32),
        shape(part, 1, f32),
    ]
    (
        w_out, shared, w_bc, w_dt, w_dt_rows, conv_own, conv_bc_own, small, skip, gain_gate, norm_gain_own,
    ) = call(
        functools.partial(prepare_kernel, dims), (1,), [whole_spec(x.shape) for x in ins],
        [whole_spec(x.shape) for x in outs], outs, [], (), *ins, wait=(tail,),
        us=0.05,
    )
    edge_far, shared_far = swap(tail, "head", 2), swap(shared, "head", 2)
    far, edge_far, shared_far = lax.optimization_barrier((far, edge_far, shared_far))
    edge_pieces = tail, swap(tail, "head", 1), edge_far, swap(edge_far, "head", 1)
    weight_pieces = shared, swap(shared, "head", 1), shared_far, swap(shared_far, "head", 1)
    diagonal = swap(far, "head", 1)
    token_pieces = tokens, near, far, diagonal

    lane_spec = pack_spec((count, LANES))
    chan_spec = pack_spec((count, inner))
    xbc_spec = pack_spec((count, chans))
    model_spec = pack_spec((features, count))
    piece_spec = pack_spec((part, count))
    edge_spec = whole_spec((part, LANES))
    pay_shape = (rows + EDGE, LANES)
    pay_specs = [side_spec(pay_shape, half, k) for k in (True, False)]
    pay = shape(half, *pay_shape, jnp.int16)
    state_spec = half_spec(pay_shape, half)
    vec = whole_spec((1, inner))
    square = whole_spec((features, inner))

    w_bc_rows, conv_all, gain_all, edge, edge_raws = call(
        functools.partial(border_kernel, dims),
        (1,),
        [edge_spec] * 4 + [whole_spec((bc_part, features + LANES))] * 4
        + [square, whole_spec((8, inner))],
        [
            whole_spec((bc, features)), whole_spec((8, chans)), whole_spec((features, 1)),
            whole_spec((features, LANES)), whole_spec((LANES, chans)),
        ],
        [
            shape(bc, features, bf16), shape(8, chans, f32), shape(features, 1, f32),
            shape(features, LANES, bf16), shape(LANES, chans, f32),
        ],
        [pltpu.VMEM((4, part, LANES), bf16), pltpu.VMEM((4, bc_part, features + LANES), bf16)],
        (meta,),
        *edge_pieces, *weight_pieces, proj_x, conv_own,
    )

    def front(keep, onto):
        spec = lambda shape_of: sided_spec(shape_of, half, keep)
        return call(
            functools.partial(front_kernel, dims, keep),
            (half,),
            [spec((part, count))] * 4
            + [
                square, whole_spec((bc, features)), whole_spec((LANES, features)),
                whole_spec((8, chans)), whole_spec((8, LANES)), whole_spec((features, 1)),
                whole_spec((LANES, chans)),
            ],
            [
                spec((features, count)), spec((1, count)), spec((ext, inner)), spec((ext, bc_part)),
                spec((count, chans)), spec((count, LANES)), pack_spec(pay_shape),
            ],
            [
                shape(packs, features, count, bf16), shape(packs, 1, count, f32),
                shape(packs, ext, inner, bf16), shape(packs, ext, bc_part, bf16),
                shape(packs, count, chans, bf16), shape(packs, count, LANES, f32), pay,
            ],
            [Each((4, part, count), bf16), Each((ext, chans), f32)],
            pre,
            *token_pieces, proj_x, w_bc_rows, w_dt_rows, conv_all, small, gain_all, edge_raws,
            us=6, onto=onto,
        )

    *early, send = front(False, ())
    kept = {}

    def keep_work(_):
        *kept["front"], kept["keep"] = front(True, early)
        order.hold(*(kept["front"][i] for i in (0, 4, 5)))

    def inner_work(_):
        *_, xbc, steps = kept["front"]
        kept["inner"] = call(
            functools.partial(inner_kernel, dims),
            grid,
            [xbc_spec, lane_spec],
            chan_spec,
            shape(packs, count, inner, f32),
            [],
            pre,
            xbc, steps,
            us=6,
        )
        order.hold(kept["inner"])

    def cot_work(newest):
        own, far = kept["cots"]
        near = swap(own, "head", 1)
        cots = own, near, far, swap(lax.optimization_barrier((far, newest))[0], "head", 1)
        kept["cot"], kept["gg"] = call(
            functools.partial(cot_kernel, dims),
            (packs // half,),
            [piece_spec] * 4 + [whole_spec((inner, features))],
            [model_spec, chan_spec],
            [shape(packs, features, count, bf16), shape(packs, count, inner, f32)],
            [Each((4, part, count), bf16)],
            pre,
            *cots, proj_out,
            us=5.5, group=half,
        )

    def gate_slope_work(_):
        normed, _, raw_x, raw_bc, *_ = kept["front"]
        own = lax.optimization_barrier((cotangent, normed))[0]
        kept["cots"] = own, swap(own, "head", 2)
        kept["slope"] = call(
            functools.partial(gate_slope_kernel, dims),
            grid,
            [model_spec, square, pack_spec((ext, inner)), pack_spec((ext, bc_part)),
             whole_spec((8, inner)), whole_spec((8, bc_part))],
            [chan_spec, chan_spec, pack_spec((count, bc_part))],
            [shape(packs, count, inner, bf16), shape(packs, count, inner, f32),
             shape(packs, count, bc_part, f32)],
            [Each((ext, inner), f32), Each((ext, bc_part), f32)],
            pre,
            normed, proj_z, raw_x, raw_bc, conv_own, conv_bc_own,
            us=7,
        )

    state_keep, state_recv = scan_states(
        lambda: kept["keep"], send, meta, packs, heads, size, 0,
        (keep_work, gate_slope_work, inner_work, cot_work),
    )
    normed, inv, raw_x, raw_bc, xbc, steps = kept["front"]
    inner_out, cot, gg = kept["inner"], kept["cot"], kept["gg"]
    gate, slope_x, slope_bc = kept["slope"]
    order.drop(inner_out)

    y, stats = call(
        functools.partial(gate_kernel, dims),
        (packs // half,),
        [
            xbc_spec, lane_spec, chan_spec, state_spec, state_spec, chan_spec, chan_spec, vec, vec,
        ],
        [chan_spec, pack_spec((2, count))],
        [shape(packs, count, inner, f32), shape(packs, 2, count, f32)],
        [],
        pre,
        xbc, steps, inner_out, state_keep, state_recv, gate, gg, gain_gate, skip,
        us=6.6, group=half,
    )
    stats = head_pieces(stats)

    gy, gated, ggate, gkeep, gsend, gate_small = call(
        functools.partial(grad_kernel, dims, total_inner),
        grid,
        [
            *[pack_spec((2, count))] * 4, xbc_spec, lane_spec, chan_spec, chan_spec, chan_spec, vec,
            vec,
        ],
        [chan_spec] * 3 + pay_specs + [whole_spec((8, inner))],
        [shape(packs, count, inner, f32)] + [shape(packs, count, inner, bf16)] * 2
        + [pay, pay, shape(8, inner, f32)],
        [],
        pre,
        *stats, xbc, steps, y, gate, gg, gain_gate, skip,
        us=8.3,
    )

    piece_shape = shape(packs, part, count, f32)
    send_spec = pack_spec((2, part, count))
    rows_half = features // 2
    half_specs = [whole_spec((rows_half, inner))] * 2
    half_shapes = [shape(rows_half, inner, f32), shape(rows_half, inner, bf16)]
    half_sums = pltpu.VMEM((2, rows_half, inner), f32)
    row8, row8_shape = whole_spec((8, features)), shape(8, features, f32)

    early_sum, late_sum = SeqSum(), SeqSum()

    def out_work(_):
        *kept["out"], keep, give = call(
            functools.partial(out_kernel, dims),
            (packs // half,),
            [chan_spec, model_spec, square],
            [piece_spec, piece_spec, send_spec] + half_specs,
            [piece_shape, piece_shape, shape(packs, 2, part, count, bf16)] + half_shapes,
            [Each((4, part, count), f32), half_sums],
            pre,
            gated, cot, w_out,
            us=6.8, group=half,
        )
        early_sum.put(keep, give)

    def z_work(_):
        keep, give, kept["gain"] = call(
            functools.partial(z_kernel, dims),
            (packs // half,),
            [model_spec, chan_spec, square],
            half_specs + [row8],
            half_shapes + [row8_shape],
            [half_sums],
            pre,
            normed, ggate, proj_z,
            us=5.3, group=half,
        )
        early_sum.put(keep, give)

    def diag_work(_):
        kept["diag"] = call(
            functools.partial(diag_kernel, dims),
            grid,
            [xbc_spec, lane_spec, chan_spec, chan_spec, state_spec, state_spec],
            [chan_spec, pack_spec((count, bc)), lane_spec],
            [
                shape(packs, count, inner, f32), shape(packs, count, bc, f32),
                shape(packs, count, LANES, f32),
            ],
            [],
            pre,
            xbc, steps, gy, y, state_keep, state_recv,
            us=12,
        )

    def early_work(_):
        early_sum.add(meta)
        own, far, send = kept["out"]
        own, far = call(
            out_gather_kernel, grid, [piece_spec, piece_spec, send_spec], [piece_spec, piece_spec],
            [piece_shape, shape(packs, part, count, bf16)], [], (), own, far, swap(send, "head", 1),
        )
        kept["out"] = own, swap(far, "head", 2)

    gstate_keep, gstate_recv = scan_states(
        gkeep, gsend, meta, packs, heads, size, 1, (out_work, z_work, diag_work, early_work),
        lambda: early_sum.got,
    )
    out_own, out_far = kept["out"]
    dx, dbc, sums = kept["diag"]

    edge_tile = (EDGE, inner)

    def pair_spec(shape_of):
        return pl.BlockSpec((half,) + shape_of, lambda p, *_: (p,) + (0,) * len(shape_of))

    pair_lane = pair_spec((count, LANES))
    share_own, share_near, grad_x, state_sums, edge_x = call(
        functools.partial(share_kernel, dims),
        (packs // half,),
        [xbc_spec, lane_spec, pack_spec((count, bc)), state_spec, state_spec, chan_spec, chan_spec,
         chan_spec, whole_spec((8, inner)), vec],
        [lane_spec, lane_spec, chan_spec, lane_spec, pack_spec(edge_tile)],
        [shape(packs, count, LANES, f32)] * 2
        + [shape(packs, count, inner, f32), shape(packs, count, LANES, f32),
           shape(packs, *edge_tile, bf16)],
        [Each((2 * EDGE, inner), f32)],
        pre,
        xbc, steps, dbc, gstate_keep, gstate_recv, gy, dx, slope_x, conv_own, skip,
        us=6.4, group=half,
    )
    share_near = swap(share_near, "head", 1)
    advance(early_sum, meta)
    two = shape(half, count, LANES, f32)
    bc_keep, bc_send = call(
        functools.partial(middle_kernel, (packs, bc_part)),
        (1,),
        [whole_spec((packs, count, LANES))] * 2,
        [whole_spec(two.shape)] * 2,
        [two, two],
        [],
        (meta,),
        share_own, share_near,
    )
    bc_recv = swap(bc_send, "head", 2)

    main_x, keep, give, grad_conv, gain_x = call(
        functools.partial(xback_kernel, dims),
        grid,
        [
            chan_spec, pack_spec((ext, inner)), model_spec, whole_spec((features, LANES)),
            pack_spec(edge_tile), whole_spec((8, inner)), square,
        ],
        [chan_spec, *half_specs, whole_spec((8, inner)), row8],
        [shape(packs, count, inner, bf16), *half_shapes, shape(8, inner, f32), row8_shape],
        [
            Each((count + EDGE, inner), f32), Each((ext, inner), f32), half_sums,
            pltpu.VMEM((LANES, inner), bf16),
        ],
        pre,
        grad_x, raw_x, normed, edge, edge_x, conv_own, proj_x,
        us=7, wait=(out_far,),
    )
    late_sum.put(keep, give)
    advance(early_sum, meta)

    gdt, gdt_rows, grad_small, gain_dt = call(
        functools.partial(step_kernel, dims),
        (packs // half,),
        [
            pair_lane, pair_lane, pair_lane, *[whole_spec((half,) + pay_shape)] * 4,
            whole_spec((8, LANES)), pair_spec((features, count)), whole_spec((features, LANES)),
        ],
        [pair_lane, row8, whole_spec((8, LANES)), row8],
        [shape(packs, count, LANES, bf16), row8_shape, shape(8, LANES, f32), row8_shape],
        [pltpu.VMEM((features, LANES), f32)],
        pre,
        steps, sums, state_sums, state_keep, state_recv, gstate_keep, gstate_recv, small, normed,
        w_dt,
        us=6,
    )
    advance(early_sum, meta)
    advance(late_sum, meta)
    give_rows = 2 * bc_part + 2 * SMALL
    gbc, edges, bc_sum, smalls = call(
        functools.partial(conv_bc_kernel, dims),
        grid,
        [
            half_spec((count, LANES), half), half_spec((count, LANES), half),
            pack_spec((count, bc_part)), pack_spec((ext, bc_part)), model_spec,
            whole_spec((features, LANES)), whole_spec((features, bc_part)),
            whole_spec((8, bc_part)), pack_spec(edge_tile), whole_spec((8, inner)), row8,
            whole_spec((8, LANES)), whole_spec((8, inner)), row8, row8, row8,
            whole_spec((features, 1)),
        ],
        [
            pack_spec((count, bc_part)), pack_spec((EDGE, inner + LANES)),
            whole_spec((give_rows, inner)), whole_spec((SMALL, inner)),
        ],
        [
            shape(packs, count, bc_part, bf16), shape(packs, EDGE, inner + LANES, bf16),
            shape(give_rows, inner, bf16), shape(SMALL, inner, f32),
        ],
        [
            Each((ext + EDGE, bc_part), f32), Each((ext, bc_part), f32),
            pltpu.VMEM((features, bc_part), f32), pltpu.VMEM((LANES, bc_part), bf16),
            pltpu.VMEM((8, bc_part), f32),
        ],
        pre,
        bc_keep, bc_recv, slope_bc, raw_bc, normed, edge, w_bc, conv_bc_own, edge_x, grad_conv,
        gdt_rows, grad_small, gate_small, kept["gain"], gain_x, gain_dt, gain_all,
        us=5,
    )
    edges = shift(edges, "seq", -1)
    bc_bits = [1 << k for k in range((lax.axis_size("seq") - 1).bit_length())]
    bc_got = swap(bc_sum, "seq", 1)
    advance(late_sum, meta)

    def bc_step(bit):
        nonlocal bc_sum, smalls, bc_got
        spec, small_spec = whole_spec(bc_sum.shape), whole_spec(smalls.shape)
        bc_sum, smalls = call(
            functools.partial(add_kernel, 1, False, [2 * bc_part], 1, True), (1,),
            [spec, spec, small_spec], [spec, small_spec],
            [shape(*bc_sum.shape, bf16), shape(*smalls.shape, f32)], [], (meta,),
            bc_sum, bc_got, smalls, us=0.01,
        )
        bc_got = swap(bc_sum, "seq", bit)

    bc_step(bc_bits[1])
    advance(early_sum, meta)

    tall = part + EDGE
    tall_send = pack_spec((2, tall, count))
    tall_spec = pack_spec((tall, count))
    row_spec, row_shape = pack_spec((1, count)), shape(packs, 1, count, f32)
    gn_own, gn_far, gn_send, dots = call(
        functools.partial(back_kernel, dims),
        (packs // half,),
        [
            chan_spec, pack_spec((EDGE, inner + LANES)), chan_spec, lane_spec,
            pack_spec((count, bc_part)), model_spec, square, square,
            whole_spec((features, bc_part)), whole_spec((features, LANES)),
        ],
        [piece_spec, piece_spec, tall_send, row_spec],
        [piece_shape, piece_shape, shape(packs, 2, tall, count, bf16), row_shape],
        [Each((4, part, count), f32)],
        pre,
        main_x, edges, ggate, gdt, gbc, normed, proj_z, proj_x, w_bc, w_dt,
        us=6, group=half,
    )
    near = swap(gn_send, "head", 1)
    order.drop(xbc, steps, normed)
    advance(late_sum, meta, 0.01, wait=(bc_got,))
    block_out = call(
        out_final_kernel, grid, [piece_spec] * 3, piece_spec, shape(packs, part, count, bf16), [],
        (), out_own, out_far, tokens, out=True, us=2,
    )
    block_out = jnp.swapaxes(block_out, 1, 2)

    gn_own, gn_far, dots = call(
        gather_kernel,
        grid,
        [piece_spec, piece_spec, tall_send, row_spec],
        [piece_spec, tall_spec, row_spec],
        [piece_shape, shape(packs, tall, count, bf16), row_shape],
        [],
        (),
        gn_own, gn_far, near, dots,
        us=0.01,
    )
    gn_far = swap(gn_far, "head", 2)
    order.hold(gn_own)
    while early_sum.bit != 0:
        advance(early_sum, meta)
    for bit in bc_bits[2:]:
        bc_step(bit)
    small_spec, give_spec = whole_spec(smalls.shape), whole_spec(bc_sum.shape)

    def head_step(x, bit):
        return call(
            plus_kernel, (1,), [small_spec, small_spec], small_spec, shape(*x.shape, f32), [], (),
            x, swap(x, "head", bit), us=0.01,
        )

    advance(late_sum, meta, 0.01)
    grads_out, grads_z = early_sum.result(meta, ("flip", "rows"), 2)
    while late_sum.bit != 0:
        advance(late_sum, meta, 0.01)
    grad_bc, smalls = call(
        functools.partial(whole_kernel, bc_part), (1,), [give_spec, give_spec, small_spec],
        [whole_spec((bc_part, features)), small_spec],
        [shape(bc_part, features, f32), shape(*smalls.shape, f32)], [], (), bc_sum, bc_got, smalls,
        us=0.01, out=1,
    )
    gains = head_step(smalls, 1)
    in_grad = call(
        functools.partial(final_kernel, (packs, count, features)),
        grid,
        [piece_spec, tall_spec, row_spec, piece_spec, row_spec, whole_spec((part, 1)), piece_spec],
        piece_spec,
        piece_shape,
        [],
        (),
        gn_own, gn_far, dots, tokens, inv, norm_gain_own, cotangent,
        us=2, out=True,
    )
    in_grad = jnp.swapaxes(in_grad, 1, 2)
    order.drop(gn_own)
    gains = head_step(gains, 2)
    vectors = [(inner,), (bc_part,), (heads,), (heads,), (heads,), (inner,), (part,)]
    tables = [(heads, features), (width, inner), (width, bc_part)]
    outs = call(
        functools.partial(unpack_kernel, (heads, features, bc_part, width)), (1,),
        [small_spec, small_spec], [whole_spec(x) for x in tables + vectors],
        [shape(*x, f32) for x in tables + vectors], [], (meta,), smalls, gains, out=True, us=0.01,
    )
    grad_dt, grad_conv, grad_conv_bc = outs[:3]
    bias_x_grad, bias_bc_grad, dt_bias_grad, a_log_grad, skip_grad, gate_grad, grad_gain = outs[3:]
    grads_x, = late_sum.result(meta, ("rows",))
    return (
        block_out,
        in_grad,
        grad_gain,
        grads_z,
        grads_x,
        grad_bc.T,
        grad_dt.T,
        grad_conv,
        grad_conv_bc,
        bias_x_grad,
        bias_bc_grad,
        dt_bias_grad,
        a_log_grad,
        skip_grad,
        gate_grad,
        grads_out,
    )


def solution(mesh):
    token, column, vector = P(None, "seq", "head"), P(None, "head"), P("head")
    row = P("head", None)
    return jax.shard_map(
        shards,
        mesh=mesh,
        in_specs=(
            token, token, P(), vector, column, column, column, column, column, column, vector,
            vector, vector, vector, vector, vector, row,
        ),
        out_specs=(
            token, token, vector, column, column, column, column, column, column, vector, vector,
            vector, vector, vector, vector, row,
        ),
        check_vma=False,
    )
```

```python
import functools

import jax
import jax.numpy as jnp
from jax import lax
from jax.experimental import pallas as pl
from jax.experimental.pallas import tpu as pltpu
from jax.sharding import PartitionSpec as P

EPSILON = 1e-05
bf16 = jnp.bfloat16
f32 = jnp.float32
LANES = 128
EDGE = 16
MIB = 1024 * 1024
STEPS = 32000.0
UNIT = 16384.0
LN2 = 0.6931471805599453
GROUP = 16
SMALL = 32


def permuted(x, axis, route):
    y = lax.ppermute(x, axis, route)
    order.near.append(y)
    return y


def swap(x, axis, bit):
    return permuted(x, axis, [(i, i ^ bit) for i in range(lax.axis_size(axis))])


def shift(x, axis, distance):
    n = lax.axis_size(axis)
    return permuted(x, axis, [(i, i + distance) for i in range(n) if 0 <= i + distance < n])


def head_pieces(x):
    far = swap(x, "head", 2)
    near = swap(x, "head", 1)
    return x, near, far, swap(far, "head", 1)


def nn(a, b):
    return lax.dot_general(a, b, (((1,), (0,)), ((), ())), preferred_element_type=f32)


def nt(a, b):
    return lax.dot_general(a, b, (((1,), (1,)), ((), ())), preferred_element_type=f32)


def tn(a, b):
    return lax.dot_general(a, b, (((0,), (0,)), ((), ())), preferred_element_type=f32)


def split2(v):
    hi = v.astype(bf16)
    return hi, (v - hi.astype(f32)).astype(bf16)


def split3(v):
    hi = v.astype(bf16)
    rest = v - hi.astype(f32)
    mid = rest.astype(bf16)
    return hi, mid, (rest - mid.astype(f32)).astype(bf16)


def spread_matrix(heads, size):
    row = lax.broadcasted_iota(jnp.int32, (LANES, heads * size), 0)
    col = lax.broadcasted_iota(jnp.int32, (LANES, heads * size), 1)
    first = (col >= row * size) & (col < (row + 1) * size)
    again = (col >= (row - GROUP) * size) & (col < (row - GROUP + 1) * size)
    return jnp.where(first | again, 1.0, 0.0).astype(bf16)


def spread(v, matrix, heads):
    hi, lo = split2(head_lanes(v, heads))
    return nn((hi.astype(f32) + to_group(lo.astype(f32), 1)).astype(bf16), matrix)


def head_lanes(v, heads):
    return jnp.where(lax.broadcasted_iota(jnp.int32, v.shape, 1) < heads, v, 0.0)


def to_group(v, k):
    return pltpu.roll(v, k * GROUP, 1)


def from_group(v, k, heads):
    return head_lanes(pltpu.roll(v, LANES - k * GROUP, 1) if k else v, heads)


def collapse(v, matrix, heads):
    return head_lanes(nt(jnp.concatenate(split2(v), axis=1), jnp.concatenate([matrix] * 2, axis=1)), heads)


def triangle(count, lower):
    row = lax.broadcasted_iota(jnp.int32, (count, count), 0)
    col = lax.broadcasted_iota(jnp.int32, (count, count), 1)
    keep = (row >= col) if lower else (row <= col)
    return jnp.where(keep, 1.0, 0.0).astype(bf16)


def exact_sums(matrix, v, heads):
    hi, mid, lo = [piece.astype(f32) for piece in split3(v)]
    sums = nn(matrix, (hi + to_group(mid, 1) + to_group(lo, 2)).astype(bf16))
    return from_group(sums, 0, heads) + from_group(sums, 1, heads) + from_group(sums, 2, heads)


def step_sizes(v, heads):
    soft = jnp.maximum(v, 0.0) + jnp.log1p(jnp.exp(-jnp.abs(v)))
    return head_lanes(soft, heads)


def steps_of(block, heads):
    return step_sizes(block, heads), from_group(block, 1, heads)


def segments(positions, lens_ref, pack, count):
    total = jnp.zeros(positions.shape, jnp.int32)
    end = jnp.int32(0)
    for k in range(count):
        end = end + lens_ref[pack, k]
        total = total + jnp.where(positions >= end, 1, 0)
    return total


def column_segments(meta_ref, lens_ref, pack, count, nseq, before):
    rows = lax.broadcasted_iota(jnp.int32, (count + before, 1), 0)
    return segments(rows + (meta_ref[0] * count - before), lens_ref, pack, nseq)


def row_segments(meta_ref, lens_ref, pack, count, nseq):
    cols = lax.broadcasted_iota(jnp.int32, (1, count), 1)
    return segments(cols + meta_ref[0] * count, lens_ref, pack, nseq)


def carry_column(meta_ref, seg_ext, before):
    same = seg_ext[before:] == seg_ext[before - 1 : before]
    return jnp.where(same & (meta_ref[0] > 0), 1.0, 0.0)


def to_int16(v):
    return jnp.floor(v + 0.5).astype(jnp.int32).astype(jnp.int16)


def encode_state(out, p, state, decay, heads, size):
    lane = lax.broadcasted_iota(jnp.int32, (1, LANES), 1)
    powers = jnp.zeros((1, LANES), f32)
    for h in range(heads):
        part = state[h * size : (h + 1) * size]
        top = jnp.max(jnp.max(jnp.abs(part), axis=0, keepdims=True), axis=1, keepdims=True)
        power = jnp.ceil(jnp.log(jnp.maximum(top, 1e-30)) / LN2)
        powers = powers + jnp.where(lane == h, power, 0.0)
        codes = jnp.clip(part * (jnp.exp(-power * LN2) * STEPS), -32767.0, 32767.0)
        out[p, h * size : (h + 1) * size, :] = to_int16(codes)
    row = lax.broadcasted_iota(jnp.int32, (EDGE, LANES), 0)
    coarse = jnp.floor(decay * UNIT)
    fine = (decay * UNIT - coarse) * UNIT
    tail = jnp.where(row == 0, powers, jnp.where(row == 1, coarse, jnp.where(row == 2, fine, 0.0)))
    out[p, heads * size :, :] = to_int16(tail)


def decode_state(block, heads, size):
    values = block.astype(jnp.int32).astype(f32)
    tail = values[heads * size :]
    scale = jnp.exp(tail[0:1] * LN2) / STEPS
    decay = (tail[1:2] + tail[2:3] / UNIT) / UNIT
    return scaled_state(values[: heads * size], scale, heads, size), decay


def sigmoid(v):
    return 1.0 / (1.0 + jnp.exp(-v))


def scaled_state(state, decay, heads, size):
    return jnp.concatenate(
        [state[h * size : (h + 1) * size] * decay[:, h : h + 1] for h in range(heads)], axis=0
    )


def tail_kernel(meta, tokens, out):
    lane = lax.broadcasted_iota(jnp.int32, out.shape, 1)
    total = jnp.zeros(out.shape, f32)
    for p in range(tokens.shape[0]):
        moved = pltpu.roll(tokens[p].astype(f32), (p + 1) * EDGE, 1)
        total = jnp.where((lane >= p * EDGE) & (lane < (p + 1) * EDGE), moved, total)
    out[...] = total.astype(bf16)


def wide_row(ref, lanes=LANES):
    row = ref[...].astype(f32)[None, :]
    blank = lanes - row.shape[1]
    return jnp.concatenate([row, jnp.zeros((1, blank), f32)], axis=1) if blank else row


def prepare_kernel(dims, *refs):
    packs, count, features, inner, bc, heads, size, width, nseq = dims
    (
        wbc, conv_bc, bias_bc, norm_gain, wdt, conv_x, bias_x, dt_bias, a_log, d_skip, gate_gain, wout,
        wout_o, shared_o, wbc_o, wdt_o, wdt_rows_o, conv_x_o, conv_bc_o, small_o, skip_o, gate_gain_o, gain_o,
    ) = refs
    bc_part, part = bc // 4, features // 4
    wout_o[...] = jnp.transpose(wout[...])
    taps = conv_bc[...].astype(f32)
    bias = wide_row(bias_bc, bc_part)
    gain = wide_row(norm_gain, part)
    pieces = [gain[:, c * bc_part : (c + 1) * bc_part] for c in range(part // bc_part)]
    rows = jnp.concatenate([taps, bias] + pieces, axis=0)
    rows = jnp.concatenate([rows, jnp.zeros((LANES - rows.shape[0], bc_part), f32)], axis=0)
    rows = jnp.concatenate([rows, jnp.zeros((LANES, LANES - bc_part), f32)], axis=1)
    extra = jnp.transpose(rows)[:bc_part].astype(bf16)
    shared_o[:, :features] = wbc[...]
    shared_o[:, features:] = extra
    wbc_o[...] = jnp.transpose(wbc[...].astype(f32)).astype(bf16)
    dt_rows = jnp.concatenate(
        [wdt[...].astype(f32), jnp.zeros((LANES - heads, features), f32)], axis=0
    )
    wdt_rows_o[...] = dt_rows.astype(bf16)
    wdt_o[...] = jnp.transpose(dt_rows).astype(bf16)
    blank = jnp.zeros((7 - width, inner), f32)
    conv_x_o[...] = jnp.concatenate(
        [conv_x[...].astype(f32), wide_row(bias_x, inner), blank], axis=0
    )
    conv_bc_o[...] = jnp.concatenate([taps, bias, blank[:, :bc_part]], axis=0)
    small_o[...] = jnp.concatenate(
        [wide_row(dt_bias), wide_row(a_log), jnp.zeros((6, LANES), f32)], axis=0
    )
    skips = jnp.concatenate([wide_row(d_skip), jnp.zeros((7, LANES), f32)], axis=0)
    matrix = spread_matrix(heads, size)
    skip_o[...] = sum(nn(piece, matrix) for piece in split3(skips))[0:1]
    gate_gain_o[...] = wide_row(gate_gain, inner)
    column = jnp.concatenate([gain, jnp.zeros((LANES - 1, part), f32)], axis=0)
    column = jnp.concatenate([column, jnp.zeros((LANES, 2 * LANES - part), f32)], axis=1)
    gain_o[...] = jnp.transpose(column)[:part, 0:1]


def normalise(values, gain, features):
    mean = jnp.sum(values * values, axis=0, keepdims=True) / features
    inv = lax.rsqrt(mean + EPSILON)
    return inv, ((values * inv) * gain).astype(bf16)


def raw_rows(normed, wx, wbc):
    return jnp.concatenate([nn(normed, wx), nt(normed, wbc)], axis=1).astype(bf16)


def border_kernel(dims, meta, *refs):
    packs, count, features, inner, bc, heads, size, width, nseq = dims
    edges, shared = refs[0:4], refs[4:8]
    wx, conv_x, wbc_o, conv_o, gain_o, edge_o, raws_o, stage, weights = refs[8:]
    head = meta[1]
    part, bc_part = features // 4, bc // 4
    for k in range(4):
        weights[head ^ k] = shared[k][...]
        stage[head ^ k] = edges[k][...]
    whole = weights[...].reshape(bc, weights.shape[2])
    wbc_o[...] = whole[:, :features]
    extra = whole[:, features:].astype(f32)
    conv_o[:, :inner] = conv_x[...]
    conv_o[:, inner:] = jnp.transpose(extra)[0:8]
    for h in range(4):
        for c in range(part // bc_part):
            gain_o[h * part + c * bc_part : h * part + (c + 1) * bc_part, :] = extra[
                h * bc_part : (h + 1) * bc_part, width + 1 + c : width + 2 + c
            ]
    _, normed = normalise(stage[...].reshape(features, stage.shape[2]).astype(f32), gain_o[...], features)
    edge_o[...] = normed
    raws_o[...] = raw_rows(jnp.transpose(normed), wx[...], wbc_o[...]).astype(f32)


def front_kernel(dims, keep, meta, lens, *refs):
    packs, count, features, inner, bc, heads, size, width, nseq = dims
    tokens, refs = refs[0:4], refs[4:]
    wx, wbc, wdt, conv, small, gain, edge_raws, *refs = refs
    normed_o, inv_o, rawx_o, rawbc_o, xbc_o, steps_o, state_o, stage, raws = refs[-9:]
    side = meta[0] & 1 if keep else 1 - (meta[0] & 1)
    pack = order.pack + (packs // 2) * side
    head = meta[1]
    for k in range(4):
        stage[head ^ k] = tokens[k][0]
    inv, normed_t = normalise(stage[...].reshape(features, count).astype(f32), gain[...], features)
    inv_o[0] = inv
    normed_o[0] = normed_t
    normed = jnp.transpose(normed_t)
    raws[EDGE:, :] = raw_rows(normed, wx[...], wbc[...]).astype(f32)
    raws[0:EDGE, :] = edge_raws[pl.ds(pl.multiple_of(pack * EDGE, EDGE), EDGE), :]

    def own_bc(values):
        bc_part = bc // 4
        parts = [values[:, inner + h * bc_part : inner + (h + 1) * bc_part] for h in range(4)]
        low = jnp.where((head & 1) == 0, parts[0], parts[1])
        high = jnp.where((head & 1) == 0, parts[2], parts[3])
        return jnp.where((head >> 1) == 0, low, high)

    rawx_o[0] = raws[:, :inner].astype(bf16)
    rawbc_o[0] = own_bc(raws[...]).astype(bf16)
    seg = column_segments(meta, lens, pack, count, nseq, EDGE)
    seg_main = seg[EDGE:]
    pre = convolved(raws, conv, seg, count, width)
    xbc = (pre * sigmoid(pre)).astype(bf16)
    xbc_o[0] = xbc
    v = head_lanes(nt(normed, wdt[...]).astype(bf16).astype(f32) + small[0:1, :], heads)
    dt = step_sizes(v, heads)
    rate = -dt * jnp.exp(small[1:2, :])
    cum = exact_sums(triangle(count, True), rate, heads)
    steps_o[0] = v + to_group(cum, 1)
    cum_end = cum[count - 1 : count]
    weight = jnp.where(seg_main == seg[count + EDGE - 1 :], jnp.exp(cum_end - cum), 0.0) * dt
    matrix = spread_matrix(heads, size)
    scaled = (xbc[:, :inner].astype(f32) * spread(weight, matrix, heads)).astype(bf16)
    state = jnp.transpose(nn(jnp.transpose(xbc[:, inner : inner + bc // 2]), scaled))
    carry = carry_column(meta, seg, EDGE)
    encode_state(state_o, 0, state, carry[count - 1 :] * jnp.exp(cum_end), heads, size)


def convolved(raws, conv, seg, count, width):
    pre = jnp.broadcast_to(conv[width : width + 1, :], (count, raws.shape[1]))
    for k in range(width):
        low = EDGE - (width - 1) + k
        mask = jnp.where(seg[low : low + count] == seg[EDGE:], 1.0, 0.0)
        pre = pre + conv[k : k + 1, :] * raws[low : low + count, :] * mask
    return pre


def gate_slope_kernel(dims, meta, lens, *refs):
    packs, count, features, inner, bc, heads, size, width, nseq = dims
    normed, wz, raw_x, raw_bc, conv_x, conv_bc, gate_o, slope_x_o, slope_bc_o, raws, raws_bc = refs
    pack = order.pack
    gate_o[0] = tn(normed[0], wz[...]).astype(bf16)
    seg = column_segments(meta, lens, pack, count, nseq, EDGE)
    for raw, wide, conv, out in ((raw_x, raws, conv_x, slope_x_o), (raw_bc, raws_bc, conv_bc, slope_bc_o)):
        wide[...] = raw[0].astype(f32)
        pre = convolved(wide, conv, seg, count, width)
        sig = sigmoid(pre)
        out[0] = sig * (1.0 + pre * (1.0 - sig))


def store_state(meta, packs, pack, keep_o, send_o, state, decay, heads, size):
    mine = (pack // (packs // 2)) == (meta[0] & 1)

    @pl.when(mine)
    def _():
        encode_state(keep_o, 0, state, decay, heads, size)

    @pl.when(jnp.logical_not(mine))
    def _():
        encode_state(send_o, 0, state, decay, heads, size)


def load_state(meta, packs, pack, keep, recv, heads, size):
    mine = (pack // (packs // 2)) == (meta[0] & 1)
    block = jnp.where(mine, keep[0].astype(jnp.int32), recv[0].astype(jnp.int32))
    return decode_state(block, heads, size)[0]


def decay_parts(cum_col, cum_row, masked):
    return masked * jnp.exp(jnp.minimum(cum_col - cum_row, 0.0))


def block_mask(meta, lens, pack, count, nseq):
    col = column_segments(meta, lens, pack, count, nseq, 0)
    row = row_segments(meta, lens, pack, count, nseq)
    tri = lax.broadcasted_iota(jnp.int32, (count, count), 0) >= lax.broadcasted_iota(
        jnp.int32, (count, count), 1
    )
    return tri & (col == row)


def inner_kernel(dims, meta, lens, *refs):
    packs, count, features, inner, bc, heads, size, width, nseq = dims
    xbc, steps, inner_o = refs
    pack = order.pack
    half = bc // 2
    b_vals, c_vals = xbc[0, :, inner : inner + half], xbc[0, :, inner + half :]
    scores = jnp.where(block_mask(meta, lens, pack, count, nseq), nt(c_vals, b_vals), 0.0)
    dt, cum_col = steps_of(steps[0], heads)
    cum_row = jnp.transpose(cum_col)
    dt_row = jnp.transpose(dt)
    lane = lax.broadcasted_iota(jnp.int32, (count, 2 * size), 1)
    for pair in range(heads // 2):
        cols = slice(2 * pair * size, (2 * pair + 2) * size)
        x_pair = xbc[0, :, cols]
        parts = []
        for h in (2 * pair, 2 * pair + 1):
            weights = decay_parts(cum_col[:, h : h + 1], cum_row[h : h + 1], scores)
            parts.append(nn((weights * dt_row[h : h + 1]).astype(bf16), x_pair))
        inner_o[0, :, cols] = jnp.where(lane < size, parts[0], parts[1])


def cot_kernel(dims, meta, lens, *refs):
    packs, count, features, inner, bc, heads, size, width, nseq = dims
    pieces, (wout, cot_o, gg_o, stage) = refs[:4], refs[4:]
    for k in range(4):
        stage[meta[1] ^ k] = pieces[k][0]
    cotangent = stage[...].reshape(features, count)
    cot_o[0] = cotangent
    gg_o[0] = jnp.transpose(nn(wout[...], cotangent))


def compose(lower, upper, heads, size):
    return scaled_state(lower[0], upper[1], heads, size) + upper[0], lower[1] * upper[1]


def choose(flag, a, b):
    return jnp.where(flag, a[0], b[0]), jnp.where(flag, a[1], b[1])


def pair_kernel(dims, rev, meta, own, other, out):
    packs, heads, size = dims
    upper_is_own = ((meta[0] & 1) ^ rev) == 1
    for p in range(packs // 2):
        a, b = decode_state(own[p], heads, size), decode_state(other[p], heads, size)
        both = compose(choose(upper_is_own, b, a), choose(upper_is_own, a, b), heads, size)
        encode_state(out, p, *both, heads, size)


def entering_from(before, b, p, heads, size):
    if before is None:
        return (jnp.zeros_like(b[0]), jnp.ones_like(b[1])), b
    entering = decode_state(before[p], heads, size)
    return entering, compose(b, entering, heads, size)


def cube_kernel(dims, rev, bit, first, meta, *refs):
    packs, heads, size = dims
    total, other = refs[0], refs[1]
    before, next_o, before_o = (None, refs[2], refs[3]) if first else refs[2:5]
    upper_is_own = (((meta[0] >> bit) & 1) ^ rev) == 1
    for p in range(packs // 2):
        a, b = decode_state(total[p], heads, size), decode_state(other[p], heads, size)
        both = compose(choose(upper_is_own, b, a), choose(upper_is_own, a, b), heads, size)
        encode_state(next_o, p, *both, heads, size)
        entering, longer = entering_from(before, b, p, heads, size)
        encode_state(before_o, p, *choose(upper_is_own, longer, entering), heads, size)


def last_kernel(dims, rev, bit, first, meta, *refs):
    packs, heads, size = dims
    own, pair, other = refs[0:3]
    before, keep_o, send_o = (None, refs[3], refs[4]) if first else refs[3:6]
    add = (((meta[0] >> bit) & 1) ^ rev) == 1
    upper_is_own = ((meta[0] & 1) ^ rev) == 1
    for p in range(packs // 2):
        entering, longer = entering_from(
            before, decode_state(other[p], heads, size), p, heads, size
        )
        low = choose(add, longer, entering)
        lower = decode_state(jnp.where(upper_is_own, pair[p].astype(jnp.int32), own[p].astype(jnp.int32)), heads, size)
        high = compose(low, lower, heads, size)
        encode_state(keep_o, p, *choose(upper_is_own, high, low), heads, size)
        encode_state(send_o, p, *choose(upper_is_own, low, high), heads, size)


def gate_kernel(dims, meta, lens, *refs):
    packs, count, features, inner, bc, heads, size, width, nseq = dims
    xbc, steps, inner_in, keep, recv, gate, gg, gain, skip, y_o, stats_o = refs
    pack = order.pack
    state = jnp.concatenate(
        split2(load_state(meta, packs, pack, keep, recv, heads, size)), axis=1
    )
    carry = carry_column(meta, column_segments(meta, lens, pack, count, nseq, EDGE), EDGE)
    matrix = spread_matrix(heads, size)
    entering = spread(carry * jnp.exp(from_group(steps[0], 1, heads)), matrix, heads)
    c_vals = xbc[0, :, inner + bc // 2 :]
    y = inner_in[0] + entering * nt(jnp.concatenate([c_vals, c_vals], axis=1), state)
    y_o[0] = y
    gate_f = gate[0].astype(f32)
    ssd = y + xbc[0, :, :inner].astype(f32) * skip[...]
    mixed = ssd * (gate_f * sigmoid(gate_f))
    squares = jnp.sum(mixed * mixed, axis=1, keepdims=True)
    dots = jnp.sum(gain[...] * gg[0] * mixed, axis=1, keepdims=True)
    lane = lax.broadcasted_iota(jnp.int32, (count, LANES), 1)
    both = jnp.where(lane == 0, squares, 0.0) + jnp.where(lane == 1, dots, 0.0)
    stats_o[0] = jnp.transpose(both)[0:2]


def grad_kernel(dims, total_inner, meta, lens, *refs):
    packs, count, features, inner, bc, heads, size, width, nseq = dims
    (
        stats, near, far, diagonal, xbc, steps, y, gate, gg, gain, skip,
        gy_o, gated_o, ggate_o, keep_o, send_o, small_o,
    ) = refs
    pack = order.pack

    @order.first
    def _():
        small_o[...] = jnp.zeros_like(small_o)

    sums = (stats[0] + near[0]) + (far[0] + diagonal[0])
    row = lax.broadcasted_iota(jnp.int32, (LANES, count), 0)
    wide = jnp.where(row == 0, sums[0:1], 0.0) + jnp.where(row == 1, sums[1:2], 0.0)
    cols = jnp.transpose(wide)
    inv = lax.rsqrt(cols[:, 0:1] / total_inner + EPSILON)
    dot = cols[:, 1:2] / total_inner
    x_f, gg_f, gate_f = xbc[0, :, :inner].astype(f32), gg[0], gate[0].astype(f32)
    ssd = y[0] + x_f * skip[...]
    sig = sigmoid(gate_f)
    act = gate_f * sig
    mixed = ssd * act
    scaled = mixed * inv
    gated_o[0] = (scaled * gain[...]).astype(bf16)
    grad_mixed = inv * gain[...] * gg_f - mixed * (inv * inv * inv * dot)
    gy_f = grad_mixed * act
    gy_o[0] = gy_f
    ggate_o[0] = (grad_mixed * ssd * sig * (1.0 + gate_f * (1.0 - sig))).astype(bf16)
    carry = carry_column(meta, column_segments(meta, lens, pack, count, nseq, EDGE), EDGE)
    cum = from_group(steps[0], 1, heads)
    entering = carry * jnp.exp(cum)
    ey_hi, ey_lo = split2(gy_f * spread(entering, spread_matrix(heads, size), heads))
    c_rows = jnp.transpose(xbc[0, :, inner + bc // 2 :])
    state_grad = jnp.transpose(nn(c_rows, ey_hi) + nn(c_rows, ey_lo))
    small_o[0:1, :] += jnp.sum(gg_f * scaled, axis=0, keepdims=True)
    small_o[1:2, :] += jnp.sum(gy_f * x_f, axis=0, keepdims=True)
    return lambda: store_state(
        meta, packs, pack, keep_o, send_o, state_grad, entering[count - 1 :], heads, size
    )


def diag_kernel(dims, meta, lens, *refs):
    packs, count, features, inner, bc, heads, size, width, nseq = dims
    xbc, steps, gy, y, keep, recv, dx_o, dbc_o, sums_o = refs
    pack = order.pack
    half = bc // 2
    b_vals, c_vals = xbc[0, :, inner : inner + half], xbc[0, :, inner + half :]
    col = column_segments(meta, lens, pack, count, nseq, 0)
    row = row_segments(meta, lens, pack, count, nseq)
    mask = (col == row) & (
        lax.broadcasted_iota(jnp.int32, (count, count), 0)
        <= lax.broadcasted_iota(jnp.int32, (count, count), 1)
    )
    scores = jnp.where(mask, nt(b_vals, c_vals), 0.0)
    dt, cum_col = steps_of(steps[0], heads)
    cum_row = jnp.transpose(cum_col)
    lane = lax.broadcasted_iota(jnp.int32, (count, 2 * size), 1)
    grad_scores = jnp.zeros((count, count), f32)
    zero = jnp.zeros((), bf16)
    for pair in range(heads // 2):
        cols = slice(2 * pair * size, (2 * pair + 2) * size)
        x_pair = xbc[0, :, cols]
        x_twice = jnp.concatenate([x_pair, x_pair], axis=1)
        gy_hi, gy_lo = split2(gy[0, :, cols])
        gy_wide = jnp.concatenate([gy_hi, gy_lo], axis=1)
        parts = []
        for h in (2 * pair, 2 * pair + 1):
            own = (lane < size) if h % 2 == 0 else (lane >= size)
            part = jnp.exp(jnp.minimum(cum_row[h : h + 1] - cum_col[:, h : h + 1], 0.0)) * dt[:, h : h + 1]
            parts.append(nn((scores * part).astype(bf16), gy_wide))
            both = jnp.concatenate([jnp.where(own, gy_hi, zero), jnp.where(own, gy_lo, zero)], axis=1)
            grad_scores = grad_scores + nt(x_twice, both) * part
        two = [part[:, : 2 * size] + part[:, 2 * size :] for part in parts]
        dx_o[0, :, cols] = jnp.where(lane < size, two[0], two[1])
    hi, lo = split2(jnp.where(mask, grad_scores, 0.0))
    state_hi, state_lo = split2(load_state(meta, packs, pack, keep, recv, heads, size))
    carry = carry_column(meta, column_segments(meta, lens, pack, count, nseq, EDGE), EDGE)
    matrix = spread_matrix(heads, size)
    ey_hi, ey_lo = split2(gy[0] * spread(carry * jnp.exp(cum_col), matrix, heads))
    dbc_o[0, :, :half] = nn(
        jnp.concatenate([hi, lo], axis=1), jnp.concatenate([c_vals, c_vals], axis=0)
    )
    b_rows = jnp.transpose(b_vals)
    dbc_o[0, :, half:] = (
        jnp.transpose(nn(b_rows, hi) + nn(b_rows, lo))
        + nn(ey_hi, state_hi) + nn(ey_hi, state_lo) + nn(ey_lo, state_hi)
    )
    row_sum = collapse(gy[0] * y[0], matrix, heads)
    col_sum = collapse(xbc[0, :, :inner].astype(f32) * dx_o[0], matrix, heads)
    sums_o[0] = row_sum + to_group(col_sum, 1)


def scatter_pieces(head, stage, own_o, far_o, send_o):
    own_o[0] = stage[head]
    send_o[0, 0] = stage[head ^ 1].astype(bf16)
    far_o[0] = stage[head ^ 2]
    send_o[0, 1] = stage[head ^ 3].astype(bf16)


def accumulate(meta, pack, packs, sums, term, keep_o, send_o):
    sums[...] += term.reshape(sums.shape)

    def finish():
        @last_pack(pack, packs)
        def _():
            side = meta[0] & 1
            keep_o[...] = sums[side]
            send_o[...] = sums[1 - side].astype(bf16)

    return finish


def last_pack(pack, packs):
    return lambda work: pl.when(pack == packs - 1)(work)


def cleared(*refs):
    @order.first
    def _():
        for ref in refs:
            ref[...] = jnp.zeros_like(ref)


def out_kernel(dims, meta, lens, *refs):
    packs, count, features, inner, bc, heads, size, width, nseq = dims
    gated, cot, wout, own_o, far_o, send_o, keep_o, give_o, stage, sums = refs
    pack = order.pack
    cleared(sums)
    stage[...] = nt(wout[...], gated[0]).reshape(stage.shape)
    scatter_pieces(meta[1], stage, own_o, far_o, send_o)
    return accumulate(meta, pack, packs, sums, nn(cot[0], gated[0]), keep_o, give_o)


def gain_row(weights, grads):
    part = jnp.sum(weights.astype(f32) * grads, axis=1, keepdims=True)
    return jnp.transpose(jnp.broadcast_to(part, (part.shape[0], LANES)))[0:8]


def z_kernel(dims, meta, lens, *refs):
    normed, ggate, wz, keep_o, give_o, gain_o, sums = refs
    pack = order.pack
    cleared(sums)
    store = accumulate(meta, pack, dims[0], sums, nn(normed[0], ggate[0]), keep_o, give_o)

    def finish():
        store()

        @last_pack(pack, dims[0])
        def _():
            gain_o[...] = gain_row(wz[...], sums[...].reshape(wz.shape))

    return finish


def end_weights(seg, seg_main, cum_col, dt_col, count):
    cum_end = cum_col[count - 1 :]
    end = seg[count + EDGE - 1 :]
    return jnp.where(seg_main == end, jnp.exp(cum_end - cum_col), 0.0) * dt_col


def share_kernel(dims, meta, lens, *refs):
    packs, count, features, inner, bc, heads, size, width, nseq = dims
    (
        xbc, steps, dbc, gkeep, grecv, gy, dx, slope, conv, skip,
        own_o, near_o, grad_o, state_sum_o, edge_o,
        gpad,
    ) = refs
    pack = order.pack
    half, quarter = bc // 2, bc // 4
    g_hi, g_lo = split2(load_state(meta, packs, pack, gkeep, grecv, heads, size))
    seg = column_segments(meta, lens, pack, count, nseq, EDGE)
    dt, cum = steps_of(steps[0], heads)
    matrix = spread_matrix(heads, size)
    wide = spread(end_weights(seg, seg[EDGE:], cum, dt, count), matrix, heads)
    x_f = xbc[0, :, :inner].astype(f32)
    hi, lo = split2(wide * x_f)
    grad_b = dbc[0, :, :half] + nn(hi, g_hi) + nn(lo, g_hi) + nn(hi, g_lo)
    grad_c = dbc[0, :, half:]
    even = jnp.concatenate([grad_b[:, :quarter], grad_c[:, :quarter]], axis=1)
    odd = jnp.concatenate([grad_b[:, quarter:], grad_c[:, quarter:]], axis=1)
    first = (meta[1] & 1) == 0
    own_o[0] = jnp.where(first, even, odd)
    near_o[0] = jnp.where(first, odd, even)
    b_vals = xbc[0, :, inner : inner + half]
    u_wide = wide * nt(
        jnp.concatenate([b_vals, b_vals], axis=1), jnp.concatenate([g_hi, g_lo], axis=1)
    )
    state_sum_o[0] = collapse(x_f * u_wide, matrix, heads)
    grad_x = (dx[0] + u_wide + gy[0] * skip[...]) * slope[0]
    grad_o[0] = grad_x
    gpad[:EDGE, :] = jnp.zeros((EDGE, inner), f32)
    gpad[EDGE:, :] = grad_x[:EDGE]
    edge_o[0] = conv_rows(gpad, conv, seg, EDGE, width).astype(bf16)


def middle_kernel(dims, meta, *refs):
    packs, quarter = dims
    own, near, keep_o, send_o = refs
    half = packs // 2
    first = (meta[1] >> 1) == 0
    for p in range(half):
        a, b = own[p] + near[p], own[p + half] + near[p + half]
        low = jnp.concatenate([a[:, :quarter], b[:, :quarter]], axis=1)
        high = jnp.concatenate([a[:, quarter:], b[:, quarter:]], axis=1)
        keep_o[p] = jnp.where(first, low, high)
        send_o[p] = jnp.where(first, high, low)


def conv_taps(grads, raws, gconv_o, seg, count, width):
    seg_main = seg[EDGE : EDGE + count]
    for k in range(width):
        low = EDGE - (width - 1) + k
        mask = jnp.where(seg[low : low + count] == seg_main, 1.0, 0.0)
        gconv_o[k : k + 1, :] += jnp.sum(
            grads * (raws[low : low + count, :] * mask), axis=0, keepdims=True
        )
    gconv_o[width : width + 1, :] += jnp.sum(grads, axis=0, keepdims=True)


def conv_rows(gpad, conv, seg, rows, width):
    total = jnp.zeros((rows, gpad.shape[1]), f32)
    for lag in range(width):
        mask = jnp.where(seg[lag : lag + rows] == seg[:rows], 1.0, 0.0)
        k = width - 1 - lag
        total = total + conv[k : k + 1, :] * (gpad[lag : lag + rows, :] * mask)
    return total


def step_kernel(dims, meta, lens, *refs):
    packs, count, features, inner, bc, heads, size, width, nseq = dims
    (
        steps, sums, state_sums, keep, recv, gkeep, grecv, small, normed, wdt,
        gdt_o, gdt_rows_o, gsmall_o, gain_o,
        gdt_sums,
    ) = refs
    group, half = pl.program_id(0), packs // 2
    matrix = spread_matrix(heads, size)
    ones = jnp.ones((8, LANES), bf16)
    decay_rate = -jnp.exp(small[1:2, :])
    upper = triangle(count, False)
    rows = lax.broadcasted_iota(jnp.int32, (count, LANES), 0)
    mine = group == (meta[0] & 1)
    bias_sum, rate_sum = jnp.zeros((1, LANES), f32), jnp.zeros((1, LANES), f32)
    term = jnp.zeros((features, LANES), f32)
    for j in range(half):
        pick = lambda a, b: jnp.where(mine, a[j].astype(jnp.int32), b[j].astype(jnp.int32))
        state = decode_state(pick(keep, recv), heads, size)[0]
        gstate = decode_state(pick(gkeep, grecv), heads, size)[0]
        seg = column_segments(meta, lens, group * half + j, count, nseq, EDGE)
        v = steps[j]
        dt, cum = steps_of(v, heads)
        sig = head_lanes(sigmoid(v), heads)
        row_sum, col_sum = from_group(sums[j], 0, heads), from_group(sums[j], 1, heads)
        state_sum = state_sums[j]
        carry = carry_column(meta, seg, EDGE)
        hi, lo = split2(gstate * state)
        by_head = collapse(nt(ones, hi) + nt(ones, lo), matrix, heads)[0:1]
        last = by_head * carry[count - 1 :] * jnp.exp(cum[count - 1 :]) + jnp.sum(
            state_sum, axis=0, keepdims=True
        )
        grad_cum = row_sum - col_sum - state_sum + jnp.where(rows == count - 1, last, 0.0)
        grad_rate = exact_sums(upper, grad_cum, heads)
        ratio = jnp.where(dt > 1e-30, sig / jnp.maximum(dt, 1e-30), 1.0)
        grad_dt = head_lanes(ratio * (col_sum + state_sum) + grad_rate * decay_rate * sig, heads)
        low = grad_dt.astype(bf16)
        gdt_o[j] = low
        bias_sum = bias_sum + jnp.sum(grad_dt, axis=0, keepdims=True)
        rate_sum = rate_sum + jnp.sum(grad_rate * dt * decay_rate, axis=0, keepdims=True)
        term = term + nn(normed[j], low)

    @pl.when(group == 0)
    def _():
        gsmall_o[...] = jnp.zeros_like(gsmall_o)
        gdt_sums[...] = jnp.zeros_like(gdt_sums)

    gsmall_o[0:1, :] += bias_sum
    gsmall_o[1:2, :] += rate_sum
    gdt_sums[...] += term

    @pl.when(group == packs // half - 1)
    def _():
        gdt_rows_o[...] = jnp.transpose(gdt_sums[...])[0:8]
        gain_o[...] = gain_row(wdt[...], gdt_sums[...])


def xback_kernel(dims, meta, lens, *refs):
    packs, count, features, inner, bc, heads, size, width, nseq = dims
    (
        grads, raw, normed, edge, edge_x, conv, wx,
        main_o, keep_o, give_o, gconv_o, gain_o,
        gpad, raws, sums, rows_x,
    ) = refs
    pack = order.pack
    seg = column_segments(meta, lens, pack, count, nseq, EDGE)

    cleared(gconv_o, rows_x, sums)
    raws[...] = raw[0].astype(f32)
    gpad[:count, :] = grads[0]
    gpad[count:, :] = jnp.zeros((EDGE, inner), f32)
    conv_taps(grads[0], raws, gconv_o, seg, count, width)
    seg_pad = jnp.concatenate([seg[EDGE:], jnp.full((8, 1), -1, jnp.int32)], axis=0)
    main = conv_rows(gpad, conv, seg_pad, count, width).astype(bf16)
    main_o[0] = main
    rows_x[pl.ds(pl.multiple_of(pack * EDGE, EDGE), EDGE), :] = edge_x[0]
    sums[...] += nn(normed[0], main).reshape(sums.shape)

    def finish():
        @last_pack(pack, packs)
        def _():
            sums[...] += nn(edge[...], rows_x[...]).reshape(sums.shape)
            side = meta[0] & 1
            keep_o[...] = sums[side]
            give_o[...] = sums[1 - side].astype(bf16)
            gain_o[...] = gain_row(wx[...], sums[...].reshape(wx.shape))

    return finish


def conv_bc_kernel(dims, meta, lens, *refs):
    packs, count, features, inner, bc, heads, size, width, nseq = dims
    (
        keep, recv, slope, raw, normed, edge, wbc, conv, edge_x,
        gconv_x, gdt_rows, gsmall, gate_small, gain_z, gain_x, gain_dt, gain,
        rows_o, edges_o, give_o, small_o,
        gpad, raws, sums, edge_bc, gconv,
    ) = refs
    pack = order.pack
    quarter = bc // 4

    cleared(gconv, edge_bc, sums)
    gpad[:EDGE, :] = jnp.zeros((EDGE, quarter), f32)
    gpad[EDGE + count :, :] = jnp.zeros((EDGE, quarter), f32)
    both = keep[0] + recv[0]
    grad = jnp.where(pack < packs // 2, both[:, :quarter], both[:, quarter:]) * slope[0]
    seg = column_segments(meta, lens, pack, count, nseq, EDGE)
    raws[...] = raw[0].astype(f32)
    gpad[EDGE : EDGE + count, :] = grad
    conv_taps(grad, raws, gconv, seg, count, width)
    seg_pad = jnp.concatenate([seg, jnp.full((8, 1), -1, jnp.int32)], axis=0)
    grad_raw = conv_rows(gpad, conv, seg_pad, count + EDGE, width).astype(bf16)
    rows_o[0] = grad_raw[EDGE:]
    edge_bc[pl.ds(pl.multiple_of(pack * EDGE, EDGE), EDGE), :] = grad_raw[:EDGE]
    edges_o[0, :, :inner] = edge_x[0]
    blank = jnp.zeros((EDGE, LANES - quarter), bf16)
    edges_o[0, :, inner:] = jnp.concatenate([grad_raw[:EDGE], blank], axis=1)
    sums[...] += nn(normed[0], grad_raw[EDGE:])

    def finish():
        @last_pack(pack, packs)
        def _():
            total = sums[...] + nn(edge[...], edge_bc[...])
            rows = jnp.transpose(total)
            taps = width + 1
            give_o[:quarter, :] = rows[:, :inner].astype(bf16)
            give_o[quarter : 2 * quarter, :] = rows[:, inner:].astype(bf16)
            small_o[...] = jnp.zeros_like(small_o)
            for h in range(heads):
                small_o[2 * h : 2 * h + 1, :] = gdt_rows[h : h + 1, :inner]
                small_o[2 * h + 1 : 2 * h + 2, :] = gdt_rows[h : h + 1, inner:]
            row = 2 * heads
            small_o[row : row + taps, :] = gconv_x[:taps, :]
            row += taps
            small_o[row : row + 1, :] = gate_small[0:1, :]
            skips = collapse(gate_small[...], spread_matrix(heads, size), heads)
            small_o[row + 1 : row + 2, :] = jnp.concatenate(
                [gsmall[0:1, :], gsmall[1:2, :], skips[1:2, :]], axis=1
            )
            blank_row = jnp.zeros((1, inner - taps * quarter), f32)
            small_o[row + 2 : row + 3, :] = jnp.concatenate(
                [gconv[k : k + 1, :] for k in range(taps)] + [blank_row], axis=1
            )
            gains = gain_row(wbc[...], total)[0:1] + gain_z[0:1, :] + gain_x[0:1, :] + gain_dt[0:1, :]
            gains = gains / jnp.transpose(jnp.broadcast_to(gain[...], (features, LANES)))[0:1]
            small_o[row + 3 : row + 4, :] = gains[:, :inner]
            small_o[row + 4 : row + 5, :] = gains[:, inner:]
            hi, lo = split2(small_o[...])
            give_o[2 * quarter : 2 * quarter + SMALL, :] = hi
            give_o[2 * quarter + SMALL :, :] = lo

    return finish


def back_kernel(dims, meta, lens, *refs):
    packs, count, features, inner, bc, heads, size, width, nseq = dims
    (
        main, edges, ggate, gdt, gbc, normed, wz, wx, wbc, wdt,
        own_o, far_o, send_o, dots_o,
        stage,
    ) = refs
    head = meta[1]
    part, quarter = features // 4, bc // 4
    late = count - EDGE

    def with_edge(rows, edge):
        low = (rows[late:].astype(f32) + edge.astype(f32)).astype(bf16)
        return jnp.concatenate([rows[:late], low], axis=0)

    grad_x = with_edge(main[0], edges[0, :, :inner])
    grad_bc = with_edge(gbc[0], edges[0, :, inner : inner + quarter])
    whole = nt(wz[...], ggate[0]) + nt(wx[...], grad_x) + nt(wbc[...], grad_bc) + nt(wdt[...], gdt[0])
    dots = jnp.sum(whole * normed[0].astype(f32), axis=0, keepdims=True)
    stage[...] = whole.reshape(stage.shape)
    dots_o[0] = dots
    own_o[0] = stage[head]
    far_o[0] = stage[head ^ 2]
    for k in range(2):
        send_o[0, k, :part, :] = stage[head ^ (1 + 2 * k)].astype(bf16)
        send_o[0, k, part:, :] = extra_rows(dots)


def extra_rows(*values):
    row = lax.broadcasted_iota(jnp.int32, (EDGE, values[0].shape[1]), 0)
    total = jnp.zeros(row.shape, f32)
    for i, value in enumerate(values):
        for k, piece in enumerate(split3(value)):
            total = total + jnp.where(row == 3 * i + k, piece.astype(f32), 0.0)
    return total.astype(bf16)


def read_extra(block, i):
    rows = block.astype(f32)
    return rows[3 * i : 3 * i + 1] + rows[3 * i + 1 : 3 * i + 2] + rows[3 * i + 2 : 3 * i + 3]


def gather_kernel(own, far, near, dots, own_o, far_o, dots_o):
    part = own.shape[1]
    own_o[0] = own[0] + near[0, 0, :part, :].astype(f32)
    far_o[0, :part, :] = (far[0] + near[0, 1, :part, :].astype(f32)).astype(bf16)
    both = dots[0] + read_extra(near[0, 0, part:, :], 0)
    dots_o[0] = both
    far_o[0, part:, :] = extra_rows(both)


def final_kernel(dims, own, far, dots, tokens, inv, gain, out_grad, in_grad_o):
    packs, count, features = dims
    part = own.shape[1]
    grad = own[0] + far[0, :part, :].astype(f32)
    mean = (dots[0] + read_extra(far[0, part:, :], 0)) / features
    unit = tokens[0].astype(f32) * inv[0]
    in_grad_o[0] = out_grad[0].astype(f32) + inv[0] * (gain[...] * grad - unit * mean)


def out_gather_kernel(own, far, near, own_o, far_o):
    own_o[0] = own[0] + near[0, 0].astype(f32)
    far_o[0] = (far[0] + near[0, 1].astype(f32)).astype(bf16)


def out_final_kernel(own, far, tokens, out):
    out[0] = (tokens[0].astype(f32) + (own[0] + far[0].astype(f32))).astype(bf16)


def add_kernel(bit, halve, segs, count, small, meta, *refs):
    keep, got, refs = refs[:count], refs[count : 2 * count], refs[2 * count :]
    end = segs[-1] if count > 1 else sum(segs)
    write = 0
    if small:
        small_in, *refs, small_o = refs
        hi, lo = split2(small_in[...])
        mine = hi.astype(f32) + lo.astype(f32)
        theirs = got[-1][end : end + SMALL, :].astype(f32) + got[-1][end + SMALL :, :].astype(f32)
        total = mine + theirs
        small_o[...] = total
        if bit is not None:
            send_o = refs[-1]
            behind = send_o.shape[0] - 2 * SMALL
            hi, lo = split2(total)
            send_o[behind : behind + SMALL, :] = hi
            send_o[behind + SMALL :, :] = lo
    read = 0
    for i, rows in enumerate(segs):
        if count > 1:
            total = keep[i][...] + got[i][:rows, :].astype(f32)
        else:
            total = keep[0][read : read + rows, :].astype(f32) + got[0][read : read + rows, :].astype(f32)
        read += rows
        if halve:
            half = rows // 2
            first = ((meta[0] >> bit) & 1) == 0
            top, bottom = total[:half], total[half:]
            refs[0][write : write + half, :] = jnp.where(first, top, bottom)
            refs[1][write : write + half, :] = jnp.where(first, bottom, top).astype(bf16)
            write += half
        else:
            refs[0][write : write + rows, :] = total.astype(bf16)
            write += rows


def whole_kernel(quarter, keep, got, small, out, small_o):
    total = keep[: 2 * quarter, :].astype(f32) + got[: 2 * quarter, :].astype(f32)
    out[...] = jnp.concatenate([total[:quarter], total[quarter:]], axis=1)
    hi, lo = split2(small[...])
    end = 2 * quarter
    theirs = got[end : end + SMALL, :].astype(f32) + got[end + SMALL :, :].astype(f32)
    small_o[...] = (hi.astype(f32) + lo.astype(f32)) + theirs


def join_kernel(bit, segs, meta, mine, got, out):
    first = ((meta[0] >> bit) & 1) == 0
    read = 0
    for rows in segs:
        a = mine[read : read + rows, :].astype(f32)
        b = got[read : read + rows, :].astype(f32)
        out[2 * read : 2 * read + rows, :] = jnp.where(first, a, b).astype(bf16)
        out[2 * read + rows : 2 * read + 2 * rows, :] = jnp.where(first, b, a).astype(bf16)
        read += rows


def part_kernel(values, out):
    out[0] = values[...].astype(f32)


def result_kernel(segs, ways, meta, mine, got, *outs):
    first = (meta[0] & 1) == 0
    read = 0
    for rows, way, out in zip(segs, ways, outs):
        a = mine[read : read + rows, :].astype(f32)
        b = got[read : read + rows, :].astype(f32)
        top, bottom = jnp.where(first, a, b), jnp.where(first, b, a)
        if way == "rows":
            out[:rows, :] = top
            out[rows:, :] = bottom
        elif way == "flip":
            out[:, :rows] = jnp.transpose(top)
            out[:, rows:] = jnp.transpose(bottom)
        else:
            out[...] = jnp.concatenate([top, bottom], axis=1)
        read += rows


def plus_kernel(a, b, out):
    out[...] = a[...] + b[...]


def unpack_kernel(dims, meta, *refs):
    heads, features, bc_part, width = dims
    smalls, gains, dt_o, taps_x_o, taps_bc_o, bias_x_o, bias_bc_o, dt_bias_o, a_log_o, skip_o, gate_o, gain_o = refs
    for h in range(heads):
        dt_o[h : h + 1, :] = jnp.concatenate(
            [smalls[2 * h : 2 * h + 1, :], smalls[2 * h + 1 : 2 * h + 2, :]], axis=1
        )
    row = 2 * heads
    taps_x_o[...] = smalls[row : row + width, :]
    bias_x_o[...] = smalls[row + width, :]
    row += width + 1
    gate_o[...] = smalls[row, :]
    for k, out in enumerate((dt_bias_o, a_log_o, skip_o)):
        out[...] = smalls[row + 1, k * LANES : k * LANES + heads]
    taps = smalls[row + 2 : row + 3, :]
    for k in range(width):
        taps_bc_o[k : k + 1, :] = taps[:, k * bc_part : (k + 1) * bc_part]
    bias_bc_o[...] = taps[0, width * bc_part : (width + 1) * bc_part]
    both = jnp.concatenate([gains[row + 3 : row + 4, :], gains[row + 4 : row + 5, :]], axis=1)
    part = features // 4
    parts = [both[:, h * part : (h + 1) * part] for h in range(4)]
    low = jnp.where((meta[1] & 1) == 0, parts[0], parts[1])
    high = jnp.where((meta[1] & 1) == 0, parts[2], parts[3])
    gain_o[...] = jnp.where((meta[1] >> 1) == 0, low, high)[0]


class Spec:
    def __init__(self, shape, index, each=True):
        self.shape, self.index, self.each = tuple(shape), index, each

    def block(self, group):
        zeros = (0,) * len(self.shape)
        if not self.each:
            return pl.BlockSpec(self.shape, lambda p, *_: zeros)
        size = group or 1
        return pl.BlockSpec(
            (size,) + self.shape, lambda p, *pre: (self.index(p, pre, bool(group)),) + zeros
        )


def whole_spec(shape):
    return Spec(shape, None, False)


def pack_spec(shape):
    return Spec(shape, lambda p, pre, grouped: p)


def half_spec(shape, half):
    return Spec(shape, lambda p, pre, grouped: 0 if grouped else p % half)


def sided_spec(shape, half, keep):
    def index(p, pre, grouped):
        side = pre[0][0] & 1 if keep else 1 - (pre[0][0] & 1)
        return side if grouped else p + half * side

    return Spec(shape, index)


def side_spec(shape, half, keep):
    def index(p, pre, grouped):
        if grouped:
            return 0
        side = pre[0][0] & 1 if keep else 1 - (pre[0][0] & 1)
        group = p // half
        return jnp.where(group == side, p % half, jnp.where(group < side, 0, half - 1))

    return Spec(shape, index)


class Each:
    def __init__(self, shape, dtype):
        self.shape, self.dtype = tuple(shape), dtype

    def scratch(self, group):
        return pltpu.VMEM(((group,) if group else ()) + self.shape, self.dtype)


class Order:
    def __init__(self):
        self.clear()

    def clear(self):
        self.last, self.near, self.held = (), [], []
        self.pack, self.lane, self.lanes = None, 0, 1

    def first(self, work):
        if self.lane == 0:
            pl.when(self.pack == 0)(work)

    def hold(self, *arrays):
        self.held += arrays

    def drop(self, *arrays):
        self.held = [x for x in self.held if not any(x is y for y in arrays)]

    def placed(self, x):
        return pltpu.with_memory_space_constraint(x, pltpu.VMEM) if self.holds(x) else x

    def holds(self, x):
        return any(x is y for y in self.near)


order = Order()


def call(
    kernel, grid, in_specs, out_specs, out_shape, scratch, prefetch, *args, limit=28, wait=(), us=1,
    out=False, onto=(), group=0,
):
    first = len(prefetch) + len(args)
    args = args + tuple(onto)
    in_specs = list(in_specs) + [pl.BlockSpec(memory_space=pl.ANY)] * len(onto)
    given = len(prefetch) + len(args)
    held = order.last + tuple(wait)
    held += tuple(x for x in order.held if not any(x is y for y in args + held))
    late = len(held)
    single = not isinstance(out_shape, (list, tuple))
    out_specs, out_shape = ([out_specs], [out_shape]) if single else (list(out_specs), list(out_shape))
    token = jax.ShapeDtypeStruct((8, LANES), f32)
    count = len(out_shape)
    results = count if out is True else int(out)

    specs = list(in_specs[: len(in_specs) - len(onto)]) + out_specs
    blocks = lambda items: [x.block(group) if isinstance(x, Spec) else x for x in items]

    def body(*refs):
        ins, rest = refs[:first], refs[given + late :]
        fixed, blocked = ins[: len(prefetch)], (*ins[len(prefetch) :], *rest[:count])
        own = rest[count + 1 :]
        finish = []
        for lane in range(group or 1):
            order.pack, order.lane, order.lanes = pl.program_id(0), lane, group or 1
            views, scratches = blocked, own
            if group:
                order.pack = order.pack * group + lane
                views = [
                    ref.at[pl.ds(lane, 1)] if isinstance(spec, Spec) and spec.each else ref
                    for ref, spec in zip(blocked, specs)
                ]
                scratches = [
                    ref.at[lane] if isinstance(item, Each) else ref for ref, item in zip(own, scratch)
                ]
            finish.append(kernel(*fixed, *views, *scratches))
        for work in finish:
            if work is not None:
                work()

    *outs, order_out = pl.pallas_call(
        body,
        grid_spec=pltpu.PrefetchScalarGridSpec(
            num_scalar_prefetch=len(prefetch),
            grid=grid,
            in_specs=blocks(in_specs) + [pl.BlockSpec(memory_space=pl.ANY)] * late,
            out_specs=blocks(out_specs + [whole_spec(token.shape)]),
            scratch_shapes=[x.scratch(group) if isinstance(x, Each) else x for x in scratch],
        ),
        input_output_aliases={first + i: i for i in range(len(onto))},
        out_shape=[
            x if i < results else pltpu.VMEM(x.shape, x.dtype) for i, x in enumerate(out_shape + [token])
        ],
        compiler_params=pltpu.CompilerParams(vmem_limit_bytes=limit * MIB),
        cost_estimate=pl.CostEstimate(
            flops=int(us * 10e9), bytes_accessed=int(us * 3e6), transcendentals=0
        ),
    )(*[pltpu.with_memory_space_constraint(x, pltpu.VMEM) for x in prefetch], *[order.placed(x) for x in args], *[order.placed(x) for x in held])
    order.last = (order_out,)
    order.near.append(order_out)
    order.near += outs[results:]
    return outs[0] if single else outs


def shape(*dims_and_type):
    return jax.ShapeDtypeStruct(dims_and_type[:-1], dims_and_type[-1])


def scan_states(keep, send, meta, packs, heads, size, rev, beside, waits=lambda: ()):
    dims = (packs, heads, size)
    rows = heads * size
    half = packs // 2
    pay = shape(half, rows + EDGE, LANES, jnp.int16)
    spec = whole_spec(pay.shape)
    bits = (lax.axis_size("seq") - 1).bit_length()
    beside = list(beside)

    def work(newest):
        if beside:
            beside.pop(0)(newest)

    other = swap(send, "seq", 1)
    work(send)
    keep = keep() if callable(keep) else keep
    total = call(
        functools.partial(pair_kernel, dims, rev), (1,), [spec, spec], spec, pay, [], (meta,),
        keep, other,
    )
    before = None
    for bit in range(1, bits):
        got = swap(total, "seq", 1 << bit)
        extra = () if before is None else (before,)
        work(total)
        if bit < bits - 1:
            total, before = call(
                functools.partial(cube_kernel, dims, rev, bit, before is None), (1,),
                [spec] * (2 + len(extra)), [spec, spec], [pay, pay], [], (meta,),
                total, got, *extra,
            )
        else:
            own, back = call(
                functools.partial(last_kernel, dims, rev, bit, before is None), (1,),
                [spec] * (3 + len(extra)), [spec, spec], [pay, pay], [],
                (meta,), keep, other, got, *extra, wait=waits(),
            )
    recv = swap(back, "seq", 1)
    while beside:
        work(back)
    return own, recv


class SeqSum:
    def __init__(self):
        self.keep, self.got, self.segs = [], [], []
        self.small = self.bit = None
        self.bits = list(range(1, (lax.axis_size("seq") - 1).bit_length()))
        self.halved = []

    def put(self, keep, give, segs=None, small=None):
        self.keep.append(keep)
        self.got.append(swap(give, "seq", 1))
        self.segs += segs or [keep.shape[0]]
        self.small = small

    def add(self, meta, us=1, wait=()):
        bit = self.bits.pop(0) if self.bits else None
        halve = bit is not None and all(rows % (2 * EDGE) == 0 for rows in self.segs)
        cols = self.keep[0].shape[1]
        segs = [rows // 2 for rows in self.segs] if halve else self.segs
        rows = sum(segs)
        small = self.small is not None
        behind = 2 * SMALL if small and bit is not None else 0
        low = shape(rows + behind, cols, bf16)
        out = [shape(rows, cols, f32), low] if halve else [low]
        ins = [*self.keep, *self.got]
        if small:
            ins.append(self.small)
            out.append(shape(*self.small.shape, f32))
        outs = call(
            functools.partial(add_kernel, bit, halve, self.segs, len(self.keep), small), (1,),
            [whole_spec(x.shape) for x in ins], [whole_spec(x.shape) for x in out], out, [],
            (meta,), *ins, us=us, wait=wait,
        )
        if small:
            self.small = outs[-1]
        self.segs, self.keep = segs, [outs[0]]
        if bit is None:
            return True
        self.got = [swap(outs[1] if halve else outs[0], "seq", 1 << bit)]
        if halve:
            self.halved.append(bit)
        return False

    def send_back(self):
        self.bit = self.halved.pop() if self.halved else 0
        self.got = [swap(self.keep[0], "seq", 1 << self.bit)]

    def join(self, meta, us=1):
        rows, cols = self.keep[0].shape
        both = shape(2 * rows, cols, bf16)
        spec = whole_spec((rows, cols))
        self.keep = [call(
            functools.partial(join_kernel, self.bit, self.segs), (1,), [spec, spec],
            whole_spec(both.shape), both, [], (meta,), self.keep[0], self.got[0], us=us,
        )]
        self.segs = [2 * rows for rows in self.segs]

    def half_result(self, meta, mine, onto=()):
        rows, cols = self.keep[0].shape

        def index(p, pre, grouped):
            side = pre[0][0] & 1
            return side if mine else 1 - side

        return call(
            lambda meta, values, out: part_kernel(values, out), (1,), [whole_spec((rows, cols))],
            Spec((rows, cols), index), shape(2, rows, cols, f32), [], (meta,),
            self.keep[0] if mine else self.got[0], out=True, us=0.01, onto=onto,
        )

    def result(self, meta, ways, us=0.01):
        cols = self.keep[0].shape[1]
        shapes = {"rows": lambda r: (2 * r, cols), "flip": lambda r: (cols, 2 * r), "cols": lambda r: (r, 2 * cols)}
        out = [shape(*shapes[way](rows), f32) for way, rows in zip(ways, self.segs)]
        spec = whole_spec(self.keep[0].shape)
        return call(
            functools.partial(result_kernel, self.segs, ways), (1,), [spec, spec],
            [whole_spec(x.shape) for x in out], out, [], (meta,), self.keep[0], self.got[0],
            out=True, us=us,
        )


def advance(total, meta, us=1, wait=()):
    if total.bit is None:
        if total.add(meta, us, wait):
            total.send_back()
    elif total.bit:
        total.join(meta, us)
        total.send_back()


def shards(
    tokens_in, out_grad, lengths, norm_gain, proj_z, proj_x, proj_bc, proj_dt, conv_x, conv_bc,
    bias_x, bias_bc, dt_bias, a_log, d_skip, gate_gain, proj_out,
):
    packs, count, part = tokens_in.shape
    features, inner = proj_x.shape
    heads = proj_dt.shape[1]
    size = inner // heads
    width = conv_x.shape[0]
    nseq = lengths.shape[1]
    bc_part = proj_bc.shape[1]
    bc = bc_part * lax.axis_size("head")
    half = packs // 2
    chans = inner + bc
    ext = count + EDGE
    rows = heads * size
    total_inner = inner * lax.axis_size("head")
    dims = (packs, count, features, inner, bc, heads, size, width, nseq)
    seq_place, head_place = lax.axis_index("seq"), lax.axis_index("head")
    meta = jnp.stack([seq_place, head_place]).astype(jnp.int32)
    pre = (meta, lengths)
    grid = (packs,)

    order.clear()
    tokens = jnp.swapaxes(tokens_in, 1, 2)
    cotangent = jnp.swapaxes(out_grad, 1, 2)
    far = swap(tokens, "head", 2)
    near = swap(tokens, "head", 1)
    tail = call(
        tail_kernel, (1,),
        [pl.BlockSpec((packs, part, LANES), lambda p, _: (0, 0, count // LANES - 1))],
        whole_spec((part, LANES)), shape(part, LANES, bf16), [], (meta,),
        pltpu.with_memory_space_constraint(tokens, pltpu.HBM), us=0.05,
    )
    tail = shift(tail, "seq", 1)
    ins = [
        proj_bc.T, conv_bc, bias_bc, norm_gain, proj_dt.T, conv_x, bias_x, dt_bias, a_log, d_skip,
        gate_gain, proj_out,
    ]
    outs = [
        shape(features, inner, bf16),
        shape(bc_part, features + LANES, bf16), shape(features, bc_part, bf16),
        shape(features, LANES, bf16), shape(LANES, features, bf16), shape(8, inner, f32),
        shape(8, bc_part, f32), shape(8, LANES, f32), shape(1, inner, f32), shape(1, inner, f32),
        shape(part, 1, f32),
    ]
    (
        w_out, shared, w_bc, w_dt, w_dt_rows, conv_own, conv_bc_own, small, skip, gain_gate, norm_gain_own,
    ) = call(
        functools.partial(prepare_kernel, dims), (1,), [whole_spec(x.shape) for x in ins],
        [whole_spec(x.shape) for x in outs], outs, [], (), *ins, wait=(tail,),
        us=0.05,
    )
    edge_far, shared_far = swap(tail, "head", 2), swap(shared, "head", 2)
    far, edge_far, shared_far = lax.optimization_barrier((far, edge_far, shared_far))
    edge_pieces = tail, swap(tail, "head", 1), edge_far, swap(edge_far, "head", 1)
    weight_pieces = shared, swap(shared, "head", 1), shared_far, swap(shared_far, "head", 1)
    diagonal = swap(far, "head", 1)
    token_pieces = tokens, near, far, diagonal

    lane_spec = pack_spec((count, LANES))
    chan_spec = pack_spec((count, inner))
    xbc_spec = pack_spec((count, chans))
    model_spec = pack_spec((features, count))
    piece_spec = pack_spec((part, count))
    edge_spec = whole_spec((part, LANES))
    pay_shape = (rows + EDGE, LANES)
    pay_specs = [side_spec(pay_shape, half, k) for k in (True, False)]
    pay = shape(half, *pay_shape, jnp.int16)
    state_spec = half_spec(pay_shape, half)
    vec = whole_spec((1, inner))
    square = whole_spec((features, inner))

    w_bc_rows, conv_all, gain_all, edge, edge_raws = call(
        functools.partial(border_kernel, dims),
        (1,),
        [edge_spec] * 4 + [whole_spec((bc_part, features + LANES))] * 4
        + [square, whole_spec((8, inner))],
        [
            whole_spec((bc, features)), whole_spec((8, chans)), whole_spec((features, 1)),
            whole_spec((features, LANES)), whole_spec((LANES, chans)),
        ],
        [
            shape(bc, features, bf16), shape(8, chans, f32), shape(features, 1, f32),
            shape(features, LANES, bf16), shape(LANES, chans, f32),
        ],
        [pltpu.VMEM((4, part, LANES), bf16), pltpu.VMEM((4, bc_part, features + LANES), bf16)],
        (meta,),
        *edge_pieces, *weight_pieces, proj_x, conv_own,
    )

    def front(keep, onto):
        spec = lambda shape_of: sided_spec(shape_of, half, keep)
        return call(
            functools.partial(front_kernel, dims, keep),
            (half,),
            [spec((part, count))] * 4
            + [
                square, whole_spec((bc, features)), whole_spec((LANES, features)),
                whole_spec((8, chans)), whole_spec((8, LANES)), whole_spec((features, 1)),
                whole_spec((LANES, chans)),
            ],
            [
                spec((features, count)), spec((1, count)), spec((ext, inner)), spec((ext, bc_part)),
                spec((count, chans)), spec((count, LANES)), pack_spec(pay_shape),
            ],
            [
                shape(packs, features, count, bf16), shape(packs, 1, count, f32),
                shape(packs, ext, inner, bf16), shape(packs, ext, bc_part, bf16),
                shape(packs, count, chans, bf16), shape(packs, count, LANES, f32), pay,
            ],
            [Each((4, part, count), bf16), Each((ext, chans), f32)],
            pre,
            *token_pieces, proj_x, w_bc_rows, w_dt_rows, conv_all, small, gain_all, edge_raws,
            us=6, onto=onto,
        )

    *early, send = front(False, ())
    kept = {}

    def keep_work(_):
        *kept["front"], kept["keep"] = front(True, early)
        order.hold(*(kept["front"][i] for i in (0, 4, 5)))

    def inner_work(_):
        *_, xbc, steps = kept["front"]
        kept["inner"] = call(
            functools.partial(inner_kernel, dims),
            grid,
            [xbc_spec, lane_spec],
            chan_spec,
            shape(packs, count, inner, f32),
            [],
            pre,
            xbc, steps,
            us=6,
        )
        order.hold(kept["inner"])

    def cot_work(newest):
        own, far = kept["cots"]
        near = swap(own, "head", 1)
        cots = own, near, far, swap(lax.optimization_barrier((far, newest))[0], "head", 1)
        kept["cot"], kept["gg"] = call(
            functools.partial(cot_kernel, dims),
            (packs // half,),
            [piece_spec] * 4 + [whole_spec((inner, features))],
            [model_spec, chan_spec],
            [shape(packs, features, count, bf16), shape(packs, count, inner, f32)],
            [Each((4, part, count), bf16)],
            pre,
            *cots, proj_out,
            us=5.5, group=half,
        )

    def gate_slope_work(_):
        normed, _, raw_x, raw_bc, *_ = kept["front"]
        own = lax.optimization_barrier((cotangent, normed))[0]
        kept["cots"] = own, swap(own, "head", 2)
        kept["slope"] = call(
            functools.partial(gate_slope_kernel, dims),
            grid,
            [model_spec, square, pack_spec((ext, inner)), pack_spec((ext, bc_part)),
             whole_spec((8, inner)), whole_spec((8, bc_part))],
            [chan_spec, chan_spec, pack_spec((count, bc_part))],
            [shape(packs, count, inner, bf16), shape(packs, count, inner, f32),
             shape(packs, count, bc_part, f32)],
            [Each((ext, inner), f32), Each((ext, bc_part), f32)],
            pre,
            normed, proj_z, raw_x, raw_bc, conv_own, conv_bc_own,
            us=7,
        )

    state_keep, state_recv = scan_states(
        lambda: kept["keep"], send, meta, packs, heads, size, 0,
        (keep_work, gate_slope_work, inner_work, cot_work),
    )
    normed, inv, raw_x, raw_bc, xbc, steps = kept["front"]
    inner_out, cot, gg = kept["inner"], kept["cot"], kept["gg"]
    gate, slope_x, slope_bc = kept["slope"]
    order.drop(inner_out)

    y, stats = call(
        functools.partial(gate_kernel, dims),
        (packs // half,),
        [
            xbc_spec, lane_spec, chan_spec, state_spec, state_spec, chan_spec, chan_spec, vec, vec,
        ],
        [chan_spec, pack_spec((2, count))],
        [shape(packs, count, inner, f32), shape(packs, 2, count, f32)],
        [],
        pre,
        xbc, steps, inner_out, state_keep, state_recv, gate, gg, gain_gate, skip,
        us=6.6, group=half,
    )
    stats = [stats] + [swap(stats, "head", bits) for bits in (1, 2, 3)]

    gy, gated, ggate, gkeep, gsend, gate_small = call(
        functools.partial(grad_kernel, dims, total_inner),
        grid,
        [
            *[pack_spec((2, count))] * 4, xbc_spec, lane_spec, chan_spec, chan_spec, chan_spec, vec,
            vec,
        ],
        [chan_spec] * 3 + pay_specs + [whole_spec((8, inner))],
        [shape(packs, count, inner, f32)] + [shape(packs, count, inner, bf16)] * 2
        + [pay, pay, shape(8, inner, f32)],
        [],
        pre,
        *stats, xbc, steps, y, gate, gg, gain_gate, skip,
        us=8.3,
    )

    piece_shape = shape(packs, part, count, f32)
    send_spec = pack_spec((2, part, count))
    rows_half = features // 2
    half_specs = [whole_spec((rows_half, inner))] * 2
    half_shapes = [shape(rows_half, inner, f32), shape(rows_half, inner, bf16)]
    half_sums = pltpu.VMEM((2, rows_half, inner), f32)
    row8, row8_shape = whole_spec((8, features)), shape(8, features, f32)

    early_sum, late_sum = SeqSum(), SeqSum()

    def out_work(_):
        *kept["out"], keep, give = call(
            functools.partial(out_kernel, dims),
            (packs // half,),
            [chan_spec, model_spec, square],
            [piece_spec, piece_spec, send_spec] + half_specs,
            [piece_shape, piece_shape, shape(packs, 2, part, count, bf16)] + half_shapes,
            [Each((4, part, count), f32), half_sums],
            pre,
            gated, cot, w_out,
            us=6.8, group=half,
        )
        early_sum.put(keep, give)

    def z_work(_):
        keep, give, kept["gain"] = call(
            functools.partial(z_kernel, dims),
            (packs // half,),
            [model_spec, chan_spec, square],
            half_specs + [row8],
            half_shapes + [row8_shape],
            [half_sums],
            pre,
            normed, ggate, proj_z,
            us=5.3, group=half,
        )
        early_sum.put(keep, give)
        own, far, send = kept["out"]
        own, far = call(
            out_gather_kernel, grid, [piece_spec, piece_spec, send_spec], [piece_spec, piece_spec],
            [piece_shape, shape(packs, part, count, bf16)], [], (), own, far, swap(send, "head", 1),
        )
        kept["out"] = own, swap(far, "head", 2)

    def diag_work(_):
        kept["diag"] = call(
            functools.partial(diag_kernel, dims),
            grid,
            [xbc_spec, lane_spec, chan_spec, chan_spec, state_spec, state_spec],
            [chan_spec, pack_spec((count, bc)), lane_spec],
            [
                shape(packs, count, inner, f32), shape(packs, count, bc, f32),
                shape(packs, count, LANES, f32),
            ],
            [],
            pre,
            xbc, steps, gy, y, state_keep, state_recv,
            us=12,
        )

    def early_work(_):
        early_sum.add(meta)

    gstate_keep, gstate_recv = scan_states(
        gkeep, gsend, meta, packs, heads, size, 1, (out_work, z_work, diag_work, early_work),
        lambda: early_sum.got,
    )
    out_own, out_far = kept["out"]
    dx, dbc, sums = kept["diag"]

    edge_tile = (EDGE, inner)

    def pair_spec(shape_of):
        return pl.BlockSpec((half,) + shape_of, lambda p, *_: (p,) + (0,) * len(shape_of))

    pair_lane = pair_spec((count, LANES))
    share_own, share_near, grad_x, state_sums, edge_x = call(
        functools.partial(share_kernel, dims),
        (packs // half,),
        [xbc_spec, lane_spec, pack_spec((count, bc)), state_spec, state_spec, chan_spec, chan_spec,
         chan_spec, whole_spec((8, inner)), vec],
        [lane_spec, lane_spec, chan_spec, lane_spec, pack_spec(edge_tile)],
        [shape(packs, count, LANES, f32)] * 2
        + [shape(packs, count, inner, f32), shape(packs, count, LANES, f32),
           shape(packs, *edge_tile, bf16)],
        [Each((2 * EDGE, inner), f32)],
        pre,
        xbc, steps, dbc, gstate_keep, gstate_recv, gy, dx, slope_x, conv_own, skip,
        us=6.4, group=half,
    )
    share_near = swap(share_near, "head", 1)
    advance(early_sum, meta)
    two = shape(half, count, LANES, f32)
    bc_keep, bc_send = call(
        functools.partial(middle_kernel, (packs, bc_part)),
        (1,),
        [whole_spec((packs, count, LANES))] * 2,
        [whole_spec(two.shape)] * 2,
        [two, two],
        [],
        (meta,),
        share_own, share_near,
    )
    bc_recv = swap(bc_send, "head", 2)

    main_x, keep, give, grad_conv, gain_x = call(
        functools.partial(xback_kernel, dims),
        grid,
        [
            chan_spec, pack_spec((ext, inner)), model_spec, whole_spec((features, LANES)),
            pack_spec(edge_tile), whole_spec((8, inner)), square,
        ],
        [chan_spec, *half_specs, whole_spec((8, inner)), row8],
        [shape(packs, count, inner, bf16), *half_shapes, shape(8, inner, f32), row8_shape],
        [
            Each((count + EDGE, inner), f32), Each((ext, inner), f32), half_sums,
            pltpu.VMEM((LANES, inner), bf16),
        ],
        pre,
        grad_x, raw_x, normed, edge, edge_x, conv_own, proj_x,
        us=7, wait=(out_far,),
    )
    late_sum.put(keep, give)
    advance(early_sum, meta)

    gdt, gdt_rows, grad_small, gain_dt = call(
        functools.partial(step_kernel, dims),
        (packs // half,),
        [
            pair_lane, pair_lane, pair_lane, *[whole_spec((half,) + pay_shape)] * 4,
            whole_spec((8, LANES)), pair_spec((features, count)), whole_spec((features, LANES)),
        ],
        [pair_lane, row8, whole_spec((8, LANES)), row8],
        [shape(packs, count, LANES, bf16), row8_shape, shape(8, LANES, f32), row8_shape],
        [pltpu.VMEM((features, LANES), f32)],
        pre,
        steps, sums, state_sums, state_keep, state_recv, gstate_keep, gstate_recv, small, normed,
        w_dt,
        us=6,
    )
    advance(early_sum, meta)
    advance(late_sum, meta)
    give_rows = 2 * bc_part + 2 * SMALL
    gbc, edges, bc_sum, smalls = call(
        functools.partial(conv_bc_kernel, dims),
        grid,
        [
            half_spec((count, LANES), half), half_spec((count, LANES), half),
            pack_spec((count, bc_part)), pack_spec((ext, bc_part)), model_spec,
            whole_spec((features, LANES)), whole_spec((features, bc_part)),
            whole_spec((8, bc_part)), pack_spec(edge_tile), whole_spec((8, inner)), row8,
            whole_spec((8, LANES)), whole_spec((8, inner)), row8, row8, row8,
            whole_spec((features, 1)),
        ],
        [
            pack_spec((count, bc_part)), pack_spec((EDGE, inner + LANES)),
            whole_spec((give_rows, inner)), whole_spec((SMALL, inner)),
        ],
        [
            shape(packs, count, bc_part, bf16), shape(packs, EDGE, inner + LANES, bf16),
            shape(give_rows, inner, bf16), shape(SMALL, inner, f32),
        ],
        [
            Each((ext + EDGE, bc_part), f32), Each((ext, bc_part), f32),
            pltpu.VMEM((features, bc_part), f32), pltpu.VMEM((LANES, bc_part), bf16),
            pltpu.VMEM((8, bc_part), f32),
        ],
        pre,
        bc_keep, bc_recv, slope_bc, raw_bc, normed, edge, w_bc, conv_bc_own, edge_x, grad_conv,
        gdt_rows, grad_small, gate_small, kept["gain"], gain_x, gain_dt, gain_all,
        us=5,
    )
    edges = shift(edges, "seq", -1)
    bc_bits = [1 << k for k in range((lax.axis_size("seq") - 1).bit_length())]
    bc_got = swap(bc_sum, "seq", 1)
    advance(late_sum, meta)

    def bc_step(bit):
        nonlocal bc_sum, smalls, bc_got
        spec, small_spec = whole_spec(bc_sum.shape), whole_spec(smalls.shape)
        bc_sum, smalls = call(
            functools.partial(add_kernel, 1, False, [2 * bc_part], 1, True), (1,),
            [spec, spec, small_spec], [spec, small_spec],
            [shape(*bc_sum.shape, bf16), shape(*smalls.shape, f32)], [], (meta,),
            bc_sum, bc_got, smalls, us=0.01,
        )
        bc_got = swap(bc_sum, "seq", bit)

    bc_step(bc_bits[1])
    advance(early_sum, meta)

    tall = part + EDGE
    tall_send = pack_spec((2, tall, count))
    tall_spec = pack_spec((tall, count))
    row_spec, row_shape = pack_spec((1, count)), shape(packs, 1, count, f32)
    gn_own, gn_far, gn_send, dots = call(
        functools.partial(back_kernel, dims),
        (packs // half,),
        [
            chan_spec, pack_spec((EDGE, inner + LANES)), chan_spec, lane_spec,
            pack_spec((count, bc_part)), model_spec, square, square,
            whole_spec((features, bc_part)), whole_spec((features, LANES)),
        ],
        [piece_spec, piece_spec, tall_send, row_spec],
        [piece_shape, piece_shape, shape(packs, 2, tall, count, bf16), row_shape],
        [Each((4, part, count), f32)],
        pre,
        main_x, edges, ggate, gdt, gbc, normed, proj_z, proj_x, w_bc, w_dt,
        us=6, group=half,
    )
    near = swap(gn_send, "head", 1)
    order.drop(xbc, steps, normed)
    advance(late_sum, meta, 0.01, wait=(bc_got,))
    block_out = call(
        out_final_kernel, (packs // half,), [piece_spec] * 3, piece_spec, shape(packs, part, count, bf16), [],
        (), out_own, out_far, tokens, out=True, us=2, group=half,
    )
    block_out = jnp.swapaxes(block_out, 1, 2)

    gn_own, gn_far, dots = call(
        gather_kernel,
        grid,
        [piece_spec, piece_spec, tall_send, row_spec],
        [piece_spec, tall_spec, row_spec],
        [piece_shape, shape(packs, tall, count, bf16), row_shape],
        [],
        (),
        gn_own, gn_far, near, dots,
        us=0.01,
    )
    gn_far = swap(gn_far, "head", 2)
    order.hold(gn_own)
    while early_sum.bit != 0:
        advance(early_sum, meta)
    for bit in bc_bits[2:]:
        bc_step(bit)
    small_spec, give_spec = whole_spec(smalls.shape), whole_spec(bc_sum.shape)

    def head_step(x, bit):
        return call(
            plus_kernel, (1,), [small_spec, small_spec], small_spec, shape(*x.shape, f32), [], (),
            x, swap(x, "head", bit), us=0.01,
        )

    advance(late_sum, meta, 0.01)
    grads_out, grads_z = early_sum.result(meta, ("flip", "rows"), 0.4)
    while late_sum.bit != 0:
        advance(late_sum, meta, 0.01)
    grad_bc, smalls = call(
        functools.partial(whole_kernel, bc_part), (1,), [give_spec, give_spec, small_spec],
        [whole_spec((bc_part, features)), small_spec],
        [shape(bc_part, features, f32), shape(*smalls.shape, f32)], [], (), bc_sum, bc_got, smalls,
        us=0.01, out=1,
    )
    gains = head_step(smalls, 1)
    in_grad = call(
        functools.partial(final_kernel, (packs, count, features)),
        (packs // half,),
        [piece_spec, tall_spec, row_spec, piece_spec, row_spec, whole_spec((part, 1)), piece_spec],
        piece_spec,
        piece_shape,
        [],
        (),
        gn_own, gn_far, dots, tokens, inv, norm_gain_own, cotangent,
        us=2, out=True, group=half,
    )
    in_grad = jnp.swapaxes(in_grad, 1, 2)
    order.drop(gn_own)
    gains = head_step(gains, 2)
    own_half = late_sum.half_result(meta, True)
    vectors = [(inner,), (bc_part,), (heads,), (heads,), (heads,), (inner,), (part,)]
    tables = [(heads, features), (width, inner), (width, bc_part)]
    outs = call(
        functools.partial(unpack_kernel, (heads, features, bc_part, width)), (1,),
        [small_spec, small_spec], [whole_spec(x) for x in tables + vectors],
        [shape(*x, f32) for x in tables + vectors], [], (meta,), smalls, gains, out=True, us=0.01,
    )
    grad_dt, grad_conv, grad_conv_bc = outs[:3]
    bias_x_grad, bias_bc_grad, dt_bias_grad, a_log_grad, skip_grad, gate_grad, grad_gain = outs[3:]
    grads_x = late_sum.half_result(meta, False, (own_half,)).reshape(features, inner)
    return (
        block_out,
        in_grad,
        grad_gain,
        grads_z,
        grads_x,
        grad_bc.T,
        grad_dt.T,
        grad_conv,
        grad_conv_bc,
        bias_x_grad,
        bias_bc_grad,
        dt_bias_grad,
        a_log_grad,
        skip_grad,
        gate_grad,
        grads_out,
    )


def solution(mesh):
    token, column, vector = P(None, "seq", "head"), P(None, "head"), P("head")
    row = P("head", None)
    return jax.shard_map(
        shards,
        mesh=mesh,
        in_specs=(
            token, token, P(), vector, column, column, column, column, column, column, vector,
            vector, vector, vector, vector, vector, row,
        ),
        out_specs=(
            token, token, vector, column, column, column, column, column, column, vector, vector,
            vector, vector, vector, vector, row,
        ),
        check_vma=False,
    )
```

```python
import functools

import jax
import jax.numpy as jnp
from jax import lax
from jax.experimental import pallas as pl
from jax.experimental.pallas import tpu as pltpu
from jax.sharding import PartitionSpec as P

EPSILON = 1e-05
bf16 = jnp.bfloat16
f32 = jnp.float32
LANES = 128
EDGE = 16
MIB = 1024 * 1024
STEPS = 32000.0
UNIT = 16384.0
LN2 = 0.6931471805599453
GROUP = 16
SMALL = 32


def permuted(x, axis, route):
    y = lax.ppermute(x, axis, route)
    order.near.append(y)
    return y


def swap(x, axis, bit):
    return permuted(x, axis, [(i, i ^ bit) for i in range(lax.axis_size(axis))])


def shift(x, axis, distance):
    n = lax.axis_size(axis)
    return permuted(x, axis, [(i, i + distance) for i in range(n) if 0 <= i + distance < n])


def head_pieces(x):
    far = swap(x, "head", 2)
    near = swap(x, "head", 1)
    return x, near, far, swap(far, "head", 1)


def nn(a, b):
    return lax.dot_general(a, b, (((1,), (0,)), ((), ())), preferred_element_type=f32)


def nt(a, b):
    return lax.dot_general(a, b, (((1,), (1,)), ((), ())), preferred_element_type=f32)


def tn(a, b):
    return lax.dot_general(a, b, (((0,), (0,)), ((), ())), preferred_element_type=f32)


def split2(v):
    hi = v.astype(bf16)
    return hi, (v - hi.astype(f32)).astype(bf16)


def split3(v):
    hi = v.astype(bf16)
    rest = v - hi.astype(f32)
    mid = rest.astype(bf16)
    return hi, mid, (rest - mid.astype(f32)).astype(bf16)


def spread_matrix(heads, size):
    row = lax.broadcasted_iota(jnp.int32, (LANES, heads * size), 0)
    col = lax.broadcasted_iota(jnp.int32, (LANES, heads * size), 1)
    first = (col >= row * size) & (col < (row + 1) * size)
    again = (col >= (row - GROUP) * size) & (col < (row - GROUP + 1) * size)
    return jnp.where(first | again, 1.0, 0.0).astype(bf16)


def spread(v, matrix, heads):
    hi, lo = split2(head_lanes(v, heads))
    return nn((hi.astype(f32) + to_group(lo.astype(f32), 1)).astype(bf16), matrix)


def head_lanes(v, heads):
    return jnp.where(lax.broadcasted_iota(jnp.int32, v.shape, 1) < heads, v, 0.0)


def to_group(v, k):
    return pltpu.roll(v, k * GROUP, 1)


def from_group(v, k, heads):
    return head_lanes(pltpu.roll(v, LANES - k * GROUP, 1) if k else v, heads)


def collapse(v, matrix, heads):
    return head_lanes(nt(jnp.concatenate(split2(v), axis=1), jnp.concatenate([matrix] * 2, axis=1)), heads)


def triangle(count, lower):
    row = lax.broadcasted_iota(jnp.int32, (count, count), 0)
    col = lax.broadcasted_iota(jnp.int32, (count, count), 1)
    keep = (row >= col) if lower else (row <= col)
    return jnp.where(keep, 1.0, 0.0).astype(bf16)


def exact_sums(matrix, v, heads):
    hi, mid, lo = [piece.astype(f32) for piece in split3(v)]
    sums = nn(matrix, (hi + to_group(mid, 1) + to_group(lo, 2)).astype(bf16))
    return from_group(sums, 0, heads) + from_group(sums, 1, heads) + from_group(sums, 2, heads)


def step_sizes(v, heads):
    soft = jnp.maximum(v, 0.0) + jnp.log1p(jnp.exp(-jnp.abs(v)))
    return head_lanes(soft, heads)


def steps_of(block, heads):
    return step_sizes(block, heads), from_group(block, 1, heads)


def segments(positions, lens_ref, pack, count):
    total = jnp.zeros(positions.shape, jnp.int32)
    end = jnp.int32(0)
    for k in range(count):
        end = end + lens_ref[pack, k]
        total = total + jnp.where(positions >= end, 1, 0)
    return total


def column_segments(meta_ref, lens_ref, pack, count, nseq, before):
    rows = lax.broadcasted_iota(jnp.int32, (count + before, 1), 0)
    return segments(rows + (meta_ref[0] * count - before), lens_ref, pack, nseq)


def row_segments(meta_ref, lens_ref, pack, count, nseq):
    cols = lax.broadcasted_iota(jnp.int32, (1, count), 1)
    return segments(cols + meta_ref[0] * count, lens_ref, pack, nseq)


def carry_column(meta_ref, seg_ext, before):
    same = seg_ext[before:] == seg_ext[before - 1 : before]
    return jnp.where(same & (meta_ref[0] > 0), 1.0, 0.0)


def to_int16(v):
    return jnp.floor(v + 0.5).astype(jnp.int32).astype(jnp.int16)


def encode_state(out, p, state, decay, heads, size):
    lane = lax.broadcasted_iota(jnp.int32, (1, LANES), 1)
    powers = jnp.zeros((1, LANES), f32)
    for h in range(heads):
        part = state[h * size : (h + 1) * size]
        top = jnp.max(jnp.max(jnp.abs(part), axis=0, keepdims=True), axis=1, keepdims=True)
        power = jnp.ceil(jnp.log(jnp.maximum(top, 1e-30)) / LN2)
        powers = powers + jnp.where(lane == h, power, 0.0)
        codes = jnp.clip(part * (jnp.exp(-power * LN2) * STEPS), -32767.0, 32767.0)
        out[p, h * size : (h + 1) * size, :] = to_int16(codes)
    row = lax.broadcasted_iota(jnp.int32, (EDGE, LANES), 0)
    coarse = jnp.floor(decay * UNIT)
    fine = (decay * UNIT - coarse) * UNIT
    tail = jnp.where(row == 0, powers, jnp.where(row == 1, coarse, jnp.where(row == 2, fine, 0.0)))
    out[p, heads * size :, :] = to_int16(tail)


def decode_state(block, heads, size):
    values = block.astype(jnp.int32).astype(f32)
    tail = values[heads * size :]
    scale = jnp.exp(tail[0:1] * LN2) / STEPS
    decay = (tail[1:2] + tail[2:3] / UNIT) / UNIT
    return scaled_state(values[: heads * size], scale, heads, size), decay


def sigmoid(v):
    return 1.0 / (1.0 + jnp.exp(-v))


def scaled_state(state, decay, heads, size):
    return jnp.concatenate(
        [state[h * size : (h + 1) * size] * decay[:, h : h + 1] for h in range(heads)], axis=0
    )


def tail_kernel(meta, tokens, out):
    lane = lax.broadcasted_iota(jnp.int32, out.shape, 1)
    total = jnp.zeros(out.shape, f32)
    for p in range(tokens.shape[0]):
        moved = pltpu.roll(tokens[p].astype(f32), (p + 1) * EDGE, 1)
        total = jnp.where((lane >= p * EDGE) & (lane < (p + 1) * EDGE), moved, total)
    out[...] = total.astype(bf16)


def wide_row(ref, lanes=LANES):
    row = ref[...].astype(f32)[None, :]
    blank = lanes - row.shape[1]
    return jnp.concatenate([row, jnp.zeros((1, blank), f32)], axis=1) if blank else row


def prepare_kernel(dims, *refs):
    packs, count, features, inner, bc, heads, size, width, nseq = dims
    (
        wbc, conv_bc, bias_bc, norm_gain, wdt, conv_x, bias_x, dt_bias, a_log, d_skip, gate_gain, wout,
        wout_o, shared_o, wbc_o, wdt_o, wdt_rows_o, conv_x_o, conv_bc_o, small_o, skip_o, gate_gain_o, gain_o,
    ) = refs
    bc_part, part = bc // 4, features // 4
    wout_o[...] = jnp.transpose(wout[...])
    taps = conv_bc[...].astype(f32)
    bias = wide_row(bias_bc, bc_part)
    gain = wide_row(norm_gain, part)
    pieces = [gain[:, c * bc_part : (c + 1) * bc_part] for c in range(part // bc_part)]
    rows = jnp.concatenate([taps, bias] + pieces, axis=0)
    rows = jnp.concatenate([rows, jnp.zeros((LANES - rows.shape[0], bc_part), f32)], axis=0)
    rows = jnp.concatenate([rows, jnp.zeros((LANES, LANES - bc_part), f32)], axis=1)
    extra = jnp.transpose(rows)[:bc_part].astype(bf16)
    shared_o[:, :features] = wbc[...]
    shared_o[:, features:] = extra
    wbc_o[...] = jnp.transpose(wbc[...].astype(f32)).astype(bf16)
    dt_rows = jnp.concatenate(
        [wdt[...].astype(f32), jnp.zeros((LANES - heads, features), f32)], axis=0
    )
    wdt_rows_o[...] = dt_rows.astype(bf16)
    wdt_o[...] = jnp.transpose(dt_rows).astype(bf16)
    blank = jnp.zeros((7 - width, inner), f32)
    conv_x_o[...] = jnp.concatenate(
        [conv_x[...].astype(f32), wide_row(bias_x, inner), blank], axis=0
    )
    conv_bc_o[...] = jnp.concatenate([taps, bias, blank[:, :bc_part]], axis=0)
    small_o[...] = jnp.concatenate(
        [wide_row(dt_bias), wide_row(a_log), jnp.zeros((6, LANES), f32)], axis=0
    )
    skips = jnp.concatenate([wide_row(d_skip), jnp.zeros((7, LANES), f32)], axis=0)
    matrix = spread_matrix(heads, size)
    skip_o[...] = sum(nn(piece, matrix) for piece in split3(skips))[0:1]
    gate_gain_o[...] = wide_row(gate_gain, inner)
    column = jnp.concatenate([gain, jnp.zeros((LANES - 1, part), f32)], axis=0)
    column = jnp.concatenate([column, jnp.zeros((LANES, 2 * LANES - part), f32)], axis=1)
    gain_o[...] = jnp.transpose(column)[:part, 0:1]


def normalise(values, gain, features):
    mean = jnp.sum(values * values, axis=0, keepdims=True) / features
    inv = lax.rsqrt(mean + EPSILON)
    return inv, ((values * inv) * gain).astype(bf16)


def raw_rows(normed, wx, wbc):
    return jnp.concatenate([nn(normed, wx), nt(normed, wbc)], axis=1).astype(bf16)


def border_kernel(dims, meta, *refs):
    packs, count, features, inner, bc, heads, size, width, nseq = dims
    edges, shared = refs[0:4], refs[4:8]
    wx, conv_x, wbc_o, conv_o, gain_o, edge_o, raws_o, stage, weights = refs[8:]
    head = meta[1]
    part, bc_part = features // 4, bc // 4
    for k in range(4):
        weights[head ^ k] = shared[k][...]
        stage[head ^ k] = edges[k][...]
    whole = weights[...].reshape(bc, weights.shape[2])
    wbc_o[...] = whole[:, :features]
    extra = whole[:, features:].astype(f32)
    conv_o[:, :inner] = conv_x[...]
    conv_o[:, inner:] = jnp.transpose(extra)[0:8]
    for h in range(4):
        for c in range(part // bc_part):
            gain_o[h * part + c * bc_part : h * part + (c + 1) * bc_part, :] = extra[
                h * bc_part : (h + 1) * bc_part, width + 1 + c : width + 2 + c
            ]
    _, normed = normalise(stage[...].reshape(features, stage.shape[2]).astype(f32), gain_o[...], features)
    edge_o[...] = normed
    raws_o[...] = raw_rows(jnp.transpose(normed), wx[...], wbc_o[...]).astype(f32)


def front_kernel(dims, keep, meta, lens, *refs):
    packs, count, features, inner, bc, heads, size, width, nseq = dims
    tokens, refs = refs[0:4], refs[4:]
    wx, wbc, wdt, conv, small, gain, edge_raws, *refs = refs
    normed_o, inv_o, rawx_o, rawbc_o, xbc_o, steps_o, state_o, stage, raws = refs[-9:]
    side = meta[0] & 1 if keep else 1 - (meta[0] & 1)
    pack = order.pack + (packs // 2) * side
    head = meta[1]
    for k in range(4):
        stage[head ^ k] = tokens[k][0]
    inv, normed_t = normalise(stage[...].reshape(features, count).astype(f32), gain[...], features)
    inv_o[0] = inv
    normed_o[0] = normed_t
    normed = jnp.transpose(normed_t)
    raws[EDGE:, :] = raw_rows(normed, wx[...], wbc[...]).astype(f32)
    raws[0:EDGE, :] = edge_raws[pl.ds(pl.multiple_of(pack * EDGE, EDGE), EDGE), :]

    def own_bc(values):
        bc_part = bc // 4
        parts = [values[:, inner + h * bc_part : inner + (h + 1) * bc_part] for h in range(4)]
        low = jnp.where((head & 1) == 0, parts[0], parts[1])
        high = jnp.where((head & 1) == 0, parts[2], parts[3])
        return jnp.where((head >> 1) == 0, low, high)

    rawx_o[0] = raws[:, :inner].astype(bf16)
    rawbc_o[0] = own_bc(raws[...]).astype(bf16)
    seg = column_segments(meta, lens, pack, count, nseq, EDGE)
    seg_main = seg[EDGE:]
    pre = convolved(raws, conv, seg, count, width)
    xbc = (pre * sigmoid(pre)).astype(bf16)
    xbc_o[0] = xbc
    v = head_lanes(nt(normed, wdt[...]).astype(bf16).astype(f32) + small[0:1, :], heads)
    dt = step_sizes(v, heads)
    rate = -dt * jnp.exp(small[1:2, :])
    cum = exact_sums(triangle(count, True), rate, heads)
    steps_o[0] = v + to_group(cum, 1)
    cum_end = cum[count - 1 : count]
    weight = jnp.where(seg_main == seg[count + EDGE - 1 :], jnp.exp(cum_end - cum), 0.0) * dt
    matrix = spread_matrix(heads, size)
    scaled = (xbc[:, :inner].astype(f32) * spread(weight, matrix, heads)).astype(bf16)
    state = jnp.transpose(nn(jnp.transpose(xbc[:, inner : inner + bc // 2]), scaled))
    carry = carry_column(meta, seg, EDGE)
    encode_state(state_o, 0, state, carry[count - 1 :] * jnp.exp(cum_end), heads, size)


def convolved(raws, conv, seg, count, width):
    pre = jnp.broadcast_to(conv[width : width + 1, :], (count, raws.shape[1]))
    for k in range(width):
        low = EDGE - (width - 1) + k
        mask = jnp.where(seg[low : low + count] == seg[EDGE:], 1.0, 0.0)
        pre = pre + conv[k : k + 1, :] * raws[low : low + count, :] * mask
    return pre


def gate_slope_kernel(dims, meta, lens, *refs):
    packs, count, features, inner, bc, heads, size, width, nseq = dims
    normed, wz, raw_x, raw_bc, conv_x, conv_bc, gate_o, slope_x_o, slope_bc_o, raws, raws_bc = refs
    pack = order.pack
    gate_o[0] = tn(normed[0], wz[...]).astype(bf16)
    seg = column_segments(meta, lens, pack, count, nseq, EDGE)
    for raw, wide, conv, out in ((raw_x, raws, conv_x, slope_x_o), (raw_bc, raws_bc, conv_bc, slope_bc_o)):
        wide[...] = raw[0].astype(f32)
        pre = convolved(wide, conv, seg, count, width)
        sig = sigmoid(pre)
        out[0] = sig * (1.0 + pre * (1.0 - sig))


def store_state(meta, packs, pack, keep_o, send_o, state, decay, heads, size):
    mine = (pack // (packs // 2)) == (meta[0] & 1)

    @pl.when(mine)
    def _():
        encode_state(keep_o, 0, state, decay, heads, size)

    @pl.when(jnp.logical_not(mine))
    def _():
        encode_state(send_o, 0, state, decay, heads, size)


def load_state(meta, packs, pack, keep, recv, heads, size):
    mine = (pack // (packs // 2)) == (meta[0] & 1)
    block = jnp.where(mine, keep[0].astype(jnp.int32), recv[0].astype(jnp.int32))
    return decode_state(block, heads, size)[0]


def decay_parts(cum_col, cum_row, masked):
    return masked * jnp.exp(jnp.minimum(cum_col - cum_row, 0.0))


def block_mask(meta, lens, pack, count, nseq):
    col = column_segments(meta, lens, pack, count, nseq, 0)
    row = row_segments(meta, lens, pack, count, nseq)
    tri = lax.broadcasted_iota(jnp.int32, (count, count), 0) >= lax.broadcasted_iota(
        jnp.int32, (count, count), 1
    )
    return tri & (col == row)


def inner_kernel(dims, meta, lens, *refs):
    packs, count, features, inner, bc, heads, size, width, nseq = dims
    xbc, steps, inner_o = refs
    pack = order.pack
    half = bc // 2
    b_vals, c_vals = xbc[0, :, inner : inner + half], xbc[0, :, inner + half :]
    scores = jnp.where(block_mask(meta, lens, pack, count, nseq), nt(c_vals, b_vals), 0.0)
    dt, cum_col = steps_of(steps[0], heads)
    cum_row = jnp.transpose(cum_col)
    dt_row = jnp.transpose(dt)
    lane = lax.broadcasted_iota(jnp.int32, (count, 2 * size), 1)
    for pair in range(heads // 2):
        cols = slice(2 * pair * size, (2 * pair + 2) * size)
        x_pair = xbc[0, :, cols]
        parts = []
        for h in (2 * pair, 2 * pair + 1):
            weights = decay_parts(cum_col[:, h : h + 1], cum_row[h : h + 1], scores)
            parts.append(nn((weights * dt_row[h : h + 1]).astype(bf16), x_pair))
        inner_o[0, :, cols] = jnp.where(lane < size, parts[0], parts[1])


def cot_kernel(dims, meta, lens, *refs):
    packs, count, features, inner, bc, heads, size, width, nseq = dims
    pieces, (wout, cot_o, gg_o, stage) = refs[:4], refs[4:]
    for k in range(4):
        stage[meta[1] ^ k] = pieces[k][0]
    cotangent = stage[...].reshape(features, count)
    cot_o[0] = cotangent
    gg_o[0] = jnp.transpose(nn(wout[...], cotangent))


def compose(lower, upper, heads, size):
    return scaled_state(lower[0], upper[1], heads, size) + upper[0], lower[1] * upper[1]


def choose(flag, a, b):
    return jnp.where(flag, a[0], b[0]), jnp.where(flag, a[1], b[1])


def pair_kernel(dims, rev, meta, own, other, out):
    packs, heads, size = dims
    upper_is_own = ((meta[0] & 1) ^ rev) == 1
    for p in range(packs // 2):
        a, b = decode_state(own[p], heads, size), decode_state(other[p], heads, size)
        both = compose(choose(upper_is_own, b, a), choose(upper_is_own, a, b), heads, size)
        encode_state(out, p, *both, heads, size)


def entering_from(before, b, p, heads, size):
    if before is None:
        return (jnp.zeros_like(b[0]), jnp.ones_like(b[1])), b
    entering = decode_state(before[p], heads, size)
    return entering, compose(b, entering, heads, size)


def cube_kernel(dims, rev, bit, first, meta, *refs):
    packs, heads, size = dims
    total, other = refs[0], refs[1]
    before, next_o, before_o = (None, refs[2], refs[3]) if first else refs[2:5]
    upper_is_own = (((meta[0] >> bit) & 1) ^ rev) == 1
    for p in range(packs // 2):
        a, b = decode_state(total[p], heads, size), decode_state(other[p], heads, size)
        both = compose(choose(upper_is_own, b, a), choose(upper_is_own, a, b), heads, size)
        encode_state(next_o, p, *both, heads, size)
        entering, longer = entering_from(before, b, p, heads, size)
        encode_state(before_o, p, *choose(upper_is_own, longer, entering), heads, size)


def last_kernel(dims, rev, bit, first, meta, *refs):
    packs, heads, size = dims
    own, pair, other = refs[0:3]
    before, keep_o, send_o = (None, refs[3], refs[4]) if first else refs[3:6]
    add = (((meta[0] >> bit) & 1) ^ rev) == 1
    upper_is_own = ((meta[0] & 1) ^ rev) == 1
    for p in range(packs // 2):
        entering, longer = entering_from(
            before, decode_state(other[p], heads, size), p, heads, size
        )
        low = choose(add, longer, entering)
        lower = decode_state(jnp.where(upper_is_own, pair[p].astype(jnp.int32), own[p].astype(jnp.int32)), heads, size)
        high = compose(low, lower, heads, size)
        encode_state(keep_o, p, *choose(upper_is_own, high, low), heads, size)
        encode_state(send_o, p, *choose(upper_is_own, low, high), heads, size)


def gate_kernel(dims, meta, lens, *refs):
    packs, count, features, inner, bc, heads, size, width, nseq = dims
    xbc, steps, inner_in, keep, recv, gate, gg, gain, skip, y_o, stats_o = refs
    pack = order.pack
    state = jnp.concatenate(
        split2(load_state(meta, packs, pack, keep, recv, heads, size)), axis=1
    )
    carry = carry_column(meta, column_segments(meta, lens, pack, count, nseq, EDGE), EDGE)
    matrix = spread_matrix(heads, size)
    entering = spread(carry * jnp.exp(from_group(steps[0], 1, heads)), matrix, heads)
    c_vals = xbc[0, :, inner + bc // 2 :]
    y = inner_in[0] + entering * nt(jnp.concatenate([c_vals, c_vals], axis=1), state)
    y_o[0] = y
    gate_f = gate[0].astype(f32)
    ssd = y + xbc[0, :, :inner].astype(f32) * skip[...]
    mixed = ssd * (gate_f * sigmoid(gate_f))
    squares = jnp.sum(mixed * mixed, axis=1, keepdims=True)
    dots = jnp.sum(gain[...] * gg[0] * mixed, axis=1, keepdims=True)
    lane = lax.broadcasted_iota(jnp.int32, (count, LANES), 1)
    both = jnp.where(lane == 0, squares, 0.0) + jnp.where(lane == 1, dots, 0.0)
    stats_o[0] = jnp.transpose(both)[0:2]


def grad_kernel(dims, total_inner, meta, lens, *refs):
    packs, count, features, inner, bc, heads, size, width, nseq = dims
    (
        stats, near, far, diagonal, xbc, steps, y, gate, gg, gain, skip,
        gy_o, gated_o, ggate_o, keep_o, send_o, small_o,
    ) = refs
    pack = order.pack

    @order.first
    def _():
        small_o[...] = jnp.zeros_like(small_o)

    sums = (stats[0] + near[0]) + (far[0] + diagonal[0])
    row = lax.broadcasted_iota(jnp.int32, (LANES, count), 0)
    wide = jnp.where(row == 0, sums[0:1], 0.0) + jnp.where(row == 1, sums[1:2], 0.0)
    cols = jnp.transpose(wide)
    inv = lax.rsqrt(cols[:, 0:1] / total_inner + EPSILON)
    dot = cols[:, 1:2] / total_inner
    x_f, gg_f, gate_f = xbc[0, :, :inner].astype(f32), gg[0], gate[0].astype(f32)
    ssd = y[0] + x_f * skip[...]
    sig = sigmoid(gate_f)
    act = gate_f * sig
    mixed = ssd * act
    scaled = mixed * inv
    gated_o[0] = (scaled * gain[...]).astype(bf16)
    grad_mixed = inv * gain[...] * gg_f - mixed * (inv * inv * inv * dot)
    gy_f = grad_mixed * act
    gy_o[0] = gy_f
    ggate_o[0] = (grad_mixed * ssd * sig * (1.0 + gate_f * (1.0 - sig))).astype(bf16)
    carry = carry_column(meta, column_segments(meta, lens, pack, count, nseq, EDGE), EDGE)
    cum = from_group(steps[0], 1, heads)
    entering = carry * jnp.exp(cum)
    ey_hi, ey_lo = split2(gy_f * spread(entering, spread_matrix(heads, size), heads))
    c_rows = jnp.transpose(xbc[0, :, inner + bc // 2 :])
    state_grad = jnp.transpose(nn(c_rows, ey_hi) + nn(c_rows, ey_lo))
    small_o[0:1, :] += jnp.sum(gg_f * scaled, axis=0, keepdims=True)
    small_o[1:2, :] += jnp.sum(gy_f * x_f, axis=0, keepdims=True)
    return lambda: store_state(
        meta, packs, pack, keep_o, send_o, state_grad, entering[count - 1 :], heads, size
    )


def diag_kernel(dims, meta, lens, *refs):
    packs, count, features, inner, bc, heads, size, width, nseq = dims
    xbc, steps, gy, y, keep, recv, dx_o, dbc_o, sums_o = refs
    pack = order.pack
    half = bc // 2
    b_vals, c_vals = xbc[0, :, inner : inner + half], xbc[0, :, inner + half :]
    col = column_segments(meta, lens, pack, count, nseq, 0)
    row = row_segments(meta, lens, pack, count, nseq)
    mask = (col == row) & (
        lax.broadcasted_iota(jnp.int32, (count, count), 0)
        <= lax.broadcasted_iota(jnp.int32, (count, count), 1)
    )
    scores = jnp.where(mask, nt(b_vals, c_vals), 0.0)
    dt, cum_col = steps_of(steps[0], heads)
    cum_row = jnp.transpose(cum_col)
    lane = lax.broadcasted_iota(jnp.int32, (count, 2 * size), 1)
    grad_scores = jnp.zeros((count, count), f32)
    zero = jnp.zeros((), bf16)
    for pair in range(heads // 2):
        cols = slice(2 * pair * size, (2 * pair + 2) * size)
        x_pair = xbc[0, :, cols]
        x_twice = jnp.concatenate([x_pair, x_pair], axis=1)
        gy_hi, gy_lo = split2(gy[0, :, cols])
        gy_wide = jnp.concatenate([gy_hi, gy_lo], axis=1)
        parts = []
        for h in (2 * pair, 2 * pair + 1):
            own = (lane < size) if h % 2 == 0 else (lane >= size)
            part = jnp.exp(jnp.minimum(cum_row[h : h + 1] - cum_col[:, h : h + 1], 0.0)) * dt[:, h : h + 1]
            parts.append(nn((scores * part).astype(bf16), gy_wide))
            both = jnp.concatenate([jnp.where(own, gy_hi, zero), jnp.where(own, gy_lo, zero)], axis=1)
            grad_scores = grad_scores + nt(x_twice, both) * part
        two = [part[:, : 2 * size] + part[:, 2 * size :] for part in parts]
        dx_o[0, :, cols] = jnp.where(lane < size, two[0], two[1])
    hi, lo = split2(jnp.where(mask, grad_scores, 0.0))
    state_hi, state_lo = split2(load_state(meta, packs, pack, keep, recv, heads, size))
    carry = carry_column(meta, column_segments(meta, lens, pack, count, nseq, EDGE), EDGE)
    matrix = spread_matrix(heads, size)
    ey_hi, ey_lo = split2(gy[0] * spread(carry * jnp.exp(cum_col), matrix, heads))
    dbc_o[0, :, :half] = nn(
        jnp.concatenate([hi, lo], axis=1), jnp.concatenate([c_vals, c_vals], axis=0)
    )
    b_rows = jnp.transpose(b_vals)
    dbc_o[0, :, half:] = (
        jnp.transpose(nn(b_rows, hi) + nn(b_rows, lo))
        + nn(ey_hi, state_hi) + nn(ey_hi, state_lo) + nn(ey_lo, state_hi)
    )
    row_sum = collapse(gy[0] * y[0], matrix, heads)
    col_sum = collapse(xbc[0, :, :inner].astype(f32) * dx_o[0], matrix, heads)
    sums_o[0] = row_sum + to_group(col_sum, 1)


def scatter_pieces(head, stage, own_o, far_o, send_o):
    own_o[0] = stage[head]
    send_o[0, 0] = stage[head ^ 1].astype(bf16)
    far_o[0] = stage[head ^ 2]
    send_o[0, 1] = stage[head ^ 3].astype(bf16)


def accumulate(meta, pack, packs, sums, term, keep_o, send_o):
    sums[...] += term.reshape(sums.shape)

    def finish():
        @last_pack(pack, packs)
        def _():
            side = meta[0] & 1
            keep_o[...] = sums[side]
            send_o[...] = sums[1 - side].astype(bf16)

    return finish


def last_pack(pack, packs):
    return lambda work: pl.when(pack == packs - 1)(work)


def cleared(*refs):
    @order.first
    def _():
        for ref in refs:
            ref[...] = jnp.zeros_like(ref)


def out_kernel(dims, meta, lens, *refs):
    packs, count, features, inner, bc, heads, size, width, nseq = dims
    gated, cot, wout, own_o, far_o, send_o, keep_o, give_o, stage, sums = refs
    pack = order.pack
    cleared(sums)
    stage[...] = nt(wout[...], gated[0]).reshape(stage.shape)
    scatter_pieces(meta[1], stage, own_o, far_o, send_o)
    return accumulate(meta, pack, packs, sums, nn(cot[0], gated[0]), keep_o, give_o)


def gain_row(weights, grads):
    part = jnp.sum(weights.astype(f32) * grads, axis=1, keepdims=True)
    return jnp.transpose(jnp.broadcast_to(part, (part.shape[0], LANES)))[0:8]


def z_kernel(dims, meta, lens, *refs):
    normed, ggate, wz, keep_o, give_o, gain_o, sums = refs
    pack = order.pack
    cleared(sums)
    store = accumulate(meta, pack, dims[0], sums, nn(normed[0], ggate[0]), keep_o, give_o)

    def finish():
        store()

        @last_pack(pack, dims[0])
        def _():
            gain_o[...] = gain_row(wz[...], sums[...].reshape(wz.shape))

    return finish


def end_weights(seg, seg_main, cum_col, dt_col, count):
    cum_end = cum_col[count - 1 :]
    end = seg[count + EDGE - 1 :]
    return jnp.where(seg_main == end, jnp.exp(cum_end - cum_col), 0.0) * dt_col


def share_kernel(dims, meta, lens, *refs):
    packs, count, features, inner, bc, heads, size, width, nseq = dims
    (
        xbc, steps, dbc, gkeep, grecv, gy, dx, slope, conv, skip,
        own_o, near_o, grad_o, state_sum_o, edge_o,
        gpad,
    ) = refs
    pack = order.pack
    half, quarter = bc // 2, bc // 4
    g_hi, g_lo = split2(load_state(meta, packs, pack, gkeep, grecv, heads, size))
    seg = column_segments(meta, lens, pack, count, nseq, EDGE)
    dt, cum = steps_of(steps[0], heads)
    matrix = spread_matrix(heads, size)
    wide = spread(end_weights(seg, seg[EDGE:], cum, dt, count), matrix, heads)
    x_f = xbc[0, :, :inner].astype(f32)
    hi, lo = split2(wide * x_f)
    grad_b = dbc[0, :, :half] + nn(hi, g_hi) + nn(lo, g_hi) + nn(hi, g_lo)
    grad_c = dbc[0, :, half:]
    even = jnp.concatenate([grad_b[:, :quarter], grad_c[:, :quarter]], axis=1)
    odd = jnp.concatenate([grad_b[:, quarter:], grad_c[:, quarter:]], axis=1)
    first = (meta[1] & 1) == 0
    own_o[0] = jnp.where(first, even, odd)
    near_o[0] = jnp.where(first, odd, even)
    b_vals = xbc[0, :, inner : inner + half]
    u_wide = wide * nt(
        jnp.concatenate([b_vals, b_vals], axis=1), jnp.concatenate([g_hi, g_lo], axis=1)
    )
    state_sum_o[0] = collapse(x_f * u_wide, matrix, heads)
    grad_x = (dx[0] + u_wide + gy[0] * skip[...]) * slope[0]
    grad_o[0] = grad_x
    gpad[:EDGE, :] = jnp.zeros((EDGE, inner), f32)
    gpad[EDGE:, :] = grad_x[:EDGE]
    edge_o[0] = conv_rows(gpad, conv, seg, EDGE, width).astype(bf16)


def middle_kernel(dims, meta, *refs):
    packs, quarter = dims
    own, near, keep_o, send_o = refs
    half = packs // 2
    first = (meta[1] >> 1) == 0
    for p in range(half):
        a, b = own[p] + near[p], own[p + half] + near[p + half]
        low = jnp.concatenate([a[:, :quarter], b[:, :quarter]], axis=1)
        high = jnp.concatenate([a[:, quarter:], b[:, quarter:]], axis=1)
        keep_o[p] = jnp.where(first, low, high)
        send_o[p] = jnp.where(first, high, low)


def conv_taps(grads, raws, gconv_o, seg, count, width):
    seg_main = seg[EDGE : EDGE + count]
    for k in range(width):
        low = EDGE - (width - 1) + k
        mask = jnp.where(seg[low : low + count] == seg_main, 1.0, 0.0)
        gconv_o[k : k + 1, :] += jnp.sum(
            grads * (raws[low : low + count, :] * mask), axis=0, keepdims=True
        )
    gconv_o[width : width + 1, :] += jnp.sum(grads, axis=0, keepdims=True)


def conv_rows(gpad, conv, seg, rows, width):
    total = jnp.zeros((rows, gpad.shape[1]), f32)
    for lag in range(width):
        mask = jnp.where(seg[lag : lag + rows] == seg[:rows], 1.0, 0.0)
        k = width - 1 - lag
        total = total + conv[k : k + 1, :] * (gpad[lag : lag + rows, :] * mask)
    return total


def step_kernel(dims, meta, lens, *refs):
    packs, count, features, inner, bc, heads, size, width, nseq = dims
    (
        steps, sums, state_sums, keep, recv, gkeep, grecv, small, normed, wdt,
        gdt_o, gdt_rows_o, gsmall_o, gain_o,
        gdt_sums,
    ) = refs
    group, half = pl.program_id(0), packs // 2
    matrix = spread_matrix(heads, size)
    ones = jnp.ones((8, LANES), bf16)
    decay_rate = -jnp.exp(small[1:2, :])
    upper = triangle(count, False)
    rows = lax.broadcasted_iota(jnp.int32, (count, LANES), 0)
    mine = group == (meta[0] & 1)
    bias_sum, rate_sum = jnp.zeros((1, LANES), f32), jnp.zeros((1, LANES), f32)
    term = jnp.zeros((features, LANES), f32)
    for j in range(half):
        pick = lambda a, b: jnp.where(mine, a[j].astype(jnp.int32), b[j].astype(jnp.int32))
        state = decode_state(pick(keep, recv), heads, size)[0]
        gstate = decode_state(pick(gkeep, grecv), heads, size)[0]
        seg = column_segments(meta, lens, group * half + j, count, nseq, EDGE)
        v = steps[j]
        dt, cum = steps_of(v, heads)
        sig = head_lanes(sigmoid(v), heads)
        row_sum, col_sum = from_group(sums[j], 0, heads), from_group(sums[j], 1, heads)
        state_sum = state_sums[j]
        carry = carry_column(meta, seg, EDGE)
        hi, lo = split2(gstate * state)
        by_head = collapse(nt(ones, hi) + nt(ones, lo), matrix, heads)[0:1]
        last = by_head * carry[count - 1 :] * jnp.exp(cum[count - 1 :]) + jnp.sum(
            state_sum, axis=0, keepdims=True
        )
        grad_cum = row_sum - col_sum - state_sum + jnp.where(rows == count - 1, last, 0.0)
        grad_rate = exact_sums(upper, grad_cum, heads)
        ratio = jnp.where(dt > 1e-30, sig / jnp.maximum(dt, 1e-30), 1.0)
        grad_dt = head_lanes(ratio * (col_sum + state_sum) + grad_rate * decay_rate * sig, heads)
        low = grad_dt.astype(bf16)
        gdt_o[j] = low
        bias_sum = bias_sum + jnp.sum(grad_dt, axis=0, keepdims=True)
        rate_sum = rate_sum + jnp.sum(grad_rate * dt * decay_rate, axis=0, keepdims=True)
        term = term + nn(normed[j], low)

    @pl.when(group == 0)
    def _():
        gsmall_o[...] = jnp.zeros_like(gsmall_o)
        gdt_sums[...] = jnp.zeros_like(gdt_sums)

    gsmall_o[0:1, :] += bias_sum
    gsmall_o[1:2, :] += rate_sum
    gdt_sums[...] += term

    @pl.when(group == packs // half - 1)
    def _():
        gdt_rows_o[...] = jnp.transpose(gdt_sums[...])[0:8]
        gain_o[...] = gain_row(wdt[...], gdt_sums[...])


def xback_kernel(dims, meta, lens, *refs):
    packs, count, features, inner, bc, heads, size, width, nseq = dims
    (
        grads, raw, normed, edge, edge_x, conv, wx,
        main_o, keep_o, give_o, gconv_o, gain_o,
        gpad, raws, sums, rows_x,
    ) = refs
    pack = order.pack
    seg = column_segments(meta, lens, pack, count, nseq, EDGE)

    cleared(gconv_o, rows_x, sums)
    raws[...] = raw[0].astype(f32)
    gpad[:count, :] = grads[0]
    gpad[count:, :] = jnp.zeros((EDGE, inner), f32)
    conv_taps(grads[0], raws, gconv_o, seg, count, width)
    seg_pad = jnp.concatenate([seg[EDGE:], jnp.full((8, 1), -1, jnp.int32)], axis=0)
    main = conv_rows(gpad, conv, seg_pad, count, width).astype(bf16)
    main_o[0] = main
    rows_x[pl.ds(pl.multiple_of(pack * EDGE, EDGE), EDGE), :] = edge_x[0]
    sums[...] += nn(normed[0], main).reshape(sums.shape)

    def finish():
        @last_pack(pack, packs)
        def _():
            sums[...] += nn(edge[...], rows_x[...]).reshape(sums.shape)
            side = meta[0] & 1
            keep_o[...] = sums[side]
            give_o[...] = sums[1 - side].astype(bf16)
            gain_o[...] = gain_row(wx[...], sums[...].reshape(wx.shape))

    return finish


def conv_bc_kernel(dims, meta, lens, *refs):
    packs, count, features, inner, bc, heads, size, width, nseq = dims
    (
        keep, recv, slope, raw, normed, edge, wbc, conv, edge_x,
        gconv_x, gdt_rows, gsmall, gate_small, gain_z, gain_x, gain_dt, gain,
        rows_o, edges_o, give_o, small_o,
        gpad, raws, sums, edge_bc, gconv,
    ) = refs
    pack = order.pack
    quarter = bc // 4

    cleared(gconv, edge_bc, sums)
    gpad[:EDGE, :] = jnp.zeros((EDGE, quarter), f32)
    gpad[EDGE + count :, :] = jnp.zeros((EDGE, quarter), f32)
    both = keep[0] + recv[0]
    grad = jnp.where(pack < packs // 2, both[:, :quarter], both[:, quarter:]) * slope[0]
    seg = column_segments(meta, lens, pack, count, nseq, EDGE)
    raws[...] = raw[0].astype(f32)
    gpad[EDGE : EDGE + count, :] = grad
    conv_taps(grad, raws, gconv, seg, count, width)
    seg_pad = jnp.concatenate([seg, jnp.full((8, 1), -1, jnp.int32)], axis=0)
    grad_raw = conv_rows(gpad, conv, seg_pad, count + EDGE, width).astype(bf16)
    rows_o[0] = grad_raw[EDGE:]
    edge_bc[pl.ds(pl.multiple_of(pack * EDGE, EDGE), EDGE), :] = grad_raw[:EDGE]
    edges_o[0, :, :inner] = edge_x[0]
    blank = jnp.zeros((EDGE, LANES - quarter), bf16)
    edges_o[0, :, inner:] = jnp.concatenate([grad_raw[:EDGE], blank], axis=1)
    sums[...] += nn(normed[0], grad_raw[EDGE:])

    def finish():
        @last_pack(pack, packs)
        def _():
            total = sums[...] + nn(edge[...], edge_bc[...])
            rows = jnp.transpose(total)
            taps = width + 1
            give_o[:quarter, :] = rows[:, :inner].astype(bf16)
            give_o[quarter : 2 * quarter, :] = rows[:, inner:].astype(bf16)
            small_o[...] = jnp.zeros_like(small_o)
            for h in range(heads):
                small_o[2 * h : 2 * h + 1, :] = gdt_rows[h : h + 1, :inner]
                small_o[2 * h + 1 : 2 * h + 2, :] = gdt_rows[h : h + 1, inner:]
            row = 2 * heads
            small_o[row : row + taps, :] = gconv_x[:taps, :]
            row += taps
            small_o[row : row + 1, :] = gate_small[0:1, :]
            skips = collapse(gate_small[...], spread_matrix(heads, size), heads)
            small_o[row + 1 : row + 2, :] = jnp.concatenate(
                [gsmall[0:1, :], gsmall[1:2, :], skips[1:2, :]], axis=1
            )
            blank_row = jnp.zeros((1, inner - taps * quarter), f32)
            small_o[row + 2 : row + 3, :] = jnp.concatenate(
                [gconv[k : k + 1, :] for k in range(taps)] + [blank_row], axis=1
            )
            gains = gain_row(wbc[...], total)[0:1] + gain_z[0:1, :] + gain_x[0:1, :] + gain_dt[0:1, :]
            gains = gains / jnp.transpose(jnp.broadcast_to(gain[...], (features, LANES)))[0:1]
            small_o[row + 3 : row + 4, :] = gains[:, :inner]
            small_o[row + 4 : row + 5, :] = gains[:, inner:]
            hi, lo = split2(small_o[...])
            give_o[2 * quarter : 2 * quarter + SMALL, :] = hi
            give_o[2 * quarter + SMALL :, :] = lo

    return finish


def back_kernel(dims, meta, lens, *refs):
    packs, count, features, inner, bc, heads, size, width, nseq = dims
    (
        main, edges, ggate, gdt, gbc, normed, wz, wx, wbc, wdt,
        own_o, far_o, send_o, dots_o,
        stage,
    ) = refs
    head = meta[1]
    part, quarter = features // 4, bc // 4
    late = count - EDGE

    def with_edge(rows, edge):
        low = (rows[late:].astype(f32) + edge.astype(f32)).astype(bf16)
        return jnp.concatenate([rows[:late], low], axis=0)

    grad_x = with_edge(main[0], edges[0, :, :inner])
    grad_bc = with_edge(gbc[0], edges[0, :, inner : inner + quarter])
    whole = nt(wz[...], ggate[0]) + nt(wx[...], grad_x) + nt(wbc[...], grad_bc) + nt(wdt[...], gdt[0])
    dots = jnp.sum(whole * normed[0].astype(f32), axis=0, keepdims=True)
    stage[...] = whole.reshape(stage.shape)
    dots_o[0] = dots
    own_o[0] = stage[head]
    far_o[0] = stage[head ^ 2]
    for k in range(2):
        send_o[0, k, :part, :] = stage[head ^ (1 + 2 * k)].astype(bf16)
        send_o[0, k, part:, :] = extra_rows(dots)


def extra_rows(*values):
    row = lax.broadcasted_iota(jnp.int32, (EDGE, values[0].shape[1]), 0)
    total = jnp.zeros(row.shape, f32)
    for i, value in enumerate(values):
        for k, piece in enumerate(split3(value)):
            total = total + jnp.where(row == 3 * i + k, piece.astype(f32), 0.0)
    return total.astype(bf16)


def read_extra(block, i):
    rows = block.astype(f32)
    return rows[3 * i : 3 * i + 1] + rows[3 * i + 1 : 3 * i + 2] + rows[3 * i + 2 : 3 * i + 3]


def gather_kernel(own, far, near, dots, own_o, far_o, dots_o):
    part = own.shape[1]
    own_o[0] = own[0] + near[0, 0, :part, :].astype(f32)
    far_o[0, :part, :] = (far[0] + near[0, 1, :part, :].astype(f32)).astype(bf16)
    both = dots[0] + read_extra(near[0, 0, part:, :], 0)
    dots_o[0] = both
    far_o[0, part:, :] = extra_rows(both)


def final_kernel(dims, own, far, dots, tokens, inv, gain, out_grad, in_grad_o):
    packs, count, features = dims
    part = own.shape[1]
    grad = own[0] + far[0, :part, :].astype(f32)
    mean = (dots[0] + read_extra(far[0, part:, :], 0)) / features
    unit = tokens[0].astype(f32) * inv[0]
    in_grad_o[0] = out_grad[0].astype(f32) + inv[0] * (gain[...] * grad - unit * mean)


def out_gather_kernel(own, far, near, own_o, far_o):
    own_o[0] = own[0] + near[0, 0].astype(f32)
    far_o[0] = (far[0] + near[0, 1].astype(f32)).astype(bf16)


def out_final_kernel(own, far, tokens, out):
    out[0] = (tokens[0].astype(f32) + (own[0] + far[0].astype(f32))).astype(bf16)


def add_kernel(bit, halve, segs, count, small, meta, *refs):
    keep, got, refs = refs[:count], refs[count : 2 * count], refs[2 * count :]
    end = segs[-1] if count > 1 else sum(segs)
    write = 0
    if small:
        small_in, *refs, small_o = refs
        hi, lo = split2(small_in[...])
        mine = hi.astype(f32) + lo.astype(f32)
        theirs = got[-1][end : end + SMALL, :].astype(f32) + got[-1][end + SMALL :, :].astype(f32)
        total = mine + theirs
        small_o[...] = total
        if bit is not None:
            send_o = refs[-1]
            behind = send_o.shape[0] - 2 * SMALL
            hi, lo = split2(total)
            send_o[behind : behind + SMALL, :] = hi
            send_o[behind + SMALL :, :] = lo
    read = 0
    for i, rows in enumerate(segs):
        if count > 1:
            total = keep[i][...] + got[i][:rows, :].astype(f32)
        else:
            total = keep[0][read : read + rows, :].astype(f32) + got[0][read : read + rows, :].astype(f32)
        read += rows
        if halve:
            half = rows // 2
            first = ((meta[0] >> bit) & 1) == 0
            top, bottom = total[:half], total[half:]
            refs[0][write : write + half, :] = jnp.where(first, top, bottom)
            refs[1][write : write + half, :] = jnp.where(first, bottom, top).astype(bf16)
            write += half
        else:
            refs[0][write : write + rows, :] = total.astype(bf16)
            write += rows


def whole_kernel(quarter, keep, got, small, out, small_o):
    total = keep[: 2 * quarter, :].astype(f32) + got[: 2 * quarter, :].astype(f32)
    out[...] = jnp.concatenate([total[:quarter], total[quarter:]], axis=1)
    hi, lo = split2(small[...])
    end = 2 * quarter
    theirs = got[end : end + SMALL, :].astype(f32) + got[end + SMALL :, :].astype(f32)
    small_o[...] = (hi.astype(f32) + lo.astype(f32)) + theirs


def join_kernel(bit, segs, meta, mine, got, out):
    first = ((meta[0] >> bit) & 1) == 0
    read = 0
    for rows in segs:
        a = mine[read : read + rows, :].astype(f32)
        b = got[read : read + rows, :].astype(f32)
        out[2 * read : 2 * read + rows, :] = jnp.where(first, a, b).astype(bf16)
        out[2 * read + rows : 2 * read + 2 * rows, :] = jnp.where(first, b, a).astype(bf16)
        read += rows


def part_kernel(values, out):
    out[0] = values[...].astype(f32)


def result_kernel(segs, ways, meta, mine, got, *outs):
    first = (meta[0] & 1) == 0
    read = 0
    for rows, way, out in zip(segs, ways, outs):
        a = mine[read : read + rows, :].astype(f32)
        b = got[read : read + rows, :].astype(f32)
        top, bottom = jnp.where(first, a, b), jnp.where(first, b, a)
        if way == "rows":
            out[:rows, :] = top
            out[rows:, :] = bottom
        elif way == "flip":
            out[:, :rows] = jnp.transpose(top)
            out[:, rows:] = jnp.transpose(bottom)
        else:
            out[...] = jnp.concatenate([top, bottom], axis=1)
        read += rows


def plus_kernel(a, b, out):
    out[...] = a[...] + b[...]


def unpack_kernel(dims, meta, *refs):
    heads, features, bc_part, width = dims
    smalls, gains, dt_o, taps_x_o, taps_bc_o, bias_x_o, bias_bc_o, dt_bias_o, a_log_o, skip_o, gate_o, gain_o = refs
    for h in range(heads):
        dt_o[h : h + 1, :] = jnp.concatenate(
            [smalls[2 * h : 2 * h + 1, :], smalls[2 * h + 1 : 2 * h + 2, :]], axis=1
        )
    row = 2 * heads
    taps_x_o[...] = smalls[row : row + width, :]
    bias_x_o[...] = smalls[row + width, :]
    row += width + 1
    gate_o[...] = smalls[row, :]
    for k, out in enumerate((dt_bias_o, a_log_o, skip_o)):
        out[...] = smalls[row + 1, k * LANES : k * LANES + heads]
    taps = smalls[row + 2 : row + 3, :]
    for k in range(width):
        taps_bc_o[k : k + 1, :] = taps[:, k * bc_part : (k + 1) * bc_part]
    bias_bc_o[...] = taps[0, width * bc_part : (width + 1) * bc_part]
    both = jnp.concatenate([gains[row + 3 : row + 4, :], gains[row + 4 : row + 5, :]], axis=1)
    part = features // 4
    parts = [both[:, h * part : (h + 1) * part] for h in range(4)]
    low = jnp.where((meta[1] & 1) == 0, parts[0], parts[1])
    high = jnp.where((meta[1] & 1) == 0, parts[2], parts[3])
    gain_o[...] = jnp.where((meta[1] >> 1) == 0, low, high)[0]


class Spec:
    def __init__(self, shape, index, each=True):
        self.shape, self.index, self.each = tuple(shape), index, each

    def block(self, group):
        zeros = (0,) * len(self.shape)
        if not self.each:
            return pl.BlockSpec(self.shape, lambda p, *_: zeros)
        size = group or 1
        return pl.BlockSpec(
            (size,) + self.shape, lambda p, *pre: (self.index(p, pre, bool(group)),) + zeros
        )


def whole_spec(shape):
    return Spec(shape, None, False)


def pack_spec(shape):
    return Spec(shape, lambda p, pre, grouped: p)


def half_spec(shape, half):
    return Spec(shape, lambda p, pre, grouped: 0 if grouped else p % half)


def sided_spec(shape, half, keep):
    def index(p, pre, grouped):
        side = pre[0][0] & 1 if keep else 1 - (pre[0][0] & 1)
        return side if grouped else p + half * side

    return Spec(shape, index)


def side_spec(shape, half, keep):
    def index(p, pre, grouped):
        if grouped:
            return 0
        side = pre[0][0] & 1 if keep else 1 - (pre[0][0] & 1)
        group = p // half
        return jnp.where(group == side, p % half, jnp.where(group < side, 0, half - 1))

    return Spec(shape, index)


class Each:
    def __init__(self, shape, dtype):
        self.shape, self.dtype = tuple(shape), dtype

    def scratch(self, group):
        return pltpu.VMEM(((group,) if group else ()) + self.shape, self.dtype)


class Order:
    def __init__(self):
        self.clear()

    def clear(self):
        self.last, self.near, self.held = (), [], []
        self.pack, self.lane, self.lanes = None, 0, 1

    def first(self, work):
        if self.lane == 0:
            pl.when(self.pack == 0)(work)

    def hold(self, *arrays):
        self.held += arrays

    def drop(self, *arrays):
        self.held = [x for x in self.held if not any(x is y for y in arrays)]

    def placed(self, x):
        return pltpu.with_memory_space_constraint(x, pltpu.VMEM) if self.holds(x) else x

    def holds(self, x):
        return any(x is y for y in self.near)


order = Order()


def call(
    kernel, grid, in_specs, out_specs, out_shape, scratch, prefetch, *args, limit=28, wait=(), us=1,
    out=False, onto=(), group=0,
):
    first = len(prefetch) + len(args)
    args = args + tuple(onto)
    in_specs = list(in_specs) + [pl.BlockSpec(memory_space=pl.ANY)] * len(onto)
    given = len(prefetch) + len(args)
    held = order.last + tuple(wait)
    held += tuple(x for x in order.held if not any(x is y for y in args + held))
    late = len(held)
    single = not isinstance(out_shape, (list, tuple))
    out_specs, out_shape = ([out_specs], [out_shape]) if single else (list(out_specs), list(out_shape))
    token = jax.ShapeDtypeStruct((8, LANES), f32)
    count = len(out_shape)
    results = count if out is True else int(out)

    specs = list(in_specs[: len(in_specs) - len(onto)]) + out_specs
    blocks = lambda items: [x.block(group) if isinstance(x, Spec) else x for x in items]

    def body(*refs):
        ins, rest = refs[:first], refs[given + late :]
        fixed, blocked = ins[: len(prefetch)], (*ins[len(prefetch) :], *rest[:count])
        own = rest[count + 1 :]
        finish = []
        for lane in range(group or 1):
            order.pack, order.lane, order.lanes = pl.program_id(0), lane, group or 1
            views, scratches = blocked, own
            if group:
                order.pack = order.pack * group + lane
                views = [
                    ref.at[pl.ds(lane, 1)] if isinstance(spec, Spec) and spec.each else ref
                    for ref, spec in zip(blocked, specs)
                ]
                scratches = [
                    ref.at[lane] if isinstance(item, Each) else ref for ref, item in zip(own, scratch)
                ]
            finish.append(kernel(*fixed, *views, *scratches))
        for work in finish:
            if work is not None:
                work()

    *outs, order_out = pl.pallas_call(
        body,
        grid_spec=pltpu.PrefetchScalarGridSpec(
            num_scalar_prefetch=len(prefetch),
            grid=grid,
            in_specs=blocks(in_specs) + [pl.BlockSpec(memory_space=pl.ANY)] * late,
            out_specs=blocks(out_specs + [whole_spec(token.shape)]),
            scratch_shapes=[x.scratch(group) if isinstance(x, Each) else x for x in scratch],
        ),
        input_output_aliases={first + i: i for i in range(len(onto))},
        out_shape=[
            x if i < results else pltpu.VMEM(x.shape, x.dtype) for i, x in enumerate(out_shape + [token])
        ],
        compiler_params=pltpu.CompilerParams(vmem_limit_bytes=limit * MIB),
        cost_estimate=pl.CostEstimate(
            flops=int(us * 10e9), bytes_accessed=int(us * 3e6), transcendentals=0
        ),
    )(*[pltpu.with_memory_space_constraint(x, pltpu.VMEM) for x in prefetch], *[order.placed(x) for x in args], *[order.placed(x) for x in held])
    order.last = (order_out,)
    order.near.append(order_out)
    order.near += outs[results:]
    return outs[0] if single else outs


def shape(*dims_and_type):
    return jax.ShapeDtypeStruct(dims_and_type[:-1], dims_and_type[-1])


def scan_states(keep, send, meta, packs, heads, size, rev, beside, waits=lambda: ()):
    dims = (packs, heads, size)
    rows = heads * size
    half = packs // 2
    pay = shape(half, rows + EDGE, LANES, jnp.int16)
    spec = whole_spec(pay.shape)
    bits = (lax.axis_size("seq") - 1).bit_length()
    beside = list(beside)

    def work(newest):
        if beside:
            beside.pop(0)(newest)

    other = swap(send, "seq", 1)
    work(send)
    keep = keep() if callable(keep) else keep
    total = call(
        functools.partial(pair_kernel, dims, rev), (1,), [spec, spec], spec, pay, [], (meta,),
        keep, other,
    )
    before = None
    for bit in range(1, bits):
        got = swap(total, "seq", 1 << bit)
        extra = () if before is None else (before,)
        work(total)
        if bit < bits - 1:
            total, before = call(
                functools.partial(cube_kernel, dims, rev, bit, before is None), (1,),
                [spec] * (2 + len(extra)), [spec, spec], [pay, pay], [], (meta,),
                total, got, *extra,
            )
        else:
            own, back = call(
                functools.partial(last_kernel, dims, rev, bit, before is None), (1,),
                [spec] * (3 + len(extra)), [spec, spec], [pay, pay], [],
                (meta,), keep, other, got, *extra, wait=waits(),
            )
    recv = swap(back, "seq", 1)
    while beside:
        work(back)
    return own, recv


class SeqSum:
    def __init__(self):
        self.keep, self.got, self.segs = [], [], []
        self.small = self.bit = None
        self.bits = list(range(1, (lax.axis_size("seq") - 1).bit_length()))
        self.halved = []

    def put(self, keep, give, segs=None, small=None):
        self.keep.append(keep)
        self.got.append(swap(give, "seq", 1))
        self.segs += segs or [keep.shape[0]]
        self.small = small

    def add(self, meta, us=1, wait=()):
        bit = self.bits.pop(0) if self.bits else None
        halve = bit is not None and all(rows % (2 * EDGE) == 0 for rows in self.segs)
        cols = self.keep[0].shape[1]
        segs = [rows // 2 for rows in self.segs] if halve else self.segs
        rows = sum(segs)
        small = self.small is not None
        behind = 2 * SMALL if small and bit is not None else 0
        low = shape(rows + behind, cols, bf16)
        out = [shape(rows, cols, f32), low] if halve else [low]
        ins = [*self.keep, *self.got]
        if small:
            ins.append(self.small)
            out.append(shape(*self.small.shape, f32))
        outs = call(
            functools.partial(add_kernel, bit, halve, self.segs, len(self.keep), small), (1,),
            [whole_spec(x.shape) for x in ins], [whole_spec(x.shape) for x in out], out, [],
            (meta,), *ins, us=us, wait=wait,
        )
        if small:
            self.small = outs[-1]
        self.segs, self.keep = segs, [outs[0]]
        if bit is None:
            return True
        self.got = [swap(outs[1] if halve else outs[0], "seq", 1 << bit)]
        if halve:
            self.halved.append(bit)
        return False

    def send_back(self):
        self.bit = self.halved.pop() if self.halved else 0
        self.got = [swap(self.keep[0], "seq", 1 << self.bit)]

    def join(self, meta, us=1):
        rows, cols = self.keep[0].shape
        both = shape(2 * rows, cols, bf16)
        spec = whole_spec((rows, cols))
        self.keep = [call(
            functools.partial(join_kernel, self.bit, self.segs), (1,), [spec, spec],
            whole_spec(both.shape), both, [], (meta,), self.keep[0], self.got[0], us=us,
        )]
        self.segs = [2 * rows for rows in self.segs]

    def half_result(self, meta, mine, onto=()):
        rows, cols = self.keep[0].shape

        def index(p, pre, grouped):
            side = pre[0][0] & 1
            return side if mine else 1 - side

        return call(
            lambda meta, values, out: part_kernel(values, out), (1,), [whole_spec((rows, cols))],
            Spec((rows, cols), index), shape(2, rows, cols, f32), [], (meta,),
            self.keep[0] if mine else self.got[0], out=True, us=0.01, onto=onto,
        )

    def result(self, meta, ways, us=0.01):
        cols = self.keep[0].shape[1]
        shapes = {"rows": lambda r: (2 * r, cols), "flip": lambda r: (cols, 2 * r), "cols": lambda r: (r, 2 * cols)}
        out = [shape(*shapes[way](rows), f32) for way, rows in zip(ways, self.segs)]
        spec = whole_spec(self.keep[0].shape)
        return call(
            functools.partial(result_kernel, self.segs, ways), (1,), [spec, spec],
            [whole_spec(x.shape) for x in out], out, [], (meta,), self.keep[0], self.got[0],
            out=True, us=us,
        )


def advance(total, meta, us=1, wait=()):
    if total.bit is None:
        if total.add(meta, us, wait):
            total.send_back()
    elif total.bit:
        total.join(meta, us)
        total.send_back()


def shards(
    tokens_in, out_grad, lengths, norm_gain, proj_z, proj_x, proj_bc, proj_dt, conv_x, conv_bc,
    bias_x, bias_bc, dt_bias, a_log, d_skip, gate_gain, proj_out,
):
    packs, count, part = tokens_in.shape
    features, inner = proj_x.shape
    heads = proj_dt.shape[1]
    size = inner // heads
    width = conv_x.shape[0]
    nseq = lengths.shape[1]
    bc_part = proj_bc.shape[1]
    bc = bc_part * lax.axis_size("head")
    half = packs // 2
    chans = inner + bc
    ext = count + EDGE
    rows = heads * size
    total_inner = inner * lax.axis_size("head")
    dims = (packs, count, features, inner, bc, heads, size, width, nseq)
    seq_place, head_place = lax.axis_index("seq"), lax.axis_index("head")
    meta = jnp.stack([seq_place, head_place]).astype(jnp.int32)
    pre = (meta, lengths)
    grid = (packs,)

    order.clear()
    tokens = jnp.swapaxes(tokens_in, 1, 2)
    cotangent = jnp.swapaxes(out_grad, 1, 2)
    far = swap(tokens, "head", 2)
    near = swap(tokens, "head", 1)
    tail = call(
        tail_kernel, (1,),
        [pl.BlockSpec((packs, part, LANES), lambda p, _: (0, 0, count // LANES - 1))],
        whole_spec((part, LANES)), shape(part, LANES, bf16), [], (meta,),
        pltpu.with_memory_space_constraint(tokens, pltpu.HBM), us=0.05,
    )
    tail = shift(tail, "seq", 1)
    ins = [
        proj_bc.T, conv_bc, bias_bc, norm_gain, proj_dt.T, conv_x, bias_x, dt_bias, a_log, d_skip,
        gate_gain, proj_out,
    ]
    outs = [
        shape(features, inner, bf16),
        shape(bc_part, features + LANES, bf16), shape(features, bc_part, bf16),
        shape(features, LANES, bf16), shape(LANES, features, bf16), shape(8, inner, f32),
        shape(8, bc_part, f32), shape(8, LANES, f32), shape(1, inner, f32), shape(1, inner, f32),
        shape(part, 1, f32),
    ]
    (
        w_out, shared, w_bc, w_dt, w_dt_rows, conv_own, conv_bc_own, small, skip, gain_gate, norm_gain_own,
    ) = call(
        functools.partial(prepare_kernel, dims), (1,), [whole_spec(x.shape) for x in ins],
        [whole_spec(x.shape) for x in outs], outs, [], (), *ins, wait=(tail,),
        us=0.05,
    )
    edge_far, shared_far = swap(tail, "head", 2), swap(shared, "head", 2)
    far, edge_far, shared_far = lax.optimization_barrier((far, edge_far, shared_far))
    edge_pieces = tail, swap(tail, "head", 1), edge_far, swap(edge_far, "head", 1)
    weight_pieces = shared, swap(shared, "head", 1), shared_far, swap(shared_far, "head", 1)
    diagonal = swap(far, "head", 1)
    token_pieces = tokens, near, far, diagonal

    lane_spec = pack_spec((count, LANES))
    chan_spec = pack_spec((count, inner))
    xbc_spec = pack_spec((count, chans))
    model_spec = pack_spec((features, count))
    piece_spec = pack_spec((part, count))
    edge_spec = whole_spec((part, LANES))
    pay_shape = (rows + EDGE, LANES)
    pay_specs = [side_spec(pay_shape, half, k) for k in (True, False)]
    pay = shape(half, *pay_shape, jnp.int16)
    state_spec = half_spec(pay_shape, half)
    vec = whole_spec((1, inner))
    square = whole_spec((features, inner))

    w_bc_rows, conv_all, gain_all, edge, edge_raws = call(
        functools.partial(border_kernel, dims),
        (1,),
        [edge_spec] * 4 + [whole_spec((bc_part, features + LANES))] * 4
        + [square, whole_spec((8, inner))],
        [
            whole_spec((bc, features)), whole_spec((8, chans)), whole_spec((features, 1)),
            whole_spec((features, LANES)), whole_spec((LANES, chans)),
        ],
        [
            shape(bc, features, bf16), shape(8, chans, f32), shape(features, 1, f32),
            shape(features, LANES, bf16), shape(LANES, chans, f32),
        ],
        [pltpu.VMEM((4, part, LANES), bf16), pltpu.VMEM((4, bc_part, features + LANES), bf16)],
        (meta,),
        *edge_pieces, *weight_pieces, proj_x, conv_own,
    )

    def front(keep, onto):
        spec = lambda shape_of: sided_spec(shape_of, half, keep)
        return call(
            functools.partial(front_kernel, dims, keep),
            (half,),
            [spec((part, count))] * 4
            + [
                square, whole_spec((bc, features)), whole_spec((LANES, features)),
                whole_spec((8, chans)), whole_spec((8, LANES)), whole_spec((features, 1)),
                whole_spec((LANES, chans)),
            ],
            [
                spec((features, count)), spec((1, count)), spec((ext, inner)), spec((ext, bc_part)),
                spec((count, chans)), spec((count, LANES)), pack_spec(pay_shape),
            ],
            [
                shape(packs, features, count, bf16), shape(packs, 1, count, f32),
                shape(packs, ext, inner, bf16), shape(packs, ext, bc_part, bf16),
                shape(packs, count, chans, bf16), shape(packs, count, LANES, f32), pay,
            ],
            [Each((4, part, count), bf16), Each((ext, chans), f32)],
            pre,
            *token_pieces, proj_x, w_bc_rows, w_dt_rows, conv_all, small, gain_all, edge_raws,
            us=6, onto=onto,
        )

    *early, send = front(False, ())
    kept = {}

    def keep_work(_):
        *kept["front"], kept["keep"] = front(True, early)
        order.hold(*(kept["front"][i] for i in (0, 4, 5)))

    def inner_work(_):
        *_, xbc, steps = kept["front"]
        kept["inner"] = call(
            functools.partial(inner_kernel, dims),
            grid,
            [xbc_spec, lane_spec],
            chan_spec,
            shape(packs, count, inner, f32),
            [],
            pre,
            xbc, steps,
            us=6,
        )
        order.hold(kept["inner"])

    def cot_work(newest):
        own, far = kept["cots"]
        near = swap(own, "head", 1)
        cots = own, near, far, swap(lax.optimization_barrier((far, newest))[0], "head", 1)
        kept["cot"], kept["gg"] = call(
            functools.partial(cot_kernel, dims),
            (packs // half,),
            [piece_spec] * 4 + [whole_spec((inner, features))],
            [model_spec, chan_spec],
            [shape(packs, features, count, bf16), shape(packs, count, inner, f32)],
            [Each((4, part, count), bf16)],
            pre,
            *cots, proj_out,
            us=5.5, group=half,
        )

    def gate_slope_work(_):
        normed, _, raw_x, raw_bc, *_ = kept["front"]
        own = lax.optimization_barrier((cotangent, normed))[0]
        kept["cots"] = own, swap(own, "head", 2)
        kept["slope"] = call(
            functools.partial(gate_slope_kernel, dims),
            grid,
            [model_spec, square, pack_spec((ext, inner)), pack_spec((ext, bc_part)),
             whole_spec((8, inner)), whole_spec((8, bc_part))],
            [chan_spec, chan_spec, pack_spec((count, bc_part))],
            [shape(packs, count, inner, bf16), shape(packs, count, inner, f32),
             shape(packs, count, bc_part, f32)],
            [Each((ext, inner), f32), Each((ext, bc_part), f32)],
            pre,
            normed, proj_z, raw_x, raw_bc, conv_own, conv_bc_own,
            us=7,
        )

    state_keep, state_recv = scan_states(
        lambda: kept["keep"], send, meta, packs, heads, size, 0,
        (keep_work, gate_slope_work, inner_work, cot_work),
    )
    normed, inv, raw_x, raw_bc, xbc, steps = kept["front"]
    inner_out, cot, gg = kept["inner"], kept["cot"], kept["gg"]
    gate, slope_x, slope_bc = kept["slope"]
    order.drop(inner_out)

    y, stats = call(
        functools.partial(gate_kernel, dims),
        (packs // half,),
        [
            xbc_spec, lane_spec, chan_spec, state_spec, state_spec, chan_spec, chan_spec, vec, vec,
        ],
        [chan_spec, pack_spec((2, count))],
        [shape(packs, count, inner, f32), shape(packs, 2, count, f32)],
        [],
        pre,
        xbc, steps, inner_out, state_keep, state_recv, gate, gg, gain_gate, skip,
        us=6.6, group=half,
    )
    stats = [stats] + [swap(stats, "head", bits) for bits in (1, 2, 3)]

    gy, gated, ggate, gkeep, gsend, gate_small = call(
        functools.partial(grad_kernel, dims, total_inner),
        (packs // half,),
        [
            *[pack_spec((2, count))] * 4, xbc_spec, lane_spec, chan_spec, chan_spec, chan_spec, vec,
            vec,
        ],
        [chan_spec] * 3 + pay_specs + [whole_spec((8, inner))],
        [shape(packs, count, inner, f32)] + [shape(packs, count, inner, bf16)] * 2
        + [pay, pay, shape(8, inner, f32)],
        [],
        pre,
        *stats, xbc, steps, y, gate, gg, gain_gate, skip,
        us=8.3, group=half,
    )

    piece_shape = shape(packs, part, count, f32)
    send_spec = pack_spec((2, part, count))
    rows_half = features // 2
    half_specs = [whole_spec((rows_half, inner))] * 2
    half_shapes = [shape(rows_half, inner, f32), shape(rows_half, inner, bf16)]
    half_sums = pltpu.VMEM((2, rows_half, inner), f32)
    row8, row8_shape = whole_spec((8, features)), shape(8, features, f32)

    early_sum, late_sum = SeqSum(), SeqSum()

    def out_work(_):
        *kept["out"], keep, give = call(
            functools.partial(out_kernel, dims),
            (packs // half,),
            [chan_spec, model_spec, square],
            [piece_spec, piece_spec, send_spec] + half_specs,
            [piece_shape, piece_shape, shape(packs, 2, part, count, bf16)] + half_shapes,
            [Each((4, part, count), f32), half_sums],
            pre,
            gated, cot, w_out,
            us=6.8, group=half,
        )
        early_sum.put(keep, give)

    def z_work(_):
        keep, give, kept["gain"] = call(
            functools.partial(z_kernel, dims),
            (packs // half,),
            [model_spec, chan_spec, square],
            half_specs + [row8],
            half_shapes + [row8_shape],
            [half_sums],
            pre,
            normed, ggate, proj_z,
            us=5.3, group=half,
        )
        early_sum.put(keep, give)
        own, far, send = kept["out"]
        own, far = call(
            out_gather_kernel, grid, [piece_spec, piece_spec, send_spec], [piece_spec, piece_spec],
            [piece_shape, shape(packs, part, count, bf16)], [], (), own, far, swap(send, "head", 1),
        )
        kept["out"] = own, swap(far, "head", 2)

    def diag_work(_):
        kept["diag"] = call(
            functools.partial(diag_kernel, dims),
            (packs // half,),
            [xbc_spec, lane_spec, chan_spec, chan_spec, state_spec, state_spec],
            [chan_spec, pack_spec((count, bc)), lane_spec],
            [
                shape(packs, count, inner, f32), shape(packs, count, bc, f32),
                shape(packs, count, LANES, f32),
            ],
            [],
            pre,
            xbc, steps, gy, y, state_keep, state_recv,
            us=12, group=half,
        )

    def early_work(_):
        early_sum.add(meta)

    gstate_keep, gstate_recv = scan_states(
        gkeep, gsend, meta, packs, heads, size, 1, (out_work, z_work, diag_work, early_work),
        lambda: early_sum.got,
    )
    out_own, out_far = kept["out"]
    dx, dbc, sums = kept["diag"]

    edge_tile = (EDGE, inner)

    def pair_spec(shape_of):
        return pl.BlockSpec((half,) + shape_of, lambda p, *_: (p,) + (0,) * len(shape_of))

    pair_lane = pair_spec((count, LANES))
    share_own, share_near, grad_x, state_sums, edge_x = call(
        functools.partial(share_kernel, dims),
        (packs // half,),
        [xbc_spec, lane_spec, pack_spec((count, bc)), state_spec, state_spec, chan_spec, chan_spec,
         chan_spec, whole_spec((8, inner)), vec],
        [lane_spec, lane_spec, chan_spec, lane_spec, pack_spec(edge_tile)],
        [shape(packs, count, LANES, f32)] * 2
        + [shape(packs, count, inner, f32), shape(packs, count, LANES, f32),
           shape(packs, *edge_tile, bf16)],
        [Each((2 * EDGE, inner), f32)],
        pre,
        xbc, steps, dbc, gstate_keep, gstate_recv, gy, dx, slope_x, conv_own, skip,
        us=6.4, group=half,
    )
    share_near = swap(share_near, "head", 1)
    advance(early_sum, meta)
    two = shape(half, count, LANES, f32)
    bc_keep, bc_send = call(
        functools.partial(middle_kernel, (packs, bc_part)),
        (1,),
        [whole_spec((packs, count, LANES))] * 2,
        [whole_spec(two.shape)] * 2,
        [two, two],
        [],
        (meta,),
        share_own, share_near,
    )
    bc_recv = swap(bc_send, "head", 2)

    main_x, keep, give, grad_conv, gain_x = call(
        functools.partial(xback_kernel, dims),
        (packs // half,),
        [
            chan_spec, pack_spec((ext, inner)), model_spec, whole_spec((features, LANES)),
            pack_spec(edge_tile), whole_spec((8, inner)), square,
        ],
        [chan_spec, *half_specs, whole_spec((8, inner)), row8],
        [shape(packs, count, inner, bf16), *half_shapes, shape(8, inner, f32), row8_shape],
        [
            Each((count + EDGE, inner), f32), Each((ext, inner), f32), half_sums,
            pltpu.VMEM((LANES, inner), bf16),
        ],
        pre,
        grad_x, raw_x, normed, edge, edge_x, conv_own, proj_x,
        us=7, group=half, wait=(out_far,),
    )
    late_sum.put(keep, give)
    advance(early_sum, meta)

    gdt, gdt_rows, grad_small, gain_dt = call(
        functools.partial(step_kernel, dims),
        (packs // half,),
        [
            pair_lane, pair_lane, pair_lane, *[whole_spec((half,) + pay_shape)] * 4,
            whole_spec((8, LANES)), pair_spec((features, count)), whole_spec((features, LANES)),
        ],
        [pair_lane, row8, whole_spec((8, LANES)), row8],
        [shape(packs, count, LANES, bf16), row8_shape, shape(8, LANES, f32), row8_shape],
        [pltpu.VMEM((features, LANES), f32)],
        pre,
        steps, sums, state_sums, state_keep, state_recv, gstate_keep, gstate_recv, small, normed,
        w_dt,
        us=6,
    )
    advance(early_sum, meta)
    advance(late_sum, meta)
    give_rows = 2 * bc_part + 2 * SMALL
    gbc, edges, bc_sum, smalls = call(
        functools.partial(conv_bc_kernel, dims),
        grid,
        [
            half_spec((count, LANES), half), half_spec((count, LANES), half),
            pack_spec((count, bc_part)), pack_spec((ext, bc_part)), model_spec,
            whole_spec((features, LANES)), whole_spec((features, bc_part)),
            whole_spec((8, bc_part)), pack_spec(edge_tile), whole_spec((8, inner)), row8,
            whole_spec((8, LANES)), whole_spec((8, inner)), row8, row8, row8,
            whole_spec((features, 1)),
        ],
        [
            pack_spec((count, bc_part)), pack_spec((EDGE, inner + LANES)),
            whole_spec((give_rows, inner)), whole_spec((SMALL, inner)),
        ],
        [
            shape(packs, count, bc_part, bf16), shape(packs, EDGE, inner + LANES, bf16),
            shape(give_rows, inner, bf16), shape(SMALL, inner, f32),
        ],
        [
            Each((ext + EDGE, bc_part), f32), Each((ext, bc_part), f32),
            pltpu.VMEM((features, bc_part), f32), pltpu.VMEM((LANES, bc_part), bf16),
            pltpu.VMEM((8, bc_part), f32),
        ],
        pre,
        bc_keep, bc_recv, slope_bc, raw_bc, normed, edge, w_bc, conv_bc_own, edge_x, grad_conv,
        gdt_rows, grad_small, gate_small, kept["gain"], gain_x, gain_dt, gain_all,
        us=5,
    )
    edges = shift(edges, "seq", -1)
    bc_bits = [1 << k for k in range((lax.axis_size("seq") - 1).bit_length())]
    bc_got = swap(bc_sum, "seq", 1)
    advance(late_sum, meta)

    def bc_step(bit):
        nonlocal bc_sum, smalls, bc_got
        spec, small_spec = whole_spec(bc_sum.shape), whole_spec(smalls.shape)
        bc_sum, smalls = call(
            functools.partial(add_kernel, 1, False, [2 * bc_part], 1, True), (1,),
            [spec, spec, small_spec], [spec, small_spec],
            [shape(*bc_sum.shape, bf16), shape(*smalls.shape, f32)], [], (meta,),
            bc_sum, bc_got, smalls, us=0.01,
        )
        bc_got = swap(bc_sum, "seq", bit)

    bc_step(bc_bits[1])
    advance(early_sum, meta)

    tall = part + EDGE
    tall_send = pack_spec((2, tall, count))
    tall_spec = pack_spec((tall, count))
    row_spec, row_shape = pack_spec((1, count)), shape(packs, 1, count, f32)
    gn_own, gn_far, gn_send, dots = call(
        functools.partial(back_kernel, dims),
        (packs // half,),
        [
            chan_spec, pack_spec((EDGE, inner + LANES)), chan_spec, lane_spec,
            pack_spec((count, bc_part)), model_spec, square, square,
            whole_spec((features, bc_part)), whole_spec((features, LANES)),
        ],
        [piece_spec, piece_spec, tall_send, row_spec],
        [piece_shape, piece_shape, shape(packs, 2, tall, count, bf16), row_shape],
        [Each((4, part, count), f32)],
        pre,
        main_x, edges, ggate, gdt, gbc, normed, proj_z, proj_x, w_bc, w_dt,
        us=6, group=half,
    )
    near = swap(gn_send, "head", 1)
    order.drop(xbc, steps, normed)
    advance(late_sum, meta, 0.01, wait=(bc_got,))
    block_out = call(
        out_final_kernel, (packs // half,), [piece_spec] * 3, piece_spec, shape(packs, part, count, bf16), [],
        (), out_own, out_far, tokens, out=True, us=2, group=half,
    )
    block_out = jnp.swapaxes(block_out, 1, 2)

    gn_own, gn_far, dots = call(
        gather_kernel,
        grid,
        [piece_spec, piece_spec, tall_send, row_spec],
        [piece_spec, tall_spec, row_spec],
        [piece_shape, shape(packs, tall, count, bf16), row_shape],
        [],
        (),
        gn_own, gn_far, near, dots,
        us=0.01,
    )
    gn_far = swap(gn_far, "head", 2)
    order.hold(gn_own)
    while early_sum.bit != 0:
        advance(early_sum, meta)
    for bit in bc_bits[2:]:
        bc_step(bit)
    small_spec, give_spec = whole_spec(smalls.shape), whole_spec(bc_sum.shape)

    def head_step(x, bit):
        return call(
            plus_kernel, (1,), [small_spec, small_spec], small_spec, shape(*x.shape, f32), [], (),
            x, swap(x, "head", bit), us=0.01,
        )

    advance(late_sum, meta, 0.01)
    grads_out, grads_z = early_sum.result(meta, ("flip", "rows"), 0.4)
    while late_sum.bit != 0:
        advance(late_sum, meta, 0.01)
    grad_bc, smalls = call(
        functools.partial(whole_kernel, bc_part), (1,), [give_spec, give_spec, small_spec],
        [whole_spec((bc_part, features)), small_spec],
        [shape(bc_part, features, f32), shape(*smalls.shape, f32)], [], (), bc_sum, bc_got, smalls,
        us=0.01, out=1,
    )
    gains = head_step(smalls, 1)
    in_grad = call(
        functools.partial(final_kernel, (packs, count, features)),
        (packs // half,),
        [piece_spec, tall_spec, row_spec, piece_spec, row_spec, whole_spec((part, 1)), piece_spec],
        piece_spec,
        piece_shape,
        [],
        (),
        gn_own, gn_far, dots, tokens, inv, norm_gain_own, cotangent,
        us=2, out=True, group=half,
    )
    in_grad = jnp.swapaxes(in_grad, 1, 2)
    order.drop(gn_own)
    gains = head_step(gains, 2)
    own_half = late_sum.half_result(meta, True)
    vectors = [(inner,), (bc_part,), (heads,), (heads,), (heads,), (inner,), (part,)]
    tables = [(heads, features), (width, inner), (width, bc_part)]
    outs = call(
        functools.partial(unpack_kernel, (heads, features, bc_part, width)), (1,),
        [small_spec, small_spec], [whole_spec(x) for x in tables + vectors],
        [shape(*x, f32) for x in tables + vectors], [], (meta,), smalls, gains, out=True, us=0.01,
    )
    grad_dt, grad_conv, grad_conv_bc = outs[:3]
    bias_x_grad, bias_bc_grad, dt_bias_grad, a_log_grad, skip_grad, gate_grad, grad_gain = outs[3:]
    grads_x = late_sum.half_result(meta, False, (own_half,)).reshape(features, inner)
    return (
        block_out,
        in_grad,
        grad_gain,
        grads_z,
        grads_x,
        grad_bc.T,
        grad_dt.T,
        grad_conv,
        grad_conv_bc,
        bias_x_grad,
        bias_bc_grad,
        dt_bias_grad,
        a_log_grad,
        skip_grad,
        gate_grad,
        grads_out,
    )


def solution(mesh):
    token, column, vector = P(None, "seq", "head"), P(None, "head"), P("head")
    row = P("head", None)
    return jax.shard_map(
        shards,
        mesh=mesh,
        in_specs=(
            token, token, P(), vector, column, column, column, column, column, column, vector,
            vector, vector, vector, vector, vector, row,
        ),
        out_specs=(
            token, token, vector, column, column, column, column, column, column, vector, vector,
            vector, vector, vector, vector, row,
        ),
        check_vma=False,
    )
```

```python
import functools

import jax
import jax.numpy as jnp
from jax import lax
from jax.experimental import pallas as pl
from jax.experimental.pallas import tpu as pltpu
from jax.sharding import PartitionSpec as P

EPSILON = 1e-05
bf16 = jnp.bfloat16
f32 = jnp.float32
LANES = 128
EDGE = 16
MIB = 1024 * 1024
STEPS = 32000.0
UNIT = 16384.0
LN2 = 0.6931471805599453
GROUP = 16
SMALL = 32


def permuted(x, axis, route):
    y = lax.ppermute(x, axis, route)
    order.near.append(y)
    return y


def swap(x, axis, bit):
    return permuted(x, axis, [(i, i ^ bit) for i in range(lax.axis_size(axis))])


def shift(x, axis, distance):
    n = lax.axis_size(axis)
    return permuted(x, axis, [(i, i + distance) for i in range(n) if 0 <= i + distance < n])


def head_pieces(x):
    far = swap(x, "head", 2)
    near = swap(x, "head", 1)
    return x, near, far, swap(far, "head", 1)


def nn(a, b):
    return lax.dot_general(a, b, (((1,), (0,)), ((), ())), preferred_element_type=f32)


def nt(a, b):
    return lax.dot_general(a, b, (((1,), (1,)), ((), ())), preferred_element_type=f32)


def tn(a, b):
    return lax.dot_general(a, b, (((0,), (0,)), ((), ())), preferred_element_type=f32)


def split2(v):
    hi = v.astype(bf16)
    return hi, (v - hi.astype(f32)).astype(bf16)


def split3(v):
    hi = v.astype(bf16)
    rest = v - hi.astype(f32)
    mid = rest.astype(bf16)
    return hi, mid, (rest - mid.astype(f32)).astype(bf16)


def spread_matrix(heads, size):
    row = lax.broadcasted_iota(jnp.int32, (LANES, heads * size), 0)
    col = lax.broadcasted_iota(jnp.int32, (LANES, heads * size), 1)
    first = (col >= row * size) & (col < (row + 1) * size)
    again = (col >= (row - GROUP) * size) & (col < (row - GROUP + 1) * size)
    return jnp.where(first | again, 1.0, 0.0).astype(bf16)


def spread(v, matrix, heads):
    hi, lo = split2(head_lanes(v, heads))
    return nn((hi.astype(f32) + to_group(lo.astype(f32), 1)).astype(bf16), matrix)


def head_lanes(v, heads):
    return jnp.where(lax.broadcasted_iota(jnp.int32, v.shape, 1) < heads, v, 0.0)


def to_group(v, k):
    return pltpu.roll(v, k * GROUP, 1)


def from_group(v, k, heads):
    return head_lanes(pltpu.roll(v, LANES - k * GROUP, 1) if k else v, heads)


def collapse(v, matrix, heads):
    return head_lanes(nt(jnp.concatenate(split2(v), axis=1), jnp.concatenate([matrix] * 2, axis=1)), heads)


def triangle(count, lower):
    row = lax.broadcasted_iota(jnp.int32, (count, count), 0)
    col = lax.broadcasted_iota(jnp.int32, (count, count), 1)
    keep = (row >= col) if lower else (row <= col)
    return jnp.where(keep, 1.0, 0.0).astype(bf16)


def exact_sums(matrix, v, heads):
    hi, mid, lo = [piece.astype(f32) for piece in split3(v)]
    sums = nn(matrix, (hi + to_group(mid, 1) + to_group(lo, 2)).astype(bf16))
    return from_group(sums, 0, heads) + from_group(sums, 1, heads) + from_group(sums, 2, heads)


def step_sizes(v, heads):
    soft = jnp.maximum(v, 0.0) + jnp.log1p(jnp.exp(-jnp.abs(v)))
    return head_lanes(soft, heads)


def steps_of(block, heads):
    return step_sizes(block, heads), from_group(block, 1, heads)


def segments(positions, lens_ref, pack, count):
    total = jnp.zeros(positions.shape, jnp.int32)
    end = jnp.int32(0)
    for k in range(count):
        end = end + lens_ref[pack, k]
        total = total + jnp.where(positions >= end, 1, 0)
    return total


def column_segments(meta_ref, lens_ref, pack, count, nseq, before):
    rows = lax.broadcasted_iota(jnp.int32, (count + before, 1), 0)
    return segments(rows + (meta_ref[0] * count - before), lens_ref, pack, nseq)


def row_segments(meta_ref, lens_ref, pack, count, nseq):
    cols = lax.broadcasted_iota(jnp.int32, (1, count), 1)
    return segments(cols + meta_ref[0] * count, lens_ref, pack, nseq)


def carry_column(meta_ref, seg_ext, before):
    same = seg_ext[before:] == seg_ext[before - 1 : before]
    return jnp.where(same & (meta_ref[0] > 0), 1.0, 0.0)


def to_int16(v):
    return jnp.floor(v + 0.5).astype(jnp.int32).astype(jnp.int16)


def encode_state(out, p, state, decay, heads, size):
    lane = lax.broadcasted_iota(jnp.int32, (1, LANES), 1)
    powers = jnp.zeros((1, LANES), f32)
    for h in range(heads):
        part = state[h * size : (h + 1) * size]
        top = jnp.max(jnp.max(jnp.abs(part), axis=0, keepdims=True), axis=1, keepdims=True)
        power = jnp.ceil(jnp.log(jnp.maximum(top, 1e-30)) / LN2)
        powers = powers + jnp.where(lane == h, power, 0.0)
        codes = jnp.clip(part * (jnp.exp(-power * LN2) * STEPS), -32767.0, 32767.0)
        out[p, h * size : (h + 1) * size, :] = to_int16(codes)
    row = lax.broadcasted_iota(jnp.int32, (EDGE, LANES), 0)
    coarse = jnp.floor(decay * UNIT)
    fine = (decay * UNIT - coarse) * UNIT
    tail = jnp.where(row == 0, powers, jnp.where(row == 1, coarse, jnp.where(row == 2, fine, 0.0)))
    out[p, heads * size :, :] = to_int16(tail)


def decode_state(block, heads, size):
    values = block.astype(jnp.int32).astype(f32)
    tail = values[heads * size :]
    scale = jnp.exp(tail[0:1] * LN2) / STEPS
    decay = (tail[1:2] + tail[2:3] / UNIT) / UNIT
    return scaled_state(values[: heads * size], scale, heads, size), decay


def sigmoid(v):
    return 1.0 / (1.0 + jnp.exp(-v))


def scaled_state(state, decay, heads, size):
    return jnp.concatenate(
        [state[h * size : (h + 1) * size] * decay[:, h : h + 1] for h in range(heads)], axis=0
    )


def tail_kernel(meta, tokens, out):
    lane = lax.broadcasted_iota(jnp.int32, out.shape, 1)
    total = jnp.zeros(out.shape, f32)
    for p in range(tokens.shape[0]):
        moved = pltpu.roll(tokens[p].astype(f32), (p + 1) * EDGE, 1)
        total = jnp.where((lane >= p * EDGE) & (lane < (p + 1) * EDGE), moved, total)
    out[...] = total.astype(bf16)


def wide_row(ref, lanes=LANES):
    row = ref[...].astype(f32)[None, :]
    blank = lanes - row.shape[1]
    return jnp.concatenate([row, jnp.zeros((1, blank), f32)], axis=1) if blank else row


def prepare_kernel(dims, *refs):
    packs, count, features, inner, bc, heads, size, width, nseq = dims
    (
        wbc, conv_bc, bias_bc, norm_gain, wdt, conv_x, bias_x, dt_bias, a_log, d_skip, gate_gain, wout,
        wout_o, shared_o, wbc_o, wdt_o, wdt_rows_o, conv_x_o, conv_bc_o, small_o, skip_o, gate_gain_o, gain_o,
    ) = refs
    bc_part, part = bc // 4, features // 4
    wout_o[...] = jnp.transpose(wout[...])
    taps = conv_bc[...].astype(f32)
    bias = wide_row(bias_bc, bc_part)
    gain = wide_row(norm_gain, part)
    pieces = [gain[:, c * bc_part : (c + 1) * bc_part] for c in range(part // bc_part)]
    rows = jnp.concatenate([taps, bias] + pieces, axis=0)
    rows = jnp.concatenate([rows, jnp.zeros((LANES - rows.shape[0], bc_part), f32)], axis=0)
    rows = jnp.concatenate([rows, jnp.zeros((LANES, LANES - bc_part), f32)], axis=1)
    extra = jnp.transpose(rows)[:bc_part].astype(bf16)
    shared_o[:, :features] = wbc[...]
    shared_o[:, features:] = extra
    wbc_o[...] = jnp.transpose(wbc[...].astype(f32)).astype(bf16)
    dt_rows = jnp.concatenate(
        [wdt[...].astype(f32), jnp.zeros((LANES - heads, features), f32)], axis=0
    )
    wdt_rows_o[...] = dt_rows.astype(bf16)
    wdt_o[...] = jnp.transpose(dt_rows).astype(bf16)
    blank = jnp.zeros((7 - width, inner), f32)
    conv_x_o[...] = jnp.concatenate(
        [conv_x[...].astype(f32), wide_row(bias_x, inner), blank], axis=0
    )
    conv_bc_o[...] = jnp.concatenate([taps, bias, blank[:, :bc_part]], axis=0)
    small_o[...] = jnp.concatenate(
        [wide_row(dt_bias), wide_row(a_log), jnp.zeros((6, LANES), f32)], axis=0
    )
    skips = jnp.concatenate([wide_row(d_skip), jnp.zeros((7, LANES), f32)], axis=0)
    matrix = spread_matrix(heads, size)
    skip_o[...] = sum(nn(piece, matrix) for piece in split3(skips))[0:1]
    gate_gain_o[...] = wide_row(gate_gain, inner)
    column = jnp.concatenate([gain, jnp.zeros((LANES - 1, part), f32)], axis=0)
    column = jnp.concatenate([column, jnp.zeros((LANES, 2 * LANES - part), f32)], axis=1)
    gain_o[...] = jnp.transpose(column)[:part, 0:1]


def normalise(values, gain, features):
    mean = jnp.sum(values * values, axis=0, keepdims=True) / features
    inv = lax.rsqrt(mean + EPSILON)
    return inv, ((values * inv) * gain).astype(bf16)


def raw_rows(normed, wx, wbc):
    return jnp.concatenate([nn(normed, wx), nt(normed, wbc)], axis=1).astype(bf16)


def border_kernel(dims, meta, *refs):
    packs, count, features, inner, bc, heads, size, width, nseq = dims
    edges, shared = refs[0:4], refs[4:8]
    wx, conv_x, wbc_o, conv_o, gain_o, edge_o, raws_o, stage, weights = refs[8:]
    head = meta[1]
    part, bc_part = features // 4, bc // 4
    for k in range(4):
        weights[head ^ k] = shared[k][...]
        stage[head ^ k] = edges[k][...]
    whole = weights[...].reshape(bc, weights.shape[2])
    wbc_o[...] = whole[:, :features]
    extra = whole[:, features:].astype(f32)
    conv_o[:, :inner] = conv_x[...]
    conv_o[:, inner:] = jnp.transpose(extra)[0:8]
    for h in range(4):
        for c in range(part // bc_part):
            gain_o[h * part + c * bc_part : h * part + (c + 1) * bc_part, :] = extra[
                h * bc_part : (h + 1) * bc_part, width + 1 + c : width + 2 + c
            ]
    _, normed = normalise(stage[...].reshape(features, stage.shape[2]).astype(f32), gain_o[...], features)
    edge_o[...] = normed
    raws_o[...] = raw_rows(jnp.transpose(normed), wx[...], wbc_o[...]).astype(f32)


def front_kernel(dims, keep, meta, lens, *refs):
    packs, count, features, inner, bc, heads, size, width, nseq = dims
    tokens, refs = refs[0:4], refs[4:]
    wx, wbc, wdt, conv, small, gain, edge_raws, *refs = refs
    normed_o, inv_o, rawx_o, rawbc_o, xbc_o, steps_o, state_o, stage, raws = refs[-9:]
    side = meta[0] & 1 if keep else 1 - (meta[0] & 1)
    pack = order.pack + (packs // 2) * side
    head = meta[1]
    for k in range(4):
        stage[head ^ k] = tokens[k][0]
    inv, normed_t = normalise(stage[...].reshape(features, count).astype(f32), gain[...], features)
    inv_o[0] = inv
    normed_o[0] = normed_t
    normed = jnp.transpose(normed_t)
    raws[EDGE:, :] = raw_rows(normed, wx[...], wbc[...]).astype(f32)
    raws[0:EDGE, :] = edge_raws[pl.ds(pl.multiple_of(pack * EDGE, EDGE), EDGE), :]

    def own_bc(values):
        bc_part = bc // 4
        parts = [values[:, inner + h * bc_part : inner + (h + 1) * bc_part] for h in range(4)]
        low = jnp.where((head & 1) == 0, parts[0], parts[1])
        high = jnp.where((head & 1) == 0, parts[2], parts[3])
        return jnp.where((head >> 1) == 0, low, high)

    rawx_o[0] = raws[:, :inner].astype(bf16)
    rawbc_o[0] = own_bc(raws[...]).astype(bf16)
    seg = column_segments(meta, lens, pack, count, nseq, EDGE)
    seg_main = seg[EDGE:]
    pre = convolved(raws, conv, seg, count, width)
    xbc = (pre * sigmoid(pre)).astype(bf16)
    xbc_o[0] = xbc
    v = head_lanes(nt(normed, wdt[...]).astype(bf16).astype(f32) + small[0:1, :], heads)
    dt = step_sizes(v, heads)
    rate = -dt * jnp.exp(small[1:2, :])
    cum = exact_sums(triangle(count, True), rate, heads)
    steps_o[0] = v + to_group(cum, 1)
    cum_end = cum[count - 1 : count]
    weight = jnp.where(seg_main == seg[count + EDGE - 1 :], jnp.exp(cum_end - cum), 0.0) * dt
    matrix = spread_matrix(heads, size)
    scaled = (xbc[:, :inner].astype(f32) * spread(weight, matrix, heads)).astype(bf16)
    state = jnp.transpose(nn(jnp.transpose(xbc[:, inner : inner + bc // 2]), scaled))
    carry = carry_column(meta, seg, EDGE)
    encode_state(state_o, 0, state, carry[count - 1 :] * jnp.exp(cum_end), heads, size)


def convolved(raws, conv, seg, count, width):
    pre = jnp.broadcast_to(conv[width : width + 1, :], (count, raws.shape[1]))
    for k in range(width):
        low = EDGE - (width - 1) + k
        mask = jnp.where(seg[low : low + count] == seg[EDGE:], 1.0, 0.0)
        pre = pre + conv[k : k + 1, :] * raws[low : low + count, :] * mask
    return pre


def gate_slope_kernel(dims, meta, lens, *refs):
    packs, count, features, inner, bc, heads, size, width, nseq = dims
    normed, wz, raw_x, raw_bc, conv_x, conv_bc, gate_o, slope_x_o, slope_bc_o, raws, raws_bc = refs
    pack = order.pack
    gate_o[0] = tn(normed[0], wz[...]).astype(bf16)
    seg = column_segments(meta, lens, pack, count, nseq, EDGE)
    for raw, wide, conv, out in ((raw_x, raws, conv_x, slope_x_o), (raw_bc, raws_bc, conv_bc, slope_bc_o)):
        wide[...] = raw[0].astype(f32)
        pre = convolved(wide, conv, seg, count, width)
        sig = sigmoid(pre)
        out[0] = sig * (1.0 + pre * (1.0 - sig))


def store_state(meta, packs, pack, keep_o, send_o, state, decay, heads, size):
    mine = (pack // (packs // 2)) == (meta[0] & 1)

    @pl.when(mine)
    def _():
        encode_state(keep_o, 0, state, decay, heads, size)

    @pl.when(jnp.logical_not(mine))
    def _():
        encode_state(send_o, 0, state, decay, heads, size)


def load_state(meta, packs, pack, keep, recv, heads, size):
    mine = (pack // (packs // 2)) == (meta[0] & 1)
    block = jnp.where(mine, keep[0].astype(jnp.int32), recv[0].astype(jnp.int32))
    return decode_state(block, heads, size)[0]


def decay_parts(cum_col, cum_row, masked):
    return masked * jnp.exp(jnp.minimum(cum_col - cum_row, 0.0))


def block_mask(meta, lens, pack, count, nseq):
    col = column_segments(meta, lens, pack, count, nseq, 0)
    row = row_segments(meta, lens, pack, count, nseq)
    tri = lax.broadcasted_iota(jnp.int32, (count, count), 0) >= lax.broadcasted_iota(
        jnp.int32, (count, count), 1
    )
    return tri & (col == row)


def inner_kernel(dims, meta, lens, *refs):
    packs, count, features, inner, bc, heads, size, width, nseq = dims
    xbc, steps, inner_o = refs
    pack = order.pack
    half = bc // 2
    b_vals, c_vals = xbc[0, :, inner : inner + half], xbc[0, :, inner + half :]
    scores = jnp.where(block_mask(meta, lens, pack, count, nseq), nt(c_vals, b_vals), 0.0)
    dt, cum_col = steps_of(steps[0], heads)
    cum_row = jnp.transpose(cum_col)
    dt_row = jnp.transpose(dt)
    lane = lax.broadcasted_iota(jnp.int32, (count, 2 * size), 1)
    for pair in range(heads // 2):
        cols = slice(2 * pair * size, (2 * pair + 2) * size)
        x_pair = xbc[0, :, cols]
        parts = []
        for h in (2 * pair, 2 * pair + 1):
            weights = decay_parts(cum_col[:, h : h + 1], cum_row[h : h + 1], scores)
            parts.append(nn((weights * dt_row[h : h + 1]).astype(bf16), x_pair))
        inner_o[0, :, cols] = jnp.where(lane < size, parts[0], parts[1])


def cot_kernel(dims, meta, lens, *refs):
    packs, count, features, inner, bc, heads, size, width, nseq = dims
    pieces, (wout, cot_o, gg_o, stage) = refs[:4], refs[4:]
    for k in range(4):
        stage[meta[1] ^ k] = pieces[k][0]
    cotangent = stage[...].reshape(features, count)
    cot_o[0] = cotangent
    gg_o[0] = jnp.transpose(nn(wout[...], cotangent))


def compose(lower, upper, heads, size):
    return scaled_state(lower[0], upper[1], heads, size) + upper[0], lower[1] * upper[1]


def choose(flag, a, b):
    return jnp.where(flag, a[0], b[0]), jnp.where(flag, a[1], b[1])


def pair_kernel(dims, rev, meta, own, other, out):
    packs, heads, size = dims
    upper_is_own = ((meta[0] & 1) ^ rev) == 1
    for p in range(packs // 2):
        a, b = decode_state(own[p], heads, size), decode_state(other[p], heads, size)
        both = compose(choose(upper_is_own, b, a), choose(upper_is_own, a, b), heads, size)
        encode_state(out, p, *both, heads, size)


def entering_from(before, b, p, heads, size):
    if before is None:
        return (jnp.zeros_like(b[0]), jnp.ones_like(b[1])), b
    entering = decode_state(before[p], heads, size)
    return entering, compose(b, entering, heads, size)


def cube_kernel(dims, rev, bit, first, meta, *refs):
    packs, heads, size = dims
    total, other = refs[0], refs[1]
    before, next_o, before_o = (None, refs[2], refs[3]) if first else refs[2:5]
    upper_is_own = (((meta[0] >> bit) & 1) ^ rev) == 1
    for p in range(packs // 2):
        a, b = decode_state(total[p], heads, size), decode_state(other[p], heads, size)
        both = compose(choose(upper_is_own, b, a), choose(upper_is_own, a, b), heads, size)
        encode_state(next_o, p, *both, heads, size)
        entering, longer = entering_from(before, b, p, heads, size)
        encode_state(before_o, p, *choose(upper_is_own, longer, entering), heads, size)


def last_kernel(dims, rev, bit, first, meta, *refs):
    packs, heads, size = dims
    own, pair, other = refs[0:3]
    before, keep_o, send_o = (None, refs[3], refs[4]) if first else refs[3:6]
    add = (((meta[0] >> bit) & 1) ^ rev) == 1
    upper_is_own = ((meta[0] & 1) ^ rev) == 1
    for p in range(packs // 2):
        entering, longer = entering_from(
            before, decode_state(other[p], heads, size), p, heads, size
        )
        low = choose(add, longer, entering)
        lower = decode_state(jnp.where(upper_is_own, pair[p].astype(jnp.int32), own[p].astype(jnp.int32)), heads, size)
        high = compose(low, lower, heads, size)
        encode_state(keep_o, p, *choose(upper_is_own, high, low), heads, size)
        encode_state(send_o, p, *choose(upper_is_own, low, high), heads, size)


def gate_kernel(dims, meta, lens, *refs):
    packs, count, features, inner, bc, heads, size, width, nseq = dims
    xbc, steps, inner_in, keep, recv, gate, gg, gain, skip, y_o, stats_o = refs
    pack = order.pack
    state = jnp.concatenate(
        split2(load_state(meta, packs, pack, keep, recv, heads, size)), axis=1
    )
    carry = carry_column(meta, column_segments(meta, lens, pack, count, nseq, EDGE), EDGE)
    matrix = spread_matrix(heads, size)
    entering = spread(carry * jnp.exp(from_group(steps[0], 1, heads)), matrix, heads)
    c_vals = xbc[0, :, inner + bc // 2 :]
    y = inner_in[0] + entering * nt(jnp.concatenate([c_vals, c_vals], axis=1), state)
    y_o[0] = y
    gate_f = gate[0].astype(f32)
    ssd = y + xbc[0, :, :inner].astype(f32) * skip[...]
    mixed = ssd * (gate_f * sigmoid(gate_f))
    squares = jnp.sum(mixed * mixed, axis=1, keepdims=True)
    dots = jnp.sum(gain[...] * gg[0] * mixed, axis=1, keepdims=True)
    lane = lax.broadcasted_iota(jnp.int32, (count, LANES), 1)
    both = jnp.where(lane == 0, squares, 0.0) + jnp.where(lane == 1, dots, 0.0)
    stats_o[0] = jnp.transpose(both)[0:2]


def grad_kernel(dims, total_inner, meta, lens, *refs):
    packs, count, features, inner, bc, heads, size, width, nseq = dims
    (
        stats, near, far, diagonal, xbc, steps, y, gate, gg, gain, skip,
        gy_o, gated_o, ggate_o, keep_o, send_o, small_o,
    ) = refs
    pack = order.pack

    @order.first
    def _():
        small_o[...] = jnp.zeros_like(small_o)

    sums = (stats[0] + near[0]) + (far[0] + diagonal[0])
    row = lax.broadcasted_iota(jnp.int32, (LANES, count), 0)
    wide = jnp.where(row == 0, sums[0:1], 0.0) + jnp.where(row == 1, sums[1:2], 0.0)
    cols = jnp.transpose(wide)
    inv = lax.rsqrt(cols[:, 0:1] / total_inner + EPSILON)
    dot = cols[:, 1:2] / total_inner
    x_f, gg_f, gate_f = xbc[0, :, :inner].astype(f32), gg[0], gate[0].astype(f32)
    ssd = y[0] + x_f * skip[...]
    sig = sigmoid(gate_f)
    act = gate_f * sig
    mixed = ssd * act
    scaled = mixed * inv
    gated_o[0] = (scaled * gain[...]).astype(bf16)
    grad_mixed = inv * gain[...] * gg_f - mixed * (inv * inv * inv * dot)
    gy_f = grad_mixed * act
    gy_o[0] = gy_f
    ggate_o[0] = (grad_mixed * ssd * sig * (1.0 + gate_f * (1.0 - sig))).astype(bf16)
    carry = carry_column(meta, column_segments(meta, lens, pack, count, nseq, EDGE), EDGE)
    cum = from_group(steps[0], 1, heads)
    entering = carry * jnp.exp(cum)
    ey_hi, ey_lo = split2(gy_f * spread(entering, spread_matrix(heads, size), heads))
    c_rows = jnp.transpose(xbc[0, :, inner + bc // 2 :])
    state_grad = jnp.transpose(nn(c_rows, ey_hi) + nn(c_rows, ey_lo))
    small_o[0:1, :] += jnp.sum(gg_f * scaled, axis=0, keepdims=True)
    small_o[1:2, :] += jnp.sum(gy_f * x_f, axis=0, keepdims=True)
    return lambda: store_state(
        meta, packs, pack, keep_o, send_o, state_grad, entering[count - 1 :], heads, size
    )


def diag_kernel(dims, meta, lens, *refs):
    packs, count, features, inner, bc, heads, size, width, nseq = dims
    xbc, steps, gy, y, keep, recv, dx_o, dbc_o, sums_o = refs
    pack = order.pack
    half = bc // 2
    b_vals, c_vals = xbc[0, :, inner : inner + half], xbc[0, :, inner + half :]
    col = column_segments(meta, lens, pack, count, nseq, 0)
    row = row_segments(meta, lens, pack, count, nseq)
    mask = (col == row) & (
        lax.broadcasted_iota(jnp.int32, (count, count), 0)
        <= lax.broadcasted_iota(jnp.int32, (count, count), 1)
    )
    scores = jnp.where(mask, nt(b_vals, c_vals), 0.0)
    dt, cum_col = steps_of(steps[0], heads)
    cum_row = jnp.transpose(cum_col)
    lane = lax.broadcasted_iota(jnp.int32, (count, 2 * size), 1)
    grad_scores = jnp.zeros((count, count), f32)
    zero = jnp.zeros((), bf16)
    for pair in range(heads // 2):
        cols = slice(2 * pair * size, (2 * pair + 2) * size)
        x_pair = xbc[0, :, cols]
        x_twice = jnp.concatenate([x_pair, x_pair], axis=1)
        gy_hi, gy_lo = split2(gy[0, :, cols])
        gy_wide = jnp.concatenate([gy_hi, gy_lo], axis=1)
        parts = []
        for h in (2 * pair, 2 * pair + 1):
            own = (lane < size) if h % 2 == 0 else (lane >= size)
            part = jnp.exp(jnp.minimum(cum_row[h : h + 1] - cum_col[:, h : h + 1], 0.0)) * dt[:, h : h + 1]
            parts.append(nn((scores * part).astype(bf16), gy_wide))
            both = jnp.concatenate([jnp.where(own, gy_hi, zero), jnp.where(own, gy_lo, zero)], axis=1)
            grad_scores = grad_scores + nt(x_twice, both) * part
        two = [part[:, : 2 * size] + part[:, 2 * size :] for part in parts]
        dx_o[0, :, cols] = jnp.where(lane < size, two[0], two[1])
    hi, lo = split2(jnp.where(mask, grad_scores, 0.0))
    state_hi, state_lo = split2(load_state(meta, packs, pack, keep, recv, heads, size))
    carry = carry_column(meta, column_segments(meta, lens, pack, count, nseq, EDGE), EDGE)
    matrix = spread_matrix(heads, size)
    ey_hi, ey_lo = split2(gy[0] * spread(carry * jnp.exp(cum_col), matrix, heads))
    dbc_o[0, :, :half] = nn(
        jnp.concatenate([hi, lo], axis=1), jnp.concatenate([c_vals, c_vals], axis=0)
    )
    b_rows = jnp.transpose(b_vals)
    dbc_o[0, :, half:] = (
        jnp.transpose(nn(b_rows, hi) + nn(b_rows, lo))
        + nn(ey_hi, state_hi) + nn(ey_hi, state_lo) + nn(ey_lo, state_hi)
    )
    row_sum = collapse(gy[0] * y[0], matrix, heads)
    col_sum = collapse(xbc[0, :, :inner].astype(f32) * dx_o[0], matrix, heads)
    sums_o[0] = row_sum + to_group(col_sum, 1)


def scatter_pieces(head, stage, own_o, far_o, send_o):
    own_o[0] = stage[head]
    send_o[0, 0] = stage[head ^ 1].astype(bf16)
    far_o[0] = stage[head ^ 2]
    send_o[0, 1] = stage[head ^ 3].astype(bf16)


def accumulate(meta, pack, packs, sums, term, keep_o, send_o):
    sums[...] += term.reshape(sums.shape)

    def finish():
        @last_pack(pack, packs)
        def _():
            side = meta[0] & 1
            keep_o[...] = sums[side]
            send_o[...] = sums[1 - side].astype(bf16)

    return finish


def last_pack(pack, packs):
    return lambda work: pl.when(pack == packs - 1)(work)


def cleared(*refs):
    @order.first
    def _():
        for ref in refs:
            ref[...] = jnp.zeros_like(ref)


def out_kernel(dims, meta, lens, *refs):
    packs, count, features, inner, bc, heads, size, width, nseq = dims
    gated, cot, wout, own_o, far_o, send_o, keep_o, give_o, stage, sums = refs
    pack = order.pack
    cleared(sums)
    stage[...] = nt(wout[...], gated[0]).reshape(stage.shape)
    scatter_pieces(meta[1], stage, own_o, far_o, send_o)
    return accumulate(meta, pack, packs, sums, nn(cot[0], gated[0]), keep_o, give_o)


def gain_row(weights, grads):
    part = jnp.sum(weights.astype(f32) * grads, axis=1, keepdims=True)
    return jnp.transpose(jnp.broadcast_to(part, (part.shape[0], LANES)))[0:8]


def z_kernel(dims, meta, lens, *refs):
    normed, ggate, wz, keep_o, give_o, gain_o, sums = refs
    pack = order.pack
    cleared(sums)
    store = accumulate(meta, pack, dims[0], sums, nn(normed[0], ggate[0]), keep_o, give_o)

    def finish():
        store()

        @last_pack(pack, dims[0])
        def _():
            gain_o[...] = gain_row(wz[...], sums[...].reshape(wz.shape))

    return finish


def end_weights(seg, seg_main, cum_col, dt_col, count):
    cum_end = cum_col[count - 1 :]
    end = seg[count + EDGE - 1 :]
    return jnp.where(seg_main == end, jnp.exp(cum_end - cum_col), 0.0) * dt_col


def share_kernel(dims, meta, lens, *refs):
    packs, count, features, inner, bc, heads, size, width, nseq = dims
    (
        xbc, steps, dbc, gkeep, grecv, gy, dx, slope, conv, skip,
        own_o, near_o, grad_o, state_sum_o, edge_o,
        gpad,
    ) = refs
    pack = order.pack
    half, quarter = bc // 2, bc // 4
    g_hi, g_lo = split2(load_state(meta, packs, pack, gkeep, grecv, heads, size))
    seg = column_segments(meta, lens, pack, count, nseq, EDGE)
    dt, cum = steps_of(steps[0], heads)
    matrix = spread_matrix(heads, size)
    wide = spread(end_weights(seg, seg[EDGE:], cum, dt, count), matrix, heads)
    x_f = xbc[0, :, :inner].astype(f32)
    hi, lo = split2(wide * x_f)
    grad_b = dbc[0, :, :half] + nn(hi, g_hi) + nn(lo, g_hi) + nn(hi, g_lo)
    grad_c = dbc[0, :, half:]
    even = jnp.concatenate([grad_b[:, :quarter], grad_c[:, :quarter]], axis=1)
    odd = jnp.concatenate([grad_b[:, quarter:], grad_c[:, quarter:]], axis=1)
    first = (meta[1] & 1) == 0
    own_o[0] = jnp.where(first, even, odd)
    near_o[0] = jnp.where(first, odd, even)
    b_vals = xbc[0, :, inner : inner + half]
    u_wide = wide * nt(
        jnp.concatenate([b_vals, b_vals], axis=1), jnp.concatenate([g_hi, g_lo], axis=1)
    )
    state_sum_o[0] = collapse(x_f * u_wide, matrix, heads)
    grad_x = (dx[0] + u_wide + gy[0] * skip[...]) * slope[0]
    grad_o[0] = grad_x
    gpad[:EDGE, :] = jnp.zeros((EDGE, inner), f32)
    gpad[EDGE:, :] = grad_x[:EDGE]
    edge_o[0] = conv_rows(gpad, conv, seg, EDGE, width).astype(bf16)


def middle_kernel(dims, meta, *refs):
    packs, quarter = dims
    own, near, keep_o, send_o = refs
    half = packs // 2
    first = (meta[1] >> 1) == 0
    for p in range(half):
        a, b = own[p] + near[p], own[p + half] + near[p + half]
        low = jnp.concatenate([a[:, :quarter], b[:, :quarter]], axis=1)
        high = jnp.concatenate([a[:, quarter:], b[:, quarter:]], axis=1)
        keep_o[p] = jnp.where(first, low, high)
        send_o[p] = jnp.where(first, high, low)


def conv_taps(grads, raws, gconv_o, seg, count, width):
    seg_main = seg[EDGE : EDGE + count]
    for k in range(width):
        low = EDGE - (width - 1) + k
        mask = jnp.where(seg[low : low + count] == seg_main, 1.0, 0.0)
        gconv_o[k : k + 1, :] += jnp.sum(
            grads * (raws[low : low + count, :] * mask), axis=0, keepdims=True
        )
    gconv_o[width : width + 1, :] += jnp.sum(grads, axis=0, keepdims=True)


def conv_rows(gpad, conv, seg, rows, width):
    total = jnp.zeros((rows, gpad.shape[1]), f32)
    for lag in range(width):
        mask = jnp.where(seg[lag : lag + rows] == seg[:rows], 1.0, 0.0)
        k = width - 1 - lag
        total = total + conv[k : k + 1, :] * (gpad[lag : lag + rows, :] * mask)
    return total


def step_kernel(dims, meta, lens, *refs):
    packs, count, features, inner, bc, heads, size, width, nseq = dims
    (
        steps, sums, state_sums, keep, recv, gkeep, grecv, small, normed, wdt,
        gdt_o, gdt_rows_o, gsmall_o, gain_o,
        gdt_sums,
    ) = refs
    group, half = pl.program_id(0), packs // 2
    matrix = spread_matrix(heads, size)
    ones = jnp.ones((8, LANES), bf16)
    decay_rate = -jnp.exp(small[1:2, :])
    upper = triangle(count, False)
    rows = lax.broadcasted_iota(jnp.int32, (count, LANES), 0)
    mine = group == (meta[0] & 1)
    bias_sum, rate_sum = jnp.zeros((1, LANES), f32), jnp.zeros((1, LANES), f32)
    term = jnp.zeros((features, LANES), f32)
    for j in range(half):
        pick = lambda a, b: jnp.where(mine, a[j].astype(jnp.int32), b[j].astype(jnp.int32))
        state = decode_state(pick(keep, recv), heads, size)[0]
        gstate = decode_state(pick(gkeep, grecv), heads, size)[0]
        seg = column_segments(meta, lens, group * half + j, count, nseq, EDGE)
        v = steps[j]
        dt, cum = steps_of(v, heads)
        sig = head_lanes(sigmoid(v), heads)
        row_sum, col_sum = from_group(sums[j], 0, heads), from_group(sums[j], 1, heads)
        state_sum = state_sums[j]
        carry = carry_column(meta, seg, EDGE)
        hi, lo = split2(gstate * state)
        by_head = collapse(nt(ones, hi) + nt(ones, lo), matrix, heads)[0:1]
        last = by_head * carry[count - 1 :] * jnp.exp(cum[count - 1 :]) + jnp.sum(
            state_sum, axis=0, keepdims=True
        )
        grad_cum = row_sum - col_sum - state_sum + jnp.where(rows == count - 1, last, 0.0)
        grad_rate = exact_sums(upper, grad_cum, heads)
        ratio = jnp.where(dt > 1e-30, sig / jnp.maximum(dt, 1e-30), 1.0)
        grad_dt = head_lanes(ratio * (col_sum + state_sum) + grad_rate * decay_rate * sig, heads)
        low = grad_dt.astype(bf16)
        gdt_o[j] = low
        bias_sum = bias_sum + jnp.sum(grad_dt, axis=0, keepdims=True)
        rate_sum = rate_sum + jnp.sum(grad_rate * dt * decay_rate, axis=0, keepdims=True)
        term = term + nn(normed[j], low)

    @pl.when(group == 0)
    def _():
        gsmall_o[...] = jnp.zeros_like(gsmall_o)
        gdt_sums[...] = jnp.zeros_like(gdt_sums)

    gsmall_o[0:1, :] += bias_sum
    gsmall_o[1:2, :] += rate_sum
    gdt_sums[...] += term

    @pl.when(group == packs // half - 1)
    def _():
        gdt_rows_o[...] = jnp.transpose(gdt_sums[...])[0:8]
        gain_o[...] = gain_row(wdt[...], gdt_sums[...])


def xback_kernel(dims, meta, lens, *refs):
    packs, count, features, inner, bc, heads, size, width, nseq = dims
    (
        grads, raw, normed, edge, edge_x, conv, wx,
        main_o, keep_o, give_o, gconv_o, gain_o,
        gpad, raws, sums, rows_x,
    ) = refs
    pack = order.pack
    seg = column_segments(meta, lens, pack, count, nseq, EDGE)

    cleared(gconv_o, rows_x, sums)
    raws[...] = raw[0].astype(f32)
    gpad[:count, :] = grads[0]
    gpad[count:, :] = jnp.zeros((EDGE, inner), f32)
    conv_taps(grads[0], raws, gconv_o, seg, count, width)
    seg_pad = jnp.concatenate([seg[EDGE:], jnp.full((8, 1), -1, jnp.int32)], axis=0)
    main = conv_rows(gpad, conv, seg_pad, count, width).astype(bf16)
    main_o[0] = main
    rows_x[pl.ds(pl.multiple_of(pack * EDGE, EDGE), EDGE), :] = edge_x[0]
    sums[...] += nn(normed[0], main).reshape(sums.shape)

    def finish():
        @last_pack(pack, packs)
        def _():
            sums[...] += nn(edge[...], rows_x[...]).reshape(sums.shape)
            side = meta[0] & 1
            keep_o[...] = sums[side]
            give_o[...] = sums[1 - side].astype(bf16)
            gain_o[...] = gain_row(wx[...], sums[...].reshape(wx.shape))

    return finish


def conv_bc_kernel(dims, meta, lens, *refs):
    packs, count, features, inner, bc, heads, size, width, nseq = dims
    (
        keep, recv, slope, raw, normed, edge, wbc, conv, edge_x,
        gconv_x, gdt_rows, gsmall, gate_small, gain_z, gain_x, gain_dt, gain,
        rows_o, edges_o, give_o, small_o,
        gpad, raws, sums, edge_bc, gconv,
    ) = refs
    pack = order.pack
    quarter = bc // 4

    cleared(gconv, edge_bc, sums)
    gpad[:EDGE, :] = jnp.zeros((EDGE, quarter), f32)
    gpad[EDGE + count :, :] = jnp.zeros((EDGE, quarter), f32)
    both = keep[0] + recv[0]
    grad = jnp.where(pack < packs // 2, both[:, :quarter], both[:, quarter:]) * slope[0]
    seg = column_segments(meta, lens, pack, count, nseq, EDGE)
    raws[...] = raw[0].astype(f32)
    gpad[EDGE : EDGE + count, :] = grad
    conv_taps(grad, raws, gconv, seg, count, width)
    seg_pad = jnp.concatenate([seg, jnp.full((8, 1), -1, jnp.int32)], axis=0)
    grad_raw = conv_rows(gpad, conv, seg_pad, count + EDGE, width).astype(bf16)
    rows_o[0] = grad_raw[EDGE:]
    edge_bc[pl.ds(pl.multiple_of(pack * EDGE, EDGE), EDGE), :] = grad_raw[:EDGE]
    edges_o[0, :, :inner] = edge_x[0]
    blank = jnp.zeros((EDGE, LANES - quarter), bf16)
    edges_o[0, :, inner:] = jnp.concatenate([grad_raw[:EDGE], blank], axis=1)
    sums[...] += nn(normed[0], grad_raw[EDGE:])

    def finish():
        @last_pack(pack, packs)
        def _():
            total = sums[...] + nn(edge[...], edge_bc[...])
            rows = jnp.transpose(total)
            taps = width + 1
            give_o[:quarter, :] = rows[:, :inner].astype(bf16)
            give_o[quarter : 2 * quarter, :] = rows[:, inner:].astype(bf16)
            small_o[...] = jnp.zeros_like(small_o)
            for h in range(heads):
                small_o[2 * h : 2 * h + 1, :] = gdt_rows[h : h + 1, :inner]
                small_o[2 * h + 1 : 2 * h + 2, :] = gdt_rows[h : h + 1, inner:]
            row = 2 * heads
            small_o[row : row + taps, :] = gconv_x[:taps, :]
            row += taps
            small_o[row : row + 1, :] = gate_small[0:1, :]
            skips = collapse(gate_small[...], spread_matrix(heads, size), heads)
            small_o[row + 1 : row + 2, :] = jnp.concatenate(
                [gsmall[0:1, :], gsmall[1:2, :], skips[1:2, :]], axis=1
            )
            blank_row = jnp.zeros((1, inner - taps * quarter), f32)
            small_o[row + 2 : row + 3, :] = jnp.concatenate(
                [gconv[k : k + 1, :] for k in range(taps)] + [blank_row], axis=1
            )
            gains = gain_row(wbc[...], total)[0:1] + gain_z[0:1, :] + gain_x[0:1, :] + gain_dt[0:1, :]
            gains = gains / jnp.transpose(jnp.broadcast_to(gain[...], (features, LANES)))[0:1]
            small_o[row + 3 : row + 4, :] = gains[:, :inner]
            small_o[row + 4 : row + 5, :] = gains[:, inner:]
            hi, lo = split2(small_o[...])
            give_o[2 * quarter : 2 * quarter + SMALL, :] = hi
            give_o[2 * quarter + SMALL :, :] = lo

    return finish


def back_kernel(dims, meta, lens, *refs):
    packs, count, features, inner, bc, heads, size, width, nseq = dims
    (
        main, edges, ggate, gdt, gbc, normed, wz, wx, wbc, wdt,
        own_o, far_o, send_o, dots_o,
        stage,
    ) = refs
    head = meta[1]
    part, quarter = features // 4, bc // 4
    late = count - EDGE

    def with_edge(rows, edge):
        low = (rows[late:].astype(f32) + edge.astype(f32)).astype(bf16)
        return jnp.concatenate([rows[:late], low], axis=0)

    grad_x = with_edge(main[0], edges[0, :, :inner])
    grad_bc = with_edge(gbc[0], edges[0, :, inner : inner + quarter])
    whole = nt(wz[...], ggate[0]) + nt(wx[...], grad_x) + nt(wbc[...], grad_bc) + nt(wdt[...], gdt[0])
    dots = jnp.sum(whole * normed[0].astype(f32), axis=0, keepdims=True)
    stage[...] = whole.reshape(stage.shape)
    dots_o[0] = dots
    own_o[0] = stage[head]
    far_o[0] = stage[head ^ 2]
    for k in range(2):
        send_o[0, k, :part, :] = stage[head ^ (1 + 2 * k)].astype(bf16)
        send_o[0, k, part:, :] = extra_rows(dots)


def extra_rows(*values):
    row = lax.broadcasted_iota(jnp.int32, (EDGE, values[0].shape[1]), 0)
    total = jnp.zeros(row.shape, f32)
    for i, value in enumerate(values):
        for k, piece in enumerate(split3(value)):
            total = total + jnp.where(row == 3 * i + k, piece.astype(f32), 0.0)
    return total.astype(bf16)


def read_extra(block, i):
    rows = block.astype(f32)
    return rows[3 * i : 3 * i + 1] + rows[3 * i + 1 : 3 * i + 2] + rows[3 * i + 2 : 3 * i + 3]


def gather_kernel(own, far, near, dots, own_o, far_o, dots_o):
    part = own.shape[1]
    own_o[0] = own[0] + near[0, 0, :part, :].astype(f32)
    far_o[0, :part, :] = (far[0] + near[0, 1, :part, :].astype(f32)).astype(bf16)
    both = dots[0] + read_extra(near[0, 0, part:, :], 0)
    dots_o[0] = both
    far_o[0, part:, :] = extra_rows(both)


def final_kernel(dims, own, far, dots, tokens, inv, gain, out_grad, in_grad_o):
    packs, count, features = dims
    part = own.shape[1]
    grad = own[0] + far[0, :part, :].astype(f32)
    mean = (dots[0] + read_extra(far[0, part:, :], 0)) / features
    unit = tokens[0].astype(f32) * inv[0]
    in_grad_o[0] = out_grad[0].astype(f32) + inv[0] * (gain[...] * grad - unit * mean)


def out_gather_kernel(own, far, near, own_o, far_o):
    own_o[0] = own[0] + near[0, 0].astype(f32)
    far_o[0] = (far[0] + near[0, 1].astype(f32)).astype(bf16)


def out_final_kernel(own, far, tokens, out):
    out[0] = (tokens[0].astype(f32) + (own[0] + far[0].astype(f32))).astype(bf16)


def add_kernel(bit, halve, segs, count, small, meta, *refs):
    keep, got, refs = refs[:count], refs[count : 2 * count], refs[2 * count :]
    end = segs[-1] if count > 1 else sum(segs)
    write = 0
    if small:
        small_in, *refs, small_o = refs
        hi, lo = split2(small_in[...])
        mine = hi.astype(f32) + lo.astype(f32)
        theirs = got[-1][end : end + SMALL, :].astype(f32) + got[-1][end + SMALL :, :].astype(f32)
        total = mine + theirs
        small_o[...] = total
        if bit is not None:
            send_o = refs[-1]
            behind = send_o.shape[0] - 2 * SMALL
            hi, lo = split2(total)
            send_o[behind : behind + SMALL, :] = hi
            send_o[behind + SMALL :, :] = lo
    read = 0
    for i, rows in enumerate(segs):
        if count > 1:
            total = keep[i][...] + got[i][:rows, :].astype(f32)
        else:
            total = keep[0][read : read + rows, :].astype(f32) + got[0][read : read + rows, :].astype(f32)
        read += rows
        if halve:
            half = rows // 2
            first = ((meta[0] >> bit) & 1) == 0
            top, bottom = total[:half], total[half:]
            refs[0][write : write + half, :] = jnp.where(first, top, bottom)
            refs[1][write : write + half, :] = jnp.where(first, bottom, top).astype(bf16)
            write += half
        else:
            refs[0][write : write + rows, :] = total.astype(bf16)
            write += rows


def whole_kernel(quarter, keep, got, small, out, small_o):
    total = keep[: 2 * quarter, :].astype(f32) + got[: 2 * quarter, :].astype(f32)
    out[...] = jnp.concatenate([total[:quarter], total[quarter:]], axis=1)
    hi, lo = split2(small[...])
    end = 2 * quarter
    theirs = got[end : end + SMALL, :].astype(f32) + got[end + SMALL :, :].astype(f32)
    small_o[...] = (hi.astype(f32) + lo.astype(f32)) + theirs


def join_kernel(bit, segs, meta, mine, got, out):
    first = ((meta[0] >> bit) & 1) == 0
    read = 0
    for rows in segs:
        a = mine[read : read + rows, :].astype(f32)
        b = got[read : read + rows, :].astype(f32)
        out[2 * read : 2 * read + rows, :] = jnp.where(first, a, b).astype(bf16)
        out[2 * read + rows : 2 * read + 2 * rows, :] = jnp.where(first, b, a).astype(bf16)
        read += rows


def part_kernel(values, out):
    out[0] = values[...].astype(f32)


def result_kernel(segs, ways, meta, mine, got, *outs):
    first = (meta[0] & 1) == 0
    read = 0
    for rows, way, out in zip(segs, ways, outs):
        a = mine[read : read + rows, :].astype(f32)
        b = got[read : read + rows, :].astype(f32)
        top, bottom = jnp.where(first, a, b), jnp.where(first, b, a)
        if way == "rows":
            out[:rows, :] = top
            out[rows:, :] = bottom
        elif way == "flip":
            out[:, :rows] = jnp.transpose(top)
            out[:, rows:] = jnp.transpose(bottom)
        else:
            out[...] = jnp.concatenate([top, bottom], axis=1)
        read += rows


def plus_kernel(a, b, out):
    out[...] = a[...] + b[...]


def unpack_kernel(dims, meta, *refs):
    heads, features, bc_part, width = dims
    smalls, gains, dt_o, taps_x_o, taps_bc_o, bias_x_o, bias_bc_o, dt_bias_o, a_log_o, skip_o, gate_o, gain_o = refs
    for h in range(heads):
        dt_o[h : h + 1, :] = jnp.concatenate(
            [smalls[2 * h : 2 * h + 1, :], smalls[2 * h + 1 : 2 * h + 2, :]], axis=1
        )
    row = 2 * heads
    taps_x_o[...] = smalls[row : row + width, :]
    bias_x_o[...] = smalls[row + width, :]
    row += width + 1
    gate_o[...] = smalls[row, :]
    for k, out in enumerate((dt_bias_o, a_log_o, skip_o)):
        out[...] = smalls[row + 1, k * LANES : k * LANES + heads]
    taps = smalls[row + 2 : row + 3, :]
    for k in range(width):
        taps_bc_o[k : k + 1, :] = taps[:, k * bc_part : (k + 1) * bc_part]
    bias_bc_o[...] = taps[0, width * bc_part : (width + 1) * bc_part]
    both = jnp.concatenate([gains[row + 3 : row + 4, :], gains[row + 4 : row + 5, :]], axis=1)
    part = features // 4
    parts = [both[:, h * part : (h + 1) * part] for h in range(4)]
    low = jnp.where((meta[1] & 1) == 0, parts[0], parts[1])
    high = jnp.where((meta[1] & 1) == 0, parts[2], parts[3])
    gain_o[...] = jnp.where((meta[1] >> 1) == 0, low, high)[0]


class Spec:
    def __init__(self, shape, index, each=True):
        self.shape, self.index, self.each = tuple(shape), index, each

    def block(self, group):
        zeros = (0,) * len(self.shape)
        if not self.each:
            return pl.BlockSpec(self.shape, lambda p, *_: zeros)
        size = group or 1
        return pl.BlockSpec(
            (size,) + self.shape, lambda p, *pre: (self.index(p, pre, bool(group)),) + zeros
        )


def whole_spec(shape):
    return Spec(shape, None, False)


def pack_spec(shape):
    return Spec(shape, lambda p, pre, grouped: p)


def half_spec(shape, half):
    return Spec(shape, lambda p, pre, grouped: 0 if grouped else p % half)


def sided_spec(shape, half, keep):
    def index(p, pre, grouped):
        side = pre[0][0] & 1 if keep else 1 - (pre[0][0] & 1)
        return side if grouped else p + half * side

    return Spec(shape, index)


def side_spec(shape, half, keep):
    def index(p, pre, grouped):
        if grouped:
            return 0
        side = pre[0][0] & 1 if keep else 1 - (pre[0][0] & 1)
        group = p // half
        return jnp.where(group == side, p % half, jnp.where(group < side, 0, half - 1))

    return Spec(shape, index)


class Each:
    def __init__(self, shape, dtype):
        self.shape, self.dtype = tuple(shape), dtype

    def scratch(self, group):
        return pltpu.VMEM(((group,) if group else ()) + self.shape, self.dtype)


class Order:
    def __init__(self):
        self.clear()

    def clear(self):
        self.last, self.near, self.held = (), [], []
        self.pack, self.lane, self.lanes = None, 0, 1

    def first(self, work):
        if self.lane == 0:
            pl.when(self.pack == 0)(work)

    def hold(self, *arrays):
        self.held += arrays

    def drop(self, *arrays):
        self.held = [x for x in self.held if not any(x is y for y in arrays)]

    def placed(self, x):
        return pltpu.with_memory_space_constraint(x, pltpu.VMEM) if self.holds(x) else x

    def holds(self, x):
        return any(x is y for y in self.near)


order = Order()


def call(
    kernel, grid, in_specs, out_specs, out_shape, scratch, prefetch, *args, limit=28, wait=(), us=1,
    out=False, onto=(), group=0,
):
    first = len(prefetch) + len(args)
    args = args + tuple(onto)
    in_specs = list(in_specs) + [pl.BlockSpec(memory_space=pl.ANY)] * len(onto)
    given = len(prefetch) + len(args)
    held = order.last + tuple(wait)
    held += tuple(x for x in order.held if not any(x is y for y in args + held))
    late = len(held)
    single = not isinstance(out_shape, (list, tuple))
    out_specs, out_shape = ([out_specs], [out_shape]) if single else (list(out_specs), list(out_shape))
    token = jax.ShapeDtypeStruct((8, LANES), f32)
    count = len(out_shape)
    results = count if out is True else int(out)

    specs = list(in_specs[: len(in_specs) - len(onto)]) + out_specs
    blocks = lambda items: [x.block(group) if isinstance(x, Spec) else x for x in items]

    def body(*refs):
        ins, rest = refs[:first], refs[given + late :]
        fixed, blocked = ins[: len(prefetch)], (*ins[len(prefetch) :], *rest[:count])
        own = rest[count + 1 :]
        finish = []
        for lane in range(group or 1):
            order.pack, order.lane, order.lanes = pl.program_id(0), lane, group or 1
            views, scratches = blocked, own
            if group:
                order.pack = order.pack * group + lane
                views = [
                    ref.at[pl.ds(lane, 1)] if isinstance(spec, Spec) and spec.each else ref
                    for ref, spec in zip(blocked, specs)
                ]
                scratches = [
                    ref.at[lane] if isinstance(item, Each) else ref for ref, item in zip(own, scratch)
                ]
            finish.append(kernel(*fixed, *views, *scratches))
        for work in finish:
            if work is not None:
                work()

    *outs, order_out = pl.pallas_call(
        body,
        grid_spec=pltpu.PrefetchScalarGridSpec(
            num_scalar_prefetch=len(prefetch),
            grid=grid,
            in_specs=blocks(in_specs) + [pl.BlockSpec(memory_space=pl.ANY)] * late,
            out_specs=blocks(out_specs + [whole_spec(token.shape)]),
            scratch_shapes=[x.scratch(group) if isinstance(x, Each) else x for x in scratch],
        ),
        input_output_aliases={first + i: i for i in range(len(onto))},
        out_shape=[
            x if i < results else pltpu.VMEM(x.shape, x.dtype) for i, x in enumerate(out_shape + [token])
        ],
        compiler_params=pltpu.CompilerParams(vmem_limit_bytes=limit * MIB),
        cost_estimate=pl.CostEstimate(
            flops=int(us * 10e9), bytes_accessed=int(us * 3e6), transcendentals=0
        ),
    )(*[pltpu.with_memory_space_constraint(x, pltpu.VMEM) for x in prefetch], *[order.placed(x) for x in args], *[order.placed(x) for x in held])
    order.last = (order_out,)
    order.near.append(order_out)
    order.near += outs[results:]
    return outs[0] if single else outs


def shape(*dims_and_type):
    return jax.ShapeDtypeStruct(dims_and_type[:-1], dims_and_type[-1])


def scan_states(keep, send, meta, packs, heads, size, rev, beside, waits=lambda: ()):
    dims = (packs, heads, size)
    rows = heads * size
    half = packs // 2
    pay = shape(half, rows + EDGE, LANES, jnp.int16)
    spec = whole_spec(pay.shape)
    bits = (lax.axis_size("seq") - 1).bit_length()
    beside = list(beside)

    def work(newest):
        if beside:
            beside.pop(0)(newest)

    other = swap(send, "seq", 1)
    work(send)
    keep = keep() if callable(keep) else keep
    total = call(
        functools.partial(pair_kernel, dims, rev), (1,), [spec, spec], spec, pay, [], (meta,),
        keep, other,
    )
    before = None
    for bit in range(1, bits):
        got = swap(total, "seq", 1 << bit)
        extra = () if before is None else (before,)
        work(total)
        if bit < bits - 1:
            total, before = call(
                functools.partial(cube_kernel, dims, rev, bit, before is None), (1,),
                [spec] * (2 + len(extra)), [spec, spec], [pay, pay], [], (meta,),
                total, got, *extra,
            )
        else:
            own, back = call(
                functools.partial(last_kernel, dims, rev, bit, before is None), (1,),
                [spec] * (3 + len(extra)), [spec, spec], [pay, pay], [],
                (meta,), keep, other, got, *extra, wait=waits(),
            )
    recv = swap(back, "seq", 1)
    while beside:
        work(back)
    return own, recv


class SeqSum:
    def __init__(self):
        self.keep, self.got, self.segs = [], [], []
        self.small = self.bit = None
        self.bits = list(range(1, (lax.axis_size("seq") - 1).bit_length()))
        self.halved = []

    def put(self, keep, give, segs=None, small=None):
        self.keep.append(keep)
        self.got.append(swap(give, "seq", 1))
        self.segs += segs or [keep.shape[0]]
        self.small = small

    def add(self, meta, us=1, wait=()):
        bit = self.bits.pop(0) if self.bits else None
        halve = bit is not None and all(rows % (2 * EDGE) == 0 for rows in self.segs)
        cols = self.keep[0].shape[1]
        segs = [rows // 2 for rows in self.segs] if halve else self.segs
        rows = sum(segs)
        small = self.small is not None
        behind = 2 * SMALL if small and bit is not None else 0
        low = shape(rows + behind, cols, bf16)
        out = [shape(rows, cols, f32), low] if halve else [low]
        ins = [*self.keep, *self.got]
        if small:
            ins.append(self.small)
            out.append(shape(*self.small.shape, f32))
        outs = call(
            functools.partial(add_kernel, bit, halve, self.segs, len(self.keep), small), (1,),
            [whole_spec(x.shape) for x in ins], [whole_spec(x.shape) for x in out], out, [],
            (meta,), *ins, us=us, wait=wait,
        )
        if small:
            self.small = outs[-1]
        self.segs, self.keep = segs, [outs[0]]
        if bit is None:
            return True
        self.got = [swap(outs[1] if halve else outs[0], "seq", 1 << bit)]
        if halve:
            self.halved.append(bit)
        return False

    def send_back(self):
        self.bit = self.halved.pop() if self.halved else 0
        self.got = [swap(self.keep[0], "seq", 1 << self.bit)]

    def join(self, meta, us=1):
        rows, cols = self.keep[0].shape
        both = shape(2 * rows, cols, bf16)
        spec = whole_spec((rows, cols))
        self.keep = [call(
            functools.partial(join_kernel, self.bit, self.segs), (1,), [spec, spec],
            whole_spec(both.shape), both, [], (meta,), self.keep[0], self.got[0], us=us,
        )]
        self.segs = [2 * rows for rows in self.segs]

    def half_result(self, meta, mine, onto=()):
        rows, cols = self.keep[0].shape

        def index(p, pre, grouped):
            side = pre[0][0] & 1
            return side if mine else 1 - side

        return call(
            lambda meta, values, out: part_kernel(values, out), (1,), [whole_spec((rows, cols))],
            Spec((rows, cols), index), shape(2, rows, cols, f32), [], (meta,),
            self.keep[0] if mine else self.got[0], out=True, us=0.01, onto=onto,
        )

    def result(self, meta, ways, us=0.01):
        cols = self.keep[0].shape[1]
        shapes = {"rows": lambda r: (2 * r, cols), "flip": lambda r: (cols, 2 * r), "cols": lambda r: (r, 2 * cols)}
        out = [shape(*shapes[way](rows), f32) for way, rows in zip(ways, self.segs)]
        spec = whole_spec(self.keep[0].shape)
        return call(
            functools.partial(result_kernel, self.segs, ways), (1,), [spec, spec],
            [whole_spec(x.shape) for x in out], out, [], (meta,), self.keep[0], self.got[0],
            out=True, us=us,
        )


def advance(total, meta, us=1, wait=()):
    if total.bit is None:
        if total.add(meta, us, wait):
            total.send_back()
    elif total.bit:
        total.join(meta, us)
        total.send_back()


def shards(
    tokens_in, out_grad, lengths, norm_gain, proj_z, proj_x, proj_bc, proj_dt, conv_x, conv_bc,
    bias_x, bias_bc, dt_bias, a_log, d_skip, gate_gain, proj_out,
):
    packs, count, part = tokens_in.shape
    features, inner = proj_x.shape
    heads = proj_dt.shape[1]
    size = inner // heads
    width = conv_x.shape[0]
    nseq = lengths.shape[1]
    bc_part = proj_bc.shape[1]
    bc = bc_part * lax.axis_size("head")
    half = packs // 2
    chans = inner + bc
    ext = count + EDGE
    rows = heads * size
    total_inner = inner * lax.axis_size("head")
    dims = (packs, count, features, inner, bc, heads, size, width, nseq)
    seq_place, head_place = lax.axis_index("seq"), lax.axis_index("head")
    meta = jnp.stack([seq_place, head_place]).astype(jnp.int32)
    pre = (meta, lengths)
    grid = (packs,)

    order.clear()
    tokens = jnp.swapaxes(tokens_in, 1, 2)
    cotangent = jnp.swapaxes(out_grad, 1, 2)
    far = swap(tokens, "head", 2)
    near = swap(tokens, "head", 1)
    tail = call(
        tail_kernel, (1,),
        [pl.BlockSpec((packs, part, LANES), lambda p, _: (0, 0, count // LANES - 1))],
        whole_spec((part, LANES)), shape(part, LANES, bf16), [], (meta,),
        pltpu.with_memory_space_constraint(tokens, pltpu.HBM), us=0.05,
    )
    tail = shift(tail, "seq", 1)
    ins = [
        proj_bc.T, conv_bc, bias_bc, norm_gain, proj_dt.T, conv_x, bias_x, dt_bias, a_log, d_skip,
        gate_gain, proj_out,
    ]
    outs = [
        shape(features, inner, bf16),
        shape(bc_part, features + LANES, bf16), shape(features, bc_part, bf16),
        shape(features, LANES, bf16), shape(LANES, features, bf16), shape(8, inner, f32),
        shape(8, bc_part, f32), shape(8, LANES, f32), shape(1, inner, f32), shape(1, inner, f32),
        shape(part, 1, f32),
    ]
    (
        w_out, shared, w_bc, w_dt, w_dt_rows, conv_own, conv_bc_own, small, skip, gain_gate, norm_gain_own,
    ) = call(
        functools.partial(prepare_kernel, dims), (1,), [whole_spec(x.shape) for x in ins],
        [whole_spec(x.shape) for x in outs], outs, [], (), *ins, wait=(tail,),
        us=0.05,
    )
    edge_far, shared_far = swap(tail, "head", 2), swap(shared, "head", 2)
    far, edge_far, shared_far = lax.optimization_barrier((far, edge_far, shared_far))
    edge_pieces = tail, swap(tail, "head", 1), edge_far, swap(edge_far, "head", 1)
    weight_pieces = shared, swap(shared, "head", 1), shared_far, swap(shared_far, "head", 1)
    diagonal = swap(far, "head", 1)
    token_pieces = tokens, near, far, diagonal

    lane_spec = pack_spec((count, LANES))
    chan_spec = pack_spec((count, inner))
    xbc_spec = pack_spec((count, chans))
    model_spec = pack_spec((features, count))
    piece_spec = pack_spec((part, count))
    edge_spec = whole_spec((part, LANES))
    pay_shape = (rows + EDGE, LANES)
    pay_specs = [side_spec(pay_shape, half, k) for k in (True, False)]
    pay = shape(half, *pay_shape, jnp.int16)
    state_spec = half_spec(pay_shape, half)
    vec = whole_spec((1, inner))
    square = whole_spec((features, inner))

    w_bc_rows, conv_all, gain_all, edge, edge_raws = call(
        functools.partial(border_kernel, dims),
        (1,),
        [edge_spec] * 4 + [whole_spec((bc_part, features + LANES))] * 4
        + [square, whole_spec((8, inner))],
        [
            whole_spec((bc, features)), whole_spec((8, chans)), whole_spec((features, 1)),
            whole_spec((features, LANES)), whole_spec((LANES, chans)),
        ],
        [
            shape(bc, features, bf16), shape(8, chans, f32), shape(features, 1, f32),
            shape(features, LANES, bf16), shape(LANES, chans, f32),
        ],
        [pltpu.VMEM((4, part, LANES), bf16), pltpu.VMEM((4, bc_part, features + LANES), bf16)],
        (meta,),
        *edge_pieces, *weight_pieces, proj_x, conv_own,
    )

    def front(keep, onto):
        spec = lambda shape_of: sided_spec(shape_of, half, keep)
        return call(
            functools.partial(front_kernel, dims, keep),
            (1,),
            [spec((part, count))] * 4
            + [
                square, whole_spec((bc, features)), whole_spec((LANES, features)),
                whole_spec((8, chans)), whole_spec((8, LANES)), whole_spec((features, 1)),
                whole_spec((LANES, chans)),
            ],
            [
                spec((features, count)), spec((1, count)), spec((ext, inner)), spec((ext, bc_part)),
                spec((count, chans)), spec((count, LANES)), pack_spec(pay_shape),
            ],
            [
                shape(packs, features, count, bf16), shape(packs, 1, count, f32),
                shape(packs, ext, inner, bf16), shape(packs, ext, bc_part, bf16),
                shape(packs, count, chans, bf16), shape(packs, count, LANES, f32), pay,
            ],
            [Each((4, part, count), bf16), Each((ext, chans), f32)],
            pre,
            *token_pieces, proj_x, w_bc_rows, w_dt_rows, conv_all, small, gain_all, edge_raws,
            us=6, group=half, onto=onto,
        )

    *early, send = front(False, ())
    kept = {}

    def keep_work(_):
        *kept["front"], kept["keep"] = front(True, early)
        order.hold(*(kept["front"][i] for i in (0, 4, 5)))

    def inner_work(_):
        *_, xbc, steps = kept["front"]
        kept["inner"] = call(
            functools.partial(inner_kernel, dims),
            grid,
            [xbc_spec, lane_spec],
            chan_spec,
            shape(packs, count, inner, f32),
            [],
            pre,
            xbc, steps,
            us=6,
        )
        order.hold(kept["inner"])

    def cot_work(newest):
        own, far = kept["cots"]
        near = swap(own, "head", 1)
        cots = own, near, far, swap(lax.optimization_barrier((far, newest))[0], "head", 1)
        kept["cot"], kept["gg"] = call(
            functools.partial(cot_kernel, dims),
            (packs // half,),
            [piece_spec] * 4 + [whole_spec((inner, features))],
            [model_spec, chan_spec],
            [shape(packs, features, count, bf16), shape(packs, count, inner, f32)],
            [Each((4, part, count), bf16)],
            pre,
            *cots, proj_out,
            us=5.5, group=half,
        )

    def gate_slope_work(_):
        normed, _, raw_x, raw_bc, *_ = kept["front"]
        own = lax.optimization_barrier((cotangent, normed))[0]
        kept["cots"] = own, swap(own, "head", 2)
        kept["slope"] = call(
            functools.partial(gate_slope_kernel, dims),
            grid,
            [model_spec, square, pack_spec((ext, inner)), pack_spec((ext, bc_part)),
             whole_spec((8, inner)), whole_spec((8, bc_part))],
            [chan_spec, chan_spec, pack_spec((count, bc_part))],
            [shape(packs, count, inner, bf16), shape(packs, count, inner, f32),
             shape(packs, count, bc_part, f32)],
            [Each((ext, inner), f32), Each((ext, bc_part), f32)],
            pre,
            normed, proj_z, raw_x, raw_bc, conv_own, conv_bc_own,
            us=7,
        )

    state_keep, state_recv = scan_states(
        lambda: kept["keep"], send, meta, packs, heads, size, 0,
        (keep_work, gate_slope_work, inner_work, cot_work),
    )
    normed, inv, raw_x, raw_bc, xbc, steps = kept["front"]
    inner_out, cot, gg = kept["inner"], kept["cot"], kept["gg"]
    gate, slope_x, slope_bc = kept["slope"]
    order.drop(inner_out)

    y, stats = call(
        functools.partial(gate_kernel, dims),
        (packs // half,),
        [
            xbc_spec, lane_spec, chan_spec, state_spec, state_spec, chan_spec, chan_spec, vec, vec,
        ],
        [chan_spec, pack_spec((2, count))],
        [shape(packs, count, inner, f32), shape(packs, 2, count, f32)],
        [],
        pre,
        xbc, steps, inner_out, state_keep, state_recv, gate, gg, gain_gate, skip,
        us=6.6, group=half,
    )
    stats = [stats] + [swap(stats, "head", bits) for bits in (1, 2, 3)]

    gy, gated, ggate, gkeep, gsend, gate_small = call(
        functools.partial(grad_kernel, dims, total_inner),
        (packs // half,),
        [
            *[pack_spec((2, count))] * 4, xbc_spec, lane_spec, chan_spec, chan_spec, chan_spec, vec,
            vec,
        ],
        [chan_spec] * 3 + pay_specs + [whole_spec((8, inner))],
        [shape(packs, count, inner, f32)] + [shape(packs, count, inner, bf16)] * 2
        + [pay, pay, shape(8, inner, f32)],
        [],
        pre,
        *stats, xbc, steps, y, gate, gg, gain_gate, skip,
        us=8.3, group=half,
    )

    piece_shape = shape(packs, part, count, f32)
    send_spec = pack_spec((2, part, count))
    rows_half = features // 2
    half_specs = [whole_spec((rows_half, inner))] * 2
    half_shapes = [shape(rows_half, inner, f32), shape(rows_half, inner, bf16)]
    half_sums = pltpu.VMEM((2, rows_half, inner), f32)
    row8, row8_shape = whole_spec((8, features)), shape(8, features, f32)

    early_sum, late_sum = SeqSum(), SeqSum()

    def out_work(_):
        *kept["out"], keep, give = call(
            functools.partial(out_kernel, dims),
            (packs // half,),
            [chan_spec, model_spec, square],
            [piece_spec, piece_spec, send_spec] + half_specs,
            [piece_shape, piece_shape, shape(packs, 2, part, count, bf16)] + half_shapes,
            [Each((4, part, count), f32), half_sums],
            pre,
            gated, cot, w_out,
            us=6.8, group=half,
        )
        early_sum.put(keep, give)

    def z_work(_):
        keep, give, kept["gain"] = call(
            functools.partial(z_kernel, dims),
            (packs // half,),
            [model_spec, chan_spec, square],
            half_specs + [row8],
            half_shapes + [row8_shape],
            [half_sums],
            pre,
            normed, ggate, proj_z,
            us=5.3, group=half,
        )
        early_sum.put(keep, give)
        own, far, send = kept["out"]
        own, far = call(
            out_gather_kernel, grid, [piece_spec, piece_spec, send_spec], [piece_spec, piece_spec],
            [piece_shape, shape(packs, part, count, bf16)], [], (), own, far, swap(send, "head", 1),
        )
        kept["out"] = own, swap(far, "head", 2)

    def diag_work(_):
        kept["diag"] = call(
            functools.partial(diag_kernel, dims),
            (packs // half,),
            [xbc_spec, lane_spec, chan_spec, chan_spec, state_spec, state_spec],
            [chan_spec, pack_spec((count, bc)), lane_spec],
            [
                shape(packs, count, inner, f32), shape(packs, count, bc, f32),
                shape(packs, count, LANES, f32),
            ],
            [],
            pre,
            xbc, steps, gy, y, state_keep, state_recv,
            us=12, group=half,
        )

    def early_work(_):
        early_sum.add(meta)

    gstate_keep, gstate_recv = scan_states(
        gkeep, gsend, meta, packs, heads, size, 1, (out_work, z_work, diag_work, early_work),
        lambda: early_sum.got,
    )
    out_own, out_far = kept["out"]
    dx, dbc, sums = kept["diag"]

    edge_tile = (EDGE, inner)

    def pair_spec(shape_of):
        return pl.BlockSpec((half,) + shape_of, lambda p, *_: (p,) + (0,) * len(shape_of))

    pair_lane = pair_spec((count, LANES))
    share_own, share_near, grad_x, state_sums, edge_x = call(
        functools.partial(share_kernel, dims),
        (packs // half,),
        [xbc_spec, lane_spec, pack_spec((count, bc)), state_spec, state_spec, chan_spec, chan_spec,
         chan_spec, whole_spec((8, inner)), vec],
        [lane_spec, lane_spec, chan_spec, lane_spec, pack_spec(edge_tile)],
        [shape(packs, count, LANES, f32)] * 2
        + [shape(packs, count, inner, f32), shape(packs, count, LANES, f32),
           shape(packs, *edge_tile, bf16)],
        [Each((2 * EDGE, inner), f32)],
        pre,
        xbc, steps, dbc, gstate_keep, gstate_recv, gy, dx, slope_x, conv_own, skip,
        us=6.4, group=half,
    )
    share_near = swap(share_near, "head", 1)
    advance(early_sum, meta)
    two = shape(half, count, LANES, f32)
    bc_keep, bc_send = call(
        functools.partial(middle_kernel, (packs, bc_part)),
        (1,),
        [whole_spec((packs, count, LANES))] * 2,
        [whole_spec(two.shape)] * 2,
        [two, two],
        [],
        (meta,),
        share_own, share_near,
    )
    bc_recv = swap(bc_send, "head", 2)

    main_x, keep, give, grad_conv, gain_x = call(
        functools.partial(xback_kernel, dims),
        (packs // half,),
        [
            chan_spec, pack_spec((ext, inner)), model_spec, whole_spec((features, LANES)),
            pack_spec(edge_tile), whole_spec((8, inner)), square,
        ],
        [chan_spec, *half_specs, whole_spec((8, inner)), row8],
        [shape(packs, count, inner, bf16), *half_shapes, shape(8, inner, f32), row8_shape],
        [
            Each((count + EDGE, inner), f32), Each((ext, inner), f32), half_sums,
            pltpu.VMEM((LANES, inner), bf16),
        ],
        pre,
        grad_x, raw_x, normed, edge, edge_x, conv_own, proj_x,
        us=7, group=half, wait=(out_far,),
    )
    late_sum.put(keep, give)
    advance(early_sum, meta)

    gdt, gdt_rows, grad_small, gain_dt = call(
        functools.partial(step_kernel, dims),
        (packs // half,),
        [
            pair_lane, pair_lane, pair_lane, *[whole_spec((half,) + pay_shape)] * 4,
            whole_spec((8, LANES)), pair_spec((features, count)), whole_spec((features, LANES)),
        ],
        [pair_lane, row8, whole_spec((8, LANES)), row8],
        [shape(packs, count, LANES, bf16), row8_shape, shape(8, LANES, f32), row8_shape],
        [pltpu.VMEM((features, LANES), f32)],
        pre,
        steps, sums, state_sums, state_keep, state_recv, gstate_keep, gstate_recv, small, normed,
        w_dt,
        us=6,
    )
    advance(early_sum, meta)
    advance(late_sum, meta)
    give_rows = 2 * bc_part + 2 * SMALL
    gbc, edges, bc_sum, smalls = call(
        functools.partial(conv_bc_kernel, dims),
        grid,
        [
            half_spec((count, LANES), half), half_spec((count, LANES), half),
            pack_spec((count, bc_part)), pack_spec((ext, bc_part)), model_spec,
            whole_spec((features, LANES)), whole_spec((features, bc_part)),
            whole_spec((8, bc_part)), pack_spec(edge_tile), whole_spec((8, inner)), row8,
            whole_spec((8, LANES)), whole_spec((8, inner)), row8, row8, row8,
            whole_spec((features, 1)),
        ],
        [
            pack_spec((count, bc_part)), pack_spec((EDGE, inner + LANES)),
            whole_spec((give_rows, inner)), whole_spec((SMALL, inner)),
        ],
        [
            shape(packs, count, bc_part, bf16), shape(packs, EDGE, inner + LANES, bf16),
            shape(give_rows, inner, bf16), shape(SMALL, inner, f32),
        ],
        [
            Each((ext + EDGE, bc_part), f32), Each((ext, bc_part), f32),
            pltpu.VMEM((features, bc_part), f32), pltpu.VMEM((LANES, bc_part), bf16),
            pltpu.VMEM((8, bc_part), f32),
        ],
        pre,
        bc_keep, bc_recv, slope_bc, raw_bc, normed, edge, w_bc, conv_bc_own, edge_x, grad_conv,
        gdt_rows, grad_small, gate_small, kept["gain"], gain_x, gain_dt, gain_all,
        us=5,
    )
    edges = shift(edges, "seq", -1)
    bc_bits = [1 << k for k in range((lax.axis_size("seq") - 1).bit_length())]
    bc_got = swap(bc_sum, "seq", 1)
    advance(late_sum, meta)

    def bc_step(bit):
        nonlocal bc_sum, smalls, bc_got
        spec, small_spec = whole_spec(bc_sum.shape), whole_spec(smalls.shape)
        bc_sum, smalls = call(
            functools.partial(add_kernel, 1, False, [2 * bc_part], 1, True), (1,),
            [spec, spec, small_spec], [spec, small_spec],
            [shape(*bc_sum.shape, bf16), shape(*smalls.shape, f32)], [], (meta,),
            bc_sum, bc_got, smalls, us=0.01,
        )
        bc_got = swap(bc_sum, "seq", bit)

    bc_step(bc_bits[1])
    advance(early_sum, meta)

    tall = part + EDGE
    tall_send = pack_spec((2, tall, count))
    tall_spec = pack_spec((tall, count))
    row_spec, row_shape = pack_spec((1, count)), shape(packs, 1, count, f32)
    gn_own, gn_far, gn_send, dots = call(
        functools.partial(back_kernel, dims),
        (packs // half,),
        [
            chan_spec, pack_spec((EDGE, inner + LANES)), chan_spec, lane_spec,
            pack_spec((count, bc_part)), model_spec, square, square,
            whole_spec((features, bc_part)), whole_spec((features, LANES)),
        ],
        [piece_spec, piece_spec, tall_send, row_spec],
        [piece_shape, piece_shape, shape(packs, 2, tall, count, bf16), row_shape],
        [Each((4, part, count), f32)],
        pre,
        main_x, edges, ggate, gdt, gbc, normed, proj_z, proj_x, w_bc, w_dt,
        us=6, group=half,
    )
    near = swap(gn_send, "head", 1)
    order.drop(xbc, steps, normed)
    advance(late_sum, meta, 0.01, wait=(bc_got,))
    block_out = call(
        out_final_kernel, (packs // half,), [piece_spec] * 3, piece_spec, shape(packs, part, count, bf16), [],
        (), out_own, out_far, tokens, out=True, us=2, group=half,
    )
    block_out = jnp.swapaxes(block_out, 1, 2)

    gn_own, gn_far, dots = call(
        gather_kernel,
        grid,
        [piece_spec, piece_spec, tall_send, row_spec],
        [piece_spec, tall_spec, row_spec],
        [piece_shape, shape(packs, tall, count, bf16), row_shape],
        [],
        (),
        gn_own, gn_far, near, dots,
        us=0.01,
    )
    gn_far = swap(gn_far, "head", 2)
    order.hold(gn_own)
    while early_sum.bit != 0:
        advance(early_sum, meta)
    for bit in bc_bits[2:]:
        bc_step(bit)
    small_spec, give_spec = whole_spec(smalls.shape), whole_spec(bc_sum.shape)

    def head_step(x, bit):
        return call(
            plus_kernel, (1,), [small_spec, small_spec], small_spec, shape(*x.shape, f32), [], (),
            x, swap(x, "head", bit), us=0.01,
        )

    advance(late_sum, meta, 0.01)
    grads_out, grads_z = early_sum.result(meta, ("flip", "rows"), 0.4)
    while late_sum.bit != 0:
        advance(late_sum, meta, 0.01)
    grad_bc, smalls = call(
        functools.partial(whole_kernel, bc_part), (1,), [give_spec, give_spec, small_spec],
        [whole_spec((bc_part, features)), small_spec],
        [shape(bc_part, features, f32), shape(*smalls.shape, f32)], [], (), bc_sum, bc_got, smalls,
        us=0.01, out=1,
    )
    gains = head_step(smalls, 1)
    in_grad = call(
        functools.partial(final_kernel, (packs, count, features)),
        (packs // half,),
        [piece_spec, tall_spec, row_spec, piece_spec, row_spec, whole_spec((part, 1)), piece_spec],
        piece_spec,
        piece_shape,
        [],
        (),
        gn_own, gn_far, dots, tokens, inv, norm_gain_own, cotangent,
        us=2, out=True, group=half,
    )
    in_grad = jnp.swapaxes(in_grad, 1, 2)
    order.drop(gn_own)
    gains = head_step(gains, 2)
    own_half = late_sum.half_result(meta, True)
    vectors = [(inner,), (bc_part,), (heads,), (heads,), (heads,), (inner,), (part,)]
    tables = [(heads, features), (width, inner), (width, bc_part)]
    outs = call(
        functools.partial(unpack_kernel, (heads, features, bc_part, width)), (1,),
        [small_spec, small_spec], [whole_spec(x) for x in tables + vectors],
        [shape(*x, f32) for x in tables + vectors], [], (meta,), smalls, gains, out=True, us=0.01,
    )
    grad_dt, grad_conv, grad_conv_bc = outs[:3]
    bias_x_grad, bias_bc_grad, dt_bias_grad, a_log_grad, skip_grad, gate_grad, grad_gain = outs[3:]
    grads_x = late_sum.half_result(meta, False, (own_half,)).reshape(features, inner)
    return (
        block_out,
        in_grad,
        grad_gain,
        grads_z,
        grads_x,
        grad_bc.T,
        grad_dt.T,
        grad_conv,
        grad_conv_bc,
        bias_x_grad,
        bias_bc_grad,
        dt_bias_grad,
        a_log_grad,
        skip_grad,
        gate_grad,
        grads_out,
    )


def solution(mesh):
    token, column, vector = P(None, "seq", "head"), P(None, "head"), P("head")
    row = P("head", None)
    return jax.shard_map(
        shards,
        mesh=mesh,
        in_specs=(
            token, token, P(), vector, column, column, column, column, column, column, vector,
            vector, vector, vector, vector, vector, row,
        ),
        out_specs=(
            token, token, vector, column, column, column, column, column, column, vector, vector,
            vector, vector, vector, vector, row,
        ),
        check_vma=False,
    )
```
